32 devices in a mesh: row: 8 (over y, x, core), col: 4 (over z).
Axes of the slice: x: 2, y: 2, z: 4, core: 2. Of those that a mesh axis runs over, the one named last changes fastest.
Arguments:
- block_in: bfloat16 [8192, 1024], P(('row', 'col')), may hold values from -6 to 6
- attn_gain: bfloat16 [1024], P('row'), may hold values from 0.5 to 1.5
- moe_gain: bfloat16 [1024], P('row'), may hold values from 0.5 to 1.5
- w_query: bfloat16 [1024, 1024], P('row', 'col'), may hold values from -0.1875 to 0.1875
- w_key: bfloat16 [1024, 512], P('row', 'col'), may hold values from -0.1875 to 0.1875
- w_value: bfloat16 [1024, 512], P('row', 'col'), may hold values from -0.1875 to 0.1875
- w_out: bfloat16 [1024, 1024], P('row', 'col'), may hold values from -1 to 1
- w_router: bfloat16 [1024, 32], P('row', 'col'), may hold values from -0.09375 to 0.09375
- w_gate: bfloat16 [32, 1024, 512], P('row', None, 'col'), may hold values from -0.1875 to 0.1875
- w_up: bfloat16 [32, 1024, 512], P('row', None, 'col'), may hold values from -0.1875 to 0.1875
- w_down: bfloat16 [32, 1024, 512], P('row', None, 'col'), may hold values from -1 to 1
- expert_ids: int32 [8192, 8], P(('row', 'col')), may hold values from 0 to 31, all different within a row
- fill_order: int32 [32, 256], P(('row', 'col')), may hold values from 0 to 255, each once within a row
- prefix_len: int32 [8], P('row'), may hold values from 102 to 512
- out_grad: bfloat16 [8192, 1024], P(('row', 'col')), may hold values from -6 to 6
Outputs:
- block_out: float32 [8192, 1024], P(('row', 'col'))
- block_in_grad: float32 [8192, 1024], P(('row', 'col'))
- attn_gain_grad: float32 [1024], P('row')
- moe_gain_grad: float32 [1024], P('row')
- w_query_grad: float32 [1024, 1024], P('row', 'col')
- w_key_grad: float32 [1024, 512], P('row', 'col')
- w_value_grad: float32 [1024, 512], P('row', 'col')
- w_out_grad: float32 [1024, 1024], P('row', 'col')
- w_router_grad: float32 [1024, 32], P('row', 'col')
- w_gate_grad: float32 [32, 1024, 512], P('row', None, 'col')
- w_up_grad: float32 [32, 1024, 512], P('row', None, 'col')
- w_down_grad: float32 [32, 1024, 512], P('row', None, 'col')
The draws below stay inside these ranges and needn't reach their ends.
Inputs may be any that keep to these rules, and one draw needn't show every extreme that they name: `expert_ids`: each token names 8 different experts. `fill_order`: each row lists the 256 tokens of its block, each once.
All inputs are finite; a program needn't handle non-finite values.
Results may differ from the reference program's by a relative error of at most 0.024.
Values may be sent and summed in bfloat16 or wider, within the bound.
No kernel may reach another device: no remote copies, remote signals or barrier semaphores. Data moves between devices by JAX's collectives and lax.ppermute only.
A program may use at most 192 MiB of HBM per device.

```python
import jax
import jax.numpy as jnp
from jax import lax

D = 1024
H = 16
KVH = 8
HD = 64
E = 32
FF = 512
TOPK = 8
TOK_DEV = 256
TOKENS = 8192
SEQ = 1024
NSEQ = 8
CAP = 80
DEVICES = 32


def place_ends(entries, stream_key, low, largest):
    longest = entries.shape.index(max(entries.shape))
    spots = []
    for shift in (0, 1):
        where = [jax.random.randint(jax.random.fold_in(stream_key, axis), (), 0, length) for axis, length in enumerate(entries.shape)]
        where[longest] = (where[longest] + shift) % entries.shape[longest]
        spots.append(tuple(where))
    return entries.at[spots[0]].set(low).at[spots[1]].set(largest)


def shard_levels(key, extent, cuts, low, top_value):
    def one(dim, parts):
        draws = jax.random.uniform(jax.random.fold_in(jax.random.fold_in(key, 6), dim), (parts,), jnp.float32, low / len(cuts), top_value / len(cuts))
        return jnp.repeat(jnp.exp(draws), extent[dim] // parts).reshape((-1,) + (1,) * (len(extent) - dim - 1))

    level = one(*cuts[0])
    for cut in cuts[1:]:
        level = level * one(*cut)
    return level


def different_ones(stream_key, rows, count, top, lift):
    order = jax.random.permutation(jax.random.fold_in(stream_key, 1), count)
    boost = order
    for power in range(3):
        boost = boost * boost // count
    boost = boost * lift // count
    chance = jax.random.randint(jax.random.fold_in(stream_key, 2), (rows, count), 0, 4096) + boost
    sure = jax.random.permutation(jax.random.fold_in(stream_key, 3), rows)[jnp.arange(count) % rows]
    chance = jnp.where(jnp.arange(rows)[:, None] == sure[None, :], 1 << 14, chance)
    priority = chance * count + jnp.arange(count)
    return lax.top_k(priority.astype(jnp.int32), top)[1].astype(jnp.int32)


def centred(key, shape, width, most, shards=(), kind=jnp.bfloat16):
    values = width * jax.random.normal(key, shape, jnp.float32)
    if shards:
        values = values * shard_levels(key, shape, shards, -0.22, 0.18)
    return jnp.clip(values, -most, most).astype(kind)


def setup_inputs(seed: int = 0) -> dict:
    splits = jax.random.split(jax.random.key(seed), 16)
    return {
        "block_in": centred(splits[0], (TOKENS, D), 1.0, 6.0, ((0, 32),)),
        "attn_gain": jnp.clip(1.0 + 0.1 * jax.random.normal(splits[1], (D,), jnp.float32), 0.5, 1.5).astype(jnp.bfloat16),
        "moe_gain": jnp.clip(1.0 + 0.1 * jax.random.normal(splits[2], (D,), jnp.float32), 0.5, 1.5).astype(jnp.bfloat16),
        "w_query": centred(splits[3], (D, H * HD), D ** -0.5, 0.1875, ((0, 8), (1, 4))),
        "w_key": centred(splits[4], (D, KVH * HD), D ** -0.5, 0.1875, ((0, 8), (1, 4))),
        "w_value": centred(splits[5], (D, KVH * HD), D ** -0.5, 0.1875, ((0, 8), (1, 4))),
        "w_out": centred(splits[6], (H * HD, D), (H * HD // 32) ** -0.5, 1.0, ((0, 8), (1, 4))),
        "w_router": centred(splits[7], (D, E), (4 * D) ** -0.5, 0.09375, ((0, 8), (1, 4))),
        "w_gate": centred(splits[8], (E, D, FF), D ** -0.5, 0.1875, ((0, 8), (2, 4))),
        "w_up": centred(splits[9], (E, D, FF), D ** -0.5, 0.1875, ((0, 8), (2, 4))),
        "w_down": centred(splits[10], (E, D, FF), (FF // 16) ** -0.5, 1.0, ((0, 8), (2, 4))),
        "expert_ids": different_ones(splits[11], TOKENS, E, TOPK, 2048),
        "fill_order": jax.vmap(lambda own: jax.random.permutation(own, TOK_DEV))(jax.random.split(splits[12], DEVICES)).reshape((DEVICES, TOK_DEV)).astype(jnp.int32),
        "prefix_len": place_ends(jax.random.randint(splits[13], (NSEQ,), SEQ // 10, SEQ // 2 + 1), jax.random.fold_in(splits[13], 1), SEQ // 10, (SEQ // 2 + 1) - 1).astype(jnp.int32),
        "out_grad": centred(splits[14], (TOKENS, D), 1.0, 6.0, ((0, 32),)),
    }


@jax.custom_vjp
def low(v):
    return lax.optimization_barrier(v.astype(jnp.bfloat16)).astype(jnp.float32)

@jax.custom_vjp
def low_back(v):
    return v

def low_keep(v):
    return (low(v), None)

def low_pass(kept, grad):
    return (grad,)

def back_keep(v):
    return (v, None)

def back_low(kept, grad):
    return (low(grad),)
low.defvjp(low_keep, low_pass)
low_back.defvjp(back_keep, back_low)
EPS = 1e-06
NEGATIVE = -1e+30

def product(left, right):
    return jnp.dot(left, right, precision=lax.Precision.HIGHEST)

def rope_tables():
    position = jnp.arange(SEQ, dtype=jnp.int32).astype(jnp.float32)
    inverse = 10000.0 ** (-jnp.arange(HD // 2, dtype=jnp.float32) * 2.0 / HD)
    angle = position[:, None] * inverse[None, :]
    return (jnp.cos(angle), jnp.sin(angle))

def rotate(values, cosine, sine):
    half = HD // 2
    first, second = (values[..., :half], values[..., half:])
    cos_rows = cosine[:, None, :]
    sin_rows = sine[:, None, :]
    return jnp.concatenate([first * cos_rows - second * sin_rows, second * cos_rows + first * sin_rows], axis=-1)

def normalize(values, gain):
    scale = lax.rsqrt(lax.optimization_barrier(jnp.mean(values * values, axis=1, keepdims=True)) + EPS)
    return values * scale * gain

def sequence_attend(pieces):
    query_rot, key_rot, value_rows, prefix = pieces
    group = H // KVH
    spots = jnp.arange(SEQ, dtype=jnp.int32)
    allowed = (spots[None, :] <= spots[:, None]) | (spots[None, :] < prefix)
    query_heads = query_rot.reshape(SEQ, KVH, group, HD).transpose(1, 2, 0, 3)
    key_heads = key_rot.transpose(1, 0, 2)
    value_heads = value_rows.transpose(1, 0, 2)

    def one_head(inputs):
        queries, keys, values = inputs
        scores = jnp.einsum('gqd,kd->gqk', queries, keys, precision=lax.Precision.HIGHEST) * HD ** (-0.5)
        scores = low_back(scores)
        scores = jnp.where(allowed[None], scores, NEGATIVE)
        highest = lax.optimization_barrier(jnp.max(scores, axis=-1, keepdims=True))
        expo = jnp.exp(scores - highest)
        weights = low(expo / lax.optimization_barrier(jnp.sum(expo, axis=-1, keepdims=True)))
        return jnp.einsum('gqk,kd->gqd', weights, values, precision=lax.Precision.HIGHEST)
    mixed = lax.map(jax.checkpoint(one_head), (query_heads, key_heads, value_heads))
    return mixed.transpose(2, 0, 1, 3).reshape(SEQ, H * HD)

def slot_tables(expert_ids, fill_order):
    groups = TOKENS // TOK_DEV
    ids = expert_ids.reshape(groups, TOK_DEV, TOPK)
    ranked = jnp.take_along_axis(ids, fill_order[:, :, None], axis=1)
    onehot = (ranked.reshape(groups, TOK_DEV * TOPK, 1) == jnp.arange(E, dtype=jnp.int32)).astype(jnp.int32)
    before = jnp.cumsum(onehot, axis=1) - onehot
    ranked_slot = lax.optimization_barrier(jnp.sum(before * onehot, axis=2)).reshape(groups, TOK_DEV, TOPK)
    group_index = jnp.arange(groups, dtype=jnp.int32)[:, None]
    slot = jnp.zeros((groups, TOK_DEV, TOPK), jnp.int32).at[group_index, fill_order].set(ranked_slot)
    kept = slot < CAP
    dest = jnp.where(kept, (group_index[:, :, None] * E + ids) * CAP + slot, groups * E * CAP)
    pair = jnp.arange(TOKENS * TOPK, dtype=jnp.int32)
    table = jnp.full((groups * E * CAP + 1,), TOKENS * TOPK, jnp.int32).at[dest.reshape(-1)].set(pair)
    return table[:-1].reshape(groups, E, CAP).transpose(1, 0, 2)

def layer(inputs, prefix_len, slot_pair):
    block_in, attn_gain, moe_gain, w_query, w_key, w_value, w_out, w_router, w_gate, w_up, w_down = inputs
    cosine, sine = rope_tables()
    attn_in = low(normalize(block_in, attn_gain))
    query = low_back(product(attn_in, w_query)).reshape(NSEQ, SEQ, H, HD)
    key = low_back(product(attn_in, w_key)).reshape(NSEQ, SEQ, KVH, HD)
    value = low_back(low(product(attn_in, w_value))).reshape(NSEQ, SEQ, KVH, HD)
    query_rot = low(rotate(query, cosine, sine))
    key_rot = low(rotate(key, cosine, sine))
    mixed = lax.map(jax.checkpoint(sequence_attend), (query_rot, key_rot, value, prefix_len))
    mixed = low_back(low(mixed.reshape(TOKENS, H * HD)))
    resid = block_in + low_back(product(mixed, w_out))
    moe_in = low(normalize(resid, moe_gain))
    logits = low_back(product(moe_in, w_router))
    return (resid, moe_in, logits)

def reference(block_in, attn_gain, moe_gain, w_query, w_key, w_value, w_out, w_router, w_gate, w_up, w_down, expert_ids, fill_order, prefix_len, out_grad):
    floats = (block_in.astype(jnp.float32), attn_gain.astype(jnp.float32), moe_gain.astype(jnp.float32), w_query.astype(jnp.float32), w_key.astype(jnp.float32), w_value.astype(jnp.float32), w_out.astype(jnp.float32), w_router.astype(jnp.float32), w_gate.astype(jnp.float32), w_up.astype(jnp.float32), w_down.astype(jnp.float32))
    slot_pair = slot_tables(expert_ids, fill_order)

    def forward(*inputs):
        resid, moe_in, logits = layer(inputs, prefix_len, slot_pair)
        picked = jnp.take_along_axis(logits, expert_ids, axis=1)
        highest = lax.optimization_barrier(jnp.max(picked, axis=1, keepdims=True))
        expo = jnp.exp(picked - highest)
        gates = expo / lax.optimization_barrier(jnp.sum(expo, axis=1, keepdims=True))
        gates_flat = jnp.concatenate([gates.reshape(-1), jnp.zeros((1,), jnp.float32)])
        rows_pad = jnp.concatenate([moe_in, jnp.zeros((1, D), jnp.float32)])

        def one_expert(total, pieces):
            gate_w, up_w, down_w, slots = pieces
            flat = slots.reshape(-1)
            token = flat // TOPK
            rows = low_back(rows_pad[token])
            hidden_gate = low_back(product(rows, gate_w))
            hidden_up = low_back(product(rows, up_w))
            active = low(jax.nn.silu(hidden_gate) * hidden_up)
            result = low_back(low(product(active, down_w.T)))
            weight = gates_flat[flat]
            return (total.at[token].add(weight[:, None] * result), None)
        start = jnp.zeros((TOKENS + 1, D), jnp.float32)
        moe_total, unused = lax.scan(jax.checkpoint(one_expert), start, (inputs[8], inputs[9], inputs[10], slot_pair))
        return resid + moe_total[:TOKENS]
    block_out, pullback = jax.vjp(forward, *floats)
    grads = pullback(out_grad.astype(jnp.float32))
    return (block_out, grads[0], grads[1], grads[2], grads[3], grads[4], grads[5], grads[6], grads[7], grads[8], grads[9], grads[10])
```

```python
import functools

import jax
import jax.numpy as jnp
from jax import lax
from jax.experimental import pallas as pl
from jax.experimental.pallas import tpu as pltpu
from jax.sharding import PartitionSpec as P

D = 1024
H = 16
KVH = 8
HD = 64
E = 32
TOPK = 8
CAP = 80


EPS = 1e-06
NEGATIVE = -1e30


def cross_rows(left, right):
    return lax.dot_general(
        left, right, (((0,), (0,)), ((), ())), preferred_element_type=jnp.float32
    )


def times_back(left, right):
    return lax.dot_general(
        left, right, (((1,), (1,)), ((), ())), preferred_element_type=jnp.float32
    )


def rope_tables(first_position, count):
    position = (first_position + jnp.arange(count, dtype=jnp.int32)).astype(jnp.float32)
    inverse = 10000.0 ** (-jnp.arange(HD // 2, dtype=jnp.float32) * 2.0 / HD)
    angle = position[:, None] * inverse[None, :]
    return (jnp.cos(angle), jnp.sin(angle))


def rotate(values, cosine, sine):
    half = HD // 2
    first, second = (values[..., :half], values[..., half:])
    cos_rows = cosine[:, None, :]
    sin_rows = sine[:, None, :]
    return jnp.concatenate(
        [first * cos_rows - second * sin_rows, second * cos_rows + first * sin_rows], axis=-1
    )


def rotate_back(grads, cosine, sine):
    half = HD // 2
    first, second = (grads[..., :half], grads[..., half:])
    cos_rows = cosine[:, None, :]
    sin_rows = sine[:, None, :]
    return jnp.concatenate(
        [first * cos_rows + second * sin_rows, second * cos_rows - first * sin_rows], axis=-1
    )


def norm_rows(values, gain):
    scale = lax.rsqrt(jnp.mean(values * values, axis=1, keepdims=True) + EPS)
    normed = values * scale
    return (normed, scale, (normed * gain).astype(jnp.bfloat16))


def norm_back(grad_in, normed, scale, gain):
    gain_grad = jnp.sum(grad_in * normed, axis=0)
    inner = grad_in * gain
    return (scale * (inner - normed * jnp.mean(inner * normed, axis=1, keepdims=True)), gain_grad)


def to_heads(rows, count, group):
    return rows.reshape(count, KVH, group, HD).transpose(1, 2, 0, 3).reshape(KVH, group * count, HD)


def from_heads(heads, count, group):
    return heads.reshape(KVH, group, count, HD).transpose(2, 0, 1, 3).reshape(count, H, HD)


def general(
    block_in,
    attn_gain,
    moe_gain,
    w_query,
    w_key,
    w_value,
    w_out,
    w_router,
    w_gate,
    w_up,
    w_down,
    expert_ids,
    fill_order,
    prefix_len,
    out_grad,
):
    tok_rows = block_in.shape[0]
    n_col = lax.axis_size("col")
    col_index = lax.axis_index("col")
    seq_rows = tok_rows * n_col
    group = H // KVH
    scale_attn = HD ** (-0.5)
    bf16 = jnp.bfloat16
    f32 = jnp.float32
    shared = (
        lax.all_gather(w_query, "row", axis=0, tiled=True),
        lax.all_gather(w_key, "row", axis=0, tiled=True),
        lax.all_gather(w_value, "row", axis=0, tiled=True),
        lax.all_gather(w_out, "row", axis=0, tiled=True),
        lax.all_gather(w_router, "row", axis=0, tiled=True),
        lax.all_gather(attn_gain, "row", axis=0, tiled=True),
        lax.all_gather(moe_gain, "row", axis=0, tiled=True),
    )
    wq_full, wk_full, wv_full, wo_full, wr_full = (
        lax.all_gather(shared[0], "col", axis=1, tiled=True),
        lax.all_gather(shared[1], "col", axis=1, tiled=True),
        lax.all_gather(shared[2], "col", axis=1, tiled=True),
        lax.all_gather(shared[3], "col", axis=1, tiled=True),
        lax.all_gather(shared[4], "col", axis=1, tiled=True),
    )
    gain_one = shared[5].astype(f32)
    gain_two = shared[6].astype(f32)
    x_rows = block_in.astype(f32)
    normed_one, scale_one, attn_in = norm_rows(x_rows, gain_one)
    query = jnp.dot(attn_in, wq_full, preferred_element_type=f32)
    key = jnp.dot(attn_in, wk_full, preferred_element_type=f32)
    value = jnp.dot(attn_in, wv_full, preferred_element_type=f32).astype(bf16)
    cosine, sine = rope_tables(col_index * tok_rows, tok_rows)
    query_rot = rotate(query.reshape(tok_rows, H, HD), cosine, sine).astype(bf16)
    key_rot = (
        rotate(key.reshape(tok_rows, KVH, HD), cosine, sine)
        .astype(bf16)
        .reshape(tok_rows, KVH * HD)
    )
    keys_all, values_all = (
        lax.all_gather(key_rot, "col", axis=0, tiled=True),
        lax.all_gather(value, "col", axis=0, tiled=True),
    )
    prefix = prefix_len[0]
    query_spot = col_index * tok_rows + jnp.arange(tok_rows, dtype=jnp.int32)
    key_spot = jnp.arange(seq_rows, dtype=jnp.int32)
    allowed = (key_spot[None, :] <= query_spot[:, None]) | (key_spot[None, :] < prefix)
    allowed_rows = jnp.tile(allowed, (group, 1))
    query_heads = to_heads(query_rot.reshape(tok_rows, H * HD), tok_rows, group)
    key_heads = keys_all.reshape(seq_rows, KVH, HD).transpose(1, 0, 2)
    value_heads = values_all.reshape(seq_rows, KVH, HD).transpose(1, 0, 2)

    def attend(pieces):
        queries, keys, values = pieces
        scores = times_back(queries, keys) * scale_attn
        scores = jnp.where(allowed_rows, scores, NEGATIVE)
        highest = jnp.max(scores, axis=1, keepdims=True)
        expo = jnp.exp(scores - highest)
        total = jnp.sum(expo, axis=1, keepdims=True)
        weights = (expo / total).astype(bf16)
        mixed_heads = jnp.dot(weights, values, preferred_element_type=f32).astype(bf16)
        return (mixed_heads, (highest + jnp.log(total))[:, 0])

    mixed_heads, lse_heads = lax.map(attend, (query_heads, key_heads, value_heads))
    mixed = from_heads(mixed_heads, tok_rows, group).reshape(tok_rows, H * HD)
    resid = x_rows + jnp.dot(mixed, wo_full, preferred_element_type=f32)
    normed_two, scale_two, moe_in = norm_rows(resid, gain_two)
    logits = jnp.dot(moe_in, wr_full, preferred_element_type=f32)
    choice_hot = (expert_ids[:, :, None] == jnp.arange(E, dtype=jnp.int32)).astype(f32)
    picked = jnp.sum(choice_hot * logits[:, None, :], axis=2)
    highest = jnp.max(picked, axis=1, keepdims=True)
    expo = jnp.exp(picked - highest)
    gates = expo / jnp.sum(expo, axis=1, keepdims=True)
    order = fill_order[0]
    ranked = expert_ids[order]
    onehot = (ranked.reshape(-1, 1) == jnp.arange(E, dtype=jnp.int32)).astype(jnp.int32)
    before = jnp.cumsum(onehot, axis=0) - onehot
    ranked_slot = jnp.sum(before * onehot, axis=1).reshape(tok_rows, TOPK)
    slot = jnp.zeros((tok_rows, TOPK), jnp.int32).at[order].set(ranked_slot)
    kept = slot < CAP
    dest_grid = jnp.where(kept, expert_ids * CAP + slot, E * CAP)
    pair_ids = jnp.arange(tok_rows * TOPK, dtype=jnp.int32)
    slot_pair = (
        jnp.full((E * CAP + 1,), tok_rows * TOPK, jnp.int32)
        .at[dest_grid.reshape(-1)]
        .set(pair_ids)[: E * CAP]
    )
    slot_token = slot_pair // TOPK
    gate_slot = jnp.concatenate([gates.reshape(-1), jnp.zeros((1,), f32)])[slot_pair]
    moe_pad = jnp.concatenate([moe_in, jnp.zeros((1, D), bf16)])
    dispatch = moe_pad[slot_token].reshape(E, CAP, D)
    received = lax.all_to_all(dispatch, "row", split_axis=0, concat_axis=1, tiled=True)
    gate_w, up_w, down_w = (
        lax.all_gather(w_gate, "col", axis=2, tiled=True),
        lax.all_gather(w_up, "col", axis=2, tiled=True),
        lax.all_gather(w_down, "col", axis=2, tiled=True),
    )
    hidden_gate = jnp.einsum("erd,edf->erf", received, gate_w, preferred_element_type=f32)
    hidden_up = jnp.einsum("erd,edf->erf", received, up_w, preferred_element_type=f32)
    active = (jax.nn.silu(hidden_gate) * hidden_up).astype(bf16)
    expert_out = jnp.einsum("erf,edf->erd", active, down_w, preferred_element_type=f32).astype(bf16)
    returned = lax.all_to_all(expert_out, "row", split_axis=1, concat_axis=0, tiled=True)
    out_pad = jnp.concatenate([returned.reshape(E * CAP, D), jnp.zeros((1, D), bf16)])
    pair_out = out_pad[dest_grid]
    weight_pair = gates * kept.astype(f32)
    moe_out = jnp.zeros((tok_rows, D), f32)
    for choice_index in range(TOPK):
        moe_out = moe_out + weight_pair[:, choice_index : choice_index + 1] * pair_out[
            :, choice_index
        ].astype(f32)
    block_out = resid + moe_out
    grad_out = out_grad.astype(f32)
    gate_grad = jnp.stack(
        [
            jnp.sum(pair_out[:, choice_index].astype(f32) * grad_out, axis=1)
            for choice_index in range(TOPK)
        ],
        axis=1,
    )
    grad_pad = jnp.concatenate([grad_out, jnp.zeros((1, D), f32)])
    slot_grad = (gate_slot[:, None] * grad_pad[slot_token]).astype(bf16).reshape(E, CAP, D)
    out_grads = lax.all_to_all(slot_grad, "row", split_axis=0, concat_axis=1, tiled=True)
    act_grad = jnp.einsum("erd,edf->erf", out_grads, down_w, preferred_element_type=f32)
    sigma = jax.nn.sigmoid(hidden_gate)
    gate_h_grad = (act_grad * hidden_up * sigma * (1.0 + hidden_gate * (1.0 - sigma))).astype(bf16)
    up_h_grad = (act_grad * hidden_gate * sigma).astype(bf16)
    down_wgrad = jnp.einsum("erd,erf->edf", out_grads, active, preferred_element_type=f32)
    gate_wgrad = jnp.einsum("erd,erf->edf", received, gate_h_grad, preferred_element_type=f32)
    up_wgrad = jnp.einsum("erd,erf->edf", received, up_h_grad, preferred_element_type=f32)
    in_grad = (
        jnp.einsum("erf,edf->erd", gate_h_grad, gate_w, preferred_element_type=f32)
        + jnp.einsum("erf,edf->erd", up_h_grad, up_w, preferred_element_type=f32)
    ).astype(bf16)
    back_rows = lax.all_to_all(in_grad, "row", split_axis=1, concat_axis=0, tiled=True)
    gate_sum, up_sum, down_sum = (
        lax.psum_scatter(
            gate_wgrad.astype(jnp.bfloat16), "col", scatter_dimension=2, tiled=True
        ).astype(jnp.float32),
        lax.psum_scatter(
            up_wgrad.astype(jnp.bfloat16), "col", scatter_dimension=2, tiled=True
        ).astype(jnp.float32),
        lax.psum_scatter(
            down_wgrad.astype(jnp.bfloat16), "col", scatter_dimension=2, tiled=True
        ).astype(jnp.float32),
    )
    back_pad = jnp.concatenate([back_rows.reshape(E * CAP, D), jnp.zeros((1, D), bf16)])
    pair_back = back_pad[dest_grid]
    moe_in_grad = jnp.zeros((tok_rows, D), f32)
    for choice_index in range(TOPK):
        moe_in_grad = moe_in_grad + pair_back[:, choice_index].astype(f32)
    picked_grad = gates * (gate_grad - jnp.sum(gates * gate_grad, axis=1, keepdims=True))
    logit_grad = jnp.sum(choice_hot * picked_grad[:, :, None], axis=1).astype(bf16)
    router_wgrad = cross_rows(moe_in, logit_grad)
    moe_in_grad = moe_in_grad + times_back(logit_grad, wr_full)
    norm_two_grad, gain_two_grad = norm_back(moe_in_grad, normed_two, scale_two, gain_two)
    resid_grad = grad_out + norm_two_grad
    branch_grad = resid_grad.astype(bf16)
    out_wgrad = cross_rows(mixed, branch_grad)
    mixed_grad = times_back(branch_grad, wo_full).astype(bf16)
    grad_heads = to_heads(mixed_grad, tok_rows, group)

    def query_side(pieces):
        queries, keys, values, lse_rows, grad_rows = pieces
        scores = jnp.where(allowed_rows, times_back(queries, keys) * scale_attn, NEGATIVE)
        probs = jnp.exp(scores - lse_rows[:, None])
        prob_grad = times_back(grad_rows, values)
        delta = jnp.sum(probs * prob_grad, axis=1, keepdims=True)
        score_grad = (probs * (prob_grad - delta)).astype(bf16)
        query_grad = jnp.dot(score_grad, keys, preferred_element_type=f32) * scale_attn
        return (query_grad, delta[:, 0], score_grad, probs)

    def both_sides(pieces):
        queries, keys, values, lse_rows, grad_rows = pieces
        query_grad, delta, score_grad, probs = query_side(pieces)
        key_grad = cross_rows(score_grad, queries) * scale_attn
        value_grad = cross_rows(probs.astype(bf16), grad_rows)
        return (query_grad, key_grad, value_grad)

    query_rot_grad, key_parts, value_parts = lax.map(
        both_sides, (query_heads, key_heads, value_heads, lse_heads, grad_heads)
    )
    key_rot_grad, value_grad = (
        lax.psum_scatter(
            key_parts.transpose(1, 0, 2).reshape(seq_rows, KVH * HD).astype(jnp.bfloat16),
            "col",
            scatter_dimension=0,
            tiled=True,
        ).astype(jnp.float32),
        lax.psum_scatter(
            value_parts.transpose(1, 0, 2).reshape(seq_rows, KVH * HD).astype(jnp.bfloat16),
            "col",
            scatter_dimension=0,
            tiled=True,
        ).astype(jnp.float32),
    )
    query_grad = (
        rotate_back(from_heads(query_rot_grad, tok_rows, group), cosine, sine)
        .reshape(tok_rows, H * HD)
        .astype(bf16)
    )
    key_grad = (
        rotate_back(key_rot_grad.reshape(tok_rows, KVH, HD), cosine, sine)
        .reshape(tok_rows, KVH * HD)
        .astype(bf16)
    )
    value_grad = value_grad.astype(bf16)
    query_wgrad = cross_rows(attn_in, query_grad)
    key_wgrad = cross_rows(attn_in, key_grad)
    value_wgrad = cross_rows(attn_in, value_grad)
    attn_in_grad = (
        times_back(query_grad, wq_full)
        + times_back(key_grad, wk_full)
        + times_back(value_grad, wv_full)
    )
    norm_one_grad, gain_one_grad = norm_back(attn_in_grad, normed_one, scale_one, gain_one)
    block_in_grad = resid_grad + norm_one_grad
    spread_one = jnp.broadcast_to(gain_one_grad[:, None], (D, n_col))
    spread_two = jnp.broadcast_to(gain_two_grad[:, None], (D, n_col))
    col_sums = (
        lax.psum_scatter(
            query_wgrad.astype(jnp.bfloat16), "col", scatter_dimension=1, tiled=True
        ).astype(jnp.float32),
        lax.psum_scatter(
            key_wgrad.astype(jnp.bfloat16), "col", scatter_dimension=1, tiled=True
        ).astype(jnp.float32),
        lax.psum_scatter(
            value_wgrad.astype(jnp.bfloat16), "col", scatter_dimension=1, tiled=True
        ).astype(jnp.float32),
        lax.psum_scatter(
            out_wgrad.astype(jnp.bfloat16), "col", scatter_dimension=1, tiled=True
        ).astype(jnp.float32),
        lax.psum_scatter(
            router_wgrad.astype(jnp.bfloat16), "col", scatter_dimension=1, tiled=True
        ).astype(jnp.float32),
        lax.psum_scatter(
            spread_one.astype(jnp.bfloat16), "col", scatter_dimension=1, tiled=True
        ).astype(jnp.float32),
        lax.psum_scatter(
            spread_two.astype(jnp.bfloat16), "col", scatter_dimension=1, tiled=True
        ).astype(jnp.float32),
    )
    row_sums = (
        lax.psum_scatter(
            col_sums[0].astype(jnp.bfloat16), "row", scatter_dimension=0, tiled=True
        ).astype(jnp.float32),
        lax.psum_scatter(
            col_sums[1].astype(jnp.bfloat16), "row", scatter_dimension=0, tiled=True
        ).astype(jnp.float32),
        lax.psum_scatter(
            col_sums[2].astype(jnp.bfloat16), "row", scatter_dimension=0, tiled=True
        ).astype(jnp.float32),
        lax.psum_scatter(
            col_sums[3].astype(jnp.bfloat16), "row", scatter_dimension=0, tiled=True
        ).astype(jnp.float32),
        lax.psum_scatter(
            col_sums[4].astype(jnp.bfloat16), "row", scatter_dimension=0, tiled=True
        ).astype(jnp.float32),
        lax.psum_scatter(
            col_sums[5].astype(jnp.bfloat16), "row", scatter_dimension=0, tiled=True
        ).astype(jnp.float32),
        lax.psum_scatter(
            col_sums[6].astype(jnp.bfloat16), "row", scatter_dimension=0, tiled=True
        ).astype(jnp.float32),
    )
    return (
        block_out,
        block_in_grad,
        row_sums[5][:, 0],
        row_sums[6][:, 0],
        row_sums[0],
        row_sums[1],
        row_sums[2],
        row_sums[3],
        row_sums[4],
        gate_sum,
        up_sum,
        down_sum,
    )


F32 = jnp.float32
BF16 = jnp.bfloat16
MIB = 1024 * 1024
LANES = 128


def dot_nn(a, b):
    return lax.dot_general(a, b, (((1,), (0,)), ((), ())), preferred_element_type=F32)


def dot_nt(a, b):
    return lax.dot_general(a, b, (((1,), (1,)), ((), ())), preferred_element_type=F32)


def dot_tn(a, b):
    return lax.dot_general(a, b, (((0,), (0,)), ((), ())), preferred_element_type=F32)


def in_vmem():
    return pl.BlockSpec(memory_space=pltpu.VMEM)


def in_smem():
    return pl.BlockSpec(memory_space=pltpu.SMEM)


def partner(values):
    lane = lax.broadcasted_iota(jnp.int32, values.shape, 1)
    half = HD // 2
    return jnp.where(
        lane % HD < half,
        pltpu.roll(values, LANES - half, 1),
        pltpu.roll(values, half, 1),
    )


def attend_kernel(
    spot_ref, x0, x1, x2, x3, gain_ref, w_ref, cos_ref, sin_ref,
    attn_ref, mixed_ref, q_ref, k_ref, v_ref, lse_ref,
):
    rows = x0.shape[0]
    col, prefix = spot_ref[0], spot_ref[1]
    gain = gain_ref[...]
    for step, chunk in enumerate((x0, x1, x2, x3)):
        source = lax.rem(col - step + 4, 4)
        x = chunk[...].astype(F32)
        scale = lax.rsqrt(jnp.mean(x * x, axis=1, keepdims=True) + EPS)
        attn_ref[pl.ds(pl.multiple_of(source * rows, rows), rows), :] = (x * scale * gain).astype(BF16)
    for tile in range(4):
        span = pl.ds(tile * rows, rows)
        qkv = dot_nn(attn_ref[span, :], w_ref[...])
        cosine, sine = cos_ref[span, :], sin_ref[span, :]
        for block in range(3):
            v = qkv[:, block * LANES : (block + 1) * LANES]
            y = v * cosine + partner(v) * sine
            if block < 2:
                y = (y * HD ** (-0.5)).astype(BF16)
                q_ref[2 * block, span, :] = y[:, :HD]
                q_ref[2 * block + 1, span, :] = y[:, HD:]
            else:
                y = y.astype(BF16)
                k_ref[0, span, :] = y[:, :HD]
                k_ref[1, span, :] = y[:, HD:]
        v = qkv[:, 3 * LANES :].astype(BF16)
        v_ref[0, span, :] = v[:, :HD]
        v_ref[1, span, :] = v[:, HD:]
    total = 4 * rows
    for tile in range(4):
        span = pl.ds(tile * rows, rows)
        keys = max((tile + 1) * rows, total // 2)
        key_spot = lax.broadcasted_iota(jnp.int32, (rows, keys), 1)
        query_spot = lax.broadcasted_iota(jnp.int32, (rows, keys), 0) + tile * rows
        allowed = (key_spot <= query_spot) | (key_spot < prefix)
        for pair in range(2):
            k, v = k_ref[pair, pl.ds(0, keys), :], v_ref[pair, pl.ds(0, keys), :]
            outs = []
            for head in (2 * pair, 2 * pair + 1):
                scores = jnp.where(allowed, dot_nt(q_ref[head, span, :], k), NEGATIVE)
                highest = jnp.max(scores, axis=1, keepdims=True)
                expo = jnp.exp(scores - highest)
                summed = jnp.sum(expo, axis=1, keepdims=True)
                outs.append(dot_nn(expo.astype(BF16), v) * (1.0 / summed))
                lse_ref[span, head : head + 1] = highest + jnp.log(summed)
            mixed_ref[span, pair * LANES : (pair + 1) * LANES] = jnp.concatenate(outs, axis=1).astype(BF16)


def attend(spots, chunks, gain, w_qkv, cosine, sine):
    rows = chunks[0].shape[0]
    seq = 4 * rows
    shapes = (
        jax.ShapeDtypeStruct((seq, D), BF16),
        jax.ShapeDtypeStruct((seq, 256), BF16),
        jax.ShapeDtypeStruct((4, seq, HD), BF16),
        jax.ShapeDtypeStruct((2, seq, HD), BF16),
        jax.ShapeDtypeStruct((2, seq, HD), BF16),
        jax.ShapeDtypeStruct((seq, 4), F32),
    )
    return pl.pallas_call(
        attend_kernel,
        out_shape=shapes,
        in_specs=[in_smem()] + [in_vmem()] * 8,
        out_specs=tuple(in_vmem() for _ in shapes),
        compiler_params=pltpu.CompilerParams(vmem_limit_bytes=40 * MIB),
        cost_estimate=pl.CostEstimate(flops=4 * 10**9, bytes_accessed=8 * MIB, transcendentals=3 * 10**6),
    )(spots, *chunks, gain, w_qkv, cosine, sine)


def attend_back_kernel(
    spot_ref, grad_ref, mixed_ref, q_ref, k_ref, v_ref, lse_ref, attn_ref, w_ref, cos_ref, sin_ref, gain_ref,
    wgrad_ref, in_ref, gain_grad_ref, dqkv_ref, dk_ref, dv_ref, dq_ref, mg_ref,
):
    seq = attn_ref.shape[0]
    rows = seq // 4
    prefix = spot_ref[1]
    for tile in range(4):
        span = pl.ds(tile * rows, rows)
        for pair in range(2):
            g = grad_ref[span, pair * LANES : (pair + 1) * LANES]
            mg_ref[2 * pair, span, :] = g[:, :HD]
            mg_ref[2 * pair + 1, span, :] = g[:, HD:]
    dk_ref[...] = jnp.zeros_like(dk_ref)
    dv_ref[...] = jnp.zeros_like(dv_ref)
    for tile in range(4):
        span = pl.ds(tile * rows, rows)
        keys = max((tile + 1) * rows, seq // 2)
        key_spot = lax.broadcasted_iota(jnp.int32, (rows, keys), 1)
        query_spot = lax.broadcasted_iota(jnp.int32, (rows, keys), 0) + tile * rows
        allowed = (key_spot <= query_spot) | (key_spot < prefix)
        for pair in range(2):
            k, v = k_ref[pair, pl.ds(0, keys), :], v_ref[pair, pl.ds(0, keys), :]
            both = grad_ref[span, pair * LANES : (pair + 1) * LANES].astype(F32) * mixed_ref[
                span, pair * LANES : (pair + 1) * LANES
            ].astype(F32)
            outs = []
            for at, head in enumerate((2 * pair, 2 * pair + 1)):
                q, g = q_ref[head, span, :], mg_ref[head, span, :]
                delta = jnp.sum(both[:, at * HD : (at + 1) * HD], axis=1, keepdims=True)
                scores = jnp.where(allowed, dot_nt(q, k), NEGATIVE)
                probs = jnp.exp(scores - lse_ref[span, head : head + 1])
                score_grad = (probs * (dot_nt(g, v) - delta)).astype(BF16)
                dv_ref[pair, pl.ds(0, keys), :] += dot_tn(probs.astype(BF16), g)
                dk_ref[pair, pl.ds(0, keys), :] += dot_tn(score_grad, q)
                outs.append(dot_nn(score_grad, k) * HD ** (-0.5))
            dq_ref[span, pair * LANES : (pair + 1) * LANES] = jnp.concatenate(outs, axis=1)
    for tile in range(4):
        span = pl.ds(tile * rows, rows)
        cosine, sine = cos_ref[span, :], sin_ref[span, :]
        for block in range(3):
            if block < 2:
                g = dq_ref[span, block * LANES : (block + 1) * LANES]
            else:
                g = jnp.concatenate([dk_ref[0, span, :], dk_ref[1, span, :]], axis=1)
            dqkv_ref[span, block * LANES : (block + 1) * LANES] = (g * cosine - partner(g) * sine).astype(BF16)
        dqkv_ref[span, 3 * LANES :] = jnp.concatenate([dv_ref[0, span, :], dv_ref[1, span, :]], axis=1).astype(BF16)
    gain_total = jnp.zeros((1, D), F32)
    for tile in range(4):
        span = pl.ds(tile * rows, rows)
        back = dot_nt(dqkv_ref[span, :], w_ref[...])
        in_ref[span, :] = back.astype(BF16)
        gain_total = gain_total + jnp.sum(back * attn_ref[span, :].astype(F32), axis=0, keepdims=True)
    gain_grad_ref[...] = gain_total / gain_ref[...]
    for part in range(4):
        span = pl.ds(part * 256, 256)
        wgrad_ref[span, :] = dot_tn(attn_ref[:, span], dqkv_ref[...]).astype(BF16)


def attend_back(spots, grads, mixed, q, k, v, lse, attn_in, w_qkv, cosine, sine, gain):
    seq = attn_in.shape[0]
    shapes = (
        jax.ShapeDtypeStruct((D, 512), BF16),
        jax.ShapeDtypeStruct((seq, D), BF16),
        jax.ShapeDtypeStruct((1, D), F32),
    )
    return pl.pallas_call(
        attend_back_kernel,
        out_shape=shapes,
        in_specs=[in_smem()] + [in_vmem()] * 11,
        out_specs=tuple(in_vmem() for _ in shapes),
        scratch_shapes=[
            pltpu.VMEM((seq, 512), BF16),
            pltpu.VMEM((2, seq, HD), F32),
            pltpu.VMEM((2, seq, HD), F32),
            pltpu.VMEM((seq, 256), F32),
            pltpu.VMEM((4, seq, HD), BF16),
        ],
        compiler_params=pltpu.CompilerParams(vmem_limit_bytes=48 * MIB),
        cost_estimate=pl.CostEstimate(flops=10 * 10**9, bytes_accessed=14 * MIB, transcendentals=3 * 10**6),
    )(spots, grads, mixed, q, k, v, lse, attn_in, w_qkv, cosine, sine, gain)


def route_kernel(
    mixed_ref, x_ref, wo_ref, gain_ref, wr_ref, ids_ref, order_ref,
    resid_ref, send_ref, gates_ref, kept_ref,
):
    rows = x_ref.shape[0]
    resid = x_ref[...].astype(F32)
    for part in range(4):
        resid = resid + dot_nn(mixed_ref[pl.ds(part * rows, rows), :], wo_ref[part * 256 : (part + 1) * 256, :])
    resid_ref[...] = resid
    scale = lax.rsqrt(jnp.mean(resid * resid, axis=1, keepdims=True) + EPS)
    moe_in = (resid * scale * gain_ref[...]).astype(BF16)
    send_ref[:, :D] = moe_in
    logits = dot_nn(moe_in, wr_ref[...])
    lane = lax.broadcasted_iota(jnp.int32, (rows, LANES), 1)
    chosen = jnp.zeros((rows, LANES), jnp.bool_)
    for choice in range(TOPK):
        chosen = chosen | (ids_ref[:, choice : choice + 1] == lane)
    picked = jnp.where(chosen, logits, NEGATIVE)
    expo = jnp.exp(picked - jnp.max(picked, axis=1, keepdims=True))
    gates = expo / jnp.sum(expo, axis=1, keepdims=True)
    first = lax.broadcasted_iota(jnp.int32, (rows, rows), 0)
    second = lax.broadcasted_iota(jnp.int32, (rows, rows), 1)
    place = (first == order_ref[...]).astype(BF16)
    sooner = dot_nn(place, (second < first).astype(BF16)).astype(BF16)
    sooner = dot_nt(sooner, place).astype(BF16)
    slot = dot_nn(sooner, chosen.astype(BF16))
    kept = (chosen & (slot < CAP)).astype(F32)
    gates_ref[...] = gates
    kept_ref[...] = kept
    send_ref[:, D:] = (gates * kept).astype(BF16)


def route(mixed, x, wo, gain, wr, ids, order):
    rows = x.shape[0]
    shapes = (
        jax.ShapeDtypeStruct((rows, D), F32),
        jax.ShapeDtypeStruct((rows, D + LANES), BF16),
        jax.ShapeDtypeStruct((rows, LANES), F32),
        jax.ShapeDtypeStruct((rows, LANES), F32),
    )
    return pl.pallas_call(
        route_kernel,
        out_shape=shapes,
        in_specs=[in_vmem()] * 7,
        out_specs=tuple(in_vmem() for _ in shapes),
        compiler_params=pltpu.CompilerParams(vmem_limit_bytes=32 * MIB),
        cost_estimate=pl.CostEstimate(flops=10**9, bytes_accessed=5 * MIB, transcendentals=10**5),
    )(mixed, x, wo, gain, wr, ids, order)


def expert_kernel(
    x_ref, g_ref, wg_ref, wu_ref, wd_ref,
    out_ref, back_ref, hg_ref, hu_ref, act_ref, out_acc, in_acc, gate_acc,
):
    step = pl.program_id(0)
    count = wg_ref.shape[0]
    wide = count * LANES

    @pl.when(step == 0)
    def _():
        out_acc[...] = jnp.zeros_like(out_acc)
        in_acc[...] = jnp.zeros_like(in_acc)
        gate_acc[...] = jnp.zeros_like(gate_acc)

    join = lambda ref: jnp.concatenate([ref[i] for i in range(count)], axis=1)
    wg, wu, wd = join(wg_ref), join(wu_ref), join(wd_ref)
    x = x_ref[:, :D]
    expert = lax.broadcasted_iota(jnp.int32, (LANES, wide), 0)
    column = lax.broadcasted_iota(jnp.int32, (LANES, wide), 1)
    spread = (expert == step * count + column // LANES).astype(BF16)
    gate = dot_nn(x_ref[:, D:], spread)
    hidden_gate = dot_nn(x, wg)
    hidden_up = dot_nn(x, wu)
    act_grad = dot_nn(g_ref[...], wd)
    sigma = 0.5 * jnp.tanh(0.5 * hidden_gate) + 0.5
    swish = hidden_gate * sigma
    active = swish * hidden_up
    gate_acc[...] += dot_nt((active * act_grad).astype(BF16), spread)
    gated = (active * gate).astype(BF16)
    act_ref[...] = gated
    out_acc[...] += dot_nt(gated, wd)
    act_grad = act_grad * gate
    up_grad = (act_grad * swish).astype(BF16)
    gate_grad = (act_grad * hidden_up * (sigma + swish * (1.0 - sigma))).astype(BF16)
    hg_ref[...] = gate_grad
    hu_ref[...] = up_grad
    in_acc[...] += dot_nt(gate_grad, wg) + dot_nt(up_grad, wu)

    @pl.when(step == pl.num_programs(0) - 1)
    def _():
        out_ref[...] = out_acc[...].astype(BF16)
        back_ref[:, :D] = in_acc[...].astype(BF16)
        back_ref[:, D:] = gate_acc[...].astype(BF16)


def experts(x, g, wg, wu, wd):
    rows = x.shape[0]
    count = 4
    steps = wg.shape[0] // count
    wide = count * LANES
    weight = pl.BlockSpec((count, D, LANES), lambda i: (i, 0, 0))
    hidden = pl.BlockSpec((rows, wide), lambda i: (0, i))
    whole = lambda width: pl.BlockSpec((rows, width), lambda i: (0, 0))
    return pl.pallas_call(
        expert_kernel,
        grid=(steps,),
        out_shape=(
            jax.ShapeDtypeStruct((rows, D), BF16),
            jax.ShapeDtypeStruct((rows, D + LANES), BF16),
        )
        + (jax.ShapeDtypeStruct((rows, steps * wide), BF16),) * 3,
        in_specs=[whole(D + LANES), whole(D), weight, weight, weight],
        out_specs=(whole(D), whole(D + LANES), hidden, hidden, hidden),
        scratch_shapes=[
            pltpu.VMEM((rows, D), F32),
            pltpu.VMEM((rows, D), F32),
            pltpu.VMEM((rows, LANES), F32),
        ],
        compiler_params=pltpu.CompilerParams(vmem_limit_bytes=40 * MIB),
        cost_estimate=pl.CostEstimate(flops=13 * 10**9, bytes_accessed=32 * MIB, transcendentals=10**6),
    )(x, g, wg, wu, wd)


def expert_wgrad_kernel(
    x0, x1, x2, x3, g0, g1, g2, g3, hg0, hg1, hg2, hg3, hu0, hu1, hu2, hu3, a0, a1, a2, a3,
    wg_ref, wu_ref, wd_ref, xt_ref, gt_ref,
):
    rows = x0.shape[0]

    @pl.when(pl.program_id(0) == 0)
    def _():
        for at, (x, g) in enumerate(zip((x0, x1, x2, x3), (g0, g1, g2, g3))):
            xt_ref[:, at * rows : (at + 1) * rows] = x[:, :D].T
            gt_ref[:, at * rows : (at + 1) * rows] = g[...].T

    for left, parts, out in (
        (xt_ref, (hg0, hg1, hg2, hg3), wg_ref),
        (xt_ref, (hu0, hu1, hu2, hu3), wu_ref),
        (gt_ref, (a0, a1, a2, a3), wd_ref),
    ):
        joined = jnp.concatenate([part[...] for part in parts], axis=0)
        product = dot_nn(left[...], joined).astype(BF16)
        for i in range(out.shape[0]):
            out[i] = product[:, i * LANES : (i + 1) * LANES]


def expert_wgrads(xs, gs, hgs, hus, acts):
    rows = xs[0].shape[0]
    count = 4
    wide = count * LANES
    steps = hgs[0].shape[1] // wide
    hidden = pl.BlockSpec((rows, wide), lambda i: (0, i))
    whole = lambda width: pl.BlockSpec((rows, width), lambda i: (0, 0))
    weight = pl.BlockSpec((count, D, LANES), lambda i: (i, 0, 0))
    return pl.pallas_call(
        expert_wgrad_kernel,
        grid=(steps,),
        out_shape=(jax.ShapeDtypeStruct((steps * count, D, LANES), BF16),) * 3,
        in_specs=[whole(D + LANES)] * 4 + [whole(D)] * 4 + [hidden] * 12,
        out_specs=(weight,) * 3,
        scratch_shapes=[pltpu.VMEM((D, 4 * rows), BF16), pltpu.VMEM((D, 4 * rows), BF16)],
        compiler_params=pltpu.CompilerParams(vmem_limit_bytes=48 * MIB),
        cost_estimate=pl.CostEstimate(flops=26 * 10**9, bytes_accessed=56 * MIB, transcendentals=0),
    )(*xs, *gs, *hgs, *hus, *acts)


def turn_kernel(
    back_ref, gates_ref, kept_ref, resid_ref, gain_ref, g_ref, wr_ref, wo_ref, send_ref,
    resid_grad_ref, branch_ref, mixed_grad_ref, small_ref,
):
    rows = resid_ref.shape[0]
    gates = gates_ref[...]
    gate_grad = back_ref[:, D:].astype(F32) * kept_ref[...]
    logit_grad = gates * (gate_grad - jnp.sum(gates * gate_grad, axis=1, keepdims=True))
    logit_grad = logit_grad.astype(BF16)
    moe_grad = back_ref[:, :D].astype(F32) + dot_nt(logit_grad, wr_ref[...])
    resid = resid_ref[...]
    scale = lax.rsqrt(jnp.mean(resid * resid, axis=1, keepdims=True) + EPS)
    normed = resid * scale
    small_ref[LANES:, :] = jnp.broadcast_to(jnp.sum(moe_grad * normed, axis=0, keepdims=True), (8, D))
    small_ref[:LANES, :] = dot_tn(logit_grad, send_ref[:, :D])
    inner = moe_grad * gain_ref[...]
    grad = g_ref[...].astype(F32) + scale * (inner - normed * jnp.mean(inner * normed, axis=1, keepdims=True))
    resid_grad_ref[...] = grad
    branch = grad.astype(BF16)
    branch_ref[...] = branch
    for part in range(4):
        mixed_grad_ref[pl.ds(part * rows, rows), :] = dot_nt(
            branch, wo_ref[part * 256 : (part + 1) * 256, :]
        ).astype(BF16)


def turn(back, gates, kept, resid, gain, g, wr, wo, send):
    rows = resid.shape[0]
    shapes = (
        jax.ShapeDtypeStruct((rows, D), F32),
        jax.ShapeDtypeStruct((rows, D), BF16),
        jax.ShapeDtypeStruct((4 * rows, 256), BF16),
        jax.ShapeDtypeStruct((LANES + 8, D), F32),
    )
    return pl.pallas_call(
        turn_kernel,
        out_shape=shapes,
        in_specs=[in_vmem()] * 9,
        out_specs=tuple(in_vmem() for _ in shapes),
        compiler_params=pltpu.CompilerParams(vmem_limit_bytes=32 * MIB),
        cost_estimate=pl.CostEstimate(flops=10**9, bytes_accessed=7 * MIB, transcendentals=10**5),
    )(back, gates, kept, resid, gain, g, wr, wo, send)


def ring_gather(value, n_col):
    steps = [(i, (i + 1) % n_col) for i in range(n_col)]
    chunks = [value]
    for _ in range(n_col - 1):
        chunks.append(lax.ppermute(chunks[-1], "col", steps))
    return chunks


def ring_sum(parts, n_col):
    steps = [(i, (i + 1) % n_col) for i in range(n_col)]
    total = parts[1]
    for part in parts[2:] + parts[:1]:
        total = lax.ppermute(total, "col", steps).astype(F32) + part.astype(F32)
        if part is not parts[0]:
            total = total.astype(BF16)
    return total


def fast(
    block_in,
    attn_gain,
    moe_gain,
    w_query,
    w_key,
    w_value,
    w_out,
    w_router,
    w_gate,
    w_up,
    w_down,
    expert_ids,
    fill_order,
    prefix_len,
    out_grad,
):
    rows = block_in.shape[0]
    n_col = lax.axis_size("col")
    col = lax.axis_index("col")
    seq = rows * n_col
    spots = jnp.stack([col.astype(jnp.int32), prefix_len[0]])
    w_qkv = lax.all_gather(jnp.concatenate([w_query, w_key, w_value], axis=1), "row", axis=0, tiled=True)
    gains = lax.all_gather(jnp.stack([attn_gain, moe_gain]), "row", axis=1, tiled=True).astype(F32)
    gain_one, gain_two = gains[:1], gains[1:]
    wo_col = lax.all_gather(w_out, "col", axis=1, tiled=True)
    wr_col = lax.all_gather(w_router, "col", axis=1, tiled=True)
    wo_wr = jnp.concatenate([wo_col, jnp.pad(wr_col, ((0, 0), (0, LANES - E)))], axis=1)
    wo_wr = lax.all_gather(wo_wr, "row", axis=0, tiled=True)
    wo, wr = wo_wr[:, :D], wo_wr[:, D:]
    cosine, sine = rope_tables(0, seq)
    cosine = jnp.tile(cosine, (1, 4))
    sine = jnp.concatenate([-sine, sine, -sine, sine], axis=1)

    x_chunks = ring_gather(block_in, n_col)
    attn_in, mixed, q, k, v, lse = attend(spots, x_chunks, gain_one, w_qkv, cosine, sine)
    mixed_own = lax.all_to_all(mixed, "col", split_axis=0, concat_axis=0, tiled=True)
    resid, send, gates, kept = route(mixed_own, block_in, wo, gain_two, wr, expert_ids, fill_order)

    wg = lax.all_gather(w_gate, "row", axis=0, tiled=True)
    wu = lax.all_gather(w_up, "row", axis=0, tiled=True)
    wd = lax.all_gather(w_down, "row", axis=0, tiled=True)
    g_chunks = ring_gather(out_grad, n_col)
    send_chunks = ring_gather(send, n_col)
    results = [experts(x, g, wg, wu, wd) for x, g in zip(send_chunks, g_chunks)]
    back = ring_sum([result[1] for result in results], n_col).astype(BF16)
    resid_grad, branch, mixed_grad, small = turn(back, gates, kept, resid, gain_two, out_grad, wr, wo, send)
    mixed_grads = lax.all_to_all(mixed_grad, "col", split_axis=0, concat_axis=0, tiled=True)
    qkv_wgrad, attn_back, gain_one_part = attend_back(
        spots, mixed_grads, mixed, q, k, v, lse, attn_in, w_qkv, cosine, sine, gain_one
    )
    back_parts = [
        lax.dynamic_slice(attn_back, (lax.rem(col - s + n_col, n_col) * rows, 0), (rows, D)) for s in range(n_col)
    ]
    attn_grad = ring_sum(back_parts, n_col)
    x_rows = block_in.astype(F32)
    scale = lax.rsqrt(jnp.mean(x_rows * x_rows, axis=1, keepdims=True) + EPS)
    normed = x_rows * scale
    inner = attn_grad * gain_one
    block_in_grad = resid_grad + scale * (inner - normed * jnp.mean(inner * normed, axis=1, keepdims=True))
    block_out = resid + ring_sum([result[0] for result in results], n_col)

    wgrads = expert_wgrads(
        send_chunks, g_chunks, [t[2] for t in results], [t[3] for t in results], [t[4] for t in results]
    )
    gate_sum, up_sum, down_sum = (
        lax.psum_scatter(part, "row", scatter_dimension=0, tiled=True).astype(F32) for part in wgrads
    )
    mixed_flat = mixed_own.reshape(n_col, rows, 256).transpose(1, 0, 2).reshape(rows, D)
    out_wgrad = cross_rows(mixed_flat, branch).astype(BF16)
    qkv_sum = lax.psum_scatter(qkv_wgrad, "row", scatter_dimension=0, tiled=True).astype(F32)
    out_sum = lax.psum_scatter(out_wgrad, "row", scatter_dimension=0, tiled=True)
    out_sum = lax.psum_scatter(out_sum, "col", scatter_dimension=1, tiled=True).astype(F32)
    gain_both = jnp.concatenate([small[LANES : LANES + 1], gain_one_part], axis=0)
    rest = jnp.concatenate([small[:E], gain_both], axis=0)
    rest = lax.psum(rest, ("row", "col"))
    row = lax.axis_index("row")
    own = lax.dynamic_slice(rest, (0, row * LANES), (E + 2, LANES))
    router_sum = lax.dynamic_slice(own, (col * 8, 0), (8, LANES)).T
    return (
        block_out,
        block_in_grad,
        own[E + 1],
        own[E],
        qkv_sum[:, :256],
        qkv_sum[:, 256:384],
        qkv_sum[:, 384:],
        out_sum,
        router_sum,
        gate_sum,
        up_sum,
        down_sum,
    )


def takes_fast(mesh):
    n_row, n_col = mesh.shape["row"], mesh.shape["col"]
    return n_row == 8 and n_col == 4


def solution(mesh):
    in_specs = (
        P(("row", "col"), None),
        P("row"),
        P("row"),
        P("row", "col"),
        P("row", "col"),
        P("row", "col"),
        P("row", "col"),
        P("row", "col"),
        P("row", None, "col"),
        P("row", None, "col"),
        P("row", None, "col"),
        P(("row", "col"), None),
        P(("row", "col"), None),
        P("row"),
        P(("row", "col"), None),
    )
    out_specs = (
        P(("row", "col"), None),
        P(("row", "col"), None),
        P("row"),
        P("row"),
        P("row", "col"),
        P("row", "col"),
        P("row", "col"),
        P("row", "col"),
        P("row", "col"),
        P("row", None, "col"),
        P("row", None, "col"),
        P("row", None, "col"),
    )
    local = fast if takes_fast(mesh) else general
    return jax.shard_map(local, mesh=mesh, in_specs=in_specs, out_specs=out_specs, check_vma=False)
```

```python
import functools

import jax
import jax.numpy as jnp
from jax import lax
from jax.experimental import pallas as pl
from jax.experimental.pallas import tpu as pltpu
from jax.sharding import PartitionSpec as P

D = 1024
H = 16
KVH = 8
HD = 64
E = 32
TOPK = 8
CAP = 80


EPS = 1e-06
NEGATIVE = -1e30


def cross_rows(left, right):
    return lax.dot_general(
        left, right, (((0,), (0,)), ((), ())), preferred_element_type=jnp.float32
    )


def times_back(left, right):
    return lax.dot_general(
        left, right, (((1,), (1,)), ((), ())), preferred_element_type=jnp.float32
    )


def rope_tables(first_position, count):
    position = (first_position + jnp.arange(count, dtype=jnp.int32)).astype(jnp.float32)
    inverse = 10000.0 ** (-jnp.arange(HD // 2, dtype=jnp.float32) * 2.0 / HD)
    angle = position[:, None] * inverse[None, :]
    return (jnp.cos(angle), jnp.sin(angle))


def rotate(values, cosine, sine):
    half = HD // 2
    first, second = (values[..., :half], values[..., half:])
    cos_rows = cosine[:, None, :]
    sin_rows = sine[:, None, :]
    return jnp.concatenate(
        [first * cos_rows - second * sin_rows, second * cos_rows + first * sin_rows], axis=-1
    )


def rotate_back(grads, cosine, sine):
    half = HD // 2
    first, second = (grads[..., :half], grads[..., half:])
    cos_rows = cosine[:, None, :]
    sin_rows = sine[:, None, :]
    return jnp.concatenate(
        [first * cos_rows + second * sin_rows, second * cos_rows - first * sin_rows], axis=-1
    )


def norm_rows(values, gain):
    scale = lax.rsqrt(jnp.mean(values * values, axis=1, keepdims=True) + EPS)
    normed = values * scale
    return (normed, scale, (normed * gain).astype(jnp.bfloat16))


def norm_back(grad_in, normed, scale, gain):
    gain_grad = jnp.sum(grad_in * normed, axis=0)
    inner = grad_in * gain
    return (scale * (inner - normed * jnp.mean(inner * normed, axis=1, keepdims=True)), gain_grad)


def to_heads(rows, count, group):
    return rows.reshape(count, KVH, group, HD).transpose(1, 2, 0, 3).reshape(KVH, group * count, HD)


def from_heads(heads, count, group):
    return heads.reshape(KVH, group, count, HD).transpose(2, 0, 1, 3).reshape(count, H, HD)


def general(
    block_in,
    attn_gain,
    moe_gain,
    w_query,
    w_key,
    w_value,
    w_out,
    w_router,
    w_gate,
    w_up,
    w_down,
    expert_ids,
    fill_order,
    prefix_len,
    out_grad,
):
    tok_rows = block_in.shape[0]
    n_col = lax.axis_size("col")
    col_index = lax.axis_index("col")
    seq_rows = tok_rows * n_col
    group = H // KVH
    scale_attn = HD ** (-0.5)
    bf16 = jnp.bfloat16
    f32 = jnp.float32
    shared = (
        lax.all_gather(w_query, "row", axis=0, tiled=True),
        lax.all_gather(w_key, "row", axis=0, tiled=True),
        lax.all_gather(w_value, "row", axis=0, tiled=True),
        lax.all_gather(w_out, "row", axis=0, tiled=True),
        lax.all_gather(w_router, "row", axis=0, tiled=True),
        lax.all_gather(attn_gain, "row", axis=0, tiled=True),
        lax.all_gather(moe_gain, "row", axis=0, tiled=True),
    )
    wq_full, wk_full, wv_full, wo_full, wr_full = (
        lax.all_gather(shared[0], "col", axis=1, tiled=True),
        lax.all_gather(shared[1], "col", axis=1, tiled=True),
        lax.all_gather(shared[2], "col", axis=1, tiled=True),
        lax.all_gather(shared[3], "col", axis=1, tiled=True),
        lax.all_gather(shared[4], "col", axis=1, tiled=True),
    )
    gain_one = shared[5].astype(f32)
    gain_two = shared[6].astype(f32)
    x_rows = block_in.astype(f32)
    normed_one, scale_one, attn_in = norm_rows(x_rows, gain_one)
    query = jnp.dot(attn_in, wq_full, preferred_element_type=f32)
    key = jnp.dot(attn_in, wk_full, preferred_element_type=f32)
    value = jnp.dot(attn_in, wv_full, preferred_element_type=f32).astype(bf16)
    cosine, sine = rope_tables(col_index * tok_rows, tok_rows)
    query_rot = rotate(query.reshape(tok_rows, H, HD), cosine, sine).astype(bf16)
    key_rot = (
        rotate(key.reshape(tok_rows, KVH, HD), cosine, sine)
        .astype(bf16)
        .reshape(tok_rows, KVH * HD)
    )
    keys_all, values_all = (
        lax.all_gather(key_rot, "col", axis=0, tiled=True),
        lax.all_gather(value, "col", axis=0, tiled=True),
    )
    prefix = prefix_len[0]
    query_spot = col_index * tok_rows + jnp.arange(tok_rows, dtype=jnp.int32)
    key_spot = jnp.arange(seq_rows, dtype=jnp.int32)
    allowed = (key_spot[None, :] <= query_spot[:, None]) | (key_spot[None, :] < prefix)
    allowed_rows = jnp.tile(allowed, (group, 1))
    query_heads = to_heads(query_rot.reshape(tok_rows, H * HD), tok_rows, group)
    key_heads = keys_all.reshape(seq_rows, KVH, HD).transpose(1, 0, 2)
    value_heads = values_all.reshape(seq_rows, KVH, HD).transpose(1, 0, 2)

    def attend(pieces):
        queries, keys, values = pieces
        scores = times_back(queries, keys) * scale_attn
        scores = jnp.where(allowed_rows, scores, NEGATIVE)
        highest = jnp.max(scores, axis=1, keepdims=True)
        expo = jnp.exp(scores - highest)
        total = jnp.sum(expo, axis=1, keepdims=True)
        weights = (expo / total).astype(bf16)
        mixed_heads = jnp.dot(weights, values, preferred_element_type=f32).astype(bf16)
        return (mixed_heads, (highest + jnp.log(total))[:, 0])

    mixed_heads, lse_heads = lax.map(attend, (query_heads, key_heads, value_heads))
    mixed = from_heads(mixed_heads, tok_rows, group).reshape(tok_rows, H * HD)
    resid = x_rows + jnp.dot(mixed, wo_full, preferred_element_type=f32)
    normed_two, scale_two, moe_in = norm_rows(resid, gain_two)
    logits = jnp.dot(moe_in, wr_full, preferred_element_type=f32)
    choice_hot = (expert_ids[:, :, None] == jnp.arange(E, dtype=jnp.int32)).astype(f32)
    picked = jnp.sum(choice_hot * logits[:, None, :], axis=2)
    highest = jnp.max(picked, axis=1, keepdims=True)
    expo = jnp.exp(picked - highest)
    gates = expo / jnp.sum(expo, axis=1, keepdims=True)
    order = fill_order[0]
    ranked = expert_ids[order]
    onehot = (ranked.reshape(-1, 1) == jnp.arange(E, dtype=jnp.int32)).astype(jnp.int32)
    before = jnp.cumsum(onehot, axis=0) - onehot
    ranked_slot = jnp.sum(before * onehot, axis=1).reshape(tok_rows, TOPK)
    slot = jnp.zeros((tok_rows, TOPK), jnp.int32).at[order].set(ranked_slot)
    kept = slot < CAP
    dest_grid = jnp.where(kept, expert_ids * CAP + slot, E * CAP)
    pair_ids = jnp.arange(tok_rows * TOPK, dtype=jnp.int32)
    slot_pair = (
        jnp.full((E * CAP + 1,), tok_rows * TOPK, jnp.int32)
        .at[dest_grid.reshape(-1)]
        .set(pair_ids)[: E * CAP]
    )
    slot_token = slot_pair // TOPK
    gate_slot = jnp.concatenate([gates.reshape(-1), jnp.zeros((1,), f32)])[slot_pair]
    moe_pad = jnp.concatenate([moe_in, jnp.zeros((1, D), bf16)])
    dispatch = moe_pad[slot_token].reshape(E, CAP, D)
    received = lax.all_to_all(dispatch, "row", split_axis=0, concat_axis=1, tiled=True)
    gate_w, up_w, down_w = (
        lax.all_gather(w_gate, "col", axis=2, tiled=True),
        lax.all_gather(w_up, "col", axis=2, tiled=True),
        lax.all_gather(w_down, "col", axis=2, tiled=True),
    )
    hidden_gate = jnp.einsum("erd,edf->erf", received, gate_w, preferred_element_type=f32)
    hidden_up = jnp.einsum("erd,edf->erf", received, up_w, preferred_element_type=f32)
    active = (jax.nn.silu(hidden_gate) * hidden_up).astype(bf16)
    expert_out = jnp.einsum("erf,edf->erd", active, down_w, preferred_element_type=f32).astype(bf16)
    returned = lax.all_to_all(expert_out, "row", split_axis=1, concat_axis=0, tiled=True)
    out_pad = jnp.concatenate([returned.reshape(E * CAP, D), jnp.zeros((1, D), bf16)])
    pair_out = out_pad[dest_grid]
    weight_pair = gates * kept.astype(f32)
    moe_out = jnp.zeros((tok_rows, D), f32)
    for choice_index in range(TOPK):
        moe_out = moe_out + weight_pair[:, choice_index : choice_index + 1] * pair_out[
            :, choice_index
        ].astype(f32)
    block_out = resid + moe_out
    grad_out = out_grad.astype(f32)
    gate_grad = jnp.stack(
        [
            jnp.sum(pair_out[:, choice_index].astype(f32) * grad_out, axis=1)
            for choice_index in range(TOPK)
        ],
        axis=1,
    )
    grad_pad = jnp.concatenate([grad_out, jnp.zeros((1, D), f32)])
    slot_grad = (gate_slot[:, None] * grad_pad[slot_token]).astype(bf16).reshape(E, CAP, D)
    out_grads = lax.all_to_all(slot_grad, "row", split_axis=0, concat_axis=1, tiled=True)
    act_grad = jnp.einsum("erd,edf->erf", out_grads, down_w, preferred_element_type=f32)
    sigma = jax.nn.sigmoid(hidden_gate)
    gate_h_grad = (act_grad * hidden_up * sigma * (1.0 + hidden_gate * (1.0 - sigma))).astype(bf16)
    up_h_grad = (act_grad * hidden_gate * sigma).astype(bf16)
    down_wgrad = jnp.einsum("erd,erf->edf", out_grads, active, preferred_element_type=f32)
    gate_wgrad = jnp.einsum("erd,erf->edf", received, gate_h_grad, preferred_element_type=f32)
    up_wgrad = jnp.einsum("erd,erf->edf", received, up_h_grad, preferred_element_type=f32)
    in_grad = (
        jnp.einsum("erf,edf->erd", gate_h_grad, gate_w, preferred_element_type=f32)
        + jnp.einsum("erf,edf->erd", up_h_grad, up_w, preferred_element_type=f32)
    ).astype(bf16)
    back_rows = lax.all_to_all(in_grad, "row", split_axis=1, concat_axis=0, tiled=True)
    gate_sum, up_sum, down_sum = (
        lax.psum_scatter(
            gate_wgrad.astype(jnp.bfloat16), "col", scatter_dimension=2, tiled=True
        ).astype(jnp.float32),
        lax.psum_scatter(
            up_wgrad.astype(jnp.bfloat16), "col", scatter_dimension=2, tiled=True
        ).astype(jnp.float32),
        lax.psum_scatter(
            down_wgrad.astype(jnp.bfloat16), "col", scatter_dimension=2, tiled=True
        ).astype(jnp.float32),
    )
    back_pad = jnp.concatenate([back_rows.reshape(E * CAP, D), jnp.zeros((1, D), bf16)])
    pair_back = back_pad[dest_grid]
    moe_in_grad = jnp.zeros((tok_rows, D), f32)
    for choice_index in range(TOPK):
        moe_in_grad = moe_in_grad + pair_back[:, choice_index].astype(f32)
    picked_grad = gates * (gate_grad - jnp.sum(gates * gate_grad, axis=1, keepdims=True))
    logit_grad = jnp.sum(choice_hot * picked_grad[:, :, None], axis=1).astype(bf16)
    router_wgrad = cross_rows(moe_in, logit_grad)
    moe_in_grad = moe_in_grad + times_back(logit_grad, wr_full)
    norm_two_grad, gain_two_grad = norm_back(moe_in_grad, normed_two, scale_two, gain_two)
    resid_grad = grad_out + norm_two_grad
    branch_grad = resid_grad.astype(bf16)
    out_wgrad = cross_rows(mixed, branch_grad)
    mixed_grad = times_back(branch_grad, wo_full).astype(bf16)
    grad_heads = to_heads(mixed_grad, tok_rows, group)

    def query_side(pieces):
        queries, keys, values, lse_rows, grad_rows = pieces
        scores = jnp.where(allowed_rows, times_back(queries, keys) * scale_attn, NEGATIVE)
        probs = jnp.exp(scores - lse_rows[:, None])
        prob_grad = times_back(grad_rows, values)
        delta = jnp.sum(probs * prob_grad, axis=1, keepdims=True)
        score_grad = (probs * (prob_grad - delta)).astype(bf16)
        query_grad = jnp.dot(score_grad, keys, preferred_element_type=f32) * scale_attn
        return (query_grad, delta[:, 0], score_grad, probs)

    def both_sides(pieces):
        queries, keys, values, lse_rows, grad_rows = pieces
        query_grad, delta, score_grad, probs = query_side(pieces)
        key_grad = cross_rows(score_grad, queries) * scale_attn
        value_grad = cross_rows(probs.astype(bf16), grad_rows)
        return (query_grad, key_grad, value_grad)

    query_rot_grad, key_parts, value_parts = lax.map(
        both_sides, (query_heads, key_heads, value_heads, lse_heads, grad_heads)
    )
    key_rot_grad, value_grad = (
        lax.psum_scatter(
            key_parts.transpose(1, 0, 2).reshape(seq_rows, KVH * HD).astype(jnp.bfloat16),
            "col",
            scatter_dimension=0,
            tiled=True,
        ).astype(jnp.float32),
        lax.psum_scatter(
            value_parts.transpose(1, 0, 2).reshape(seq_rows, KVH * HD).astype(jnp.bfloat16),
            "col",
            scatter_dimension=0,
            tiled=True,
        ).astype(jnp.float32),
    )
    query_grad = (
        rotate_back(from_heads(query_rot_grad, tok_rows, group), cosine, sine)
        .reshape(tok_rows, H * HD)
        .astype(bf16)
    )
    key_grad = (
        rotate_back(key_rot_grad.reshape(tok_rows, KVH, HD), cosine, sine)
        .reshape(tok_rows, KVH * HD)
        .astype(bf16)
    )
    value_grad = value_grad.astype(bf16)
    query_wgrad = cross_rows(attn_in, query_grad)
    key_wgrad = cross_rows(attn_in, key_grad)
    value_wgrad = cross_rows(attn_in, value_grad)
    attn_in_grad = (
        times_back(query_grad, wq_full)
        + times_back(key_grad, wk_full)
        + times_back(value_grad, wv_full)
    )
    norm_one_grad, gain_one_grad = norm_back(attn_in_grad, normed_one, scale_one, gain_one)
    block_in_grad = resid_grad + norm_one_grad
    spread_one = jnp.broadcast_to(gain_one_grad[:, None], (D, n_col))
    spread_two = jnp.broadcast_to(gain_two_grad[:, None], (D, n_col))
    col_sums = (
        lax.psum_scatter(
            query_wgrad.astype(jnp.bfloat16), "col", scatter_dimension=1, tiled=True
        ).astype(jnp.float32),
        lax.psum_scatter(
            key_wgrad.astype(jnp.bfloat16), "col", scatter_dimension=1, tiled=True
        ).astype(jnp.float32),
        lax.psum_scatter(
            value_wgrad.astype(jnp.bfloat16), "col", scatter_dimension=1, tiled=True
        ).astype(jnp.float32),
        lax.psum_scatter(
            out_wgrad.astype(jnp.bfloat16), "col", scatter_dimension=1, tiled=True
        ).astype(jnp.float32),
        lax.psum_scatter(
            router_wgrad.astype(jnp.bfloat16), "col", scatter_dimension=1, tiled=True
        ).astype(jnp.float32),
        lax.psum_scatter(
            spread_one.astype(jnp.bfloat16), "col", scatter_dimension=1, tiled=True
        ).astype(jnp.float32),
        lax.psum_scatter(
            spread_two.astype(jnp.bfloat16), "col", scatter_dimension=1, tiled=True
        ).astype(jnp.float32),
    )
    row_sums = (
        lax.psum_scatter(
            col_sums[0].astype(jnp.bfloat16), "row", scatter_dimension=0, tiled=True
        ).astype(jnp.float32),
        lax.psum_scatter(
            col_sums[1].astype(jnp.bfloat16), "row", scatter_dimension=0, tiled=True
        ).astype(jnp.float32),
        lax.psum_scatter(
            col_sums[2].astype(jnp.bfloat16), "row", scatter_dimension=0, tiled=True
        ).astype(jnp.float32),
        lax.psum_scatter(
            col_sums[3].astype(jnp.bfloat16), "row", scatter_dimension=0, tiled=True
        ).astype(jnp.float32),
        lax.psum_scatter(
            col_sums[4].astype(jnp.bfloat16), "row", scatter_dimension=0, tiled=True
        ).astype(jnp.float32),
        lax.psum_scatter(
            col_sums[5].astype(jnp.bfloat16), "row", scatter_dimension=0, tiled=True
        ).astype(jnp.float32),
        lax.psum_scatter(
            col_sums[6].astype(jnp.bfloat16), "row", scatter_dimension=0, tiled=True
        ).astype(jnp.float32),
    )
    return (
        block_out,
        block_in_grad,
        row_sums[5][:, 0],
        row_sums[6][:, 0],
        row_sums[0],
        row_sums[1],
        row_sums[2],
        row_sums[3],
        row_sums[4],
        gate_sum,
        up_sum,
        down_sum,
    )


F32 = jnp.float32
BF16 = jnp.bfloat16
MIB = 1024 * 1024
LANES = 128


def dot_nn(a, b):
    return lax.dot_general(a, b, (((1,), (0,)), ((), ())), preferred_element_type=F32)


def dot_nt(a, b):
    return lax.dot_general(a, b, (((1,), (1,)), ((), ())), preferred_element_type=F32)


def dot_tn(a, b):
    return lax.dot_general(a, b, (((0,), (0,)), ((), ())), preferred_element_type=F32)


def in_vmem():
    return pl.BlockSpec(memory_space=pltpu.VMEM)


def in_smem():
    return pl.BlockSpec(memory_space=pltpu.SMEM)


def partner(values):
    lane = lax.broadcasted_iota(jnp.int32, values.shape, 1)
    half = HD // 2
    return jnp.where(
        lane % HD < half,
        pltpu.roll(values, LANES - half, 1),
        pltpu.roll(values, half, 1),
    )


def attend_kernel(
    spot_ref, x0, x1, x2, x3, pack_ref, cos_ref, sin_ref,
    attn_ref, mixed_ref, q_ref, k_ref, v_ref, lse_ref, w_ref, gain_ref,
):
    rows = x0.shape[0]
    col, prefix = spot_ref[0], spot_ref[1]
    for part in range(8):
        span = pl.ds(part * LANES, LANES)
        w_ref[span, :] = pack_ref[part, :LANES, :]
        gain_ref[0:1, span] = pack_ref[part, LANES : LANES + 1, :LANES].astype(F32)
        gain_ref[1:2, span] = pack_ref[part, LANES : LANES + 1, LANES : 2 * LANES].astype(F32)
    gain = gain_ref[0:1, :]
    for step, chunk in enumerate((x0, x1, x2, x3)):
        source = lax.rem(col - step + 4, 4)
        x = chunk[...].astype(F32)
        scale = lax.rsqrt(jnp.mean(x * x, axis=1, keepdims=True) + EPS)
        attn_ref[pl.ds(pl.multiple_of(source * rows, rows), rows), :] = (x * scale * gain).astype(BF16)
    for tile in range(4):
        span = pl.ds(tile * rows, rows)
        qkv = dot_nn(attn_ref[span, :], w_ref[...])
        cosine, sine = cos_ref[span, :], sin_ref[span, :]
        for block in range(3):
            v = qkv[:, block * LANES : (block + 1) * LANES]
            y = v * cosine + partner(v) * sine
            if block < 2:
                y = (y * HD ** (-0.5)).astype(BF16)
                q_ref[2 * block, span, :] = y[:, :HD]
                q_ref[2 * block + 1, span, :] = y[:, HD:]
            else:
                y = y.astype(BF16)
                k_ref[0, span, :] = y[:, :HD]
                k_ref[1, span, :] = y[:, HD:]
        v = qkv[:, 3 * LANES :].astype(BF16)
        v_ref[0, span, :] = v[:, :HD]
        v_ref[1, span, :] = v[:, HD:]
    total = 4 * rows
    for tile in range(4):
        span = pl.ds(tile * rows, rows)
        keys = max((tile + 1) * rows, total // 2)
        key_spot = lax.broadcasted_iota(jnp.int32, (rows, keys), 1)
        query_spot = lax.broadcasted_iota(jnp.int32, (rows, keys), 0) + tile * rows
        allowed = (key_spot <= query_spot) | (key_spot < prefix)
        for pair in range(2):
            k, v = k_ref[pair, pl.ds(0, keys), :], v_ref[pair, pl.ds(0, keys), :]
            outs = []
            for head in (2 * pair, 2 * pair + 1):
                scores = jnp.where(allowed, dot_nt(q_ref[head, span, :], k), NEGATIVE)
                highest = jnp.max(scores, axis=1, keepdims=True)
                expo = jnp.exp(scores - highest)
                summed = jnp.sum(expo, axis=1, keepdims=True)
                outs.append(dot_nn(expo.astype(BF16), v) * (1.0 / summed))
                lse_ref[span, head : head + 1] = highest + jnp.log(summed)
            mixed_ref[span, pair * LANES : (pair + 1) * LANES] = jnp.concatenate(outs, axis=1).astype(BF16)


def attend(spots, chunks, pack, cosine, sine):
    rows = chunks[0].shape[0]
    seq = 4 * rows
    shapes = (
        jax.ShapeDtypeStruct((seq, D), BF16),
        jax.ShapeDtypeStruct((seq, 256), BF16),
        jax.ShapeDtypeStruct((4, seq, HD), BF16),
        jax.ShapeDtypeStruct((2, seq, HD), BF16),
        jax.ShapeDtypeStruct((2, seq, HD), BF16),
        jax.ShapeDtypeStruct((seq, 4), F32),
        jax.ShapeDtypeStruct((D, 512), BF16),
        jax.ShapeDtypeStruct((2, D), F32),
    )
    return pl.pallas_call(
        attend_kernel,
        out_shape=shapes,
        in_specs=[in_smem()] + [in_vmem()] * 7,
        out_specs=tuple(in_vmem() for _ in shapes),
        compiler_params=pltpu.CompilerParams(vmem_limit_bytes=40 * MIB),
        cost_estimate=pl.CostEstimate(flops=4 * 10**9, bytes_accessed=8 * MIB, transcendentals=3 * 10**6),
    )(spots, *chunks, pack, cosine, sine)


def attend_back_kernel(
    spot_ref, grad_ref, mixed_ref, q_ref, k_ref, v_ref, lse_ref, attn_ref, w_ref, cos_ref, sin_ref, gain_ref,
    wgrad_ref, in0, in1, in2, in3, dqkv_ref, dk_ref, dv_ref, dq_ref, mg_ref,
):
    seq = attn_ref.shape[0]
    rows = seq // 4
    prefix = spot_ref[1]
    for tile in range(4):
        span = pl.ds(tile * rows, rows)
        for pair in range(2):
            g = grad_ref[span, pair * LANES : (pair + 1) * LANES]
            mg_ref[2 * pair, span, :] = g[:, :HD]
            mg_ref[2 * pair + 1, span, :] = g[:, HD:]
    dk_ref[...] = jnp.zeros_like(dk_ref)
    dv_ref[...] = jnp.zeros_like(dv_ref)
    for tile in range(4):
        span = pl.ds(tile * rows, rows)
        keys = max((tile + 1) * rows, seq // 2)
        key_spot = lax.broadcasted_iota(jnp.int32, (rows, keys), 1)
        query_spot = lax.broadcasted_iota(jnp.int32, (rows, keys), 0) + tile * rows
        allowed = (key_spot <= query_spot) | (key_spot < prefix)
        for pair in range(2):
            k, v = k_ref[pair, pl.ds(0, keys), :], v_ref[pair, pl.ds(0, keys), :]
            both = grad_ref[span, pair * LANES : (pair + 1) * LANES].astype(F32) * mixed_ref[
                span, pair * LANES : (pair + 1) * LANES
            ].astype(F32)
            outs = []
            for at, head in enumerate((2 * pair, 2 * pair + 1)):
                q, g = q_ref[head, span, :], mg_ref[head, span, :]
                delta = jnp.sum(both[:, at * HD : (at + 1) * HD], axis=1, keepdims=True)
                scores = jnp.where(allowed, dot_nt(q, k), NEGATIVE)
                probs = jnp.exp(scores - lse_ref[span, head : head + 1])
                score_grad = (probs * (dot_nt(g, v) - delta)).astype(BF16)
                dv_ref[pair, pl.ds(0, keys), :] += dot_tn(probs.astype(BF16), g)
                dk_ref[pair, pl.ds(0, keys), :] += dot_tn(score_grad, q)
                outs.append(dot_nn(score_grad, k) * HD ** (-0.5))
            dq_ref[span, pair * LANES : (pair + 1) * LANES] = jnp.concatenate(outs, axis=1)
    for tile in range(4):
        span = pl.ds(tile * rows, rows)
        cosine, sine = cos_ref[span, :], sin_ref[span, :]
        for block in range(3):
            if block < 2:
                g = dq_ref[span, block * LANES : (block + 1) * LANES]
            else:
                g = jnp.concatenate([dk_ref[0, span, :], dk_ref[1, span, :]], axis=1)
            dqkv_ref[span, block * LANES : (block + 1) * LANES] = (g * cosine - partner(g) * sine).astype(BF16)
        dqkv_ref[span, 3 * LANES :] = jnp.concatenate([dv_ref[0, span, :], dv_ref[1, span, :]], axis=1).astype(BF16)
    gain_total = jnp.zeros((1, D), F32)
    for step, out in enumerate((in0, in1, in2, in3)):
        source = lax.rem(spot_ref[0] - step + 4, 4)
        span = pl.ds(pl.multiple_of(source * rows, rows), rows)
        back = dot_nt(dqkv_ref[span, :], w_ref[...])
        out[...] = back.astype(BF16)
        gain_total = gain_total + jnp.sum(back * attn_ref[span, :].astype(F32), axis=0, keepdims=True)
    gain_total = gain_total / gain_ref[0:1, :]
    for part in range(8):
        span = pl.ds(part * LANES, LANES)
        wgrad_ref[part, LANES:, :LANES] = jnp.broadcast_to(gain_total[:, part * LANES : (part + 1) * LANES], (8, LANES)).astype(BF16)
        wgrad_ref[part, LANES:, LANES:] = jnp.zeros((8, 3 * LANES), BF16)
        wgrad_ref[part, :LANES, :] = dot_tn(attn_ref[:, span], dqkv_ref[...]).astype(BF16)


def attend_back(spots, grads, mixed, q, k, v, lse, attn_in, w_qkv, cosine, sine, gain):
    seq = attn_in.shape[0]
    shapes = (
        jax.ShapeDtypeStruct((8, 136, 512), BF16),
    ) + (jax.ShapeDtypeStruct((seq // 4, D), BF16),) * 4
    return pl.pallas_call(
        attend_back_kernel,
        out_shape=shapes,
        in_specs=[in_smem()] + [in_vmem()] * 11,
        out_specs=tuple(in_vmem() for _ in shapes),
        scratch_shapes=[
            pltpu.VMEM((seq, 512), BF16),
            pltpu.VMEM((2, seq, HD), F32),
            pltpu.VMEM((2, seq, HD), F32),
            pltpu.VMEM((seq, 256), F32),
            pltpu.VMEM((4, seq, HD), BF16),
        ],
        compiler_params=pltpu.CompilerParams(vmem_limit_bytes=48 * MIB),
        cost_estimate=pl.CostEstimate(flops=10 * 10**9, bytes_accessed=14 * MIB, transcendentals=3 * 10**6),
    )(spots, grads, mixed, q, k, v, lse, attn_in, w_qkv, cosine, sine, gain)


def route_kernel(
    spot_ref, mixed_ref, x_ref, pack_ref, gain_ref, wr_ref, ids_ref, order_ref,
    resid_ref, send_ref, gates_ref, kept_ref, wo_ref,
):
    rows = x_ref.shape[0]
    for part in range(32):
        wo_ref[pl.ds(part // 4 * LANES, LANES), pl.ds(part % 4 * 256, 256)] = pack_ref[part, :LANES, :]
    resid = x_ref[...].astype(F32)
    for part in range(4):
        resid = resid + dot_nn(mixed_ref[pl.ds(part * rows, rows), :], wo_ref[part * 256 : (part + 1) * 256, :])
    resid_ref[...] = resid
    scale = lax.rsqrt(jnp.mean(resid * resid, axis=1, keepdims=True) + EPS)
    moe_in = (resid * scale * gain_ref[1:2, :]).astype(BF16)
    send_ref[:, :D] = moe_in
    logits = dot_nn(moe_in, wr_ref[...])
    lane = lax.broadcasted_iota(jnp.int32, (rows, LANES), 1)
    chosen = jnp.zeros((rows, LANES), jnp.bool_)
    for choice in range(TOPK):
        chosen = chosen | (ids_ref[:, choice : choice + 1] == lane)
    picked = jnp.where(chosen, logits, NEGATIVE)
    expo = jnp.exp(picked - jnp.max(picked, axis=1, keepdims=True))
    gates = expo / jnp.sum(expo, axis=1, keepdims=True)
    first = lax.broadcasted_iota(jnp.int32, (rows, rows), 0)
    second = lax.broadcasted_iota(jnp.int32, (rows, rows), 1)
    place = (first == order_ref[...]).astype(BF16)
    sooner = dot_nn(place, (second < first).astype(BF16)).astype(BF16)
    sooner = dot_nt(sooner, place).astype(BF16)
    slot = dot_nn(sooner, chosen.astype(BF16))
    kept = (chosen & (slot < CAP)).astype(F32)
    gates_ref[...] = gates
    kept_ref[...] = kept
    send_ref[:, D:] = dot_nn((gates * kept).astype(BF16), relabel(spot_ref[2])).astype(BF16)


def relabel(row):
    first = lax.broadcasted_iota(jnp.int32, (LANES, LANES), 0)
    second = lax.broadcasted_iota(jnp.int32, (LANES, LANES), 1)
    return (first == (second ^ (row * 4))).astype(BF16)


def route(spots, mixed, x, pack, gain, wr, ids, order):
    rows = x.shape[0]
    shapes = (
        jax.ShapeDtypeStruct((rows, D), F32),
        jax.ShapeDtypeStruct((rows, D + LANES), BF16),
        jax.ShapeDtypeStruct((rows, LANES), F32),
        jax.ShapeDtypeStruct((rows, LANES), F32),
        jax.ShapeDtypeStruct((D, D), BF16),
    )
    return pl.pallas_call(
        route_kernel,
        out_shape=shapes,
        in_specs=[in_smem()] + [in_vmem()] * 7,
        out_specs=tuple(in_vmem() for _ in shapes),
        compiler_params=pltpu.CompilerParams(vmem_limit_bytes=32 * MIB),
        cost_estimate=pl.CostEstimate(flops=10**9, bytes_accessed=5 * MIB, transcendentals=10**5),
    )(spots, mixed, x, pack, gain, wr, ids, order)


def expert_kernel(
    x_ref, g_ref, w0, w1, w2, w3, w4, w5, w6a, w6b, w7a, w7b,
    out_ref, back_ref, hg_ref, hu_ref, act_ref, out_acc, in_acc, gate_acc, held, sems,
):
    step = pl.program_id(0)
    count = held.shape[1]
    wide = count * LANES
    sources = ((w0,), (w1,), (w2,), (w3,), (w4,), (w5,), (w6a, w6b), (w7a, w7b))

    def fetch(at, slot):
        for k, parts in enumerate(sources):

            @pl.when(at == k)
            def _():
                size = count // len(parts)
                for i, part in enumerate(parts):
                    pltpu.make_async_copy(part, held.at[slot, pl.ds(i * size, size)], sems.at[slot]).start()

    @pl.when(step == 0)
    def _():
        fetch(step, 0)
        out_acc[...] = jnp.zeros_like(out_acc)
        in_acc[...] = jnp.zeros_like(in_acc)
        gate_acc[...] = jnp.zeros_like(gate_acc)

    now = lax.rem(step, 2)
    pltpu.make_async_copy(w0, held.at[now], sems.at[now]).wait()
    fetch(step + 1, 1 - now)

    join = lambda kind: jnp.concatenate([held[now, i, kind] for i in range(count)], axis=1)
    wg, wu, wd = join(0), join(1), join(2)
    x = x_ref[:, :D]
    expert = lax.broadcasted_iota(jnp.int32, (LANES, wide), 0)
    column = lax.broadcasted_iota(jnp.int32, (LANES, wide), 1)
    spread = (expert == step * count + column // LANES).astype(BF16)
    gate = dot_nn(x_ref[:, D:], spread)
    hidden_gate = dot_nn(x, wg)
    hidden_up = dot_nn(x, wu)
    act_grad = dot_nn(g_ref[...], wd)
    sigma = 0.5 * jnp.tanh(0.5 * hidden_gate) + 0.5
    swish = hidden_gate * sigma
    active = swish * hidden_up
    gate_acc[...] += dot_nt((active * act_grad).astype(BF16), spread)
    gated = (active * gate).astype(BF16)
    act_ref[...] = gated
    out_acc[...] += dot_nt(gated, wd)
    act_grad = act_grad * gate
    up_grad = (act_grad * swish).astype(BF16)
    gate_grad = (act_grad * hidden_up * (sigma + swish * (1.0 - sigma))).astype(BF16)
    hg_ref[...] = gate_grad
    hu_ref[...] = up_grad
    in_acc[...] += dot_nt(gate_grad, wg) + dot_nt(up_grad, wu)

    @pl.when(step == pl.num_programs(0) - 1)
    def _():
        out_ref[...] = out_acc[...].astype(BF16)
        back_ref[:, :D] = in_acc[...].astype(BF16)
        back_ref[:, D:] = gate_acc[...].astype(BF16)


def experts(x, g, weights):
    rows = x.shape[0]
    count = 4
    steps = 8
    wide = count * LANES
    hidden = pl.BlockSpec((rows, wide), lambda i: (0, i))
    whole = lambda width: pl.BlockSpec((rows, width), lambda i: (0, 0))
    return pl.pallas_call(
        expert_kernel,
        grid=(steps,),
        out_shape=(
            jax.ShapeDtypeStruct((rows, D), BF16),
            jax.ShapeDtypeStruct((rows, D + LANES), BF16),
        )
        + (jax.ShapeDtypeStruct((rows, steps * wide), BF16),) * 3,
        in_specs=[whole(D + LANES), whole(D)] + [pl.BlockSpec(memory_space=pl.ANY)] * 10,
        out_specs=(whole(D), whole(D + LANES), hidden, hidden, hidden),
        scratch_shapes=[
            pltpu.VMEM((rows, D), F32),
            pltpu.VMEM((rows, D), F32),
            pltpu.VMEM((rows, LANES), F32),
            pltpu.VMEM((2, count, 3, D, LANES), BF16),
            pltpu.SemaphoreType.DMA((2,)),
        ],
        compiler_params=pltpu.CompilerParams(vmem_limit_bytes=56 * MIB),
        cost_estimate=pl.CostEstimate(flops=20 * 10**9, bytes_accessed=32 * MIB, transcendentals=10**6),
    )(x, g, *weights)


def flip_kernel(x0, x1, x2, x3, g0, g1, g2, g3, xt_ref, gt_ref):
    rows = x0.shape[0]
    for at, (x, g) in enumerate(zip((x0, x1, x2, x3), (g0, g1, g2, g3))):
        xt_ref[:, at * rows : (at + 1) * rows] = x[:, :D].T
        gt_ref[:, at * rows : (at + 1) * rows] = g[...].T


def flip(xs, gs):
    seq = 4 * xs[0].shape[0]
    return pl.pallas_call(
        flip_kernel,
        out_shape=(jax.ShapeDtypeStruct((D, seq), BF16),) * 2,
        in_specs=[in_vmem()] * 8,
        out_specs=(in_vmem(),) * 2,
        compiler_params=pltpu.CompilerParams(vmem_limit_bytes=24 * MIB),
        cost_estimate=pl.CostEstimate(flops=10**9, bytes_accessed=8 * MIB, transcendentals=0),
    )(*xs, *gs)


def expert_wgrad_kernel(places, added, halved, *refs):
    xt_ref, gt_ref = refs[:2]
    hidden = refs[2:14]
    more = refs[14:]
    half = pl.program_id(0) % 2
    extra = more[0] if added else None
    outs = more[1:] if added else more
    for kind, left in enumerate((xt_ref, xt_ref, gt_ref)):
        joined = jnp.concatenate([part[...] for part in hidden[kind * 4 : kind * 4 + 4]], axis=0)
        product = dot_nn(left[...], joined)
        for i in range(2):
            piece = product[:, i * LANES : (i + 1) * LANES]
            if added:
                piece = piece + extra[0, i, kind].astype(F32)
            outs[0][0, i, kind] = piece.astype(BF16)


def expert_wgrads(flipped, hidden, places, extra=None):
    rows = hidden[0][0].shape[0]
    wide = 2 * LANES
    seq = flipped[0].shape[1]
    first = places[0] * 2
    jump = (places[1] - places[0]) * 2 if len(places) > 1 else 0
    lane = pl.BlockSpec((rows, wide), lambda i: (0, first + (i // 2) * jump + i % 2))
    whole = pl.BlockSpec((D, seq), lambda i: (0, 0))
    weight = pl.BlockSpec((1, 2, 3, D, LANES), lambda i: (i, 0, 0, 0, 0))
    steps = 2 * len(places)
    return pl.pallas_call(
        functools.partial(expert_wgrad_kernel, places, extra is not None, False),
        grid=(steps,),
        out_shape=jax.ShapeDtypeStruct((steps, 2, 3, D, LANES), BF16),
        in_specs=[whole] * 2 + [lane] * 12 + ([weight] if extra is not None else []),
        out_specs=weight,
        compiler_params=pltpu.CompilerParams(vmem_limit_bytes=32 * MIB),
        cost_estimate=pl.CostEstimate(
            flops=len(places) * 5 * 10**9, bytes_accessed=(4 + 6 * len(places)) * MIB, transcendentals=0
        ),
    )(*flipped, *hidden[0], *hidden[1], *hidden[2], *(() if extra is None else (extra,)))


def turn_kernel(
    spot_ref, back_ref, gates_ref, kept_ref, resid_ref, gain_ref, g_ref, wr_ref, wo_ref, send_ref,
    resid_grad_ref, branch_ref, mixed_grad_ref, small_ref,
):
    rows = resid_ref.shape[0]
    gates = gates_ref[...]
    gate_grad = dot_nn(back_ref[:, D:], relabel(spot_ref[2])) * kept_ref[...]
    logit_grad = gates * (gate_grad - jnp.sum(gates * gate_grad, axis=1, keepdims=True))
    logit_grad = logit_grad.astype(BF16)
    moe_grad = back_ref[:, :D].astype(F32) + dot_nt(logit_grad, wr_ref[...])
    resid = resid_ref[...]
    scale = lax.rsqrt(jnp.mean(resid * resid, axis=1, keepdims=True) + EPS)
    normed = resid * scale
    small_ref[LANES:, :] = jnp.broadcast_to(jnp.sum(moe_grad * normed, axis=0, keepdims=True), (8, D))
    small_ref[:LANES, :] = dot_tn(logit_grad, send_ref[:, :D])
    inner = moe_grad * gain_ref[1:2, :]
    grad = g_ref[...].astype(F32) + scale * (inner - normed * jnp.mean(inner * normed, axis=1, keepdims=True))
    resid_grad_ref[...] = grad
    branch = grad.astype(BF16)
    branch_ref[...] = branch
    for part in range(4):
        mixed_grad_ref[pl.ds(part * rows, rows), :] = dot_nt(
            branch, wo_ref[part * 256 : (part + 1) * 256, :]
        ).astype(BF16)


def turn(spots, back, gates, kept, resid, gain, g, wr, wo, send):
    rows = resid.shape[0]
    shapes = (
        jax.ShapeDtypeStruct((rows, D), F32),
        jax.ShapeDtypeStruct((rows, D), BF16),
        jax.ShapeDtypeStruct((4 * rows, 256), BF16),
        jax.ShapeDtypeStruct((LANES + 8, D), F32),
    )
    return pl.pallas_call(
        turn_kernel,
        out_shape=shapes,
        in_specs=[in_smem()] + [in_vmem()] * 9,
        out_specs=tuple(in_vmem() for _ in shapes),
        compiler_params=pltpu.CompilerParams(vmem_limit_bytes=32 * MIB),
        cost_estimate=pl.CostEstimate(flops=2 * 10**9, bytes_accessed=7 * MIB, transcendentals=10**5),
    )(spots, back, gates, kept, resid, gain, g, wr, wo, send)


def out_wgrad_kernel(mixed_ref, branch_ref, small_ref, pack_ref):
    rows = branch_ref.shape[0]
    for part in range(4):
        product = dot_tn(mixed_ref[pl.ds(part * rows, rows), :], branch_ref[...]).astype(BF16)
        pack_ref[2 * part, :LANES, :] = product[:LANES]
        pack_ref[2 * part + 1, :LANES, :] = product[LANES:]
    for row in range(8):
        span = pl.ds(row * LANES, LANES)
        for col in range(4):
            pack_ref[row, LANES:, col * 256 : col * 256 + LANES] = small_ref[col * 8 : col * 8 + 8, span].astype(BF16)
            pack_ref[row, LANES:, col * 256 + LANES : col * 256 + 256] = small_ref[LANES:, span].astype(BF16)


def out_wgrad(mixed, branch, small):
    return pl.pallas_call(
        out_wgrad_kernel,
        out_shape=jax.ShapeDtypeStruct((8, LANES + 8, D), BF16),
        in_specs=[in_vmem()] * 3,
        out_specs=in_vmem(),
        compiler_params=pltpu.CompilerParams(vmem_limit_bytes=24 * MIB),
        cost_estimate=pl.CostEstimate(flops=2 * 10**9, bytes_accessed=4 * MIB, transcendentals=0),
    )(mixed, branch, small)


def ring_gather(value, n_col):
    steps = [(i, (i + 1) % n_col) for i in range(n_col)]
    chunks = [value]
    for _ in range(n_col - 1):
        chunks.append(lax.ppermute(chunks[-1], "col", steps))
    return chunks


def ring_sum(parts, n_col):
    steps = [(i, (i + 1) % n_col) for i in range(n_col)]
    total = parts[1]
    for part in parts[2:] + parts[:1]:
        total = lax.ppermute(total, "col", steps).astype(F32) + part.astype(F32)
        if part is not parts[0]:
            total = total.astype(BF16)
    return total


CORE, ACROSS_X, ACROSS_Y = 1, 2, 4


def swap(value, mask):
    return lax.ppermute(value, "row", [(i, i ^ mask) for i in range(8)])


def gather_weights(own):
    from_x, from_y = swap(own, ACROSS_X), swap(own, ACROSS_Y)
    other = swap(own, CORE)
    half = own.shape[0] // 2
    far_a, far_b = swap(from_y[:half], ACROSS_X), swap(from_x[half:], ACROSS_Y)
    return (
        own, other, from_x, swap(from_x, CORE), from_y, swap(from_y, CORE),
        far_a, far_b, swap(far_a, CORE), swap(far_b, CORE),
    )


def sum_weights(flipped, hidden):
    p7 = expert_wgrads(flipped, hidden, (7,))
    r7 = swap(p7, CORE)
    p35 = expert_wgrads(flipped, hidden, (3, 5))
    r35 = swap(p35, CORE)
    q6 = expert_wgrads(flipped, hidden, (6,), r7)
    from_x, from_y = swap(q6[:1], ACROSS_X), swap(q6[1:], ACROSS_Y)
    p1 = expert_wgrads(flipped, hidden, (1,))
    r1 = swap(p1, CORE)
    q24 = expert_wgrads(flipped, hidden, (2, 4), r35)
    q2a, q2b, q4a, q4b = (q24[i : i + 1] for i in range(4))
    from_x2a, from_y4b = swap(q2a, ACROSS_X), swap(q4b, ACROSS_Y)
    add = lambda a, b: (a.astype(F32) + b.astype(F32)).astype(BF16)
    from_x2b = swap(add(q2b, from_y), ACROSS_X)
    from_y4a = swap(add(q4a, from_x), ACROSS_Y)
    q0 = expert_wgrads(flipped, hidden, (0,), r1)
    low = q0[0].astype(F32) + from_x2a[0].astype(F32) + from_y4a[0].astype(F32)
    high = q0[1].astype(F32) + from_x2b[0].astype(F32) + from_y4b[0].astype(F32)
    return low, high


def fast(
    block_in,
    attn_gain,
    moe_gain,
    w_query,
    w_key,
    w_value,
    w_out,
    w_router,
    w_gate,
    w_up,
    w_down,
    expert_ids,
    fill_order,
    prefix_len,
    out_grad,
):
    rows = block_in.shape[0]
    n_col = lax.axis_size("col")
    col = lax.axis_index("col")
    row = lax.axis_index("row")
    seq = rows * n_col
    spots = jnp.stack([col.astype(jnp.int32), prefix_len[0], row.astype(jnp.int32)])
    gains = jnp.concatenate([attn_gain, moe_gain, jnp.zeros((256,), BF16)])[None]
    pack_qkv = jnp.concatenate(
        [jnp.concatenate([w_query, w_key, w_value], axis=1), gains, jnp.zeros((7, 512), BF16)], axis=0
    )
    pack_qkv = lax.all_gather(pack_qkv, "row", axis=0)
    pack_out = jnp.concatenate([w_out, w_router.reshape(4, 256), jnp.zeros((4, 256), BF16)], axis=0)
    pack_out = lax.all_gather(pack_out, ("row", "col"), axis=0)
    wr = pack_out[:, LANES : LANES + 4].reshape(8, 4, LANES, 8).transpose(0, 2, 1, 3).reshape(D, E)
    wr = jnp.pad(wr, ((0, 0), (0, LANES - E)))
    cosine, sine = rope_tables(0, seq)
    cosine = jnp.tile(cosine, (1, 4))
    sine = jnp.concatenate([-sine, sine, -sine, sine], axis=1)

    weights = gather_weights(jnp.stack([w_gate, w_up, w_down], axis=1))
    x_chunks = ring_gather(block_in, n_col)
    attn_in, mixed, q, k, v, lse, w_qkv, gains = attend(spots, x_chunks, pack_qkv, cosine, sine)
    g_chunks = ring_gather(out_grad, n_col)
    mixed_own = lax.all_to_all(mixed, "col", split_axis=0, concat_axis=0, tiled=True)
    resid, send, gates, kept, wo = route(spots, mixed_own, block_in, pack_out, gains, wr, expert_ids, fill_order)

    send_chunks = ring_gather(send, n_col)
    results = [experts(x, g, weights) for x, g in zip(send_chunks, g_chunks)]
    back = ring_sum([result[1] for result in results], n_col).astype(BF16)
    resid_grad, branch, mixed_grad, small = turn(
        spots, back, gates, kept, resid, gains, out_grad, wr, wo, send
    )
    mixed_grads = lax.all_to_all(mixed_grad, "col", split_axis=0, concat_axis=0, tiled=True)
    qkv_wgrad, *back_parts = attend_back(
        spots, mixed_grads, mixed, q, k, v, lse, attn_in, w_qkv, cosine, sine, gains
    )
    attn_grad = ring_sum(back_parts, n_col)
    x_rows = block_in.astype(F32)
    scale = lax.rsqrt(jnp.mean(x_rows * x_rows, axis=1, keepdims=True) + EPS)
    normed = x_rows * scale
    inner = attn_grad * gains[:1]
    block_in_grad = resid_grad + scale * (inner - normed * jnp.mean(inner * normed, axis=1, keepdims=True))
    block_out = resid + ring_sum([result[0] for result in results], n_col)

    low, high = sum_weights(
        flip(send_chunks, g_chunks), [[result[kind] for result in results] for kind in (2, 3, 4)]
    )
    gate_sum, up_sum, down_sum = (jnp.concatenate([low[:, i], high[:, i]], axis=0) for i in range(3))

    out_sum = lax.psum_scatter(out_wgrad(mixed_own, branch, small), "row", scatter_dimension=0)
    out_sum = lax.psum_scatter(out_sum, "col", scatter_dimension=1, tiled=True).astype(F32)
    qkv_sum = lax.psum_scatter(qkv_wgrad, "row", scatter_dimension=0).astype(F32)
    gain_one_sum = lax.psum(qkv_sum[LANES, :LANES], "col")
    return (
        block_out,
        block_in_grad,
        gain_one_sum,
        out_sum[LANES, LANES:],
        qkv_sum[:LANES, :256],
        qkv_sum[:LANES, 256:384],
        qkv_sum[:LANES, 384:],
        out_sum[:LANES],
        out_sum[LANES:, :LANES].T,
        gate_sum,
        up_sum,
        down_sum,
    )


def takes_fast(mesh):
    n_row, n_col = mesh.shape["row"], mesh.shape["col"]
    return n_row == 8 and n_col == 4


def solution(mesh):
    in_specs = (
        P(("row", "col"), None),
        P("row"),
        P("row"),
        P("row", "col"),
        P("row", "col"),
        P("row", "col"),
        P("row", "col"),
        P("row", "col"),
        P("row", None, "col"),
        P("row", None, "col"),
        P("row", None, "col"),
        P(("row", "col"), None),
        P(("row", "col"), None),
        P("row"),
        P(("row", "col"), None),
    )
    out_specs = (
        P(("row", "col"), None),
        P(("row", "col"), None),
        P("row"),
        P("row"),
        P("row", "col"),
        P("row", "col"),
        P("row", "col"),
        P("row", "col"),
        P("row", "col"),
        P("row", None, "col"),
        P("row", None, "col"),
        P("row", None, "col"),
    )
    local = fast if takes_fast(mesh) else general
    return jax.shard_map(local, mesh=mesh, in_specs=in_specs, out_specs=out_specs, check_vma=False)
```

```python
import functools

import jax
import jax.numpy as jnp
from jax import lax
from jax.experimental import pallas as pl
from jax.experimental.pallas import tpu as pltpu
from jax.sharding import PartitionSpec as P

D = 1024
H = 16
KVH = 8
HD = 64
E = 32
TOPK = 8
CAP = 80


EPS = 1e-06
NEGATIVE = -1e30


def cross_rows(left, right):
    return lax.dot_general(
        left, right, (((0,), (0,)), ((), ())), preferred_element_type=jnp.float32
    )


def times_back(left, right):
    return lax.dot_general(
        left, right, (((1,), (1,)), ((), ())), preferred_element_type=jnp.float32
    )


def rope_tables(first_position, count):
    position = (first_position + jnp.arange(count, dtype=jnp.int32)).astype(jnp.float32)
    inverse = 10000.0 ** (-jnp.arange(HD // 2, dtype=jnp.float32) * 2.0 / HD)
    angle = position[:, None] * inverse[None, :]
    return (jnp.cos(angle), jnp.sin(angle))


def rotate(values, cosine, sine):
    half = HD // 2
    first, second = (values[..., :half], values[..., half:])
    cos_rows = cosine[:, None, :]
    sin_rows = sine[:, None, :]
    return jnp.concatenate(
        [first * cos_rows - second * sin_rows, second * cos_rows + first * sin_rows], axis=-1
    )


def rotate_back(grads, cosine, sine):
    half = HD // 2
    first, second = (grads[..., :half], grads[..., half:])
    cos_rows = cosine[:, None, :]
    sin_rows = sine[:, None, :]
    return jnp.concatenate(
        [first * cos_rows + second * sin_rows, second * cos_rows - first * sin_rows], axis=-1
    )


def norm_rows(values, gain):
    scale = lax.rsqrt(jnp.mean(values * values, axis=1, keepdims=True) + EPS)
    normed = values * scale
    return (normed, scale, (normed * gain).astype(jnp.bfloat16))


def norm_back(grad_in, normed, scale, gain):
    gain_grad = jnp.sum(grad_in * normed, axis=0)
    inner = grad_in * gain
    return (scale * (inner - normed * jnp.mean(inner * normed, axis=1, keepdims=True)), gain_grad)


def to_heads(rows, count, group):
    return rows.reshape(count, KVH, group, HD).transpose(1, 2, 0, 3).reshape(KVH, group * count, HD)


def from_heads(heads, count, group):
    return heads.reshape(KVH, group, count, HD).transpose(2, 0, 1, 3).reshape(count, H, HD)


def general(
    block_in,
    attn_gain,
    moe_gain,
    w_query,
    w_key,
    w_value,
    w_out,
    w_router,
    w_gate,
    w_up,
    w_down,
    expert_ids,
    fill_order,
    prefix_len,
    out_grad,
):
    tok_rows = block_in.shape[0]
    n_col = lax.axis_size("col")
    col_index = lax.axis_index("col")
    seq_rows = tok_rows * n_col
    group = H // KVH
    scale_attn = HD ** (-0.5)
    bf16 = jnp.bfloat16
    f32 = jnp.float32
    shared = (
        lax.all_gather(w_query, "row", axis=0, tiled=True),
        lax.all_gather(w_key, "row", axis=0, tiled=True),
        lax.all_gather(w_value, "row", axis=0, tiled=True),
        lax.all_gather(w_out, "row", axis=0, tiled=True),
        lax.all_gather(w_router, "row", axis=0, tiled=True),
        lax.all_gather(attn_gain, "row", axis=0, tiled=True),
        lax.all_gather(moe_gain, "row", axis=0, tiled=True),
    )
    wq_full, wk_full, wv_full, wo_full, wr_full = (
        lax.all_gather(shared[0], "col", axis=1, tiled=True),
        lax.all_gather(shared[1], "col", axis=1, tiled=True),
        lax.all_gather(shared[2], "col", axis=1, tiled=True),
        lax.all_gather(shared[3], "col", axis=1, tiled=True),
        lax.all_gather(shared[4], "col", axis=1, tiled=True),
    )
    gain_one = shared[5].astype(f32)
    gain_two = shared[6].astype(f32)
    x_rows = block_in.astype(f32)
    normed_one, scale_one, attn_in = norm_rows(x_rows, gain_one)
    query = jnp.dot(attn_in, wq_full, preferred_element_type=f32)
    key = jnp.dot(attn_in, wk_full, preferred_element_type=f32)
    value = jnp.dot(attn_in, wv_full, preferred_element_type=f32).astype(bf16)
    cosine, sine = rope_tables(col_index * tok_rows, tok_rows)
    query_rot = rotate(query.reshape(tok_rows, H, HD), cosine, sine).astype(bf16)
    key_rot = (
        rotate(key.reshape(tok_rows, KVH, HD), cosine, sine)
        .astype(bf16)
        .reshape(tok_rows, KVH * HD)
    )
    keys_all, values_all = (
        lax.all_gather(key_rot, "col", axis=0, tiled=True),
        lax.all_gather(value, "col", axis=0, tiled=True),
    )
    prefix = prefix_len[0]
    query_spot = col_index * tok_rows + jnp.arange(tok_rows, dtype=jnp.int32)
    key_spot = jnp.arange(seq_rows, dtype=jnp.int32)
    allowed = (key_spot[None, :] <= query_spot[:, None]) | (key_spot[None, :] < prefix)
    allowed_rows = jnp.tile(allowed, (group, 1))
    query_heads = to_heads(query_rot.reshape(tok_rows, H * HD), tok_rows, group)
    key_heads = keys_all.reshape(seq_rows, KVH, HD).transpose(1, 0, 2)
    value_heads = values_all.reshape(seq_rows, KVH, HD).transpose(1, 0, 2)

    def attend(pieces):
        queries, keys, values = pieces
        scores = times_back(queries, keys) * scale_attn
        scores = jnp.where(allowed_rows, scores, NEGATIVE)
        highest = jnp.max(scores, axis=1, keepdims=True)
        expo = jnp.exp(scores - highest)
        total = jnp.sum(expo, axis=1, keepdims=True)
        weights = (expo / total).astype(bf16)
        mixed_heads = jnp.dot(weights, values, preferred_element_type=f32).astype(bf16)
        return (mixed_heads, (highest + jnp.log(total))[:, 0])

    mixed_heads, lse_heads = lax.map(attend, (query_heads, key_heads, value_heads))
    mixed = from_heads(mixed_heads, tok_rows, group).reshape(tok_rows, H * HD)
    resid = x_rows + jnp.dot(mixed, wo_full, preferred_element_type=f32)
    normed_two, scale_two, moe_in = norm_rows(resid, gain_two)
    logits = jnp.dot(moe_in, wr_full, preferred_element_type=f32)
    choice_hot = (expert_ids[:, :, None] == jnp.arange(E, dtype=jnp.int32)).astype(f32)
    picked = jnp.sum(choice_hot * logits[:, None, :], axis=2)
    highest = jnp.max(picked, axis=1, keepdims=True)
    expo = jnp.exp(picked - highest)
    gates = expo / jnp.sum(expo, axis=1, keepdims=True)
    order = fill_order[0]
    ranked = expert_ids[order]
    onehot = (ranked.reshape(-1, 1) == jnp.arange(E, dtype=jnp.int32)).astype(jnp.int32)
    before = jnp.cumsum(onehot, axis=0) - onehot
    ranked_slot = jnp.sum(before * onehot, axis=1).reshape(tok_rows, TOPK)
    slot = jnp.zeros((tok_rows, TOPK), jnp.int32).at[order].set(ranked_slot)
    kept = slot < CAP
    dest_grid = jnp.where(kept, expert_ids * CAP + slot, E * CAP)
    pair_ids = jnp.arange(tok_rows * TOPK, dtype=jnp.int32)
    slot_pair = (
        jnp.full((E * CAP + 1,), tok_rows * TOPK, jnp.int32)
        .at[dest_grid.reshape(-1)]
        .set(pair_ids)[: E * CAP]
    )
    slot_token = slot_pair // TOPK
    gate_slot = jnp.concatenate([gates.reshape(-1), jnp.zeros((1,), f32)])[slot_pair]
    moe_pad = jnp.concatenate([moe_in, jnp.zeros((1, D), bf16)])
    dispatch = moe_pad[slot_token].reshape(E, CAP, D)
    received = lax.all_to_all(dispatch, "row", split_axis=0, concat_axis=1, tiled=True)
    gate_w, up_w, down_w = (
        lax.all_gather(w_gate, "col", axis=2, tiled=True),
        lax.all_gather(w_up, "col", axis=2, tiled=True),
        lax.all_gather(w_down, "col", axis=2, tiled=True),
    )
    hidden_gate = jnp.einsum("erd,edf->erf", received, gate_w, preferred_element_type=f32)
    hidden_up = jnp.einsum("erd,edf->erf", received, up_w, preferred_element_type=f32)
    active = (jax.nn.silu(hidden_gate) * hidden_up).astype(bf16)
    expert_out = jnp.einsum("erf,edf->erd", active, down_w, preferred_element_type=f32).astype(bf16)
    returned = lax.all_to_all(expert_out, "row", split_axis=1, concat_axis=0, tiled=True)
    out_pad = jnp.concatenate([returned.reshape(E * CAP, D), jnp.zeros((1, D), bf16)])
    pair_out = out_pad[dest_grid]
    weight_pair = gates * kept.astype(f32)
    moe_out = jnp.zeros((tok_rows, D), f32)
    for choice_index in range(TOPK):
        moe_out = moe_out + weight_pair[:, choice_index : choice_index + 1] * pair_out[
            :, choice_index
        ].astype(f32)
    block_out = resid + moe_out
    grad_out = out_grad.astype(f32)
    gate_grad = jnp.stack(
        [
            jnp.sum(pair_out[:, choice_index].astype(f32) * grad_out, axis=1)
            for choice_index in range(TOPK)
        ],
        axis=1,
    )
    grad_pad = jnp.concatenate([grad_out, jnp.zeros((1, D), f32)])
    slot_grad = (gate_slot[:, None] * grad_pad[slot_token]).astype(bf16).reshape(E, CAP, D)
    out_grads = lax.all_to_all(slot_grad, "row", split_axis=0, concat_axis=1, tiled=True)
    act_grad = jnp.einsum("erd,edf->erf", out_grads, down_w, preferred_element_type=f32)
    sigma = jax.nn.sigmoid(hidden_gate)
    gate_h_grad = (act_grad * hidden_up * sigma * (1.0 + hidden_gate * (1.0 - sigma))).astype(bf16)
    up_h_grad = (act_grad * hidden_gate * sigma).astype(bf16)
    down_wgrad = jnp.einsum("erd,erf->edf", out_grads, active, preferred_element_type=f32)
    gate_wgrad = jnp.einsum("erd,erf->edf", received, gate_h_grad, preferred_element_type=f32)
    up_wgrad = jnp.einsum("erd,erf->edf", received, up_h_grad, preferred_element_type=f32)
    in_grad = (
        jnp.einsum("erf,edf->erd", gate_h_grad, gate_w, preferred_element_type=f32)
        + jnp.einsum("erf,edf->erd", up_h_grad, up_w, preferred_element_type=f32)
    ).astype(bf16)
    back_rows = lax.all_to_all(in_grad, "row", split_axis=1, concat_axis=0, tiled=True)
    gate_sum, up_sum, down_sum = (
        lax.psum_scatter(
            gate_wgrad.astype(jnp.bfloat16), "col", scatter_dimension=2, tiled=True
        ).astype(jnp.float32),
        lax.psum_scatter(
            up_wgrad.astype(jnp.bfloat16), "col", scatter_dimension=2, tiled=True
        ).astype(jnp.float32),
        lax.psum_scatter(
            down_wgrad.astype(jnp.bfloat16), "col", scatter_dimension=2, tiled=True
        ).astype(jnp.float32),
    )
    back_pad = jnp.concatenate([back_rows.reshape(E * CAP, D), jnp.zeros((1, D), bf16)])
    pair_back = back_pad[dest_grid]
    moe_in_grad = jnp.zeros((tok_rows, D), f32)
    for choice_index in range(TOPK):
        moe_in_grad = moe_in_grad + pair_back[:, choice_index].astype(f32)
    picked_grad = gates * (gate_grad - jnp.sum(gates * gate_grad, axis=1, keepdims=True))
    logit_grad = jnp.sum(choice_hot * picked_grad[:, :, None], axis=1).astype(bf16)
    router_wgrad = cross_rows(moe_in, logit_grad)
    moe_in_grad = moe_in_grad + times_back(logit_grad, wr_full)
    norm_two_grad, gain_two_grad = norm_back(moe_in_grad, normed_two, scale_two, gain_two)
    resid_grad = grad_out + norm_two_grad
    branch_grad = resid_grad.astype(bf16)
    out_wgrad = cross_rows(mixed, branch_grad)
    mixed_grad = times_back(branch_grad, wo_full).astype(bf16)
    grad_heads = to_heads(mixed_grad, tok_rows, group)

    def query_side(pieces):
        queries, keys, values, lse_rows, grad_rows = pieces
        scores = jnp.where(allowed_rows, times_back(queries, keys) * scale_attn, NEGATIVE)
        probs = jnp.exp(scores - lse_rows[:, None])
        prob_grad = times_back(grad_rows, values)
        delta = jnp.sum(probs * prob_grad, axis=1, keepdims=True)
        score_grad = (probs * (prob_grad - delta)).astype(bf16)
        query_grad = jnp.dot(score_grad, keys, preferred_element_type=f32) * scale_attn
        return (query_grad, delta[:, 0], score_grad, probs)

    def both_sides(pieces):
        queries, keys, values, lse_rows, grad_rows = pieces
        query_grad, delta, score_grad, probs = query_side(pieces)
        key_grad = cross_rows(score_grad, queries) * scale_attn
        value_grad = cross_rows(probs.astype(bf16), grad_rows)
        return (query_grad, key_grad, value_grad)

    query_rot_grad, key_parts, value_parts = lax.map(
        both_sides, (query_heads, key_heads, value_heads, lse_heads, grad_heads)
    )
    key_rot_grad, value_grad = (
        lax.psum_scatter(
            key_parts.transpose(1, 0, 2).reshape(seq_rows, KVH * HD).astype(jnp.bfloat16),
            "col",
            scatter_dimension=0,
            tiled=True,
        ).astype(jnp.float32),
        lax.psum_scatter(
            value_parts.transpose(1, 0, 2).reshape(seq_rows, KVH * HD).astype(jnp.bfloat16),
            "col",
            scatter_dimension=0,
            tiled=True,
        ).astype(jnp.float32),
    )
    query_grad = (
        rotate_back(from_heads(query_rot_grad, tok_rows, group), cosine, sine)
        .reshape(tok_rows, H * HD)
        .astype(bf16)
    )
    key_grad = (
        rotate_back(key_rot_grad.reshape(tok_rows, KVH, HD), cosine, sine)
        .reshape(tok_rows, KVH * HD)
        .astype(bf16)
    )
    value_grad = value_grad.astype(bf16)
    query_wgrad = cross_rows(attn_in, query_grad)
    key_wgrad = cross_rows(attn_in, key_grad)
    value_wgrad = cross_rows(attn_in, value_grad)
    attn_in_grad = (
        times_back(query_grad, wq_full)
        + times_back(key_grad, wk_full)
        + times_back(value_grad, wv_full)
    )
    norm_one_grad, gain_one_grad = norm_back(attn_in_grad, normed_one, scale_one, gain_one)
    block_in_grad = resid_grad + norm_one_grad
    spread_one = jnp.broadcast_to(gain_one_grad[:, None], (D, n_col))
    spread_two = jnp.broadcast_to(gain_two_grad[:, None], (D, n_col))
    col_sums = (
        lax.psum_scatter(
            query_wgrad.astype(jnp.bfloat16), "col", scatter_dimension=1, tiled=True
        ).astype(jnp.float32),
        lax.psum_scatter(
            key_wgrad.astype(jnp.bfloat16), "col", scatter_dimension=1, tiled=True
        ).astype(jnp.float32),
        lax.psum_scatter(
            value_wgrad.astype(jnp.bfloat16), "col", scatter_dimension=1, tiled=True
        ).astype(jnp.float32),
        lax.psum_scatter(
            out_wgrad.astype(jnp.bfloat16), "col", scatter_dimension=1, tiled=True
        ).astype(jnp.float32),
        lax.psum_scatter(
            router_wgrad.astype(jnp.bfloat16), "col", scatter_dimension=1, tiled=True
        ).astype(jnp.float32),
        lax.psum_scatter(
            spread_one.astype(jnp.bfloat16), "col", scatter_dimension=1, tiled=True
        ).astype(jnp.float32),
        lax.psum_scatter(
            spread_two.astype(jnp.bfloat16), "col", scatter_dimension=1, tiled=True
        ).astype(jnp.float32),
    )
    row_sums = (
        lax.psum_scatter(
            col_sums[0].astype(jnp.bfloat16), "row", scatter_dimension=0, tiled=True
        ).astype(jnp.float32),
        lax.psum_scatter(
            col_sums[1].astype(jnp.bfloat16), "row", scatter_dimension=0, tiled=True
        ).astype(jnp.float32),
        lax.psum_scatter(
            col_sums[2].astype(jnp.bfloat16), "row", scatter_dimension=0, tiled=True
        ).astype(jnp.float32),
        lax.psum_scatter(
            col_sums[3].astype(jnp.bfloat16), "row", scatter_dimension=0, tiled=True
        ).astype(jnp.float32),
        lax.psum_scatter(
            col_sums[4].astype(jnp.bfloat16), "row", scatter_dimension=0, tiled=True
        ).astype(jnp.float32),
        lax.psum_scatter(
            col_sums[5].astype(jnp.bfloat16), "row", scatter_dimension=0, tiled=True
        ).astype(jnp.float32),
        lax.psum_scatter(
            col_sums[6].astype(jnp.bfloat16), "row", scatter_dimension=0, tiled=True
        ).astype(jnp.float32),
    )
    return (
        block_out,
        block_in_grad,
        row_sums[5][:, 0],
        row_sums[6][:, 0],
        row_sums[0],
        row_sums[1],
        row_sums[2],
        row_sums[3],
        row_sums[4],
        gate_sum,
        up_sum,
        down_sum,
    )


F32 = jnp.float32
BF16 = jnp.bfloat16
MIB = 1024 * 1024
LANES = 128
VMEM_MOST = 60 * MIB
COST_SCALE = 10**6


def cost(microseconds):
    return pl.CostEstimate(flops=int(microseconds * COST_SCALE), bytes_accessed=10**5, transcendentals=0)


def dot_nn(a, b):
    return lax.dot_general(a, b, (((1,), (0,)), ((), ())), preferred_element_type=F32)


def dot_nt(a, b):
    return lax.dot_general(a, b, (((1,), (1,)), ((), ())), preferred_element_type=F32)


def dot_tn(a, b):
    return lax.dot_general(a, b, (((0,), (0,)), ((), ())), preferred_element_type=F32)


def in_vmem():
    return pl.BlockSpec(memory_space=pltpu.VMEM)


def in_smem():
    return pl.BlockSpec(memory_space=pltpu.SMEM)


def in_hbm():
    return pl.BlockSpec(memory_space=pl.ANY)


def behind(kernel, n_in, after):
    if not after:
        return kernel
    return lambda *refs: kernel(*refs[:n_in], *refs[n_in + len(after) :])


def partner(values):
    lane = lax.broadcasted_iota(jnp.int32, values.shape, 1)
    half = HD // 2
    return jnp.where(
        lane % HD < half,
        pltpu.roll(values, LANES - half, 1),
        pltpu.roll(values, half, 1),
    )


def attend_kernel(
    spot_ref, x0, x1, x2, x3, pack_ref, cos_ref, sin_ref,
    attn_ref, q_ref, k_ref, v_ref, lse_ref, w_ref, gain_ref, mixed_ref,
):
    rows = x0.shape[0]
    col, prefix = spot_ref[0], spot_ref[1]
    for part in range(8):
        span = pl.ds(part * LANES, LANES)
        w_ref[span, :] = pack_ref[part, :LANES, :]
        gain_ref[0:1, span] = pack_ref[part, LANES : LANES + 1, :LANES].astype(F32)
        gain_ref[1:2, span] = pack_ref[part, LANES : LANES + 1, LANES : 2 * LANES].astype(F32)
    gain = gain_ref[0:1, :]
    for step, chunk in enumerate((x0, x1, x2, x3)):
        source = lax.rem(col - step + 4, 4)
        x = chunk[...].astype(F32)
        scale = lax.rsqrt(jnp.mean(x * x, axis=1, keepdims=True) + EPS)
        attn_ref[pl.ds(pl.multiple_of(source * rows, rows), rows), :] = (x * scale * gain).astype(BF16)
    for tile in range(4):
        span = pl.ds(tile * rows, rows)
        qkv = dot_nn(attn_ref[span, :], w_ref[...])
        cosine, sine = cos_ref[span, :], sin_ref[span, :]
        for block in range(3):
            v = qkv[:, block * LANES : (block + 1) * LANES]
            y = v * cosine + partner(v) * sine
            if block < 2:
                y = (y * HD ** (-0.5)).astype(BF16)
                q_ref[2 * block, span, :] = y[:, :HD]
                q_ref[2 * block + 1, span, :] = y[:, HD:]
            else:
                y = y.astype(BF16)
                k_ref[0, span, :] = y[:, :HD]
                k_ref[1, span, :] = y[:, HD:]
        v = qkv[:, 3 * LANES :].astype(BF16)
        v_ref[0, span, :] = v[:, :HD]
        v_ref[1, span, :] = v[:, HD:]
    total = 4 * rows
    for tile in range(4):
        span = pl.ds(tile * rows, rows)
        keys = max((tile + 1) * rows, total // 2)
        key_spot = lax.broadcasted_iota(jnp.int32, (rows, keys), 1)
        query_spot = lax.broadcasted_iota(jnp.int32, (rows, keys), 0) + tile * rows
        allowed = (key_spot <= query_spot) | (key_spot < prefix)
        for pair in range(2):
            k, v = k_ref[pair, pl.ds(0, keys), :], v_ref[pair, pl.ds(0, keys), :]
            outs = []
            for head in (2 * pair, 2 * pair + 1):
                scores = jnp.where(allowed, dot_nt(q_ref[head, span, :], k), NEGATIVE)
                highest = jnp.max(scores, axis=1, keepdims=True)
                expo = jnp.exp(scores - highest)
                summed = jnp.sum(expo, axis=1, keepdims=True)
                outs.append(dot_nn(expo.astype(BF16), v) * (1.0 / summed))
                lse_ref[span, head : head + 1] = highest + jnp.log(summed)
            mixed_ref[span, pair * LANES : (pair + 1) * LANES] = jnp.concatenate(outs, axis=1).astype(BF16)


def attend(spots, chunks, pack, cosine, sine, after=()):
    rows = chunks[0].shape[0]
    seq = 4 * rows
    shapes = (
        jax.ShapeDtypeStruct((seq, D), BF16),
        jax.ShapeDtypeStruct((4, seq, HD), BF16),
        jax.ShapeDtypeStruct((2, seq, HD), BF16),
        jax.ShapeDtypeStruct((2, seq, HD), BF16),
        jax.ShapeDtypeStruct((seq, 4), F32),
        jax.ShapeDtypeStruct((D, 512), BF16),
        jax.ShapeDtypeStruct((2, D), F32),
        jax.ShapeDtypeStruct((seq, 256), BF16),
    )
    return pl.pallas_call(
        behind(attend_kernel, 8, after),
        out_shape=shapes,
        in_specs=[in_smem()] + [in_vmem()] * 7 + [in_hbm()] * len(after),
        out_specs=tuple(in_vmem() for _ in shapes),
        compiler_params=pltpu.CompilerParams(vmem_limit_bytes=VMEM_MOST),
        cost_estimate=cost(10),
    )(spots, *chunks, pack, cosine, sine, *after)


def attend_back_kernel(
    spot_ref, grad_ref, mixed_ref, q_ref, k_ref, v_ref, lse_ref, attn_ref, w_ref, cos_ref, sin_ref, gain_ref,
    wgrad_ref, in0, in1, in2, in3, dqkv_ref, dk_ref, dv_ref, dq_ref, mg_ref,
):
    seq = attn_ref.shape[0]
    rows = seq // 4
    prefix = spot_ref[1]
    for tile in range(4):
        span = pl.ds(tile * rows, rows)
        for pair in range(2):
            g = grad_ref[span, pair * LANES : (pair + 1) * LANES]
            mg_ref[2 * pair, span, :] = g[:, :HD]
            mg_ref[2 * pair + 1, span, :] = g[:, HD:]
    dk_ref[...] = jnp.zeros_like(dk_ref)
    dv_ref[...] = jnp.zeros_like(dv_ref)
    for tile in range(4):
        span = pl.ds(tile * rows, rows)
        keys = max((tile + 1) * rows, seq // 2)
        key_spot = lax.broadcasted_iota(jnp.int32, (rows, keys), 1)
        query_spot = lax.broadcasted_iota(jnp.int32, (rows, keys), 0) + tile * rows
        allowed = (key_spot <= query_spot) | (key_spot < prefix)
        for pair in range(2):
            k, v = k_ref[pair, pl.ds(0, keys), :], v_ref[pair, pl.ds(0, keys), :]
            both = grad_ref[span, pair * LANES : (pair + 1) * LANES].astype(F32) * mixed_ref[
                span, pair * LANES : (pair + 1) * LANES
            ].astype(F32)
            outs = []
            for at, head in enumerate((2 * pair, 2 * pair + 1)):
                q, g = q_ref[head, span, :], mg_ref[head, span, :]
                delta = jnp.sum(both[:, at * HD : (at + 1) * HD], axis=1, keepdims=True)
                scores = jnp.where(allowed, dot_nt(q, k), NEGATIVE)
                probs = jnp.exp(scores - lse_ref[span, head : head + 1])
                score_grad = (probs * (dot_nt(g, v) - delta)).astype(BF16)
                dv_ref[pair, pl.ds(0, keys), :] += dot_tn(probs.astype(BF16), g)
                dk_ref[pair, pl.ds(0, keys), :] += dot_tn(score_grad, q)
                outs.append(dot_nn(score_grad, k) * HD ** (-0.5))
            dq_ref[span, pair * LANES : (pair + 1) * LANES] = jnp.concatenate(outs, axis=1)
    for tile in range(4):
        span = pl.ds(tile * rows, rows)
        cosine, sine = cos_ref[span, :], sin_ref[span, :]
        for block in range(3):
            if block < 2:
                g = dq_ref[span, block * LANES : (block + 1) * LANES]
            else:
                g = jnp.concatenate([dk_ref[0, span, :], dk_ref[1, span, :]], axis=1)
            dqkv_ref[span, block * LANES : (block + 1) * LANES] = (g * cosine - partner(g) * sine).astype(BF16)
        dqkv_ref[span, 3 * LANES :] = jnp.concatenate([dv_ref[0, span, :], dv_ref[1, span, :]], axis=1).astype(BF16)
    gain_total = jnp.zeros((1, D), F32)
    for step, out in enumerate((in0, in1, in2, in3)):
        source = lax.rem(spot_ref[0] - step + 4, 4)
        span = pl.ds(pl.multiple_of(source * rows, rows), rows)
        back = dot_nt(dqkv_ref[span, :], w_ref[...])
        out[...] = back.astype(BF16)
        gain_total = gain_total + jnp.sum(back * attn_ref[span, :].astype(F32), axis=0, keepdims=True)
    gain_total = gain_total / gain_ref[0:1, :]
    for part in range(8):
        span = pl.ds(part * LANES, LANES)
        wgrad_ref[part, LANES:, :LANES] = jnp.broadcast_to(gain_total[:, part * LANES : (part + 1) * LANES], (8, LANES)).astype(BF16)
        wgrad_ref[part, LANES:, LANES:] = jnp.zeros((8, 3 * LANES), BF16)
        wgrad_ref[part, :LANES, :] = dot_tn(attn_ref[:, span], dqkv_ref[...]).astype(BF16)


def attend_back(spots, grads, mixed, q, k, v, lse, attn_in, w_qkv, cosine, sine, gain, after=()):
    seq = attn_in.shape[0]
    shapes = (
        jax.ShapeDtypeStruct((8, 136, 512), BF16),
    ) + (jax.ShapeDtypeStruct((seq // 4, D), BF16),) * 4
    return pl.pallas_call(
        behind(attend_back_kernel, 12, after),
        out_shape=shapes,
        in_specs=[in_smem()] + [in_vmem()] * 11 + [in_hbm()] * len(after),
        out_specs=tuple(in_vmem() for _ in shapes),
        scratch_shapes=[
            pltpu.VMEM((seq, 512), BF16),
            pltpu.VMEM((2, seq, HD), F32),
            pltpu.VMEM((2, seq, HD), F32),
            pltpu.VMEM((seq, 256), F32),
            pltpu.VMEM((4, seq, HD), BF16),
        ],
        compiler_params=pltpu.CompilerParams(vmem_limit_bytes=VMEM_MOST),
        cost_estimate=cost(16),
    )(spots, grads, mixed, q, k, v, lse, attn_in, w_qkv, cosine, sine, gain, *after)


def route_kernel(
    spot_ref, mixed_ref, x_ref, pack_ref, gain_ref, ids_ref, order_ref,
    resid_ref, send_ref, gates_ref, kept_ref, wo_ref, wr_ref, wr_wide,
):
    rows = x_ref.shape[0]
    wr_wide[...] = jnp.zeros_like(wr_wide)
    for row in range(8):
        span = pl.ds(row * LANES, LANES)
        for col in range(4):
            wo_ref[span, col * 256 : (col + 1) * 256] = pack_ref[4 * row + col, :LANES, :]
            wr_wide[col * 8 : (col + 1) * 8, span] = pack_ref[4 * row + col, LANES:, :LANES].astype(F32)
    wr_ref[...] = wr_wide[...].astype(BF16)
    resid = x_ref[...].astype(F32)
    for part in range(4):
        resid = resid + dot_nn(mixed_ref[pl.ds(part * rows, rows), :], wo_ref[part * 256 : (part + 1) * 256, :])
    resid_ref[...] = resid
    scale = lax.rsqrt(jnp.mean(resid * resid, axis=1, keepdims=True) + EPS)
    moe_in = (resid * scale * gain_ref[1:2, :]).astype(BF16)
    send_ref[:, :D] = moe_in
    logits = dot_nt(moe_in, wr_ref[...])
    lane = lax.broadcasted_iota(jnp.int32, (rows, LANES), 1)
    chosen = jnp.zeros((rows, LANES), jnp.bool_)
    for choice in range(TOPK):
        chosen = chosen | (ids_ref[:, choice : choice + 1] == lane)
    picked = jnp.where(chosen, logits, NEGATIVE)
    expo = jnp.exp(picked - jnp.max(picked, axis=1, keepdims=True))
    gates = expo / jnp.sum(expo, axis=1, keepdims=True)
    first = lax.broadcasted_iota(jnp.int32, (rows, rows), 0)
    second = lax.broadcasted_iota(jnp.int32, (rows, rows), 1)
    place = (first == order_ref[...]).astype(BF16)
    sooner = dot_nn(place, (second < first).astype(BF16)).astype(BF16)
    sooner = dot_nt(sooner, place).astype(BF16)
    slot = dot_nn(sooner, chosen.astype(BF16))
    kept = (chosen & (slot < CAP)).astype(F32)
    gates_ref[...] = gates
    kept_ref[...] = kept
    send_ref[:, D:] = dot_nn((gates * kept).astype(BF16), relabel(spot_ref[2])).astype(BF16)


def relabel(row):
    first = lax.broadcasted_iota(jnp.int32, (LANES, LANES), 0)
    second = lax.broadcasted_iota(jnp.int32, (LANES, LANES), 1)
    return (first == (second ^ (row * 4))).astype(BF16)


def route(spots, mixed, x, pack, gain, ids, order):
    rows = x.shape[0]
    shapes = (
        jax.ShapeDtypeStruct((rows, D), F32),
        jax.ShapeDtypeStruct((rows, D + LANES), BF16),
        jax.ShapeDtypeStruct((rows, LANES), F32),
        jax.ShapeDtypeStruct((rows, LANES), F32),
        jax.ShapeDtypeStruct((D, D), BF16),
        jax.ShapeDtypeStruct((LANES, D), BF16),
    )
    return pl.pallas_call(
        route_kernel,
        out_shape=shapes,
        in_specs=[in_smem()] + [in_vmem()] * 6,
        out_specs=tuple(in_vmem() for _ in shapes),
        scratch_shapes=[pltpu.VMEM((LANES, D), F32)],
        compiler_params=pltpu.CompilerParams(vmem_limit_bytes=VMEM_MOST),
        cost_estimate=cost(2),
    )(spots, mixed, x, pack, gain, ids, order)


def expert_kernel(x_ref, g_ref, *refs):
    weights, refs = refs[:10], refs[10:]
    back_ref, hg_ref, hu_ref, act_ref, out_acc, in_acc, gate_acc, held, sems = refs
    step = pl.program_id(0)
    count = held.shape[1]
    wide = count * LANES

    def fetch(at, slot):
        for k in range(8):

            @pl.when(at == k)
            def _():
                for i in range(2):
                    half = weights[k].at[pl.ds(2 * i, 2)] if k < 6 else weights[2 * k - 6 + i]
                    pltpu.make_async_copy(half, held.at[slot, pl.ds(2 * i, 2)], sems.at[slot, i]).start()

    @pl.when(step == 0)
    def _():
        fetch(step, 0)
        out_acc[...] = jnp.zeros_like(out_acc)
        in_acc[...] = jnp.zeros_like(in_acc)
        gate_acc[...] = jnp.zeros_like(gate_acc)

    now = lax.rem(step, 2)
    for i in range(2):
        pltpu.make_async_copy(weights[6], held.at[now, pl.ds(2 * i, 2)], sems.at[now, i]).wait()
    fetch(step + 1, 1 - now)

    join = lambda kind: jnp.concatenate([held[now, i, kind] for i in range(count)], axis=1)
    wg, wu, wd = join(0), join(1), join(2)
    x = x_ref[:, :D]
    expert = lax.broadcasted_iota(jnp.int32, (LANES, wide), 0)
    column = lax.broadcasted_iota(jnp.int32, (LANES, wide), 1)
    spread = (expert == step * count + column // LANES).astype(BF16)
    gate = dot_nn(x_ref[:, D:], spread)
    hidden_gate = dot_nn(x, wg)
    hidden_up = dot_nn(x, wu)
    act_grad = dot_nn(g_ref[...], wd)
    sigma = 0.5 * jnp.tanh(0.5 * hidden_gate) + 0.5
    swish = hidden_gate * sigma
    active = swish * hidden_up
    gate_acc[...] += dot_nt((active * act_grad).astype(BF16), spread)
    gated = (active * gate).astype(BF16)
    act_ref[...] = gated
    out_acc[...] += dot_nt(gated, wd)
    act_grad = act_grad * gate
    up_grad = (act_grad * swish).astype(BF16)
    gate_grad = (act_grad * hidden_up * (sigma + swish * (1.0 - sigma))).astype(BF16)
    hg_ref[...] = gate_grad
    hu_ref[...] = up_grad
    in_acc[...] += dot_nt(gate_grad, wg) + dot_nt(up_grad, wu)

    @pl.when(step == pl.num_programs(0) - 1)
    def _():
        back_ref[:, :D] = in_acc[...].astype(BF16)
        back_ref[:, D : 2 * D] = out_acc[...].astype(BF16)
        back_ref[:, 2 * D :] = gate_acc[...].astype(BF16)


def experts(x, g, weights, after=()):
    rows = x.shape[0]
    count = 4
    steps = 8
    wide = count * LANES
    hidden = pl.BlockSpec((rows, wide), lambda i: (0, i))
    whole = lambda width: pl.BlockSpec((rows, width), lambda i: (0, 0))
    return pl.pallas_call(
        behind(expert_kernel, 12, after),
        out_shape=(jax.ShapeDtypeStruct((rows, 2 * D + LANES), BF16),)
        + (jax.ShapeDtypeStruct((rows, steps * wide), BF16),) * 3,
        grid_spec=pltpu.PrefetchScalarGridSpec(
            num_scalar_prefetch=0,
            grid=(steps,),
            in_specs=[whole(D + LANES), whole(D)] + [in_hbm()] * (10 + len(after)),
            out_specs=(whole(2 * D + LANES), hidden, hidden, hidden),
            scratch_shapes=[
                pltpu.VMEM((rows, D), F32),
                pltpu.VMEM((rows, D), F32),
                pltpu.VMEM((rows, LANES), F32),
                pltpu.VMEM((2, count, 3, D, LANES), BF16),
                pltpu.SemaphoreType.DMA((2, 2)),
            ],
        ),
        compiler_params=pltpu.CompilerParams(vmem_limit_bytes=VMEM_MOST),
        cost_estimate=cost(21),
    )(x, g, *weights, *after)


def flip_kernel(x0, x1, x2, x3, g0, g1, g2, g3, xt_ref, gt_ref):
    rows = x0.shape[0]
    for at, (x, g) in enumerate(zip((x0, x1, x2, x3), (g0, g1, g2, g3))):
        xt_ref[:, at * rows : (at + 1) * rows] = x[:, :D].T
        gt_ref[:, at * rows : (at + 1) * rows] = g[...].T


def flip(xs, gs, after=()):
    seq = 4 * xs[0].shape[0]
    return pl.pallas_call(
        behind(flip_kernel, 8, after),
        out_shape=(jax.ShapeDtypeStruct((D, seq), BF16),) * 2,
        in_specs=[in_vmem()] * 8 + [in_hbm()] * len(after),
        out_specs=(in_vmem(),) * 2,
        compiler_params=pltpu.CompilerParams(vmem_limit_bytes=VMEM_MOST),
        cost_estimate=cost(2),
    )(*xs, *gs, *after)


def expert_wgrad_kernel(places, added, late, xt_ref, gt_ref, *refs):
    hidden, refs = refs[:12], refs[12:]
    count = len(places)
    n_extra = len({place[0] for place in added if place}) + len(late)
    plain = [k for k, place in enumerate(added) if not place]
    extras, refs = refs[:n_extra], refs[n_extra:]
    n_out = len({which for which, _ in places})
    outs, refs = refs[:n_out], refs[n_out:]
    held, out_sems, got, in_sems = refs
    step = pl.program_id(0)
    now = lax.rem(step, 2)

    def fetch(at, slot):
        for k, place in enumerate(added):
            if not place:
                continue
            which, half = place

            @pl.when(at == k)
            def _():
                pltpu.make_async_copy(extras[which].at[half], got.at[slot, 0], in_sems.at[slot, 0]).start()
                if k in late:
                    pltpu.make_async_copy(extras[late[k]].at[0], got.at[slot, 1], in_sems.at[slot, 1]).start()

    if added:

        @pl.when(step == 0)
        def _():
            fetch(step, 0)

        fetch(step + 1, 1 - now)

    def sent(slot):
        pltpu.make_async_copy(held.at[slot], outs[0].at[0], out_sems.at[slot]).wait()

    @pl.when(step >= 2)
    def _():
        sent(now)

    first = functools.reduce(jnp.logical_and, [step != k for k in plain], step >= 0)
    second = functools.reduce(jnp.logical_or, [step == k for k in late], False)
    if added:

        @pl.when(functools.reduce(jnp.logical_and, [step != k for k in plain], step >= 0))
        def _():
            pltpu.make_async_copy(extras[0].at[0], got.at[now, 0], in_sems.at[now, 0]).wait()

        for k in late:

            @pl.when(step == k)
            def _():
                pltpu.make_async_copy(extras[0].at[0], got.at[now, 1], in_sems.at[now, 1]).wait()


    for kind, left in enumerate((xt_ref, xt_ref, gt_ref)):
        joined = jnp.concatenate([part[...] for part in hidden[kind * 4 : kind * 4 + 4]], axis=0)
        product = dot_nn(left[...], joined)
        for i in range(2):
            piece = product[:, i * LANES : (i + 1) * LANES]
            if plain:
                piece = piece + jnp.where(first, got[now, 0, i, kind].astype(F32), 0.0)
            elif added:
                piece = piece + got[now, 0, i, kind].astype(F32)
            if late:
                piece = piece + jnp.where(second, got[now, 1, i, kind].astype(F32), 0.0)
            held[now, i, kind] = piece.astype(BF16)

    for k, (which, half) in enumerate(places):

        @pl.when(step == k)
        def _():
            pltpu.make_async_copy(held.at[now], outs[which].at[half], out_sems.at[now]).start()

    @pl.when(step == count - 1)
    def _():
        sent(now)
        if count > 1:
            sent(1 - now)


def expert_wgrads(flipped, hidden, entries, places, extras=(), added=(), late=None, after=(), time=None):
    rows = hidden[0][0].shape[0]
    wide = 2 * LANES
    seq = flipped[0].shape[1]
    count = len(entries)

    def entry(i):
        place = entries[0]
        for k in range(1, count):
            place = jnp.where(i == k, entries[k], place)
        return (0, place)

    lane = pl.BlockSpec((rows, wide), entry)
    whole = pl.BlockSpec((D, seq), lambda i: (0, 0))
    kernel = functools.partial(expert_wgrad_kernel, places, added, late or {})
    sizes = [sum(which == o for which, _ in places) for o in range(max(which for which, _ in places) + 1)]
    return pl.pallas_call(
        behind(kernel, 14 + len(extras), after),
        grid=(count,),
        out_shape=tuple(jax.ShapeDtypeStruct((size, 2, 3, D, LANES), BF16) for size in sizes),
        in_specs=[whole] * 2 + [lane] * 12 + [in_hbm()] * (len(extras) + len(after)),
        out_specs=(in_hbm(),) * len(sizes),
        scratch_shapes=[
            pltpu.VMEM((2, 2, 3, D, LANES), BF16),
            pltpu.SemaphoreType.DMA((2,)),
            pltpu.VMEM((2, 2, 2, 3, D, LANES), BF16),
            pltpu.SemaphoreType.DMA((2, 2)),
        ],
        compiler_params=pltpu.CompilerParams(vmem_limit_bytes=VMEM_MOST),
        cost_estimate=cost(time or 2.2 * count),
    )(*flipped, *hidden[0], *hidden[1], *hidden[2], *extras, *after)


def expert_total_kernel(own_ref, xa_ref, xb_ref, ya_ref, yb_ref, gate_ref, up_ref, down_ref):
    for kind, out in enumerate((gate_ref, up_ref, down_ref)):
        for half, (x_ref, y_ref) in enumerate(((xa_ref, ya_ref), (xb_ref, yb_ref))):
            out[half, 0] = (
                own_ref[half, 0, kind].astype(F32) + x_ref[0, 0, kind].astype(F32) + y_ref[0, 0, kind].astype(F32)
            )


def expert_total(after, own, *parts):
    block = pl.BlockSpec((2, 1, 3, D, LANES), lambda i: (0, i, 0, 0, 0))
    part = pl.BlockSpec((1, 1, 3, D, LANES), lambda i: (0, i, 0, 0, 0))
    out = pl.BlockSpec((2, 1, D, LANES), lambda i: (0, i, 0, 0))
    sums = pl.pallas_call(
        behind(expert_total_kernel, 5, after),
        grid=(2,),
        out_shape=(jax.ShapeDtypeStruct((2, 2, D, LANES), F32),) * 3,
        in_specs=[block] + [part] * 4 + [in_hbm()] * len(after),
        out_specs=(out,) * 3,
        compiler_params=pltpu.CompilerParams(vmem_limit_bytes=VMEM_MOST),
        cost_estimate=cost(5),
    )(own, *parts, *after)
    return [total.reshape(4, D, LANES) for total in sums]


def halves_kernel(x_ref, y_ref, low_ref, high_ref):
    low_ref[...] = y_ref[...]
    high_ref[...] = x_ref[...]


def halves(from_x, from_y, after):
    half = jax.ShapeDtypeStruct((2, 3, D, LANES), BF16)
    first = pl.BlockSpec((1, 1, D, LANES), lambda i, j: (i, j, 0, 0))
    second = pl.BlockSpec((1, 1, D, LANES), lambda i, j: (i + 2, j, 0, 0))
    return pl.pallas_call(
        behind(halves_kernel, 2, after),
        grid=(2, 3),
        out_shape=(half, half),
        in_specs=[second, first] + [in_hbm()] * len(after),
        out_specs=(first,) * 2,
        compiler_params=pltpu.CompilerParams(vmem_limit_bytes=VMEM_MOST),
        cost_estimate=cost(3),
    )(from_x, from_y, *after)


def turn_kernel(
    spot_ref, came_ref, back_ref, gates_ref, kept_ref, resid_ref, gain_ref, g_ref, wr_ref, wo_ref, send_ref,
    out_ref, resid_grad_ref, branch_ref, mixed_grad_ref, small_ref,
):
    rows = resid_ref.shape[0]
    gates = gates_ref[...]
    both = lambda span: came_ref[:, span].astype(F32) + back_ref[:, span].astype(F32)
    out_ref[...] = resid_ref[...] + both(slice(D, 2 * D))
    gate_grad = dot_nn(both(slice(2 * D, None)).astype(BF16), relabel(spot_ref[2])) * kept_ref[...]
    logit_grad = gates * (gate_grad - jnp.sum(gates * gate_grad, axis=1, keepdims=True))
    logit_grad = logit_grad.astype(BF16)
    moe_grad = both(slice(0, D)) + dot_nn(logit_grad, wr_ref[...])
    resid = resid_ref[...]
    scale = lax.rsqrt(jnp.mean(resid * resid, axis=1, keepdims=True) + EPS)
    normed = resid * scale
    small_ref[LANES:, :] = jnp.broadcast_to(jnp.sum(moe_grad * normed, axis=0, keepdims=True), (8, D))
    small_ref[:LANES, :] = dot_tn(logit_grad, send_ref[:, :D])
    inner = moe_grad * gain_ref[1:2, :]
    grad = g_ref[...].astype(F32) + scale * (inner - normed * jnp.mean(inner * normed, axis=1, keepdims=True))
    resid_grad_ref[...] = grad
    branch = grad.astype(BF16)
    branch_ref[...] = branch
    for part in range(4):
        mixed_grad_ref[pl.ds(part * rows, rows), :] = dot_nt(
            branch, wo_ref[part * 256 : (part + 1) * 256, :]
        ).astype(BF16)


def turn(spots, came, back, gates, kept, resid, gain, g, wr, wo, send, after=()):
    rows = resid.shape[0]
    shapes = (
        jax.ShapeDtypeStruct((rows, D), F32),
        jax.ShapeDtypeStruct((rows, D), F32),
        jax.ShapeDtypeStruct((rows, D), BF16),
        jax.ShapeDtypeStruct((4 * rows, 256), BF16),
        jax.ShapeDtypeStruct((LANES + 8, D), F32),
    )
    return pl.pallas_call(
        behind(turn_kernel, 11, after),
        out_shape=shapes,
        in_specs=[in_smem()] + [in_vmem()] * 10 + [in_hbm()] * len(after),
        out_specs=tuple(in_vmem() for _ in shapes),
        compiler_params=pltpu.CompilerParams(vmem_limit_bytes=VMEM_MOST),
        cost_estimate=cost(2),
    )(spots, came, back, gates, kept, resid, gain, g, wr, wo, send, *after)


def out_wgrad_kernel(mixed_ref, branch_ref, small_ref, pack_ref):
    rows = branch_ref.shape[0]
    for part in range(4):
        product = dot_tn(mixed_ref[pl.ds(part * rows, rows), :], branch_ref[...]).astype(BF16)
        pack_ref[2 * part, :LANES, :] = product[:LANES]
        pack_ref[2 * part + 1, :LANES, :] = product[LANES:]
    for row in range(8):
        span = pl.ds(row * LANES, LANES)
        for col in range(4):
            pack_ref[row, LANES:, col * 256 : col * 256 + LANES] = small_ref[col * 8 : col * 8 + 8, span].astype(BF16)
            pack_ref[row, LANES:, col * 256 + LANES : col * 256 + 256] = small_ref[LANES:, span].astype(BF16)


def out_wgrad(mixed, branch, small, after=()):
    return pl.pallas_call(
        behind(out_wgrad_kernel, 3, after),
        out_shape=jax.ShapeDtypeStruct((8, LANES + 8, D), BF16),
        in_specs=[in_vmem()] * 3 + [in_hbm()] * len(after),
        out_specs=in_vmem(),
        compiler_params=pltpu.CompilerParams(vmem_limit_bytes=VMEM_MOST),
        cost_estimate=cost(3),
    )(mixed, branch, small, *after)


def ring_gather(value, n_col):
    steps = [(i, (i + 1) % n_col) for i in range(n_col)]
    chunks = [value]
    for _ in range(n_col - 1):
        chunks.append(lax.ppermute(chunks[-1], "col", steps))
    return chunks


def ring_sum(parts, n_col):
    steps = [(i, (i + 1) % n_col) for i in range(n_col)]
    total = parts[1]
    for part in parts[2:] + parts[:1]:
        total = lax.ppermute(total, "col", steps).astype(F32) + part.astype(F32)
        if part is not parts[0]:
            total = total.astype(BF16)
    return total


def shift_all(parts, n_col):
    return [
        lax.ppermute(part, "col", [(i, (i + s) % n_col) for i in range(n_col)]) if s else part
        for s, part in enumerate(parts)
    ]


def hold(value, *until):
    return lax.optimization_barrier((value, *until))[0]


CORE, ACROSS_X, ACROSS_Y = 1, 2, 4


def swap(value, mask):
    return lax.ppermute(value, "row", [(i, i ^ mask) for i in range(8)])


def fast(
    block_in,
    attn_gain,
    moe_gain,
    w_query,
    w_key,
    w_value,
    w_out,
    w_router,
    w_gate,
    w_up,
    w_down,
    expert_ids,
    fill_order,
    prefix_len,
    out_grad,
):
    rows = block_in.shape[0]
    n_col = lax.axis_size("col")
    col = lax.axis_index("col")
    row = lax.axis_index("row")
    seq = rows * n_col
    spots = jnp.stack([col.astype(jnp.int32), prefix_len[0], row.astype(jnp.int32)])
    gains = jnp.concatenate([attn_gain, moe_gain, jnp.zeros((256,), BF16)])[None]
    pack_qkv = jnp.concatenate(
        [jnp.concatenate([w_query, w_key, w_value], axis=1), gains, jnp.zeros((7, 512), BF16)], axis=0
    )
    pack_qkv = lax.all_gather(pack_qkv, "row", axis=0)
    x_chunks = ring_gather(block_in, n_col)
    own = jnp.stack([w_gate, w_up, w_down], axis=1)
    from_x, from_y, other = swap(own, ACROSS_X), swap(own, ACROSS_Y), swap(own, CORE)
    pack_out = jnp.concatenate([w_out, jnp.pad(w_router.T, ((0, 0), (0, 256 - LANES)))], axis=0)
    pack_out = lax.all_gather(pack_out, ("row", "col"), axis=0)
    cosine, sine = rope_tables(0, seq)
    cosine = jnp.tile(cosine, (1, 4))
    sine = jnp.concatenate([-sine, sine, -sine, sine], axis=1)

    attn_in, q, k, v, lse, w_qkv, gains, mixed_all = attend(spots, x_chunks, pack_qkv, cosine, sine, [other])
    g_chunks = ring_gather(hold(out_grad, x_chunks[3]), n_col)
    mixed_own = lax.all_to_all(mixed_all, "col", split_axis=0, concat_axis=0, tiled=True)
    resid, send, gates, kept, wo, wr = route(
        spots, mixed_own, block_in, pack_out, gains, expert_ids, fill_order
    )
    low, high = halves(from_x, from_y, [mixed_own])
    far = swap(low, ACROSS_X), swap(high, ACROSS_Y)
    weights = [own, other, from_x, swap(from_x, CORE), from_y, swap(from_y, CORE), *far]

    send_chunks = [send, *ring_gather(hold(send, g_chunks[3]), n_col)[1:]]
    weights += [swap(hold(part, send_chunks[3]), CORE) for part in far]
    results, backs, back = {}, [], None
    steps = [(i, (i + 1) % n_col) for i in range(n_col)]
    order = (1, 2, 3, 0)
    for at, chunk in enumerate(order):
        after = [results[order[at - 1]][1]] if at else [send_chunks[3]]
        if at >= 2:
            after.append(backs[at - 2])
        results[chunk] = experts(send_chunks[chunk], g_chunks[chunk], weights, after)
        if chunk:
            part = results[chunk][0]
            back = part if back is None else (back.astype(F32) + part.astype(F32)).astype(BF16)
            back = lax.ppermute(back, "col", steps)
            backs.append(back)
    results = [results[chunk] for chunk in range(n_col)]

    flipped = flip(send_chunks, g_chunks, [results[2][1]])
    hidden = [[result[kind] for result in results] for kind in (1, 2, 3)]
    wgrads = functools.partial(expert_wgrads, flipped, hidden)
    (p7,) = wgrads((14, 15), ((0, 0), (0, 1)), after=[backs[2]])
    r7 = swap(p7, CORE)
    block_out, resid_grad, branch, mixed_grad, small = turn(
        spots, backs[2], results[0][0], gates, kept, resid, gains, out_grad, wr, wo, send, [p7]
    )
    mixed_grads = lax.all_to_all(mixed_grad, "col", split_axis=0, concat_axis=0, tiled=True)
    (p53,) = wgrads((6, 7, 10, 11), tuple((0, i) for i in range(4)), after=[branch, r7])
    r53 = swap(p53, CORE)
    q6 = wgrads((12, 13), ((0, 0), (1, 0)), [r7], ((0, 0), (0, 1)), after=[p53])
    far_x, far_y = swap(q6[0], ACROSS_X), swap(q6[1], ACROSS_Y)
    pack = out_wgrad(mixed_own, branch, small, q6[:1])
    out_sum = lax.psum_scatter(pack, "row", scatter_dimension=0, tiled=True)
    q2a, q4b = wgrads((4, 9), ((0, 0), (1, 0)), [r53], ((0, 0), (0, 3)), after=[pack, mixed_grads])
    x2a, y4b = swap(q2a, ACROSS_X), swap(q4b, ACROSS_Y)
    q2b, q4a, p1 = wgrads(
        (5, 8, 2, 3),
        ((0, 0), (1, 0), (2, 0), (2, 1)),
        [r53, far_y, far_x],
        ((0, 1), (0, 2), None, None),
        {0: 1, 1: 2},
        [q2a],
    )
    r1 = swap(p1, CORE)
    x2b, y4a = swap(q2b, ACROSS_X), swap(q4a, ACROSS_Y)
    qkv_wgrad, *back_parts = attend_back(
        spots, mixed_grads, mixed_all, q, k, v, lse, attn_in, w_qkv, cosine, sine, gains, [q2b]
    )
    (q0,) = wgrads((0, 1), ((0, 0), (0, 1)), [r1], ((0, 0), (0, 1)), after=[qkv_wgrad])
    moving = lax.ppermute(back_parts[1], "col", steps)
    moving = (hold(moving, q0, x2a, y4b).astype(F32) + back_parts[2].astype(F32)).astype(BF16)
    moving = lax.ppermute(moving, "col", steps)
    moving = (moving.astype(F32) + back_parts[3].astype(F32)).astype(BF16)
    third_step = moving
    attn_grad = lax.ppermute(moving, "col", steps).astype(F32) + back_parts[0].astype(F32)
    x_rows = block_in.astype(F32)
    scale = lax.rsqrt(jnp.mean(x_rows * x_rows, axis=1, keepdims=True) + EPS)
    normed = x_rows * scale
    inner = attn_grad * gains[:1]
    block_in_grad = resid_grad + scale * (inner - normed * jnp.mean(inner * normed, axis=1, keepdims=True))
    gate_sum, up_sum, down_sum = expert_total([third_step], q0, x2a, x2b, y4a, y4b)

    qkv_sum = lax.psum_scatter(qkv_wgrad, "row", scatter_dimension=0, tiled=True)[0].astype(F32)
    out_sum = lax.psum_scatter(hold(out_sum, q2b), "col", scatter_dimension=2, tiled=True)[0].astype(F32)
    gain_one = qkv_sum[LANES:, :LANES]
    gain_one_sum = functools.reduce(jnp.add, shift_all([gain_one] * n_col, n_col))[0]
    return (
        block_out,
        block_in_grad,
        gain_one_sum,
        out_sum[LANES, LANES:],
        qkv_sum[:LANES, :256],
        qkv_sum[:LANES, 256:384],
        qkv_sum[:LANES, 384:],
        out_sum[:LANES],
        out_sum[LANES:, :LANES].T,
        gate_sum,
        up_sum,
        down_sum,
    )


def takes_fast(mesh):
    n_row, n_col = mesh.shape["row"], mesh.shape["col"]
    return n_row == 8 and n_col == 4


def solution(mesh):
    in_specs = (
        P(("row", "col"), None),
        P("row"),
        P("row"),
        P("row", "col"),
        P("row", "col"),
        P("row", "col"),
        P("row", "col"),
        P("row", "col"),
        P("row", None, "col"),
        P("row", None, "col"),
        P("row", None, "col"),
        P(("row", "col"), None),
        P(("row", "col"), None),
        P("row"),
        P(("row", "col"), None),
    )
    out_specs = (
        P(("row", "col"), None),
        P(("row", "col"), None),
        P("row"),
        P("row"),
        P("row", "col"),
        P("row", "col"),
        P("row", "col"),
        P("row", "col"),
        P("row", "col"),
        P("row", None, "col"),
        P("row", None, "col"),
        P("row", None, "col"),
    )
    local = fast if takes_fast(mesh) else general
    return jax.shard_map(local, mesh=mesh, in_specs=in_specs, out_specs=out_specs, check_vma=False)
```

```python
import functools

import jax
import jax.numpy as jnp
from jax import lax
from jax.experimental import pallas as pl
from jax.experimental.pallas import tpu as pltpu
from jax.sharding import PartitionSpec as P

D = 1024
H = 16
KVH = 8
HD = 64
E = 32
TOPK = 8
CAP = 80


EPS = 1e-06
NEGATIVE = -1e30


def cross_rows(left, right):
    return lax.dot_general(
        left, right, (((0,), (0,)), ((), ())), preferred_element_type=jnp.float32
    )


def times_back(left, right):
    return lax.dot_general(
        left, right, (((1,), (1,)), ((), ())), preferred_element_type=jnp.float32
    )


def rope_tables(first_position, count):
    position = (first_position + jnp.arange(count, dtype=jnp.int32)).astype(jnp.float32)
    inverse = 10000.0 ** (-jnp.arange(HD // 2, dtype=jnp.float32) * 2.0 / HD)
    angle = position[:, None] * inverse[None, :]
    return (jnp.cos(angle), jnp.sin(angle))


def rotate(values, cosine, sine):
    half = HD // 2
    first, second = (values[..., :half], values[..., half:])
    cos_rows = cosine[:, None, :]
    sin_rows = sine[:, None, :]
    return jnp.concatenate(
        [first * cos_rows - second * sin_rows, second * cos_rows + first * sin_rows], axis=-1
    )


def rotate_back(grads, cosine, sine):
    half = HD // 2
    first, second = (grads[..., :half], grads[..., half:])
    cos_rows = cosine[:, None, :]
    sin_rows = sine[:, None, :]
    return jnp.concatenate(
        [first * cos_rows + second * sin_rows, second * cos_rows - first * sin_rows], axis=-1
    )


def norm_rows(values, gain):
    scale = lax.rsqrt(jnp.mean(values * values, axis=1, keepdims=True) + EPS)
    normed = values * scale
    return (normed, scale, (normed * gain).astype(jnp.bfloat16))


def norm_back(grad_in, normed, scale, gain):
    gain_grad = jnp.sum(grad_in * normed, axis=0)
    inner = grad_in * gain
    return (scale * (inner - normed * jnp.mean(inner * normed, axis=1, keepdims=True)), gain_grad)


def to_heads(rows, count, group):
    return rows.reshape(count, KVH, group, HD).transpose(1, 2, 0, 3).reshape(KVH, group * count, HD)


def from_heads(heads, count, group):
    return heads.reshape(KVH, group, count, HD).transpose(2, 0, 1, 3).reshape(count, H, HD)


def general(
    block_in,
    attn_gain,
    moe_gain,
    w_query,
    w_key,
    w_value,
    w_out,
    w_router,
    w_gate,
    w_up,
    w_down,
    expert_ids,
    fill_order,
    prefix_len,
    out_grad,
):
    tok_rows = block_in.shape[0]
    n_col = lax.axis_size("col")
    col_index = lax.axis_index("col")
    seq_rows = tok_rows * n_col
    group = H // KVH
    scale_attn = HD ** (-0.5)
    bf16 = jnp.bfloat16
    f32 = jnp.float32
    shared = (
        lax.all_gather(w_query, "row", axis=0, tiled=True),
        lax.all_gather(w_key, "row", axis=0, tiled=True),
        lax.all_gather(w_value, "row", axis=0, tiled=True),
        lax.all_gather(w_out, "row", axis=0, tiled=True),
        lax.all_gather(w_router, "row", axis=0, tiled=True),
        lax.all_gather(attn_gain, "row", axis=0, tiled=True),
        lax.all_gather(moe_gain, "row", axis=0, tiled=True),
    )
    wq_full, wk_full, wv_full, wo_full, wr_full = (
        lax.all_gather(shared[0], "col", axis=1, tiled=True),
        lax.all_gather(shared[1], "col", axis=1, tiled=True),
        lax.all_gather(shared[2], "col", axis=1, tiled=True),
        lax.all_gather(shared[3], "col", axis=1, tiled=True),
        lax.all_gather(shared[4], "col", axis=1, tiled=True),
    )
    gain_one = shared[5].astype(f32)
    gain_two = shared[6].astype(f32)
    x_rows = block_in.astype(f32)
    normed_one, scale_one, attn_in = norm_rows(x_rows, gain_one)
    query = jnp.dot(attn_in, wq_full, preferred_element_type=f32)
    key = jnp.dot(attn_in, wk_full, preferred_element_type=f32)
    value = jnp.dot(attn_in, wv_full, preferred_element_type=f32).astype(bf16)
    cosine, sine = rope_tables(col_index * tok_rows, tok_rows)
    query_rot = rotate(query.reshape(tok_rows, H, HD), cosine, sine).astype(bf16)
    key_rot = (
        rotate(key.reshape(tok_rows, KVH, HD), cosine, sine)
        .astype(bf16)
        .reshape(tok_rows, KVH * HD)
    )
    keys_all, values_all = (
        lax.all_gather(key_rot, "col", axis=0, tiled=True),
        lax.all_gather(value, "col", axis=0, tiled=True),
    )
    prefix = prefix_len[0]
    query_spot = col_index * tok_rows + jnp.arange(tok_rows, dtype=jnp.int32)
    key_spot = jnp.arange(seq_rows, dtype=jnp.int32)
    allowed = (key_spot[None, :] <= query_spot[:, None]) | (key_spot[None, :] < prefix)
    allowed_rows = jnp.tile(allowed, (group, 1))
    query_heads = to_heads(query_rot.reshape(tok_rows, H * HD), tok_rows, group)
    key_heads = keys_all.reshape(seq_rows, KVH, HD).transpose(1, 0, 2)
    value_heads = values_all.reshape(seq_rows, KVH, HD).transpose(1, 0, 2)

    def attend(pieces):
        queries, keys, values = pieces
        scores = times_back(queries, keys) * scale_attn
        scores = jnp.where(allowed_rows, scores, NEGATIVE)
        highest = jnp.max(scores, axis=1, keepdims=True)
        expo = jnp.exp(scores - highest)
        total = jnp.sum(expo, axis=1, keepdims=True)
        weights = (expo / total).astype(bf16)
        mixed_heads = jnp.dot(weights, values, preferred_element_type=f32).astype(bf16)
        return (mixed_heads, (highest + jnp.log(total))[:, 0])

    mixed_heads, lse_heads = lax.map(attend, (query_heads, key_heads, value_heads))
    mixed = from_heads(mixed_heads, tok_rows, group).reshape(tok_rows, H * HD)
    resid = x_rows + jnp.dot(mixed, wo_full, preferred_element_type=f32)
    normed_two, scale_two, moe_in = norm_rows(resid, gain_two)
    logits = jnp.dot(moe_in, wr_full, preferred_element_type=f32)
    choice_hot = (expert_ids[:, :, None] == jnp.arange(E, dtype=jnp.int32)).astype(f32)
    picked = jnp.sum(choice_hot * logits[:, None, :], axis=2)
    highest = jnp.max(picked, axis=1, keepdims=True)
    expo = jnp.exp(picked - highest)
    gates = expo / jnp.sum(expo, axis=1, keepdims=True)
    order = fill_order[0]
    ranked = expert_ids[order]
    onehot = (ranked.reshape(-1, 1) == jnp.arange(E, dtype=jnp.int32)).astype(jnp.int32)
    before = jnp.cumsum(onehot, axis=0) - onehot
    ranked_slot = jnp.sum(before * onehot, axis=1).reshape(tok_rows, TOPK)
    slot = jnp.zeros((tok_rows, TOPK), jnp.int32).at[order].set(ranked_slot)
    kept = slot < CAP
    dest_grid = jnp.where(kept, expert_ids * CAP + slot, E * CAP)
    pair_ids = jnp.arange(tok_rows * TOPK, dtype=jnp.int32)
    slot_pair = (
        jnp.full((E * CAP + 1,), tok_rows * TOPK, jnp.int32)
        .at[dest_grid.reshape(-1)]
        .set(pair_ids)[: E * CAP]
    )
    slot_token = slot_pair // TOPK
    gate_slot = jnp.concatenate([gates.reshape(-1), jnp.zeros((1,), f32)])[slot_pair]
    moe_pad = jnp.concatenate([moe_in, jnp.zeros((1, D), bf16)])
    dispatch = moe_pad[slot_token].reshape(E, CAP, D)
    received = lax.all_to_all(dispatch, "row", split_axis=0, concat_axis=1, tiled=True)
    gate_w, up_w, down_w = (
        lax.all_gather(w_gate, "col", axis=2, tiled=True),
        lax.all_gather(w_up, "col", axis=2, tiled=True),
        lax.all_gather(w_down, "col", axis=2, tiled=True),
    )
    hidden_gate = jnp.einsum("erd,edf->erf", received, gate_w, preferred_element_type=f32)
    hidden_up = jnp.einsum("erd,edf->erf", received, up_w, preferred_element_type=f32)
    active = (jax.nn.silu(hidden_gate) * hidden_up).astype(bf16)
    expert_out = jnp.einsum("erf,edf->erd", active, down_w, preferred_element_type=f32).astype(bf16)
    returned = lax.all_to_all(expert_out, "row", split_axis=1, concat_axis=0, tiled=True)
    out_pad = jnp.concatenate([returned.reshape(E * CAP, D), jnp.zeros((1, D), bf16)])
    pair_out = out_pad[dest_grid]
    weight_pair = gates * kept.astype(f32)
    moe_out = jnp.zeros((tok_rows, D), f32)
    for choice_index in range(TOPK):
        moe_out = moe_out + weight_pair[:, choice_index : choice_index + 1] * pair_out[
            :, choice_index
        ].astype(f32)
    block_out = resid + moe_out
    grad_out = out_grad.astype(f32)
    gate_grad = jnp.stack(
        [
            jnp.sum(pair_out[:, choice_index].astype(f32) * grad_out, axis=1)
            for choice_index in range(TOPK)
        ],
        axis=1,
    )
    grad_pad = jnp.concatenate([grad_out, jnp.zeros((1, D), f32)])
    slot_grad = (gate_slot[:, None] * grad_pad[slot_token]).astype(bf16).reshape(E, CAP, D)
    out_grads = lax.all_to_all(slot_grad, "row", split_axis=0, concat_axis=1, tiled=True)
    act_grad = jnp.einsum("erd,edf->erf", out_grads, down_w, preferred_element_type=f32)
    sigma = jax.nn.sigmoid(hidden_gate)
    gate_h_grad = (act_grad * hidden_up * sigma * (1.0 + hidden_gate * (1.0 - sigma))).astype(bf16)
    up_h_grad = (act_grad * hidden_gate * sigma).astype(bf16)
    down_wgrad = jnp.einsum("erd,erf->edf", out_grads, active, preferred_element_type=f32)
    gate_wgrad = jnp.einsum("erd,erf->edf", received, gate_h_grad, preferred_element_type=f32)
    up_wgrad = jnp.einsum("erd,erf->edf", received, up_h_grad, preferred_element_type=f32)
    in_grad = (
        jnp.einsum("erf,edf->erd", gate_h_grad, gate_w, preferred_element_type=f32)
        + jnp.einsum("erf,edf->erd", up_h_grad, up_w, preferred_element_type=f32)
    ).astype(bf16)
    back_rows = lax.all_to_all(in_grad, "row", split_axis=1, concat_axis=0, tiled=True)
    gate_sum, up_sum, down_sum = (
        lax.psum_scatter(
            gate_wgrad.astype(jnp.bfloat16), "col", scatter_dimension=2, tiled=True
        ).astype(jnp.float32),
        lax.psum_scatter(
            up_wgrad.astype(jnp.bfloat16), "col", scatter_dimension=2, tiled=True
        ).astype(jnp.float32),
        lax.psum_scatter(
            down_wgrad.astype(jnp.bfloat16), "col", scatter_dimension=2, tiled=True
        ).astype(jnp.float32),
    )
    back_pad = jnp.concatenate([back_rows.reshape(E * CAP, D), jnp.zeros((1, D), bf16)])
    pair_back = back_pad[dest_grid]
    moe_in_grad = jnp.zeros((tok_rows, D), f32)
    for choice_index in range(TOPK):
        moe_in_grad = moe_in_grad + pair_back[:, choice_index].astype(f32)
    picked_grad = gates * (gate_grad - jnp.sum(gates * gate_grad, axis=1, keepdims=True))
    logit_grad = jnp.sum(choice_hot * picked_grad[:, :, None], axis=1).astype(bf16)
    router_wgrad = cross_rows(moe_in, logit_grad)
    moe_in_grad = moe_in_grad + times_back(logit_grad, wr_full)
    norm_two_grad, gain_two_grad = norm_back(moe_in_grad, normed_two, scale_two, gain_two)
    resid_grad = grad_out + norm_two_grad
    branch_grad = resid_grad.astype(bf16)
    out_wgrad = cross_rows(mixed, branch_grad)
    mixed_grad = times_back(branch_grad, wo_full).astype(bf16)
    grad_heads = to_heads(mixed_grad, tok_rows, group)

    def query_side(pieces):
        queries, keys, values, lse_rows, grad_rows = pieces
        scores = jnp.where(allowed_rows, times_back(queries, keys) * scale_attn, NEGATIVE)
        probs = jnp.exp(scores - lse_rows[:, None])
        prob_grad = times_back(grad_rows, values)
        delta = jnp.sum(probs * prob_grad, axis=1, keepdims=True)
        score_grad = (probs * (prob_grad - delta)).astype(bf16)
        query_grad = jnp.dot(score_grad, keys, preferred_element_type=f32) * scale_attn
        return (query_grad, delta[:, 0], score_grad, probs)

    def both_sides(pieces):
        queries, keys, values, lse_rows, grad_rows = pieces
        query_grad, delta, score_grad, probs = query_side(pieces)
        key_grad = cross_rows(score_grad, queries) * scale_attn
        value_grad = cross_rows(probs.astype(bf16), grad_rows)
        return (query_grad, key_grad, value_grad)

    query_rot_grad, key_parts, value_parts = lax.map(
        both_sides, (query_heads, key_heads, value_heads, lse_heads, grad_heads)
    )
    key_rot_grad, value_grad = (
        lax.psum_scatter(
            key_parts.transpose(1, 0, 2).reshape(seq_rows, KVH * HD).astype(jnp.bfloat16),
            "col",
            scatter_dimension=0,
            tiled=True,
        ).astype(jnp.float32),
        lax.psum_scatter(
            value_parts.transpose(1, 0, 2).reshape(seq_rows, KVH * HD).astype(jnp.bfloat16),
            "col",
            scatter_dimension=0,
            tiled=True,
        ).astype(jnp.float32),
    )
    query_grad = (
        rotate_back(from_heads(query_rot_grad, tok_rows, group), cosine, sine)
        .reshape(tok_rows, H * HD)
        .astype(bf16)
    )
    key_grad = (
        rotate_back(key_rot_grad.reshape(tok_rows, KVH, HD), cosine, sine)
        .reshape(tok_rows, KVH * HD)
        .astype(bf16)
    )
    value_grad = value_grad.astype(bf16)
    query_wgrad = cross_rows(attn_in, query_grad)
    key_wgrad = cross_rows(attn_in, key_grad)
    value_wgrad = cross_rows(attn_in, value_grad)
    attn_in_grad = (
        times_back(query_grad, wq_full)
        + times_back(key_grad, wk_full)
        + times_back(value_grad, wv_full)
    )
    norm_one_grad, gain_one_grad = norm_back(attn_in_grad, normed_one, scale_one, gain_one)
    block_in_grad = resid_grad + norm_one_grad
    spread_one = jnp.broadcast_to(gain_one_grad[:, None], (D, n_col))
    spread_two = jnp.broadcast_to(gain_two_grad[:, None], (D, n_col))
    col_sums = (
        lax.psum_scatter(
            query_wgrad.astype(jnp.bfloat16), "col", scatter_dimension=1, tiled=True
        ).astype(jnp.float32),
        lax.psum_scatter(
            key_wgrad.astype(jnp.bfloat16), "col", scatter_dimension=1, tiled=True
        ).astype(jnp.float32),
        lax.psum_scatter(
            value_wgrad.astype(jnp.bfloat16), "col", scatter_dimension=1, tiled=True
        ).astype(jnp.float32),
        lax.psum_scatter(
            out_wgrad.astype(jnp.bfloat16), "col", scatter_dimension=1, tiled=True
        ).astype(jnp.float32),
        lax.psum_scatter(
            router_wgrad.astype(jnp.bfloat16), "col", scatter_dimension=1, tiled=True
        ).astype(jnp.float32),
        lax.psum_scatter(
            spread_one.astype(jnp.bfloat16), "col", scatter_dimension=1, tiled=True
        ).astype(jnp.float32),
        lax.psum_scatter(
            spread_two.astype(jnp.bfloat16), "col", scatter_dimension=1, tiled=True
        ).astype(jnp.float32),
    )
    row_sums = (
        lax.psum_scatter(
            col_sums[0].astype(jnp.bfloat16), "row", scatter_dimension=0, tiled=True
        ).astype(jnp.float32),
        lax.psum_scatter(
            col_sums[1].astype(jnp.bfloat16), "row", scatter_dimension=0, tiled=True
        ).astype(jnp.float32),
        lax.psum_scatter(
            col_sums[2].astype(jnp.bfloat16), "row", scatter_dimension=0, tiled=True
        ).astype(jnp.float32),
        lax.psum_scatter(
            col_sums[3].astype(jnp.bfloat16), "row", scatter_dimension=0, tiled=True
        ).astype(jnp.float32),
        lax.psum_scatter(
            col_sums[4].astype(jnp.bfloat16), "row", scatter_dimension=0, tiled=True
        ).astype(jnp.float32),
        lax.psum_scatter(
            col_sums[5].astype(jnp.bfloat16), "row", scatter_dimension=0, tiled=True
        ).astype(jnp.float32),
        lax.psum_scatter(
            col_sums[6].astype(jnp.bfloat16), "row", scatter_dimension=0, tiled=True
        ).astype(jnp.float32),
    )
    return (
        block_out,
        block_in_grad,
        row_sums[5][:, 0],
        row_sums[6][:, 0],
        row_sums[0],
        row_sums[1],
        row_sums[2],
        row_sums[3],
        row_sums[4],
        gate_sum,
        up_sum,
        down_sum,
    )


F32 = jnp.float32
BF16 = jnp.bfloat16
MIB = 1024 * 1024
LANES = 128
VMEM_MOST = 60 * MIB
COST_SCALE = 10**6


def cost(microseconds):
    return pl.CostEstimate(flops=int(microseconds * COST_SCALE), bytes_accessed=10**5, transcendentals=0)


def dot_nn(a, b):
    return lax.dot_general(a, b, (((1,), (0,)), ((), ())), preferred_element_type=F32)


def dot_nt(a, b):
    return lax.dot_general(a, b, (((1,), (1,)), ((), ())), preferred_element_type=F32)


def dot_tn(a, b):
    return lax.dot_general(a, b, (((0,), (0,)), ((), ())), preferred_element_type=F32)


def in_vmem():
    return pl.BlockSpec(memory_space=pltpu.VMEM)


def in_smem():
    return pl.BlockSpec(memory_space=pltpu.SMEM)


def in_hbm():
    return pl.BlockSpec(memory_space=pl.ANY)


def behind(kernel, n_in, after):
    if not after:
        return kernel
    return lambda *refs: kernel(*refs[:n_in], *refs[n_in + len(after) :])


def partner(values):
    lane = lax.broadcasted_iota(jnp.int32, values.shape, 1)
    half = HD // 2
    return jnp.where(
        lane % HD < half,
        pltpu.roll(values, LANES - half, 1),
        pltpu.roll(values, half, 1),
    )


def attend_kernel(
    spot_ref, x0, x1, x2, x3, pack_ref, cos_ref, sin_ref,
    attn_ref, q_ref, k_ref, v_ref, lse_ref, w_ref, gain_ref, mixed_ref,
):
    rows = x0.shape[0]
    col, prefix = spot_ref[0], spot_ref[1]
    for part in range(8):
        span = pl.ds(part * LANES, LANES)
        w_ref[span, :] = pack_ref[part, :LANES, :]
        gain_ref[0:1, span] = pack_ref[part, LANES : LANES + 1, :LANES].astype(F32)
        gain_ref[1:2, span] = pack_ref[part, LANES : LANES + 1, LANES : 2 * LANES].astype(F32)
    gain = gain_ref[0:1, :]
    for step, chunk in enumerate((x0, x1, x2, x3)):
        source = lax.rem(col - step + 4, 4)
        x = chunk[...].astype(F32)
        scale = lax.rsqrt(jnp.mean(x * x, axis=1, keepdims=True) + EPS)
        attn_ref[pl.ds(pl.multiple_of(source * rows, rows), rows), :] = (x * scale * gain).astype(BF16)
    for tile in range(4):
        span = pl.ds(tile * rows, rows)
        qkv = dot_nn(attn_ref[span, :], w_ref[...])
        cosine, sine = cos_ref[span, :], sin_ref[span, :]
        for block in range(3):
            v = qkv[:, block * LANES : (block + 1) * LANES]
            y = v * cosine + partner(v) * sine
            if block < 2:
                y = (y * HD ** (-0.5)).astype(BF16)
                q_ref[2 * block, span, :] = y[:, :HD]
                q_ref[2 * block + 1, span, :] = y[:, HD:]
            else:
                y = y.astype(BF16)
                k_ref[0, span, :] = y[:, :HD]
                k_ref[1, span, :] = y[:, HD:]
        v = qkv[:, 3 * LANES :].astype(BF16)
        v_ref[0, span, :] = v[:, :HD]
        v_ref[1, span, :] = v[:, HD:]
    total = 4 * rows
    for tile in range(4):
        span = pl.ds(tile * rows, rows)
        keys = max((tile + 1) * rows, total // 2)
        key_spot = lax.broadcasted_iota(jnp.int32, (rows, keys), 1)
        query_spot = lax.broadcasted_iota(jnp.int32, (rows, keys), 0) + tile * rows
        allowed = (key_spot <= query_spot) | (key_spot < prefix)
        for pair in range(2):
            k, v = k_ref[pair, pl.ds(0, keys), :], v_ref[pair, pl.ds(0, keys), :]
            outs = []
            for head in (2 * pair, 2 * pair + 1):
                scores = jnp.where(allowed, dot_nt(q_ref[head, span, :], k), NEGATIVE)
                highest = jnp.max(scores, axis=1, keepdims=True)
                expo = jnp.exp(scores - highest)
                summed = jnp.sum(expo, axis=1, keepdims=True)
                outs.append(dot_nn(expo.astype(BF16), v) * (1.0 / summed))
                lse_ref[span, head : head + 1] = highest + jnp.log(summed)
            mixed_ref[span, pair * LANES : (pair + 1) * LANES] = jnp.concatenate(outs, axis=1).astype(BF16)


def attend(spots, chunks, pack, cosine, sine, after=()):
    rows = chunks[0].shape[0]
    seq = 4 * rows
    shapes = (
        jax.ShapeDtypeStruct((seq, D), BF16),
        jax.ShapeDtypeStruct((4, seq, HD), BF16),
        jax.ShapeDtypeStruct((2, seq, HD), BF16),
        jax.ShapeDtypeStruct((2, seq, HD), BF16),
        jax.ShapeDtypeStruct((seq, 4), F32),
        jax.ShapeDtypeStruct((D, 512), BF16),
        jax.ShapeDtypeStruct((2, D), F32),
        jax.ShapeDtypeStruct((seq, 256), BF16),
    )
    return pl.pallas_call(
        behind(attend_kernel, 8, after),
        out_shape=shapes,
        in_specs=[in_smem()] + [in_vmem()] * 7 + [in_hbm()] * len(after),
        out_specs=tuple(in_vmem() for _ in shapes),
        compiler_params=pltpu.CompilerParams(vmem_limit_bytes=VMEM_MOST),
        cost_estimate=cost(10),
    )(spots, *chunks, pack, cosine, sine, *after)


def attend_back_kernel(
    spot_ref, grad_ref, mixed_ref, q_ref, k_ref, v_ref, lse_ref, attn_ref, w_ref, cos_ref, sin_ref, gain_ref,
    wgrad_ref, in0, in1, in2, in3, dqkv_ref, dk_ref, dv_ref, dq_ref, mg_ref,
):
    seq = attn_ref.shape[0]
    rows = seq // 4
    prefix = spot_ref[1]
    for tile in range(4):
        span = pl.ds(tile * rows, rows)
        for pair in range(2):
            g = grad_ref[span, pair * LANES : (pair + 1) * LANES]
            mg_ref[2 * pair, span, :] = g[:, :HD]
            mg_ref[2 * pair + 1, span, :] = g[:, HD:]
    dk_ref[...] = jnp.zeros_like(dk_ref)
    dv_ref[...] = jnp.zeros_like(dv_ref)
    for tile in range(4):
        span = pl.ds(tile * rows, rows)
        keys = max((tile + 1) * rows, seq // 2)
        key_spot = lax.broadcasted_iota(jnp.int32, (rows, keys), 1)
        query_spot = lax.broadcasted_iota(jnp.int32, (rows, keys), 0) + tile * rows
        allowed = (key_spot <= query_spot) | (key_spot < prefix)
        for pair in range(2):
            k, v = k_ref[pair, pl.ds(0, keys), :], v_ref[pair, pl.ds(0, keys), :]
            both = grad_ref[span, pair * LANES : (pair + 1) * LANES].astype(F32) * mixed_ref[
                span, pair * LANES : (pair + 1) * LANES
            ].astype(F32)
            outs = []
            for at, head in enumerate((2 * pair, 2 * pair + 1)):
                q, g = q_ref[head, span, :], mg_ref[head, span, :]
                delta = jnp.sum(both[:, at * HD : (at + 1) * HD], axis=1, keepdims=True)
                scores = jnp.where(allowed, dot_nt(q, k), NEGATIVE)
                probs = jnp.exp(scores - lse_ref[span, head : head + 1])
                score_grad = (probs * (dot_nt(g, v) - delta)).astype(BF16)
                dv_ref[pair, pl.ds(0, keys), :] += dot_tn(probs.astype(BF16), g)
                dk_ref[pair, pl.ds(0, keys), :] += dot_tn(score_grad, q)
                outs.append(dot_nn(score_grad, k) * HD ** (-0.5))
            dq_ref[span, pair * LANES : (pair + 1) * LANES] = jnp.concatenate(outs, axis=1)
    for tile in range(4):
        span = pl.ds(tile * rows, rows)
        cosine, sine = cos_ref[span, :], sin_ref[span, :]
        for block in range(3):
            if block < 2:
                g = dq_ref[span, block * LANES : (block + 1) * LANES]
            else:
                g = jnp.concatenate([dk_ref[0, span, :], dk_ref[1, span, :]], axis=1)
            dqkv_ref[span, block * LANES : (block + 1) * LANES] = (g * cosine - partner(g) * sine).astype(BF16)
        dqkv_ref[span, 3 * LANES :] = jnp.concatenate([dv_ref[0, span, :], dv_ref[1, span, :]], axis=1).astype(BF16)
    gain_total = jnp.zeros((1, D), F32)
    for step, out in enumerate((in0, in1, in2, in3)):
        source = lax.rem(spot_ref[0] - step + 4, 4)
        span = pl.ds(pl.multiple_of(source * rows, rows), rows)
        back = dot_nt(dqkv_ref[span, :], w_ref[...])
        out[...] = back.astype(BF16)
        gain_total = gain_total + jnp.sum(back * attn_ref[span, :].astype(F32), axis=0, keepdims=True)
    gain_total = gain_total / gain_ref[0:1, :]
    for part in range(8):
        span = pl.ds(part * LANES, LANES)
        wgrad_ref[part, LANES:, :LANES] = jnp.broadcast_to(gain_total[:, part * LANES : (part + 1) * LANES], (8, LANES)).astype(BF16)
        wgrad_ref[part, LANES:, LANES:] = jnp.zeros((8, 3 * LANES), BF16)
        wgrad_ref[part, :LANES, :] = dot_tn(attn_ref[:, span], dqkv_ref[...]).astype(BF16)


def attend_back(spots, grads, mixed, q, k, v, lse, attn_in, w_qkv, cosine, sine, gain, after=()):
    seq = attn_in.shape[0]
    shapes = (
        jax.ShapeDtypeStruct((8, 136, 512), BF16),
    ) + (jax.ShapeDtypeStruct((seq // 4, D), BF16),) * 4
    return pl.pallas_call(
        behind(attend_back_kernel, 12, after),
        out_shape=shapes,
        in_specs=[in_smem()] + [in_vmem()] * 11 + [in_hbm()] * len(after),
        out_specs=tuple(in_vmem() for _ in shapes),
        scratch_shapes=[
            pltpu.VMEM((seq, 512), BF16),
            pltpu.VMEM((2, seq, HD), F32),
            pltpu.VMEM((2, seq, HD), F32),
            pltpu.VMEM((seq, 256), F32),
            pltpu.VMEM((4, seq, HD), BF16),
        ],
        compiler_params=pltpu.CompilerParams(vmem_limit_bytes=VMEM_MOST),
        cost_estimate=cost(16),
    )(spots, grads, mixed, q, k, v, lse, attn_in, w_qkv, cosine, sine, gain, *after)


def route_kernel(
    spot_ref, mixed_ref, x_ref, pack_ref, gain_ref, ids_ref, order_ref,
    resid_ref, send_ref, gates_ref, kept_ref, wo_ref, wr_ref, wr_wide,
):
    rows = x_ref.shape[0]
    wr_wide[...] = jnp.zeros_like(wr_wide)
    for row in range(8):
        span = pl.ds(row * LANES, LANES)
        for col in range(4):
            wo_ref[span, col * 256 : (col + 1) * 256] = pack_ref[row, col, :LANES, :]
            wr_wide[col * 8 : (col + 1) * 8, span] = pack_ref[row, col, LANES:, :LANES].astype(F32)
    wr_ref[...] = wr_wide[...].astype(BF16)
    resid = x_ref[...].astype(F32)
    for part in range(4):
        resid = resid + dot_nn(mixed_ref[pl.ds(part * rows, rows), :], wo_ref[part * 256 : (part + 1) * 256, :])
    resid_ref[...] = resid
    scale = lax.rsqrt(jnp.mean(resid * resid, axis=1, keepdims=True) + EPS)
    moe_in = (resid * scale * gain_ref[1:2, :]).astype(BF16)
    send_ref[:, :D] = moe_in
    logits = dot_nt(moe_in, wr_ref[...])
    lane = lax.broadcasted_iota(jnp.int32, (rows, LANES), 1)
    chosen = jnp.zeros((rows, LANES), jnp.bool_)
    for choice in range(TOPK):
        chosen = chosen | (ids_ref[:, choice : choice + 1] == lane)
    picked = jnp.where(chosen, logits, NEGATIVE)
    expo = jnp.exp(picked - jnp.max(picked, axis=1, keepdims=True))
    gates = expo / jnp.sum(expo, axis=1, keepdims=True)
    first = lax.broadcasted_iota(jnp.int32, (rows, rows), 0)
    second = lax.broadcasted_iota(jnp.int32, (rows, rows), 1)
    place = (first == order_ref[...]).astype(BF16)
    sooner = dot_nn(place, (second < first).astype(BF16)).astype(BF16)
    sooner = dot_nt(sooner, place).astype(BF16)
    slot = dot_nn(sooner, chosen.astype(BF16))
    kept = (chosen & (slot < CAP)).astype(F32)
    gates_ref[...] = gates
    kept_ref[...] = kept
    send_ref[:, D:] = dot_nn((gates * kept).astype(BF16), relabel(spot_ref[2])).astype(BF16)


def relabel(row):
    first = lax.broadcasted_iota(jnp.int32, (LANES, LANES), 0)
    second = lax.broadcasted_iota(jnp.int32, (LANES, LANES), 1)
    return (first == (second ^ (row * 4))).astype(BF16)


def route(spots, mixed, x, pack, gain, ids, order, after=()):
    rows = x.shape[0]
    shapes = (
        jax.ShapeDtypeStruct((rows, D), F32),
        jax.ShapeDtypeStruct((rows, D + LANES), BF16),
        jax.ShapeDtypeStruct((rows, LANES), F32),
        jax.ShapeDtypeStruct((rows, LANES), F32),
        jax.ShapeDtypeStruct((D, D), BF16),
        jax.ShapeDtypeStruct((LANES, D), BF16),
    )
    return pl.pallas_call(
        behind(route_kernel, 7, after),
        out_shape=shapes,
        in_specs=[in_smem()] + [in_vmem()] * 6 + [in_hbm()] * len(after),
        out_specs=tuple(in_vmem() for _ in shapes),
        scratch_shapes=[pltpu.VMEM((LANES, D), F32)],
        compiler_params=pltpu.CompilerParams(vmem_limit_bytes=VMEM_MOST),
        cost_estimate=cost(2),
    )(spots, mixed, x, pack, gain, ids, order, *after)


def expert_kernel(x_ref, g_ref, *refs):
    weights, refs = refs[:10], refs[10:]
    back_ref, hg_ref, hu_ref, act_ref, out_acc, in_acc, gate_acc, held, sems = refs
    step = pl.program_id(0)
    count = held.shape[1]
    wide = count * LANES

    def fetch(at, slot):
        for k in range(8):

            @pl.when(at == k)
            def _():
                for i in range(2):
                    half = weights[k].at[pl.ds(2 * i, 2)] if k < 6 else weights[2 * k - 6 + i]
                    pltpu.make_async_copy(half, held.at[slot, pl.ds(2 * i, 2)], sems.at[slot, i]).start()

    @pl.when(step == 0)
    def _():
        fetch(step, 0)
        out_acc[...] = jnp.zeros_like(out_acc)
        in_acc[...] = jnp.zeros_like(in_acc)
        gate_acc[...] = jnp.zeros_like(gate_acc)

    now = lax.rem(step, 2)
    for i in range(2):
        pltpu.make_async_copy(weights[6], held.at[now, pl.ds(2 * i, 2)], sems.at[now, i]).wait()
    fetch(step + 1, 1 - now)

    join = lambda kind: jnp.concatenate([held[now, i, kind] for i in range(count)], axis=1)
    wg, wu, wd = join(0), join(1), join(2)
    x = x_ref[:, :D]
    expert = lax.broadcasted_iota(jnp.int32, (LANES, wide), 0)
    column = lax.broadcasted_iota(jnp.int32, (LANES, wide), 1)
    spread = (expert == step * count + column // LANES).astype(BF16)
    gate = dot_nn(x_ref[:, D:], spread)
    hidden_gate = dot_nn(x, wg)
    hidden_up = dot_nn(x, wu)
    act_grad = dot_nn(g_ref[...], wd)
    sigma = 0.5 * jnp.tanh(0.5 * hidden_gate) + 0.5
    swish = hidden_gate * sigma
    active = swish * hidden_up
    gate_acc[...] += dot_nt((active * act_grad).astype(BF16), spread)
    gated = (active * gate).astype(BF16)
    act_ref[...] = gated
    out_acc[...] += dot_nt(gated, wd)
    act_grad = act_grad * gate
    up_grad = (act_grad * swish).astype(BF16)
    gate_grad = (act_grad * hidden_up * (sigma + swish * (1.0 - sigma))).astype(BF16)
    hg_ref[...] = gate_grad
    hu_ref[...] = up_grad
    in_acc[...] += dot_nt(gate_grad, wg) + dot_nt(up_grad, wu)

    @pl.when(step == pl.num_programs(0) - 1)
    def _():
        back_ref[:, :D] = in_acc[...].astype(BF16)
        back_ref[:, D : 2 * D] = out_acc[...].astype(BF16)
        back_ref[:, 2 * D :] = gate_acc[...].astype(BF16)


def experts(x, g, weights, after=()):
    rows = x.shape[0]
    count = 4
    steps = 8
    wide = count * LANES
    hidden = pl.BlockSpec((rows, wide), lambda i: (0, i))
    whole = lambda width: pl.BlockSpec((rows, width), lambda i: (0, 0))
    return pl.pallas_call(
        behind(expert_kernel, 12, after),
        out_shape=(jax.ShapeDtypeStruct((rows, 2 * D + LANES), BF16),)
        + (jax.ShapeDtypeStruct((rows, steps * wide), BF16),) * 3,
        grid_spec=pltpu.PrefetchScalarGridSpec(
            num_scalar_prefetch=0,
            grid=(steps,),
            in_specs=[whole(D + LANES), whole(D)] + [in_hbm()] * (10 + len(after)),
            out_specs=(whole(2 * D + LANES), hidden, hidden, hidden),
            scratch_shapes=[
                pltpu.VMEM((rows, D), F32),
                pltpu.VMEM((rows, D), F32),
                pltpu.VMEM((rows, LANES), F32),
                pltpu.VMEM((2, count, 3, D, LANES), BF16),
                pltpu.SemaphoreType.DMA((2, 2)),
            ],
        ),
        compiler_params=pltpu.CompilerParams(vmem_limit_bytes=VMEM_MOST),
        cost_estimate=cost(21),
    )(x, g, *weights, *after)


def flip_kernel(x0, x1, x2, x3, g0, g1, g2, g3, xt_ref, gt_ref):
    rows = x0.shape[0]
    for at, (x, g) in enumerate(zip((x0, x1, x2, x3), (g0, g1, g2, g3))):
        xt_ref[:, at * rows : (at + 1) * rows] = x[:, :D].T
        gt_ref[:, at * rows : (at + 1) * rows] = g[...].T


def flip(xs, gs, after=()):
    seq = 4 * xs[0].shape[0]
    return pl.pallas_call(
        behind(flip_kernel, 8, after),
        out_shape=(jax.ShapeDtypeStruct((D, seq), BF16),) * 2,
        in_specs=[in_vmem()] * 8 + [in_hbm()] * len(after),
        out_specs=(in_vmem(),) * 2,
        compiler_params=pltpu.CompilerParams(vmem_limit_bytes=VMEM_MOST),
        cost_estimate=cost(2),
    )(*xs, *gs, *after)


def expert_wgrad_kernel(places, added, late, xt_ref, gt_ref, *refs):
    hidden, refs = refs[:12], refs[12:]
    count = len(places)
    n_extra = len({place[0] for place in added if place}) + len(late)
    plain = [k for k, place in enumerate(added) if not place]
    extras, refs = refs[:n_extra], refs[n_extra:]
    n_out = len({which for which, _ in places})
    outs, refs = refs[:n_out], refs[n_out:]
    held, out_sems, got, in_sems = refs
    step = pl.program_id(0)
    now = lax.rem(step, 2)

    def fetch(at, slot):
        for k, place in enumerate(added):
            if not place:
                continue
            which, half = place

            @pl.when(at == k)
            def _():
                pltpu.make_async_copy(extras[which].at[half], got.at[slot, 0], in_sems.at[slot, 0]).start()
                if k in late:
                    pltpu.make_async_copy(extras[late[k]].at[0], got.at[slot, 1], in_sems.at[slot, 1]).start()

    if added:

        @pl.when(step == 0)
        def _():
            fetch(step, 0)

        fetch(step + 1, 1 - now)

    def sent(slot):
        pltpu.make_async_copy(held.at[slot], outs[0].at[0], out_sems.at[slot]).wait()

    @pl.when(step >= 2)
    def _():
        sent(now)

    first = functools.reduce(jnp.logical_and, [step != k for k in plain], step >= 0)
    second = functools.reduce(jnp.logical_or, [step == k for k in late], False)
    if added:

        @pl.when(functools.reduce(jnp.logical_and, [step != k for k in plain], step >= 0))
        def _():
            pltpu.make_async_copy(extras[0].at[0], got.at[now, 0], in_sems.at[now, 0]).wait()

        for k in late:

            @pl.when(step == k)
            def _():
                pltpu.make_async_copy(extras[0].at[0], got.at[now, 1], in_sems.at[now, 1]).wait()


    for kind, left in enumerate((xt_ref, xt_ref, gt_ref)):
        joined = jnp.concatenate([part[...] for part in hidden[kind * 4 : kind * 4 + 4]], axis=0)
        product = dot_nn(left[...], joined)
        for i in range(2):
            piece = product[:, i * LANES : (i + 1) * LANES]
            if plain:
                piece = piece + jnp.where(first, got[now, 0, i, kind].astype(F32), 0.0)
            elif added:
                piece = piece + got[now, 0, i, kind].astype(F32)
            if late:
                piece = piece + jnp.where(second, got[now, 1, i, kind].astype(F32), 0.0)
            held[now, i, kind] = piece.astype(BF16)

    for k, (which, half) in enumerate(places):

        @pl.when(step == k)
        def _():
            pltpu.make_async_copy(held.at[now], outs[which].at[half], out_sems.at[now]).start()

    @pl.when(step == count - 1)
    def _():
        sent(now)
        if count > 1:
            sent(1 - now)


def expert_wgrads(flipped, hidden, entries, places, extras=(), added=(), late=None, after=(), time=None):
    rows = hidden[0][0].shape[0]
    wide = 2 * LANES
    seq = flipped[0].shape[1]
    count = len(entries)

    def entry(i):
        place = entries[0]
        for k in range(1, count):
            place = jnp.where(i == k, entries[k], place)
        return (0, place)

    lane = pl.BlockSpec((rows, wide), entry)
    whole = pl.BlockSpec((D, seq), lambda i: (0, 0))
    kernel = functools.partial(expert_wgrad_kernel, places, added, late or {})
    sizes = [sum(which == o for which, _ in places) for o in range(max(which for which, _ in places) + 1)]
    return pl.pallas_call(
        behind(kernel, 14 + len(extras), after),
        grid=(count,),
        out_shape=tuple(jax.ShapeDtypeStruct((size, 2, 3, D, LANES), BF16) for size in sizes),
        in_specs=[whole] * 2 + [lane] * 12 + [in_hbm()] * (len(extras) + len(after)),
        out_specs=(in_hbm(),) * len(sizes),
        scratch_shapes=[
            pltpu.VMEM((2, 2, 3, D, LANES), BF16),
            pltpu.SemaphoreType.DMA((2,)),
            pltpu.VMEM((2, 2, 2, 3, D, LANES), BF16),
            pltpu.SemaphoreType.DMA((2, 2)),
        ],
        compiler_params=pltpu.CompilerParams(vmem_limit_bytes=VMEM_MOST),
        cost_estimate=cost(time or 2.2 * count),
    )(*flipped, *hidden[0], *hidden[1], *hidden[2], *extras, *after)


def expert_total_kernel(own_ref, xa_ref, xb_ref, ya_ref, yb_ref, gate_ref, up_ref, down_ref):
    for kind, out in enumerate((gate_ref, up_ref, down_ref)):
        for half, (x_ref, y_ref) in enumerate(((xa_ref, ya_ref), (xb_ref, yb_ref))):
            out[half, 0] = (
                own_ref[half, 0, kind].astype(F32) + x_ref[0, 0, kind].astype(F32) + y_ref[0, 0, kind].astype(F32)
            )


def expert_total(after, own, *parts):
    block = pl.BlockSpec((2, 1, 3, D, LANES), lambda i: (0, i, 0, 0, 0))
    part = pl.BlockSpec((1, 1, 3, D, LANES), lambda i: (0, i, 0, 0, 0))
    out = pl.BlockSpec((2, 1, D, LANES), lambda i: (0, i, 0, 0))
    sums = pl.pallas_call(
        behind(expert_total_kernel, 5, after),
        grid=(2,),
        out_shape=(jax.ShapeDtypeStruct((2, 2, D, LANES), F32),) * 3,
        in_specs=[block] + [part] * 4 + [in_hbm()] * len(after),
        out_specs=(out,) * 3,
        compiler_params=pltpu.CompilerParams(vmem_limit_bytes=VMEM_MOST),
        cost_estimate=cost(5),
    )(own, *parts, *after)
    return [total.reshape(4, D, LANES) for total in sums]


def halves_kernel(x_ref, y_ref, low_ref, high_ref):
    low_ref[...] = y_ref[...]
    high_ref[...] = x_ref[...]


def halves(from_x, from_y, after):
    half = jax.ShapeDtypeStruct((2, 3, D, LANES), BF16)
    first = pl.BlockSpec((1, 1, D, LANES), lambda i, j: (i, j, 0, 0))
    second = pl.BlockSpec((1, 1, D, LANES), lambda i, j: (i + 2, j, 0, 0))
    return pl.pallas_call(
        behind(halves_kernel, 2, after),
        grid=(2, 3),
        out_shape=(half, half),
        in_specs=[second, first] + [in_hbm()] * len(after),
        out_specs=(first,) * 2,
        compiler_params=pltpu.CompilerParams(vmem_limit_bytes=VMEM_MOST),
        cost_estimate=cost(3),
    )(from_x, from_y, *after)


def turn_kernel(
    spot_ref, came_ref, back_ref, gates_ref, kept_ref, resid_ref, gain_ref, g_ref, wr_ref, wo_ref, send_ref,
    out_ref, resid_grad_ref, branch_ref, mixed_grad_ref, small_ref,
):
    rows = resid_ref.shape[0]
    gates = gates_ref[...]
    both = lambda span: came_ref[:, span].astype(F32) + back_ref[:, span].astype(F32)
    out_ref[...] = resid_ref[...] + both(slice(D, 2 * D))
    gate_grad = dot_nn(both(slice(2 * D, None)).astype(BF16), relabel(spot_ref[2])) * kept_ref[...]
    logit_grad = gates * (gate_grad - jnp.sum(gates * gate_grad, axis=1, keepdims=True))
    logit_grad = logit_grad.astype(BF16)
    moe_grad = both(slice(0, D)) + dot_nn(logit_grad, wr_ref[...])
    resid = resid_ref[...]
    scale = lax.rsqrt(jnp.mean(resid * resid, axis=1, keepdims=True) + EPS)
    normed = resid * scale
    small_ref[LANES:, :] = jnp.broadcast_to(jnp.sum(moe_grad * normed, axis=0, keepdims=True), (8, D))
    small_ref[:LANES, :] = dot_tn(logit_grad, send_ref[:, :D])
    inner = moe_grad * gain_ref[1:2, :]
    grad = g_ref[...].astype(F32) + scale * (inner - normed * jnp.mean(inner * normed, axis=1, keepdims=True))
    resid_grad_ref[...] = grad
    branch = grad.astype(BF16)
    branch_ref[...] = branch
    for part in range(4):
        mixed_grad_ref[pl.ds(part * rows, rows), :] = dot_nt(
            branch, wo_ref[part * 256 : (part + 1) * 256, :]
        ).astype(BF16)


def turn(spots, came, back, gates, kept, resid, gain, g, wr, wo, send, after=()):
    rows = resid.shape[0]
    shapes = (
        jax.ShapeDtypeStruct((rows, D), F32),
        jax.ShapeDtypeStruct((rows, D), F32),
        jax.ShapeDtypeStruct((rows, D), BF16),
        jax.ShapeDtypeStruct((4 * rows, 256), BF16),
        jax.ShapeDtypeStruct((LANES + 8, D), F32),
    )
    return pl.pallas_call(
        behind(turn_kernel, 11, after),
        out_shape=shapes,
        in_specs=[in_smem()] + [in_vmem()] * 10 + [in_hbm()] * len(after),
        out_specs=tuple(in_vmem() for _ in shapes),
        compiler_params=pltpu.CompilerParams(vmem_limit_bytes=VMEM_MOST),
        cost_estimate=cost(2),
    )(spots, came, back, gates, kept, resid, gain, g, wr, wo, send, *after)


def out_wgrad_kernel(mixed_ref, branch_ref, small_ref, pack_ref):
    rows = branch_ref.shape[0]
    for part in range(4):
        product = dot_tn(mixed_ref[pl.ds(part * rows, rows), :], branch_ref[...]).astype(BF16)
        pack_ref[2 * part, :LANES, :] = product[:LANES]
        pack_ref[2 * part + 1, :LANES, :] = product[LANES:]
    for row in range(8):
        span = pl.ds(row * LANES, LANES)
        for col in range(4):
            pack_ref[row, LANES:, col * 256 : col * 256 + LANES] = small_ref[col * 8 : col * 8 + 8, span].astype(BF16)
            pack_ref[row, LANES:, col * 256 + LANES : col * 256 + 256] = small_ref[LANES:, span].astype(BF16)


def out_wgrad(mixed, branch, small, after=()):
    return pl.pallas_call(
        behind(out_wgrad_kernel, 3, after),
        out_shape=jax.ShapeDtypeStruct((8, LANES + 8, D), BF16),
        in_specs=[in_vmem()] * 3 + [in_hbm()] * len(after),
        out_specs=in_vmem(),
        compiler_params=pltpu.CompilerParams(vmem_limit_bytes=VMEM_MOST),
        cost_estimate=cost(3),
    )(mixed, branch, small, *after)


def unpack_kernel(sum_ref, query_ref, key_ref, value_ref, gain_ref):
    query_ref[...] = sum_ref[:LANES, :256].astype(F32)
    key_ref[...] = sum_ref[:LANES, 256:384].astype(F32)
    value_ref[...] = sum_ref[:LANES, 384:].astype(F32)
    gain_ref[...] = sum_ref[LANES:, :LANES].astype(F32)


def unpack(sums, after):
    return pl.pallas_call(
        behind(unpack_kernel, 1, after),
        out_shape=tuple(jax.ShapeDtypeStruct(shape, F32) for shape in ((LANES, 256), (LANES, LANES), (LANES, LANES), (8, LANES))),
        in_specs=[in_vmem()] + [in_hbm()] * len(after),
        out_specs=(in_vmem(),) * 4,
        compiler_params=pltpu.CompilerParams(vmem_limit_bytes=VMEM_MOST),
        cost_estimate=cost(2),
    )(sums, *after)


def ring_gather(value, n_col):
    steps = [(i, (i + 1) % n_col) for i in range(n_col)]
    chunks = [value]
    for _ in range(n_col - 1):
        chunks.append(lax.ppermute(chunks[-1], "col", steps))
    return chunks


def ring_sum(parts, n_col):
    steps = [(i, (i + 1) % n_col) for i in range(n_col)]
    total = parts[1]
    for part in parts[2:] + parts[:1]:
        total = lax.ppermute(total, "col", steps).astype(F32) + part.astype(F32)
        if part is not parts[0]:
            total = total.astype(BF16)
    return total


def shift_all(parts, n_col):
    return [
        lax.ppermute(part, "col", [(i, (i + s) % n_col) for i in range(n_col)]) if s else part
        for s, part in enumerate(parts)
    ]


def hold(value, *until):
    return lax.optimization_barrier((value, *until))[0]


CORE, ACROSS_X, ACROSS_Y = 1, 2, 4


def swap(value, mask):
    return lax.ppermute(value, "row", [(i, i ^ mask) for i in range(8)])


def fast(
    block_in,
    attn_gain,
    moe_gain,
    w_query,
    w_key,
    w_value,
    w_out,
    w_router,
    w_gate,
    w_up,
    w_down,
    expert_ids,
    fill_order,
    prefix_len,
    out_grad,
):
    rows = block_in.shape[0]
    n_col = lax.axis_size("col")
    col = lax.axis_index("col")
    row = lax.axis_index("row")
    seq = rows * n_col
    spots = jnp.stack([col.astype(jnp.int32), prefix_len[0], row.astype(jnp.int32)])
    gains = jnp.concatenate([attn_gain, moe_gain, jnp.zeros((256,), BF16)])[None]
    pack_qkv = jnp.concatenate(
        [jnp.concatenate([w_query, w_key, w_value], axis=1), gains, jnp.zeros((7, 512), BF16)], axis=0
    )
    pack_out = jnp.concatenate([w_out, jnp.pad(w_router.T, ((0, 0), (0, 256 - LANES)))], axis=0)
    pack_out = lax.all_gather(pack_out, "col", axis=0)
    pack_qkv = lax.all_gather(pack_qkv, "row", axis=0)
    pack_out = lax.all_gather(pack_out, "row", axis=0)
    cosine, sine = rope_tables(0, seq)
    cosine = jnp.tile(cosine, (1, 4))
    sine = jnp.concatenate([-sine, sine, -sine, sine], axis=1)
    ring = [(i, (i + 1) % n_col) for i in range(n_col)]
    x_chunks = [block_in, lax.ppermute(block_in, "col", ring)]
    x_chunks += ring_gather(hold(x_chunks[1], cosine, sine), n_col)[1:3]
    own = jnp.stack([w_gate, w_up, w_down], axis=1)
    from_x, from_y, other = swap(own, ACROSS_X), swap(own, ACROSS_Y), swap(own, CORE)

    attn_in, q, k, v, lse, w_qkv, gains, mixed_all = attend(spots, x_chunks, pack_qkv, cosine, sine, [other])
    g_chunks = [out_grad, lax.ppermute(hold(out_grad, x_chunks[3]), "col", ring)]
    g_chunks += ring_gather(hold(g_chunks[1], attn_in), n_col)[1:3]
    mixed_own = lax.all_to_all(mixed_all, "col", split_axis=0, concat_axis=0, tiled=True)
    low, high = halves(from_x, from_y, [g_chunks[2]])
    resid, send, gates, kept, wo, wr = route(
        spots, mixed_own, block_in, pack_out, gains, expert_ids, fill_order, [low]
    )
    far = swap(low, ACROSS_X), swap(high, ACROSS_Y)
    weights = [own, other, from_x, swap(from_x, CORE), from_y, swap(from_y, CORE), *far]

    send_chunks = [send, *ring_gather(hold(send, g_chunks[3]), n_col)[1:]]
    weights += [swap(hold(part, send_chunks[2]), CORE) for part in far]
    results, backs, back = {}, [], None
    steps = [(i, (i + 1) % n_col) for i in range(n_col)]
    order = (1, 2, 3, 0)
    for at, chunk in enumerate(order):
        after = [results[order[at - 1]][1]] if at else [send_chunks[3]]
        if at >= 2:
            after.append(backs[at - 2])
        if at == 2:
            flipped = flip(send_chunks, g_chunks, [results[2][1]])
            after.append(flipped[0])
        results[chunk] = experts(send_chunks[chunk], g_chunks[chunk], weights, after)
        if chunk:
            part = results[chunk][0]
            back = part if back is None else (back.astype(F32) + part.astype(F32)).astype(BF16)
            back = lax.ppermute(back, "col", steps)
            backs.append(back)
    results = [results[chunk] for chunk in range(n_col)]

    hidden = [[result[kind] for result in results] for kind in (1, 2, 3)]
    wgrads = functools.partial(expert_wgrads, flipped, hidden)
    (p7,) = wgrads((14, 15), ((0, 0), (0, 1)), after=[backs[2]])
    r7 = swap(p7, CORE)
    block_out, resid_grad, branch, mixed_grad, small = turn(
        spots, backs[2], results[0][0], gates, kept, resid, gains, out_grad, wr, wo, send, [p7]
    )
    mixed_grads = lax.all_to_all(mixed_grad, "col", split_axis=0, concat_axis=0, tiled=True)
    (p53,) = wgrads((6, 7, 10, 11), tuple((0, i) for i in range(4)), after=[branch, r7])
    r53 = swap(p53, CORE)
    q6 = wgrads((12, 13), ((0, 0), (1, 0)), [r7], ((0, 0), (0, 1)), after=[p53])
    far_x, far_y = swap(q6[0], ACROSS_X), swap(q6[1], ACROSS_Y)
    pack = out_wgrad(mixed_own, branch, small, q6[:1])
    out_sum = lax.psum_scatter(pack, "row", scatter_dimension=0, tiled=True)
    q2a, q4b = wgrads((4, 9), ((0, 0), (1, 0)), [r53], ((0, 0), (0, 3)), after=[pack, mixed_grads])
    x2a, y4b = swap(q2a, ACROSS_X), swap(q4b, ACROSS_Y)
    q2b, q4a, p1 = wgrads(
        (5, 8, 2, 3),
        ((0, 0), (1, 0), (2, 0), (2, 1)),
        [r53, far_y, far_x],
        ((0, 1), (0, 2), None, None),
        {0: 1, 1: 2},
        [q2a],
    )
    r1 = swap(p1, CORE)
    x2b, y4a = swap(q2b, ACROSS_X), swap(q4a, ACROSS_Y)
    qkv_wgrad, *back_parts = attend_back(
        spots, mixed_grads, mixed_all, q, k, v, lse, attn_in, w_qkv, cosine, sine, gains, [q2b]
    )
    (q0,) = wgrads((0, 1), ((0, 0), (0, 1)), [r1], ((0, 0), (0, 1)), after=[qkv_wgrad])
    moving = lax.ppermute(back_parts[1], "col", steps)
    moving = (hold(moving, q0, x2a, y4b).astype(F32) + back_parts[2].astype(F32)).astype(BF16)
    moving = lax.ppermute(moving, "col", steps)
    moving = (moving.astype(F32) + back_parts[3].astype(F32)).astype(BF16)
    third_step = moving
    last_step = lax.ppermute(moving, "col", steps)
    attn_grad = last_step.astype(F32) + back_parts[0].astype(F32)
    x_rows = block_in.astype(F32)
    scale = lax.rsqrt(jnp.mean(x_rows * x_rows, axis=1, keepdims=True) + EPS)
    normed = x_rows * scale
    inner = attn_grad * gains[:1]
    block_in_grad = resid_grad + scale * (inner - normed * jnp.mean(inner * normed, axis=1, keepdims=True))
    gate_sum, up_sum, down_sum = expert_total([third_step], q0, x2a, x2b, y4a, y4b)

    qkv_sum = lax.psum_scatter(qkv_wgrad, "row", scatter_dimension=0, tiled=True)[0]
    *qkv_sums, gain_one = unpack(qkv_sum, [last_step])
    out_sum = lax.psum_scatter(hold(out_sum, q2b), "col", scatter_dimension=2, tiled=True)[0].astype(F32)
    gain_one_sum = functools.reduce(jnp.add, shift_all([gain_one] * n_col, n_col))[0]
    return (
        block_out,
        block_in_grad,
        gain_one_sum,
        out_sum[LANES, LANES:],
        *qkv_sums,
        out_sum[:LANES],
        out_sum[LANES:, :LANES].T,
        gate_sum,
        up_sum,
        down_sum,
    )


def takes_fast(mesh):
    n_row, n_col = mesh.shape["row"], mesh.shape["col"]
    return n_row == 8 and n_col == 4


def solution(mesh):
    in_specs = (
        P(("row", "col"), None),
        P("row"),
        P("row"),
        P("row", "col"),
        P("row", "col"),
        P("row", "col"),
        P("row", "col"),
        P("row", "col"),
        P("row", None, "col"),
        P("row", None, "col"),
        P("row", None, "col"),
        P(("row", "col"), None),
        P(("row", "col"), None),
        P("row"),
        P(("row", "col"), None),
    )
    out_specs = (
        P(("row", "col"), None),
        P(("row", "col"), None),
        P("row"),
        P("row"),
        P("row", "col"),
        P("row", "col"),
        P("row", "col"),
        P("row", "col"),
        P("row", "col"),
        P("row", None, "col"),
        P("row", None, "col"),
        P("row", None, "col"),
    )
    local = fast if takes_fast(mesh) else general
    return jax.shard_map(local, mesh=mesh, in_specs=in_specs, out_specs=out_specs, check_vma=False)
```

```python
import functools

import jax
import jax.numpy as jnp
from jax import lax
from jax.experimental import pallas as pl
from jax.experimental.pallas import tpu as pltpu
from jax.sharding import PartitionSpec as P

D = 1024
H = 16
KVH = 8
HD = 64
E = 32
TOPK = 8
CAP = 80


EPS = 1e-06
NEGATIVE = -1e30


def cross_rows(left, right):
    return lax.dot_general(
        left, right, (((0,), (0,)), ((), ())), preferred_element_type=jnp.float32
    )


def times_back(left, right):
    return lax.dot_general(
        left, right, (((1,), (1,)), ((), ())), preferred_element_type=jnp.float32
    )


def rope_tables(first_position, count):
    position = (first_position + jnp.arange(count, dtype=jnp.int32)).astype(jnp.float32)
    inverse = 10000.0 ** (-jnp.arange(HD // 2, dtype=jnp.float32) * 2.0 / HD)
    angle = position[:, None] * inverse[None, :]
    return (jnp.cos(angle), jnp.sin(angle))


def rotate(values, cosine, sine):
    half = HD // 2
    first, second = (values[..., :half], values[..., half:])
    cos_rows = cosine[:, None, :]
    sin_rows = sine[:, None, :]
    return jnp.concatenate(
        [first * cos_rows - second * sin_rows, second * cos_rows + first * sin_rows], axis=-1
    )


def rotate_back(grads, cosine, sine):
    half = HD // 2
    first, second = (grads[..., :half], grads[..., half:])
    cos_rows = cosine[:, None, :]
    sin_rows = sine[:, None, :]
    return jnp.concatenate(
        [first * cos_rows + second * sin_rows, second * cos_rows - first * sin_rows], axis=-1
    )


def norm_rows(values, gain):
    scale = lax.rsqrt(jnp.mean(values * values, axis=1, keepdims=True) + EPS)
    normed = values * scale
    return (normed, scale, (normed * gain).astype(jnp.bfloat16))


def norm_back(grad_in, normed, scale, gain):
    gain_grad = jnp.sum(grad_in * normed, axis=0)
    inner = grad_in * gain
    return (scale * (inner - normed * jnp.mean(inner * normed, axis=1, keepdims=True)), gain_grad)


def to_heads(rows, count, group):
    return rows.reshape(count, KVH, group, HD).transpose(1, 2, 0, 3).reshape(KVH, group * count, HD)


def from_heads(heads, count, group):
    return heads.reshape(KVH, group, count, HD).transpose(2, 0, 1, 3).reshape(count, H, HD)


def general(
    block_in,
    attn_gain,
    moe_gain,
    w_query,
    w_key,
    w_value,
    w_out,
    w_router,
    w_gate,
    w_up,
    w_down,
    expert_ids,
    fill_order,
    prefix_len,
    out_grad,
):
    tok_rows = block_in.shape[0]
    n_col = lax.axis_size("col")
    col_index = lax.axis_index("col")
    seq_rows = tok_rows * n_col
    group = H // KVH
    scale_attn = HD ** (-0.5)
    bf16 = jnp.bfloat16
    f32 = jnp.float32
    shared = (
        lax.all_gather(w_query, "row", axis=0, tiled=True),
        lax.all_gather(w_key, "row", axis=0, tiled=True),
        lax.all_gather(w_value, "row", axis=0, tiled=True),
        lax.all_gather(w_out, "row", axis=0, tiled=True),
        lax.all_gather(w_router, "row", axis=0, tiled=True),
        lax.all_gather(attn_gain, "row", axis=0, tiled=True),
        lax.all_gather(moe_gain, "row", axis=0, tiled=True),
    )
    wq_full, wk_full, wv_full, wo_full, wr_full = (
        lax.all_gather(shared[0], "col", axis=1, tiled=True),
        lax.all_gather(shared[1], "col", axis=1, tiled=True),
        lax.all_gather(shared[2], "col", axis=1, tiled=True),
        lax.all_gather(shared[3], "col", axis=1, tiled=True),
        lax.all_gather(shared[4], "col", axis=1, tiled=True),
    )
    gain_one = shared[5].astype(f32)
    gain_two = shared[6].astype(f32)
    x_rows = block_in.astype(f32)
    normed_one, scale_one, attn_in = norm_rows(x_rows, gain_one)
    query = jnp.dot(attn_in, wq_full, preferred_element_type=f32)
    key = jnp.dot(attn_in, wk_full, preferred_element_type=f32)
    value = jnp.dot(attn_in, wv_full, preferred_element_type=f32).astype(bf16)
    cosine, sine = rope_tables(col_index * tok_rows, tok_rows)
    query_rot = rotate(query.reshape(tok_rows, H, HD), cosine, sine).astype(bf16)
    key_rot = (
        rotate(key.reshape(tok_rows, KVH, HD), cosine, sine)
        .astype(bf16)
        .reshape(tok_rows, KVH * HD)
    )
    keys_all, values_all = (
        lax.all_gather(key_rot, "col", axis=0, tiled=True),
        lax.all_gather(value, "col", axis=0, tiled=True),
    )
    prefix = prefix_len[0]
    query_spot = col_index * tok_rows + jnp.arange(tok_rows, dtype=jnp.int32)
    key_spot = jnp.arange(seq_rows, dtype=jnp.int32)
    allowed = (key_spot[None, :] <= query_spot[:, None]) | (key_spot[None, :] < prefix)
    allowed_rows = jnp.tile(allowed, (group, 1))
    query_heads = to_heads(query_rot.reshape(tok_rows, H * HD), tok_rows, group)
    key_heads = keys_all.reshape(seq_rows, KVH, HD).transpose(1, 0, 2)
    value_heads = values_all.reshape(seq_rows, KVH, HD).transpose(1, 0, 2)

    def attend(pieces):
        queries, keys, values = pieces
        scores = times_back(queries, keys) * scale_attn
        scores = jnp.where(allowed_rows, scores, NEGATIVE)
        highest = jnp.max(scores, axis=1, keepdims=True)
        expo = jnp.exp(scores - highest)
        total = jnp.sum(expo, axis=1, keepdims=True)
        weights = (expo / total).astype(bf16)
        mixed_heads = jnp.dot(weights, values, preferred_element_type=f32).astype(bf16)
        return (mixed_heads, (highest + jnp.log(total))[:, 0])

    mixed_heads, lse_heads = lax.map(attend, (query_heads, key_heads, value_heads))
    mixed = from_heads(mixed_heads, tok_rows, group).reshape(tok_rows, H * HD)
    resid = x_rows + jnp.dot(mixed, wo_full, preferred_element_type=f32)
    normed_two, scale_two, moe_in = norm_rows(resid, gain_two)
    logits = jnp.dot(moe_in, wr_full, preferred_element_type=f32)
    choice_hot = (expert_ids[:, :, None] == jnp.arange(E, dtype=jnp.int32)).astype(f32)
    picked = jnp.sum(choice_hot * logits[:, None, :], axis=2)
    highest = jnp.max(picked, axis=1, keepdims=True)
    expo = jnp.exp(picked - highest)
    gates = expo / jnp.sum(expo, axis=1, keepdims=True)
    order = fill_order[0]
    ranked = expert_ids[order]
    onehot = (ranked.reshape(-1, 1) == jnp.arange(E, dtype=jnp.int32)).astype(jnp.int32)
    before = jnp.cumsum(onehot, axis=0) - onehot
    ranked_slot = jnp.sum(before * onehot, axis=1).reshape(tok_rows, TOPK)
    slot = jnp.zeros((tok_rows, TOPK), jnp.int32).at[order].set(ranked_slot)
    kept = slot < CAP
    dest_grid = jnp.where(kept, expert_ids * CAP + slot, E * CAP)
    pair_ids = jnp.arange(tok_rows * TOPK, dtype=jnp.int32)
    slot_pair = (
        jnp.full((E * CAP + 1,), tok_rows * TOPK, jnp.int32)
        .at[dest_grid.reshape(-1)]
        .set(pair_ids)[: E * CAP]
    )
    slot_token = slot_pair // TOPK
    gate_slot = jnp.concatenate([gates.reshape(-1), jnp.zeros((1,), f32)])[slot_pair]
    moe_pad = jnp.concatenate([moe_in, jnp.zeros((1, D), bf16)])
    dispatch = moe_pad[slot_token].reshape(E, CAP, D)
    received = lax.all_to_all(dispatch, "row", split_axis=0, concat_axis=1, tiled=True)
    gate_w, up_w, down_w = (
        lax.all_gather(w_gate, "col", axis=2, tiled=True),
        lax.all_gather(w_up, "col", axis=2, tiled=True),
        lax.all_gather(w_down, "col", axis=2, tiled=True),
    )
    hidden_gate = jnp.einsum("erd,edf->erf", received, gate_w, preferred_element_type=f32)
    hidden_up = jnp.einsum("erd,edf->erf", received, up_w, preferred_element_type=f32)
    active = (jax.nn.silu(hidden_gate) * hidden_up).astype(bf16)
    expert_out = jnp.einsum("erf,edf->erd", active, down_w, preferred_element_type=f32).astype(bf16)
    returned = lax.all_to_all(expert_out, "row", split_axis=1, concat_axis=0, tiled=True)
    out_pad = jnp.concatenate([returned.reshape(E * CAP, D), jnp.zeros((1, D), bf16)])
    pair_out = out_pad[dest_grid]
    weight_pair = gates * kept.astype(f32)
    moe_out = jnp.zeros((tok_rows, D), f32)
    for choice_index in range(TOPK):
        moe_out = moe_out + weight_pair[:, choice_index : choice_index + 1] * pair_out[
            :, choice_index
        ].astype(f32)
    block_out = resid + moe_out
    grad_out = out_grad.astype(f32)
    gate_grad = jnp.stack(
        [
            jnp.sum(pair_out[:, choice_index].astype(f32) * grad_out, axis=1)
            for choice_index in range(TOPK)
        ],
        axis=1,
    )
    grad_pad = jnp.concatenate([grad_out, jnp.zeros((1, D), f32)])
    slot_grad = (gate_slot[:, None] * grad_pad[slot_token]).astype(bf16).reshape(E, CAP, D)
    out_grads = lax.all_to_all(slot_grad, "row", split_axis=0, concat_axis=1, tiled=True)
    act_grad = jnp.einsum("erd,edf->erf", out_grads, down_w, preferred_element_type=f32)
    sigma = jax.nn.sigmoid(hidden_gate)
    gate_h_grad = (act_grad * hidden_up * sigma * (1.0 + hidden_gate * (1.0 - sigma))).astype(bf16)
    up_h_grad = (act_grad * hidden_gate * sigma).astype(bf16)
    down_wgrad = jnp.einsum("erd,erf->edf", out_grads, active, preferred_element_type=f32)
    gate_wgrad = jnp.einsum("erd,erf->edf", received, gate_h_grad, preferred_element_type=f32)
    up_wgrad = jnp.einsum("erd,erf->edf", received, up_h_grad, preferred_element_type=f32)
    in_grad = (
        jnp.einsum("erf,edf->erd", gate_h_grad, gate_w, preferred_element_type=f32)
        + jnp.einsum("erf,edf->erd", up_h_grad, up_w, preferred_element_type=f32)
    ).astype(bf16)
    back_rows = lax.all_to_all(in_grad, "row", split_axis=1, concat_axis=0, tiled=True)
    gate_sum, up_sum, down_sum = (
        lax.psum_scatter(
            gate_wgrad.astype(jnp.bfloat16), "col", scatter_dimension=2, tiled=True
        ).astype(jnp.float32),
        lax.psum_scatter(
            up_wgrad.astype(jnp.bfloat16), "col", scatter_dimension=2, tiled=True
        ).astype(jnp.float32),
        lax.psum_scatter(
            down_wgrad.astype(jnp.bfloat16), "col", scatter_dimension=2, tiled=True
        ).astype(jnp.float32),
    )
    back_pad = jnp.concatenate([back_rows.reshape(E * CAP, D), jnp.zeros((1, D), bf16)])
    pair_back = back_pad[dest_grid]
    moe_in_grad = jnp.zeros((tok_rows, D), f32)
    for choice_index in range(TOPK):
        moe_in_grad = moe_in_grad + pair_back[:, choice_index].astype(f32)
    picked_grad = gates * (gate_grad - jnp.sum(gates * gate_grad, axis=1, keepdims=True))
    logit_grad = jnp.sum(choice_hot * picked_grad[:, :, None], axis=1).astype(bf16)
    router_wgrad = cross_rows(moe_in, logit_grad)
    moe_in_grad = moe_in_grad + times_back(logit_grad, wr_full)
    norm_two_grad, gain_two_grad = norm_back(moe_in_grad, normed_two, scale_two, gain_two)
    resid_grad = grad_out + norm_two_grad
    branch_grad = resid_grad.astype(bf16)
    out_wgrad = cross_rows(mixed, branch_grad)
    mixed_grad = times_back(branch_grad, wo_full).astype(bf16)
    grad_heads = to_heads(mixed_grad, tok_rows, group)

    def query_side(pieces):
        queries, keys, values, lse_rows, grad_rows = pieces
        scores = jnp.where(allowed_rows, times_back(queries, keys) * scale_attn, NEGATIVE)
        probs = jnp.exp(scores - lse_rows[:, None])
        prob_grad = times_back(grad_rows, values)
        delta = jnp.sum(probs * prob_grad, axis=1, keepdims=True)
        score_grad = (probs * (prob_grad - delta)).astype(bf16)
        query_grad = jnp.dot(score_grad, keys, preferred_element_type=f32) * scale_attn
        return (query_grad, delta[:, 0], score_grad, probs)

    def both_sides(pieces):
        queries, keys, values, lse_rows, grad_rows = pieces
        query_grad, delta, score_grad, probs = query_side(pieces)
        key_grad = cross_rows(score_grad, queries) * scale_attn
        value_grad = cross_rows(probs.astype(bf16), grad_rows)
        return (query_grad, key_grad, value_grad)

    query_rot_grad, key_parts, value_parts = lax.map(
        both_sides, (query_heads, key_heads, value_heads, lse_heads, grad_heads)
    )
    key_rot_grad, value_grad = (
        lax.psum_scatter(
            key_parts.transpose(1, 0, 2).reshape(seq_rows, KVH * HD).astype(jnp.bfloat16),
            "col",
            scatter_dimension=0,
            tiled=True,
        ).astype(jnp.float32),
        lax.psum_scatter(
            value_parts.transpose(1, 0, 2).reshape(seq_rows, KVH * HD).astype(jnp.bfloat16),
            "col",
            scatter_dimension=0,
            tiled=True,
        ).astype(jnp.float32),
    )
    query_grad = (
        rotate_back(from_heads(query_rot_grad, tok_rows, group), cosine, sine)
        .reshape(tok_rows, H * HD)
        .astype(bf16)
    )
    key_grad = (
        rotate_back(key_rot_grad.reshape(tok_rows, KVH, HD), cosine, sine)
        .reshape(tok_rows, KVH * HD)
        .astype(bf16)
    )
    value_grad = value_grad.astype(bf16)
    query_wgrad = cross_rows(attn_in, query_grad)
    key_wgrad = cross_rows(attn_in, key_grad)
    value_wgrad = cross_rows(attn_in, value_grad)
    attn_in_grad = (
        times_back(query_grad, wq_full)
        + times_back(key_grad, wk_full)
        + times_back(value_grad, wv_full)
    )
    norm_one_grad, gain_one_grad = norm_back(attn_in_grad, normed_one, scale_one, gain_one)
    block_in_grad = resid_grad + norm_one_grad
    spread_one = jnp.broadcast_to(gain_one_grad[:, None], (D, n_col))
    spread_two = jnp.broadcast_to(gain_two_grad[:, None], (D, n_col))
    col_sums = (
        lax.psum_scatter(
            query_wgrad.astype(jnp.bfloat16), "col", scatter_dimension=1, tiled=True
        ).astype(jnp.float32),
        lax.psum_scatter(
            key_wgrad.astype(jnp.bfloat16), "col", scatter_dimension=1, tiled=True
        ).astype(jnp.float32),
        lax.psum_scatter(
            value_wgrad.astype(jnp.bfloat16), "col", scatter_dimension=1, tiled=True
        ).astype(jnp.float32),
        lax.psum_scatter(
            out_wgrad.astype(jnp.bfloat16), "col", scatter_dimension=1, tiled=True
        ).astype(jnp.float32),
        lax.psum_scatter(
            router_wgrad.astype(jnp.bfloat16), "col", scatter_dimension=1, tiled=True
        ).astype(jnp.float32),
        lax.psum_scatter(
            spread_one.astype(jnp.bfloat16), "col", scatter_dimension=1, tiled=True
        ).astype(jnp.float32),
        lax.psum_scatter(
            spread_two.astype(jnp.bfloat16), "col", scatter_dimension=1, tiled=True
        ).astype(jnp.float32),
    )
    row_sums = (
        lax.psum_scatter(
            col_sums[0].astype(jnp.bfloat16), "row", scatter_dimension=0, tiled=True
        ).astype(jnp.float32),
        lax.psum_scatter(
            col_sums[1].astype(jnp.bfloat16), "row", scatter_dimension=0, tiled=True
        ).astype(jnp.float32),
        lax.psum_scatter(
            col_sums[2].astype(jnp.bfloat16), "row", scatter_dimension=0, tiled=True
        ).astype(jnp.float32),
        lax.psum_scatter(
            col_sums[3].astype(jnp.bfloat16), "row", scatter_dimension=0, tiled=True
        ).astype(jnp.float32),
        lax.psum_scatter(
            col_sums[4].astype(jnp.bfloat16), "row", scatter_dimension=0, tiled=True
        ).astype(jnp.float32),
        lax.psum_scatter(
            col_sums[5].astype(jnp.bfloat16), "row", scatter_dimension=0, tiled=True
        ).astype(jnp.float32),
        lax.psum_scatter(
            col_sums[6].astype(jnp.bfloat16), "row", scatter_dimension=0, tiled=True
        ).astype(jnp.float32),
    )
    return (
        block_out,
        block_in_grad,
        row_sums[5][:, 0],
        row_sums[6][:, 0],
        row_sums[0],
        row_sums[1],
        row_sums[2],
        row_sums[3],
        row_sums[4],
        gate_sum,
        up_sum,
        down_sum,
    )


F32 = jnp.float32
BF16 = jnp.bfloat16
MIB = 1024 * 1024
LANES = 128
VMEM_MOST = 60 * MIB
COST_SCALE = 10**6


def cost(microseconds):
    return pl.CostEstimate(flops=int(microseconds * COST_SCALE), bytes_accessed=10**5, transcendentals=0)


def dot_nn(a, b):
    return lax.dot_general(a, b, (((1,), (0,)), ((), ())), preferred_element_type=F32)


def dot_nt(a, b):
    return lax.dot_general(a, b, (((1,), (1,)), ((), ())), preferred_element_type=F32)


def dot_tn(a, b):
    return lax.dot_general(a, b, (((0,), (0,)), ((), ())), preferred_element_type=F32)


def in_vmem():
    return pl.BlockSpec(memory_space=pltpu.VMEM)


def in_smem():
    return pl.BlockSpec(memory_space=pltpu.SMEM)


def in_hbm():
    return pl.BlockSpec(memory_space=pl.ANY)


def behind(kernel, n_in, after):
    if not after:
        return kernel
    return lambda *refs: kernel(*refs[:n_in], *refs[n_in + len(after) :])


def partner(values):
    lane = lax.broadcasted_iota(jnp.int32, values.shape, 1)
    half = HD // 2
    return jnp.where(
        lane % HD < half,
        pltpu.roll(values, LANES - half, 1),
        pltpu.roll(values, half, 1),
    )


def attend_kernel(
    spot_ref, x0, x1, x2, x3, pack_ref, cos_ref, sin_ref,
    attn_ref, q_ref, k_ref, v_ref, lse_ref, w_ref, gain_ref, mixed_ref,
):
    rows = x0.shape[0]
    col, prefix = spot_ref[0], spot_ref[1]
    for part in range(8):
        span = pl.ds(part * LANES, LANES)
        w_ref[span, :] = pack_ref[part, :LANES, :]
        gain_ref[0:1, span] = pack_ref[part, LANES : LANES + 1, :LANES].astype(F32)
        gain_ref[1:2, span] = pack_ref[part, LANES : LANES + 1, LANES : 2 * LANES].astype(F32)
    gain = gain_ref[0:1, :]
    for step, chunk in enumerate((x0, x1, x2, x3)):
        source = lax.rem(col - step + 4, 4)
        x = chunk[...].astype(F32)
        scale = lax.rsqrt(jnp.mean(x * x, axis=1, keepdims=True) + EPS)
        attn_ref[pl.ds(pl.multiple_of(source * rows, rows), rows), :] = (x * scale * gain).astype(BF16)
    for tile in range(4):
        span = pl.ds(tile * rows, rows)
        qkv = dot_nn(attn_ref[span, :], w_ref[...])
        cosine, sine = cos_ref[span, :], sin_ref[span, :]
        for block in range(3):
            v = qkv[:, block * LANES : (block + 1) * LANES]
            y = v * cosine + partner(v) * sine
            if block < 2:
                y = (y * HD ** (-0.5)).astype(BF16)
                q_ref[2 * block, span, :] = y[:, :HD]
                q_ref[2 * block + 1, span, :] = y[:, HD:]
            else:
                y = y.astype(BF16)
                k_ref[0, span, :] = y[:, :HD]
                k_ref[1, span, :] = y[:, HD:]
        v = qkv[:, 3 * LANES :].astype(BF16)
        v_ref[0, span, :] = v[:, :HD]
        v_ref[1, span, :] = v[:, HD:]
    total = 4 * rows
    for tile in range(4):
        span = pl.ds(tile * rows, rows)
        keys = max((tile + 1) * rows, total // 2)
        key_spot = lax.broadcasted_iota(jnp.int32, (rows, keys), 1)
        query_spot = lax.broadcasted_iota(jnp.int32, (rows, keys), 0) + tile * rows
        allowed = (key_spot <= query_spot) | (key_spot < prefix)
        for pair in range(2):
            k, v = k_ref[pair, pl.ds(0, keys), :], v_ref[pair, pl.ds(0, keys), :]
            outs = []
            for head in (2 * pair, 2 * pair + 1):
                scores = jnp.where(allowed, dot_nt(q_ref[head, span, :], k), NEGATIVE)
                highest = jnp.max(scores, axis=1, keepdims=True)
                expo = jnp.exp(scores - highest)
                summed = jnp.sum(expo, axis=1, keepdims=True)
                outs.append(dot_nn(expo.astype(BF16), v) * (1.0 / summed))
                lse_ref[span, head : head + 1] = highest + jnp.log(summed)
            mixed_ref[span, pair * LANES : (pair + 1) * LANES] = jnp.concatenate(outs, axis=1).astype(BF16)


def attend(spots, chunks, pack, cosine, sine, after=()):
    rows = chunks[0].shape[0]
    seq = 4 * rows
    shapes = (
        jax.ShapeDtypeStruct((seq, D), BF16),
        jax.ShapeDtypeStruct((4, seq, HD), BF16),
        jax.ShapeDtypeStruct((2, seq, HD), BF16),
        jax.ShapeDtypeStruct((2, seq, HD), BF16),
        jax.ShapeDtypeStruct((seq, 4), F32),
        jax.ShapeDtypeStruct((D, 512), BF16),
        jax.ShapeDtypeStruct((2, D), F32),
        jax.ShapeDtypeStruct((seq, 256), BF16),
    )
    return pl.pallas_call(
        behind(attend_kernel, 8, after),
        out_shape=shapes,
        in_specs=[in_smem()] + [in_vmem()] * 7 + [in_hbm()] * len(after),
        out_specs=tuple(in_vmem() for _ in shapes),
        compiler_params=pltpu.CompilerParams(vmem_limit_bytes=VMEM_MOST),
        cost_estimate=cost(10),
    )(spots, *chunks, pack, cosine, sine, *after)


def attend_back_kernel(
    spot_ref, grad_ref, mixed_ref, q_ref, k_ref, v_ref, lse_ref, attn_ref, w_ref, cos_ref, sin_ref, gain_ref,
    wgrad_ref, in0, in1, in2, in3, dqkv_ref, dk_ref, dv_ref, dq_ref, mg_ref,
):
    seq = attn_ref.shape[0]
    rows = seq // 4
    prefix = spot_ref[1]
    for tile in range(4):
        span = pl.ds(tile * rows, rows)
        for pair in range(2):
            g = grad_ref[span, pair * LANES : (pair + 1) * LANES]
            mg_ref[2 * pair, span, :] = g[:, :HD]
            mg_ref[2 * pair + 1, span, :] = g[:, HD:]
    dk_ref[...] = jnp.zeros_like(dk_ref)
    dv_ref[...] = jnp.zeros_like(dv_ref)
    for tile in range(4):
        span = pl.ds(tile * rows, rows)
        keys = max((tile + 1) * rows, seq // 2)
        key_spot = lax.broadcasted_iota(jnp.int32, (rows, keys), 1)
        query_spot = lax.broadcasted_iota(jnp.int32, (rows, keys), 0) + tile * rows
        allowed = (key_spot <= query_spot) | (key_spot < prefix)
        for pair in range(2):
            k, v = k_ref[pair, pl.ds(0, keys), :], v_ref[pair, pl.ds(0, keys), :]
            both = grad_ref[span, pair * LANES : (pair + 1) * LANES].astype(F32) * mixed_ref[
                span, pair * LANES : (pair + 1) * LANES
            ].astype(F32)
            outs = []
            for at, head in enumerate((2 * pair, 2 * pair + 1)):
                q, g = q_ref[head, span, :], mg_ref[head, span, :]
                delta = jnp.sum(both[:, at * HD : (at + 1) * HD], axis=1, keepdims=True)
                scores = jnp.where(allowed, dot_nt(q, k), NEGATIVE)
                probs = jnp.exp(scores - lse_ref[span, head : head + 1])
                score_grad = (probs * (dot_nt(g, v) - delta)).astype(BF16)
                dv_ref[pair, pl.ds(0, keys), :] += dot_tn(probs.astype(BF16), g)
                dk_ref[pair, pl.ds(0, keys), :] += dot_tn(score_grad, q)
                outs.append(dot_nn(score_grad, k) * HD ** (-0.5))
            dq_ref[span, pair * LANES : (pair + 1) * LANES] = jnp.concatenate(outs, axis=1)
    for tile in range(4):
        span = pl.ds(tile * rows, rows)
        cosine, sine = cos_ref[span, :], sin_ref[span, :]
        for block in range(3):
            if block < 2:
                g = dq_ref[span, block * LANES : (block + 1) * LANES]
            else:
                g = jnp.concatenate([dk_ref[0, span, :], dk_ref[1, span, :]], axis=1)
            dqkv_ref[span, block * LANES : (block + 1) * LANES] = (g * cosine - partner(g) * sine).astype(BF16)
        dqkv_ref[span, 3 * LANES :] = jnp.concatenate([dv_ref[0, span, :], dv_ref[1, span, :]], axis=1).astype(BF16)
    gain_total = jnp.zeros((1, D), F32)
    for step, out in enumerate((in0, in1, in2, in3)):
        source = lax.rem(spot_ref[0] - step + 4, 4)
        span = pl.ds(pl.multiple_of(source * rows, rows), rows)
        back = dot_nt(dqkv_ref[span, :], w_ref[...])
        out[...] = back.astype(BF16)
        gain_total = gain_total + jnp.sum(back * attn_ref[span, :].astype(F32), axis=0, keepdims=True)
    gain_total = gain_total / gain_ref[0:1, :]
    for part in range(8):
        span = pl.ds(part * LANES, LANES)
        wgrad_ref[part, LANES:, :LANES] = jnp.broadcast_to(gain_total[:, part * LANES : (part + 1) * LANES], (8, LANES)).astype(BF16)
        wgrad_ref[part, LANES:, LANES:] = jnp.zeros((8, 3 * LANES), BF16)
        wgrad_ref[part, :LANES, :] = dot_tn(attn_ref[:, span], dqkv_ref[...]).astype(BF16)


def attend_back(spots, grads, mixed, q, k, v, lse, attn_in, w_qkv, cosine, sine, gain, after=()):
    seq = attn_in.shape[0]
    shapes = (
        jax.ShapeDtypeStruct((8, 136, 512), BF16),
    ) + (jax.ShapeDtypeStruct((seq // 4, D), BF16),) * 4
    return pl.pallas_call(
        behind(attend_back_kernel, 12, after),
        out_shape=shapes,
        in_specs=[in_smem()] + [in_vmem()] * 11 + [in_hbm()] * len(after),
        out_specs=tuple(in_vmem() for _ in shapes),
        scratch_shapes=[
            pltpu.VMEM((seq, 512), BF16),
            pltpu.VMEM((2, seq, HD), F32),
            pltpu.VMEM((2, seq, HD), F32),
            pltpu.VMEM((seq, 256), F32),
            pltpu.VMEM((4, seq, HD), BF16),
        ],
        compiler_params=pltpu.CompilerParams(vmem_limit_bytes=VMEM_MOST),
        cost_estimate=cost(16),
    )(spots, grads, mixed, q, k, v, lse, attn_in, w_qkv, cosine, sine, gain, *after)


def route_kernel(
    spot_ref, mixed_ref, x_ref, pack_ref, gain_ref, ids_ref, order_ref,
    resid_ref, send_ref, gates_ref, kept_ref, wo_ref, wr_ref, wr_wide,
):
    rows = x_ref.shape[0]
    wr_wide[...] = jnp.zeros_like(wr_wide)
    for row in range(8):
        span = pl.ds(row * LANES, LANES)
        for col in range(4):
            wo_ref[span, col * 256 : (col + 1) * 256] = pack_ref[row, col, :LANES, :]
            wr_wide[col * 8 : (col + 1) * 8, span] = pack_ref[row, col, LANES:, :LANES].astype(F32)
    wr_ref[...] = wr_wide[...].astype(BF16)
    resid = x_ref[...].astype(F32)
    for part in range(4):
        resid = resid + dot_nn(mixed_ref[pl.ds(part * rows, rows), :], wo_ref[part * 256 : (part + 1) * 256, :])
    resid_ref[...] = resid
    scale = lax.rsqrt(jnp.mean(resid * resid, axis=1, keepdims=True) + EPS)
    moe_in = (resid * scale * gain_ref[1:2, :]).astype(BF16)
    send_ref[:, :D] = moe_in
    logits = dot_nt(moe_in, wr_ref[...])
    lane = lax.broadcasted_iota(jnp.int32, (rows, LANES), 1)
    chosen = jnp.zeros((rows, LANES), jnp.bool_)
    for choice in range(TOPK):
        chosen = chosen | (ids_ref[:, choice : choice + 1] == lane)
    picked = jnp.where(chosen, logits, NEGATIVE)
    expo = jnp.exp(picked - jnp.max(picked, axis=1, keepdims=True))
    gates = expo / jnp.sum(expo, axis=1, keepdims=True)
    first = lax.broadcasted_iota(jnp.int32, (rows, rows), 0)
    second = lax.broadcasted_iota(jnp.int32, (rows, rows), 1)
    place = (first == order_ref[...]).astype(BF16)
    sooner = dot_nn(place, (second < first).astype(BF16)).astype(BF16)
    sooner = dot_nt(sooner, place).astype(BF16)
    slot = dot_nn(sooner, chosen.astype(BF16))
    kept = (chosen & (slot < CAP)).astype(F32)
    gates_ref[...] = gates
    kept_ref[...] = kept
    send_ref[:, D:] = dot_nn((gates * kept).astype(BF16), relabel(spot_ref[2])).astype(BF16)


def relabel(row):
    first = lax.broadcasted_iota(jnp.int32, (LANES, LANES), 0)
    second = lax.broadcasted_iota(jnp.int32, (LANES, LANES), 1)
    return (first == (second ^ (row * 4))).astype(BF16)


def route(spots, mixed, x, pack, gain, ids, order, after=()):
    rows = x.shape[0]
    shapes = (
        jax.ShapeDtypeStruct((rows, D), F32),
        jax.ShapeDtypeStruct((rows, D + LANES), BF16),
        jax.ShapeDtypeStruct((rows, LANES), F32),
        jax.ShapeDtypeStruct((rows, LANES), F32),
        jax.ShapeDtypeStruct((D, D), BF16),
        jax.ShapeDtypeStruct((LANES, D), BF16),
    )
    return pl.pallas_call(
        behind(route_kernel, 7, after),
        out_shape=shapes,
        in_specs=[in_smem()] + [in_vmem()] * 6 + [in_hbm()] * len(after),
        out_specs=tuple(in_vmem() for _ in shapes),
        scratch_shapes=[pltpu.VMEM((LANES, D), F32)],
        compiler_params=pltpu.CompilerParams(vmem_limit_bytes=VMEM_MOST),
        cost_estimate=cost(2),
    )(spots, mixed, x, pack, gain, ids, order, *after)


def expert_kernel(x_ref, g_ref, *refs):
    weights, refs = refs[:10], refs[10:]
    back_ref, hg_ref, hu_ref, act_ref, out_acc, in_acc, gate_acc, held, sems = refs
    step = pl.program_id(0)
    count = held.shape[1]
    wide = count * LANES

    def fetch(at, slot):
        for k in range(8):

            @pl.when(at == k)
            def _():
                for i in range(2):
                    half = weights[k].at[pl.ds(2 * i, 2)] if k < 6 else weights[2 * k - 6 + i]
                    pltpu.make_async_copy(half, held.at[slot, pl.ds(2 * i, 2)], sems.at[slot, i]).start()

    @pl.when(step == 0)
    def _():
        fetch(step, 0)
        out_acc[...] = jnp.zeros_like(out_acc)
        in_acc[...] = jnp.zeros_like(in_acc)
        gate_acc[...] = jnp.zeros_like(gate_acc)

    now = lax.rem(step, 2)
    for i in range(2):
        pltpu.make_async_copy(weights[6], held.at[now, pl.ds(2 * i, 2)], sems.at[now, i]).wait()
    fetch(step + 1, 1 - now)

    join = lambda kind: jnp.concatenate([held[now, i, kind] for i in range(count)], axis=1)
    wg, wu, wd = join(0), join(1), join(2)
    x = x_ref[:, :D]
    expert = lax.broadcasted_iota(jnp.int32, (LANES, wide), 0)
    column = lax.broadcasted_iota(jnp.int32, (LANES, wide), 1)
    spread = (expert == step * count + column // LANES).astype(BF16)
    gate = dot_nn(x_ref[:, D:], spread)
    hidden_gate = dot_nn(x, wg)
    hidden_up = dot_nn(x, wu)
    act_grad = dot_nn(g_ref[...], wd)
    sigma = 0.5 * jnp.tanh(0.5 * hidden_gate) + 0.5
    swish = hidden_gate * sigma
    active = swish * hidden_up
    gate_acc[...] += dot_nt((active * act_grad).astype(BF16), spread)
    gated = (active * gate).astype(BF16)
    act_ref[...] = gated
    out_acc[...] += dot_nt(gated, wd)
    act_grad = act_grad * gate
    up_grad = (act_grad * swish).astype(BF16)
    gate_grad = (act_grad * hidden_up * (sigma + swish * (1.0 - sigma))).astype(BF16)
    hg_ref[...] = gate_grad
    hu_ref[...] = up_grad
    in_acc[...] += dot_nt(gate_grad, wg) + dot_nt(up_grad, wu)

    @pl.when(step == pl.num_programs(0) - 1)
    def _():
        back_ref[:, :D] = in_acc[...].astype(BF16)
        back_ref[:, D : 2 * D] = out_acc[...].astype(BF16)
        back_ref[:, 2 * D :] = gate_acc[...].astype(BF16)


def experts(x, g, weights, after=()):
    rows = x.shape[0]
    count = 4
    steps = 8
    wide = count * LANES
    hidden = pl.BlockSpec((rows, wide), lambda i: (0, i))
    whole = lambda width: pl.BlockSpec((rows, width), lambda i: (0, 0))
    return pl.pallas_call(
        behind(expert_kernel, 12, after),
        out_shape=(jax.ShapeDtypeStruct((rows, 2 * D + LANES), BF16),)
        + (jax.ShapeDtypeStruct((rows, steps * wide), BF16),) * 3,
        grid_spec=pltpu.PrefetchScalarGridSpec(
            num_scalar_prefetch=0,
            grid=(steps,),
            in_specs=[whole(D + LANES), whole(D)] + [in_hbm()] * (10 + len(after)),
            out_specs=(whole(2 * D + LANES), hidden, hidden, hidden),
            scratch_shapes=[
                pltpu.VMEM((rows, D), F32),
                pltpu.VMEM((rows, D), F32),
                pltpu.VMEM((rows, LANES), F32),
                pltpu.VMEM((2, count, 3, D, LANES), BF16),
                pltpu.SemaphoreType.DMA((2, 2)),
            ],
        ),
        compiler_params=pltpu.CompilerParams(vmem_limit_bytes=VMEM_MOST),
        cost_estimate=cost(21),
    )(x, g, *weights, *after)


def flip_kernel(x0, x1, x2, x3, g0, g1, g2, g3, xt_ref, gt_ref):
    rows = x0.shape[0]
    for at, (x, g) in enumerate(zip((x0, x1, x2, x3), (g0, g1, g2, g3))):
        xt_ref[:, at * rows : (at + 1) * rows] = x[:, :D].T
        gt_ref[:, at * rows : (at + 1) * rows] = g[...].T


def flip(xs, gs, after=()):
    seq = 4 * xs[0].shape[0]
    return pl.pallas_call(
        behind(flip_kernel, 8, after),
        out_shape=(jax.ShapeDtypeStruct((D, seq), BF16),) * 2,
        in_specs=[in_vmem()] * 8 + [in_hbm()] * len(after),
        out_specs=(in_vmem(),) * 2,
        compiler_params=pltpu.CompilerParams(vmem_limit_bytes=VMEM_MOST),
        cost_estimate=cost(2),
    )(*xs, *gs, *after)


def expert_wgrad_kernel(places, added, late, xt_ref, gt_ref, *refs):
    hidden, refs = refs[:12], refs[12:]
    count = len(places)
    n_extra = len({place[0] for place in added if place}) + len(late)
    plain = [k for k, place in enumerate(added) if not place]
    extras, refs = refs[:n_extra], refs[n_extra:]
    n_out = len({which for which, _ in places})
    outs, refs = refs[:n_out], refs[n_out:]
    held, out_sems, got, in_sems = refs
    step = pl.program_id(0)
    now = lax.rem(step, 2)

    def fetch(at, slot):
        for k, place in enumerate(added):
            if not place:
                continue
            which, half = place

            @pl.when(at == k)
            def _():
                pltpu.make_async_copy(extras[which].at[half], got.at[slot, 0], in_sems.at[slot, 0]).start()
                if k in late:
                    pltpu.make_async_copy(extras[late[k]].at[0], got.at[slot, 1], in_sems.at[slot, 1]).start()

    if added:

        @pl.when(step == 0)
        def _():
            fetch(step, 0)

        fetch(step + 1, 1 - now)

    def sent(slot):
        pltpu.make_async_copy(held.at[slot], outs[0].at[0], out_sems.at[slot]).wait()

    @pl.when(step >= 2)
    def _():
        sent(now)

    first = functools.reduce(jnp.logical_and, [step != k for k in plain], step >= 0)
    second = functools.reduce(jnp.logical_or, [step == k for k in late], False)
    if added:

        @pl.when(functools.reduce(jnp.logical_and, [step != k for k in plain], step >= 0))
        def _():
            pltpu.make_async_copy(extras[0].at[0], got.at[now, 0], in_sems.at[now, 0]).wait()

        for k in late:

            @pl.when(step == k)
            def _():
                pltpu.make_async_copy(extras[0].at[0], got.at[now, 1], in_sems.at[now, 1]).wait()


    for kind, left in enumerate((xt_ref, xt_ref, gt_ref)):
        joined = jnp.concatenate([part[...] for part in hidden[kind * 4 : kind * 4 + 4]], axis=0)
        product = dot_nn(left[...], joined)
        for i in range(2):
            piece = product[:, i * LANES : (i + 1) * LANES]
            if plain:
                piece = piece + jnp.where(first, got[now, 0, i, kind].astype(F32), 0.0)
            elif added:
                piece = piece + got[now, 0, i, kind].astype(F32)
            if late:
                piece = piece + jnp.where(second, got[now, 1, i, kind].astype(F32), 0.0)
            held[now, i, kind] = piece.astype(BF16)

    for k, (which, half) in enumerate(places):

        @pl.when(step == k)
        def _():
            pltpu.make_async_copy(held.at[now], outs[which].at[half], out_sems.at[now]).start()

    @pl.when(step == count - 1)
    def _():
        sent(now)
        if count > 1:
            sent(1 - now)


def expert_wgrads(flipped, hidden, entries, places, extras=(), added=(), late=None, after=(), into=None, halves=None):
    rows = hidden[0][0].shape[0]
    wide = 2 * LANES
    seq = flipped[0].shape[1]
    count = len(entries)

    def entry(i):
        place = entries[0]
        for k in range(1, count):
            place = jnp.where(i == k, entries[k], place)
        return (0, place)

    lane = pl.BlockSpec((rows, wide), entry)
    whole = pl.BlockSpec((D, seq), lambda i: (0, 0))
    kernel = functools.partial(expert_wgrad_kernel, places, added, late or {})
    if into is not None:
        after = [into, *after]
    sizes = halves or [sum(which == o for which, _ in places) for o in range(max(which for which, _ in places) + 1)]
    return pl.pallas_call(
        behind(kernel, 14 + len(extras), after),
        grid=(count,),
        out_shape=tuple(jax.ShapeDtypeStruct((size, 2, 3, D, LANES), BF16) for size in sizes),
        in_specs=[whole] * 2 + [lane] * 12 + [in_hbm()] * (len(extras) + len(after)),
        out_specs=(in_hbm(),) * len(sizes),
        scratch_shapes=[
            pltpu.VMEM((2, 2, 3, D, LANES), BF16),
            pltpu.SemaphoreType.DMA((2,)),
            pltpu.VMEM((2, 2, 2, 3, D, LANES), BF16),
            pltpu.SemaphoreType.DMA((2, 2)),
        ],
        compiler_params=pltpu.CompilerParams(vmem_limit_bytes=VMEM_MOST),
        cost_estimate=cost(2.2 * count),
        input_output_aliases={} if into is None else {14 + len(extras): 0},
    )(*flipped, *hidden[0], *hidden[1], *hidden[2], *extras, *after)


def expert_total_kernel(own_ref, xa_ref, xb_ref, ya_ref, yb_ref, gate_ref, up_ref, down_ref):
    for kind, out in enumerate((gate_ref, up_ref, down_ref)):
        for half, (x_ref, y_ref) in enumerate(((xa_ref, ya_ref), (xb_ref, yb_ref))):
            out[half, 0] = (
                own_ref[half, 0, kind].astype(F32) + x_ref[0, 0, kind].astype(F32) + y_ref[0, 0, kind].astype(F32)
            )


def expert_total(after, own, *parts):
    block = pl.BlockSpec((2, 1, 3, D, LANES), lambda i: (0, i, 0, 0, 0))
    part = pl.BlockSpec((1, 1, 3, D, LANES), lambda i: (0, i, 0, 0, 0))
    out = pl.BlockSpec((2, 1, D, LANES), lambda i: (0, i, 0, 0))
    sums = pl.pallas_call(
        behind(expert_total_kernel, 5, after),
        grid=(2,),
        out_shape=(jax.ShapeDtypeStruct((2, 2, D, LANES), F32),) * 3,
        in_specs=[block] + [part] * 4 + [in_hbm()] * len(after),
        out_specs=(out,) * 3,
        compiler_params=pltpu.CompilerParams(vmem_limit_bytes=VMEM_MOST),
        cost_estimate=cost(5),
    )(own, *parts, *after)
    return [total.reshape(4, D, LANES) for total in sums]


def halves_kernel(x_ref, y_ref, low_ref, high_ref):
    low_ref[...] = y_ref[...]
    high_ref[...] = x_ref[...]


def halves(from_x, from_y, after):
    half = jax.ShapeDtypeStruct((2, 3, D, LANES), BF16)
    first = pl.BlockSpec((1, 1, D, LANES), lambda i, j: (i, j, 0, 0))
    second = pl.BlockSpec((1, 1, D, LANES), lambda i, j: (i + 2, j, 0, 0))
    return pl.pallas_call(
        behind(halves_kernel, 2, after),
        grid=(2, 3),
        out_shape=(half, half),
        in_specs=[second, first] + [in_hbm()] * len(after),
        out_specs=(first,) * 2,
        compiler_params=pltpu.CompilerParams(vmem_limit_bytes=VMEM_MOST),
        cost_estimate=cost(3),
    )(from_x, from_y, *after)


def turn_kernel(
    spot_ref, came_ref, back_ref, gates_ref, kept_ref, resid_ref, gain_ref, g_ref, wr_ref, wo_ref, send_ref,
    out_ref, resid_grad_ref, branch_ref, mixed_grad_ref, small_ref,
):
    rows = resid_ref.shape[0]
    gates = gates_ref[...]
    both = lambda span: came_ref[:, span].astype(F32) + back_ref[:, span].astype(F32)
    out_ref[...] = resid_ref[...] + both(slice(D, 2 * D))
    gate_grad = dot_nn(both(slice(2 * D, None)).astype(BF16), relabel(spot_ref[2])) * kept_ref[...]
    logit_grad = gates * (gate_grad - jnp.sum(gates * gate_grad, axis=1, keepdims=True))
    logit_grad = logit_grad.astype(BF16)
    moe_grad = both(slice(0, D)) + dot_nn(logit_grad, wr_ref[...])
    resid = resid_ref[...]
    scale = lax.rsqrt(jnp.mean(resid * resid, axis=1, keepdims=True) + EPS)
    normed = resid * scale
    small_ref[LANES:, :] = jnp.broadcast_to(jnp.sum(moe_grad * normed, axis=0, keepdims=True), (8, D))
    small_ref[:LANES, :] = dot_tn(logit_grad, send_ref[:, :D])
    inner = moe_grad * gain_ref[1:2, :]
    grad = g_ref[...].astype(F32) + scale * (inner - normed * jnp.mean(inner * normed, axis=1, keepdims=True))
    resid_grad_ref[...] = grad
    branch = grad.astype(BF16)
    branch_ref[...] = branch
    for part in range(4):
        mixed_grad_ref[pl.ds(part * rows, rows), :] = dot_nt(
            branch, wo_ref[part * 256 : (part + 1) * 256, :]
        ).astype(BF16)


def turn(spots, came, back, gates, kept, resid, gain, g, wr, wo, send, after=()):
    rows = resid.shape[0]
    shapes = (
        jax.ShapeDtypeStruct((rows, D), F32),
        jax.ShapeDtypeStruct((rows, D), F32),
        jax.ShapeDtypeStruct((rows, D), BF16),
        jax.ShapeDtypeStruct((4 * rows, 256), BF16),
        jax.ShapeDtypeStruct((LANES + 8, D), F32),
    )
    return pl.pallas_call(
        behind(turn_kernel, 11, after),
        out_shape=shapes,
        in_specs=[in_smem()] + [in_vmem()] * 10 + [in_hbm()] * len(after),
        out_specs=tuple(in_vmem() for _ in shapes),
        compiler_params=pltpu.CompilerParams(vmem_limit_bytes=VMEM_MOST),
        cost_estimate=cost(2),
    )(spots, came, back, gates, kept, resid, gain, g, wr, wo, send, *after)


def out_wgrad_kernel(mixed_ref, branch_ref, small_ref, pack_ref):
    rows = branch_ref.shape[0]
    for part in range(4):
        product = dot_tn(mixed_ref[pl.ds(part * rows, rows), :], branch_ref[...]).astype(BF16)
        pack_ref[2 * part, :LANES, :] = product[:LANES]
        pack_ref[2 * part + 1, :LANES, :] = product[LANES:]
    for row in range(8):
        span = pl.ds(row * LANES, LANES)
        for col in range(4):
            pack_ref[row, LANES:, col * 256 : col * 256 + LANES] = small_ref[col * 8 : col * 8 + 8, span].astype(BF16)
            pack_ref[row, LANES:, col * 256 + LANES : col * 256 + 256] = small_ref[LANES:, span].astype(BF16)


def out_wgrad(mixed, branch, small, after=()):
    return pl.pallas_call(
        behind(out_wgrad_kernel, 3, after),
        out_shape=jax.ShapeDtypeStruct((8, LANES + 8, D), BF16),
        in_specs=[in_vmem()] * 3 + [in_hbm()] * len(after),
        out_specs=in_vmem(),
        compiler_params=pltpu.CompilerParams(vmem_limit_bytes=VMEM_MOST),
        cost_estimate=cost(3),
    )(mixed, branch, small, *after)


def unpack_kernel(sum_ref, query_ref, key_ref, value_ref, gain_ref):
    query_ref[...] = sum_ref[:LANES, :256].astype(F32)
    key_ref[...] = sum_ref[:LANES, 256:384].astype(F32)
    value_ref[...] = sum_ref[:LANES, 384:].astype(F32)
    gain_ref[...] = sum_ref[LANES:, :LANES].astype(F32)


def unpack(sums, after):
    return pl.pallas_call(
        behind(unpack_kernel, 1, after),
        out_shape=tuple(jax.ShapeDtypeStruct(shape, F32) for shape in ((LANES, 256), (LANES, LANES), (LANES, LANES), (8, LANES))),
        in_specs=[in_vmem()] + [in_hbm()] * len(after),
        out_specs=(in_vmem(),) * 4,
        compiler_params=pltpu.CompilerParams(vmem_limit_bytes=VMEM_MOST),
        cost_estimate=cost(2),
    )(sums, *after)


def ring_gather(value, n_col):
    steps = [(i, (i + 1) % n_col) for i in range(n_col)]
    chunks = [value]
    for _ in range(n_col - 1):
        chunks.append(lax.ppermute(chunks[-1], "col", steps))
    return chunks


def ring_sum(parts, n_col):
    steps = [(i, (i + 1) % n_col) for i in range(n_col)]
    total = parts[1]
    for part in parts[2:] + parts[:1]:
        total = lax.ppermute(total, "col", steps).astype(F32) + part.astype(F32)
        if part is not parts[0]:
            total = total.astype(BF16)
    return total


def shift_all(parts, n_col):
    return [
        lax.ppermute(part, "col", [(i, (i + s) % n_col) for i in range(n_col)]) if s else part
        for s, part in enumerate(parts)
    ]


def hold(value, *until):
    return lax.optimization_barrier((value, *until))[0]


CORE, ACROSS_X, ACROSS_Y = 1, 2, 4


def swap(value, mask):
    return lax.ppermute(value, "row", [(i, i ^ mask) for i in range(8)])


def fast(
    block_in,
    attn_gain,
    moe_gain,
    w_query,
    w_key,
    w_value,
    w_out,
    w_router,
    w_gate,
    w_up,
    w_down,
    expert_ids,
    fill_order,
    prefix_len,
    out_grad,
):
    rows = block_in.shape[0]
    n_col = lax.axis_size("col")
    col = lax.axis_index("col")
    row = lax.axis_index("row")
    seq = rows * n_col
    spots = jnp.stack([col.astype(jnp.int32), prefix_len[0], row.astype(jnp.int32)])
    gains = jnp.concatenate([attn_gain, moe_gain, jnp.zeros((256,), BF16)])[None]
    pack_qkv = jnp.concatenate(
        [jnp.concatenate([w_query, w_key, w_value], axis=1), gains, jnp.zeros((7, 512), BF16)], axis=0
    )
    pack_out = jnp.concatenate([w_out, jnp.pad(w_router.T, ((0, 0), (0, 256 - LANES)))], axis=0)
    pack_out = lax.all_gather(pack_out, "col", axis=0)
    pack_qkv = lax.all_gather(pack_qkv, "row", axis=0)
    pack_out = lax.all_gather(pack_out, "row", axis=0)
    cosine, sine = rope_tables(0, seq)
    cosine = jnp.tile(cosine, (1, 4))
    sine = jnp.concatenate([-sine, sine, -sine, sine], axis=1)
    ring = [(i, (i + 1) % n_col) for i in range(n_col)]
    x_chunks = [block_in, lax.ppermute(block_in, "col", ring)]
    x_chunks += ring_gather(hold(x_chunks[1], cosine, sine), n_col)[1:3]
    own = jnp.stack([w_gate, w_up, w_down], axis=1)
    from_x, from_y, other = swap(own, ACROSS_X), swap(own, ACROSS_Y), swap(own, CORE)

    attn_in, q, k, v, lse, w_qkv, gains, mixed_all = attend(spots, x_chunks, pack_qkv, cosine, sine, [other])
    g_chunks = [out_grad, lax.ppermute(hold(out_grad, x_chunks[3]), "col", ring)]
    g_chunks += ring_gather(hold(g_chunks[1], attn_in), n_col)[1:3]
    mixed_own = lax.all_to_all(mixed_all, "col", split_axis=0, concat_axis=0, tiled=True)
    low, high = halves(from_x, from_y, [g_chunks[2]])
    resid, send, gates, kept, wo, wr = route(
        spots, mixed_own, block_in, pack_out, gains, expert_ids, fill_order, [low]
    )
    far = swap(low, ACROSS_X), swap(high, ACROSS_Y)
    weights = [own, other, from_x, swap(from_x, CORE), from_y, swap(from_y, CORE), *far]

    send_chunks = [send, *ring_gather(hold(send, g_chunks[3]), n_col)[1:]]
    weights += [swap(hold(part, send_chunks[2]), CORE) for part in far]
    results, backs, back = {}, [], None
    steps = [(i, (i + 1) % n_col) for i in range(n_col)]
    order = (1, 2, 3, 0)
    for at, chunk in enumerate(order):
        after = [results[order[at - 1]][1]] if at else [send_chunks[3]]
        if at >= 2:
            after.append(backs[at - 2])
        if at == 2:
            flipped = flip(send_chunks, g_chunks, [results[2][1]])
            after.append(flipped[0])
        results[chunk] = experts(send_chunks[chunk], g_chunks[chunk], weights, after)
        if chunk:
            part = results[chunk][0]
            back = part if back is None else (back.astype(F32) + part.astype(F32)).astype(BF16)
            back = lax.ppermute(back, "col", steps)
            backs.append(back)
    results = [results[chunk] for chunk in range(n_col)]

    hidden = [[result[kind] for result in results] for kind in (1, 2, 3)]
    wgrads = functools.partial(expert_wgrads, flipped, hidden)
    (p7,) = wgrads((14, 15), ((0, 0), (0, 1)), after=[backs[2]])
    r7 = swap(p7, CORE)
    (p5,) = wgrads((10, 11), ((0, 2), (0, 3)), after=[p7], halves=[4])
    (p53,) = wgrads((6, 7), ((0, 0), (0, 1)), after=[r7], into=p5, halves=[4])
    r53 = swap(p53, CORE)
    q6 = wgrads((12, 13), ((0, 0), (1, 0)), [r7], ((0, 0), (0, 1)), after=[p53])
    far_x, far_y = swap(q6[0], ACROSS_X), swap(q6[1], ACROSS_Y)
    block_out, resid_grad, branch, mixed_grad, small = turn(
        spots, backs[2], results[0][0], gates, kept, resid, gains, out_grad, wr, wo, send, q6[:1]
    )
    mixed_grads = lax.all_to_all(mixed_grad, "col", split_axis=0, concat_axis=0, tiled=True)
    pack = out_wgrad(mixed_own, branch, small)
    out_sum = lax.psum_scatter(pack, "row", scatter_dimension=0, tiled=True)
    q2a, q4b = wgrads(
        (4, 9), ((0, 0), (1, 0)), [r53], ((0, 0), (0, 3)), after=[pack, mixed_grads, far_x, far_y]
    )
    x2a, y4b = swap(q2a, ACROSS_X), swap(q4b, ACROSS_Y)
    q2b, q4a, p1 = wgrads(
        (5, 8, 2, 3),
        ((0, 0), (1, 0), (2, 0), (2, 1)),
        [r53, far_y, far_x],
        ((0, 1), (0, 2), None, None),
        {0: 1, 1: 2},
        [q2a],
    )
    r1 = swap(p1, CORE)
    x2b, y4a = swap(q2b, ACROSS_X), swap(q4a, ACROSS_Y)
    qkv_wgrad, *back_parts = attend_back(
        spots, mixed_grads, mixed_all, q, k, v, lse, attn_in, w_qkv, cosine, sine, gains, [q2b]
    )
    (q0,) = wgrads((0, 1), ((0, 0), (0, 1)), [r1], ((0, 0), (0, 1)), after=[qkv_wgrad])
    moving = lax.ppermute(back_parts[1], "col", steps)
    moving = (hold(moving, q0, x2a, y4b).astype(F32) + back_parts[2].astype(F32)).astype(BF16)
    moving = lax.ppermute(moving, "col", steps)
    moving = (moving.astype(F32) + back_parts[3].astype(F32)).astype(BF16)
    third_step = moving
    last_step = lax.ppermute(moving, "col", steps)
    attn_grad = last_step.astype(F32) + back_parts[0].astype(F32)
    x_rows = block_in.astype(F32)
    scale = lax.rsqrt(jnp.mean(x_rows * x_rows, axis=1, keepdims=True) + EPS)
    normed = x_rows * scale
    inner = attn_grad * gains[:1]
    block_in_grad = resid_grad + scale * (inner - normed * jnp.mean(inner * normed, axis=1, keepdims=True))
    gate_sum, up_sum, down_sum = expert_total([third_step], q0, x2a, x2b, y4a, y4b)

    qkv_sum = lax.psum_scatter(qkv_wgrad, "row", scatter_dimension=0, tiled=True)[0]
    *qkv_sums, gain_one = unpack(qkv_sum, [last_step])
    out_sum = lax.psum_scatter(hold(out_sum, q2b), "col", scatter_dimension=2, tiled=True)[0].astype(F32)
    gain_one_sum = functools.reduce(jnp.add, shift_all([gain_one] * n_col, n_col))[0]
    return (
        block_out,
        block_in_grad,
        gain_one_sum,
        out_sum[LANES, LANES:],
        *qkv_sums,
        out_sum[:LANES],
        out_sum[LANES:, :LANES].T,
        gate_sum,
        up_sum,
        down_sum,
    )


def takes_fast(mesh):
    n_row, n_col = mesh.shape["row"], mesh.shape["col"]
    return n_row == 8 and n_col == 4


def solution(mesh):
    in_specs = (
        P(("row", "col"), None),
        P("row"),
        P("row"),
        P("row", "col"),
        P("row", "col"),
        P("row", "col"),
        P("row", "col"),
        P("row", "col"),
        P("row", None, "col"),
        P("row", None, "col"),
        P("row", None, "col"),
        P(("row", "col"), None),
        P(("row", "col"), None),
        P("row"),
        P(("row", "col"), None),
    )
    out_specs = (
        P(("row", "col"), None),
        P(("row", "col"), None),
        P("row"),
        P("row"),
        P("row", "col"),
        P("row", "col"),
        P("row", "col"),
        P("row", "col"),
        P("row", "col"),
        P("row", None, "col"),
        P("row", None, "col"),
        P("row", None, "col"),
    )
    local = fast if takes_fast(mesh) else general
    return jax.shard_map(local, mesh=mesh, in_specs=in_specs, out_specs=out_specs, check_vma=False)
```

```python
import functools

import jax
import jax.numpy as jnp
from jax import lax
from jax.experimental import pallas as pl
from jax.experimental.pallas import tpu as pltpu
from jax.sharding import PartitionSpec as P

D = 1024
H = 16
KVH = 8
HD = 64
E = 32
TOPK = 8
CAP = 80


EPS = 1e-06
NEGATIVE = -1e30


def cross_rows(left, right):
    return lax.dot_general(
        left, right, (((0,), (0,)), ((), ())), preferred_element_type=jnp.float32
    )


def times_back(left, right):
    return lax.dot_general(
        left, right, (((1,), (1,)), ((), ())), preferred_element_type=jnp.float32
    )


def rope_tables(first_position, count):
    position = (first_position + jnp.arange(count, dtype=jnp.int32)).astype(jnp.float32)
    inverse = 10000.0 ** (-jnp.arange(HD // 2, dtype=jnp.float32) * 2.0 / HD)
    angle = position[:, None] * inverse[None, :]
    return (jnp.cos(angle), jnp.sin(angle))


def rotate(values, cosine, sine):
    half = HD // 2
    first, second = (values[..., :half], values[..., half:])
    cos_rows = cosine[:, None, :]
    sin_rows = sine[:, None, :]
    return jnp.concatenate(
        [first * cos_rows - second * sin_rows, second * cos_rows + first * sin_rows], axis=-1
    )


def rotate_back(grads, cosine, sine):
    half = HD // 2
    first, second = (grads[..., :half], grads[..., half:])
    cos_rows = cosine[:, None, :]
    sin_rows = sine[:, None, :]
    return jnp.concatenate(
        [first * cos_rows + second * sin_rows, second * cos_rows - first * sin_rows], axis=-1
    )


def norm_rows(values, gain):
    scale = lax.rsqrt(jnp.mean(values * values, axis=1, keepdims=True) + EPS)
    normed = values * scale
    return (normed, scale, (normed * gain).astype(jnp.bfloat16))


def norm_back(grad_in, normed, scale, gain):
    gain_grad = jnp.sum(grad_in * normed, axis=0)
    inner = grad_in * gain
    return (scale * (inner - normed * jnp.mean(inner * normed, axis=1, keepdims=True)), gain_grad)


def to_heads(rows, count, group):
    return rows.reshape(count, KVH, group, HD).transpose(1, 2, 0, 3).reshape(KVH, group * count, HD)


def from_heads(heads, count, group):
    return heads.reshape(KVH, group, count, HD).transpose(2, 0, 1, 3).reshape(count, H, HD)


def general(
    block_in,
    attn_gain,
    moe_gain,
    w_query,
    w_key,
    w_value,
    w_out,
    w_router,
    w_gate,
    w_up,
    w_down,
    expert_ids,
    fill_order,
    prefix_len,
    out_grad,
):
    tok_rows = block_in.shape[0]
    n_col = lax.axis_size("col")
    col_index = lax.axis_index("col")
    seq_rows = tok_rows * n_col
    group = H // KVH
    scale_attn = HD ** (-0.5)
    bf16 = jnp.bfloat16
    f32 = jnp.float32
    shared = (
        lax.all_gather(w_query, "row", axis=0, tiled=True),
        lax.all_gather(w_key, "row", axis=0, tiled=True),
        lax.all_gather(w_value, "row", axis=0, tiled=True),
        lax.all_gather(w_out, "row", axis=0, tiled=True),
        lax.all_gather(w_router, "row", axis=0, tiled=True),
        lax.all_gather(attn_gain, "row", axis=0, tiled=True),
        lax.all_gather(moe_gain, "row", axis=0, tiled=True),
    )
    wq_full, wk_full, wv_full, wo_full, wr_full = (
        lax.all_gather(shared[0], "col", axis=1, tiled=True),
        lax.all_gather(shared[1], "col", axis=1, tiled=True),
        lax.all_gather(shared[2], "col", axis=1, tiled=True),
        lax.all_gather(shared[3], "col", axis=1, tiled=True),
        lax.all_gather(shared[4], "col", axis=1, tiled=True),
    )
    gain_one = shared[5].astype(f32)
    gain_two = shared[6].astype(f32)
    x_rows = block_in.astype(f32)
    normed_one, scale_one, attn_in = norm_rows(x_rows, gain_one)
    query = jnp.dot(attn_in, wq_full, preferred_element_type=f32)
    key = jnp.dot(attn_in, wk_full, preferred_element_type=f32)
    value = jnp.dot(attn_in, wv_full, preferred_element_type=f32).astype(bf16)
    cosine, sine = rope_tables(col_index * tok_rows, tok_rows)
    query_rot = rotate(query.reshape(tok_rows, H, HD), cosine, sine).astype(bf16)
    key_rot = (
        rotate(key.reshape(tok_rows, KVH, HD), cosine, sine)
        .astype(bf16)
        .reshape(tok_rows, KVH * HD)
    )
    keys_all, values_all = (
        lax.all_gather(key_rot, "col", axis=0, tiled=True),
        lax.all_gather(value, "col", axis=0, tiled=True),
    )
    prefix = prefix_len[0]
    query_spot = col_index * tok_rows + jnp.arange(tok_rows, dtype=jnp.int32)
    key_spot = jnp.arange(seq_rows, dtype=jnp.int32)
    allowed = (key_spot[None, :] <= query_spot[:, None]) | (key_spot[None, :] < prefix)
    allowed_rows = jnp.tile(allowed, (group, 1))
    query_heads = to_heads(query_rot.reshape(tok_rows, H * HD), tok_rows, group)
    key_heads = keys_all.reshape(seq_rows, KVH, HD).transpose(1, 0, 2)
    value_heads = values_all.reshape(seq_rows, KVH, HD).transpose(1, 0, 2)

    def attend(pieces):
        queries, keys, values = pieces
        scores = times_back(queries, keys) * scale_attn
        scores = jnp.where(allowed_rows, scores, NEGATIVE)
        highest = jnp.max(scores, axis=1, keepdims=True)
        expo = jnp.exp(scores - highest)
        total = jnp.sum(expo, axis=1, keepdims=True)
        weights = (expo / total).astype(bf16)
        mixed_heads = jnp.dot(weights, values, preferred_element_type=f32).astype(bf16)
        return (mixed_heads, (highest + jnp.log(total))[:, 0])

    mixed_heads, lse_heads = lax.map(attend, (query_heads, key_heads, value_heads))
    mixed = from_heads(mixed_heads, tok_rows, group).reshape(tok_rows, H * HD)
    resid = x_rows + jnp.dot(mixed, wo_full, preferred_element_type=f32)
    normed_two, scale_two, moe_in = norm_rows(resid, gain_two)
    logits = jnp.dot(moe_in, wr_full, preferred_element_type=f32)
    choice_hot = (expert_ids[:, :, None] == jnp.arange(E, dtype=jnp.int32)).astype(f32)
    picked = jnp.sum(choice_hot * logits[:, None, :], axis=2)
    highest = jnp.max(picked, axis=1, keepdims=True)
    expo = jnp.exp(picked - highest)
    gates = expo / jnp.sum(expo, axis=1, keepdims=True)
    order = fill_order[0]
    ranked = expert_ids[order]
    onehot = (ranked.reshape(-1, 1) == jnp.arange(E, dtype=jnp.int32)).astype(jnp.int32)
    before = jnp.cumsum(onehot, axis=0) - onehot
    ranked_slot = jnp.sum(before * onehot, axis=1).reshape(tok_rows, TOPK)
    slot = jnp.zeros((tok_rows, TOPK), jnp.int32).at[order].set(ranked_slot)
    kept = slot < CAP
    dest_grid = jnp.where(kept, expert_ids * CAP + slot, E * CAP)
    pair_ids = jnp.arange(tok_rows * TOPK, dtype=jnp.int32)
    slot_pair = (
        jnp.full((E * CAP + 1,), tok_rows * TOPK, jnp.int32)
        .at[dest_grid.reshape(-1)]
        .set(pair_ids)[: E * CAP]
    )
    slot_token = slot_pair // TOPK
    gate_slot = jnp.concatenate([gates.reshape(-1), jnp.zeros((1,), f32)])[slot_pair]
    moe_pad = jnp.concatenate([moe_in, jnp.zeros((1, D), bf16)])
    dispatch = moe_pad[slot_token].reshape(E, CAP, D)
    received = lax.all_to_all(dispatch, "row", split_axis=0, concat_axis=1, tiled=True)
    gate_w, up_w, down_w = (
        lax.all_gather(w_gate, "col", axis=2, tiled=True),
        lax.all_gather(w_up, "col", axis=2, tiled=True),
        lax.all_gather(w_down, "col", axis=2, tiled=True),
    )
    hidden_gate = jnp.einsum("erd,edf->erf", received, gate_w, preferred_element_type=f32)
    hidden_up = jnp.einsum("erd,edf->erf", received, up_w, preferred_element_type=f32)
    active = (jax.nn.silu(hidden_gate) * hidden_up).astype(bf16)
    expert_out = jnp.einsum("erf,edf->erd", active, down_w, preferred_element_type=f32).astype(bf16)
    returned = lax.all_to_all(expert_out, "row", split_axis=1, concat_axis=0, tiled=True)
    out_pad = jnp.concatenate([returned.reshape(E * CAP, D), jnp.zeros((1, D), bf16)])
    pair_out = out_pad[dest_grid]
    weight_pair = gates * kept.astype(f32)
    moe_out = jnp.zeros((tok_rows, D), f32)
    for choice_index in range(TOPK):
        moe_out = moe_out + weight_pair[:, choice_index : choice_index + 1] * pair_out[
            :, choice_index
        ].astype(f32)
    block_out = resid + moe_out
    grad_out = out_grad.astype(f32)
    gate_grad = jnp.stack(
        [
            jnp.sum(pair_out[:, choice_index].astype(f32) * grad_out, axis=1)
            for choice_index in range(TOPK)
        ],
        axis=1,
    )
    grad_pad = jnp.concatenate([grad_out, jnp.zeros((1, D), f32)])
    slot_grad = (gate_slot[:, None] * grad_pad[slot_token]).astype(bf16).reshape(E, CAP, D)
    out_grads = lax.all_to_all(slot_grad, "row", split_axis=0, concat_axis=1, tiled=True)
    act_grad = jnp.einsum("erd,edf->erf", out_grads, down_w, preferred_element_type=f32)
    sigma = jax.nn.sigmoid(hidden_gate)
    gate_h_grad = (act_grad * hidden_up * sigma * (1.0 + hidden_gate * (1.0 - sigma))).astype(bf16)
    up_h_grad = (act_grad * hidden_gate * sigma).astype(bf16)
    down_wgrad = jnp.einsum("erd,erf->edf", out_grads, active, preferred_element_type=f32)
    gate_wgrad = jnp.einsum("erd,erf->edf", received, gate_h_grad, preferred_element_type=f32)
    up_wgrad = jnp.einsum("erd,erf->edf", received, up_h_grad, preferred_element_type=f32)
    in_grad = (
        jnp.einsum("erf,edf->erd", gate_h_grad, gate_w, preferred_element_type=f32)
        + jnp.einsum("erf,edf->erd", up_h_grad, up_w, preferred_element_type=f32)
    ).astype(bf16)
    back_rows = lax.all_to_all(in_grad, "row", split_axis=1, concat_axis=0, tiled=True)
    gate_sum, up_sum, down_sum = (
        lax.psum_scatter(
            gate_wgrad.astype(jnp.bfloat16), "col", scatter_dimension=2, tiled=True
        ).astype(jnp.float32),
        lax.psum_scatter(
            up_wgrad.astype(jnp.bfloat16), "col", scatter_dimension=2, tiled=True
        ).astype(jnp.float32),
        lax.psum_scatter(
            down_wgrad.astype(jnp.bfloat16), "col", scatter_dimension=2, tiled=True
        ).astype(jnp.float32),
    )
    back_pad = jnp.concatenate([back_rows.reshape(E * CAP, D), jnp.zeros((1, D), bf16)])
    pair_back = back_pad[dest_grid]
    moe_in_grad = jnp.zeros((tok_rows, D), f32)
    for choice_index in range(TOPK):
        moe_in_grad = moe_in_grad + pair_back[:, choice_index].astype(f32)
    picked_grad = gates * (gate_grad - jnp.sum(gates * gate_grad, axis=1, keepdims=True))
    logit_grad = jnp.sum(choice_hot * picked_grad[:, :, None], axis=1).astype(bf16)
    router_wgrad = cross_rows(moe_in, logit_grad)
    moe_in_grad = moe_in_grad + times_back(logit_grad, wr_full)
    norm_two_grad, gain_two_grad = norm_back(moe_in_grad, normed_two, scale_two, gain_two)
    resid_grad = grad_out + norm_two_grad
    branch_grad = resid_grad.astype(bf16)
    out_wgrad = cross_rows(mixed, branch_grad)
    mixed_grad = times_back(branch_grad, wo_full).astype(bf16)
    grad_heads = to_heads(mixed_grad, tok_rows, group)

    def query_side(pieces):
        queries, keys, values, lse_rows, grad_rows = pieces
        scores = jnp.where(allowed_rows, times_back(queries, keys) * scale_attn, NEGATIVE)
        probs = jnp.exp(scores - lse_rows[:, None])
        prob_grad = times_back(grad_rows, values)
        delta = jnp.sum(probs * prob_grad, axis=1, keepdims=True)
        score_grad = (probs * (prob_grad - delta)).astype(bf16)
        query_grad = jnp.dot(score_grad, keys, preferred_element_type=f32) * scale_attn
        return (query_grad, delta[:, 0], score_grad, probs)

    def both_sides(pieces):
        queries, keys, values, lse_rows, grad_rows = pieces
        query_grad, delta, score_grad, probs = query_side(pieces)
        key_grad = cross_rows(score_grad, queries) * scale_attn
        value_grad = cross_rows(probs.astype(bf16), grad_rows)
        return (query_grad, key_grad, value_grad)

    query_rot_grad, key_parts, value_parts = lax.map(
        both_sides, (query_heads, key_heads, value_heads, lse_heads, grad_heads)
    )
    key_rot_grad, value_grad = (
        lax.psum_scatter(
            key_parts.transpose(1, 0, 2).reshape(seq_rows, KVH * HD).astype(jnp.bfloat16),
            "col",
            scatter_dimension=0,
            tiled=True,
        ).astype(jnp.float32),
        lax.psum_scatter(
            value_parts.transpose(1, 0, 2).reshape(seq_rows, KVH * HD).astype(jnp.bfloat16),
            "col",
            scatter_dimension=0,
            tiled=True,
        ).astype(jnp.float32),
    )
    query_grad = (
        rotate_back(from_heads(query_rot_grad, tok_rows, group), cosine, sine)
        .reshape(tok_rows, H * HD)
        .astype(bf16)
    )
    key_grad = (
        rotate_back(key_rot_grad.reshape(tok_rows, KVH, HD), cosine, sine)
        .reshape(tok_rows, KVH * HD)
        .astype(bf16)
    )
    value_grad = value_grad.astype(bf16)
    query_wgrad = cross_rows(attn_in, query_grad)
    key_wgrad = cross_rows(attn_in, key_grad)
    value_wgrad = cross_rows(attn_in, value_grad)
    attn_in_grad = (
        times_back(query_grad, wq_full)
        + times_back(key_grad, wk_full)
        + times_back(value_grad, wv_full)
    )
    norm_one_grad, gain_one_grad = norm_back(attn_in_grad, normed_one, scale_one, gain_one)
    block_in_grad = resid_grad + norm_one_grad
    spread_one = jnp.broadcast_to(gain_one_grad[:, None], (D, n_col))
    spread_two = jnp.broadcast_to(gain_two_grad[:, None], (D, n_col))
    col_sums = (
        lax.psum_scatter(
            query_wgrad.astype(jnp.bfloat16), "col", scatter_dimension=1, tiled=True
        ).astype(jnp.float32),
        lax.psum_scatter(
            key_wgrad.astype(jnp.bfloat16), "col", scatter_dimension=1, tiled=True
        ).astype(jnp.float32),
        lax.psum_scatter(
            value_wgrad.astype(jnp.bfloat16), "col", scatter_dimension=1, tiled=True
        ).astype(jnp.float32),
        lax.psum_scatter(
            out_wgrad.astype(jnp.bfloat16), "col", scatter_dimension=1, tiled=True
        ).astype(jnp.float32),
        lax.psum_scatter(
            router_wgrad.astype(jnp.bfloat16), "col", scatter_dimension=1, tiled=True
        ).astype(jnp.float32),
        lax.psum_scatter(
            spread_one.astype(jnp.bfloat16), "col", scatter_dimension=1, tiled=True
        ).astype(jnp.float32),
        lax.psum_scatter(
            spread_two.astype(jnp.bfloat16), "col", scatter_dimension=1, tiled=True
        ).astype(jnp.float32),
    )
    row_sums = (
        lax.psum_scatter(
            col_sums[0].astype(jnp.bfloat16), "row", scatter_dimension=0, tiled=True
        ).astype(jnp.float32),
        lax.psum_scatter(
            col_sums[1].astype(jnp.bfloat16), "row", scatter_dimension=0, tiled=True
        ).astype(jnp.float32),
        lax.psum_scatter(
            col_sums[2].astype(jnp.bfloat16), "row", scatter_dimension=0, tiled=True
        ).astype(jnp.float32),
        lax.psum_scatter(
            col_sums[3].astype(jnp.bfloat16), "row", scatter_dimension=0, tiled=True
        ).astype(jnp.float32),
        lax.psum_scatter(
            col_sums[4].astype(jnp.bfloat16), "row", scatter_dimension=0, tiled=True
        ).astype(jnp.float32),
        lax.psum_scatter(
            col_sums[5].astype(jnp.bfloat16), "row", scatter_dimension=0, tiled=True
        ).astype(jnp.float32),
        lax.psum_scatter(
            col_sums[6].astype(jnp.bfloat16), "row", scatter_dimension=0, tiled=True
        ).astype(jnp.float32),
    )
    return (
        block_out,
        block_in_grad,
        row_sums[5][:, 0],
        row_sums[6][:, 0],
        row_sums[0],
        row_sums[1],
        row_sums[2],
        row_sums[3],
        row_sums[4],
        gate_sum,
        up_sum,
        down_sum,
    )


F32 = jnp.float32
BF16 = jnp.bfloat16
MIB = 1024 * 1024
LANES = 128
VMEM_MOST = 60 * MIB
COST_SCALE = 10**6


def cost(microseconds):
    return pl.CostEstimate(flops=int(microseconds * COST_SCALE), bytes_accessed=10**5, transcendentals=0)


def dot_nn(a, b):
    return lax.dot_general(a, b, (((1,), (0,)), ((), ())), preferred_element_type=F32)


def dot_nt(a, b):
    return lax.dot_general(a, b, (((1,), (1,)), ((), ())), preferred_element_type=F32)


def dot_tn(a, b):
    return lax.dot_general(a, b, (((0,), (0,)), ((), ())), preferred_element_type=F32)


def in_vmem():
    return pl.BlockSpec(memory_space=pltpu.VMEM)


def in_smem():
    return pl.BlockSpec(memory_space=pltpu.SMEM)


def in_hbm():
    return pl.BlockSpec(memory_space=pl.ANY)


def behind(kernel, n_in, after):
    if not after:
        return kernel
    return lambda *refs: kernel(*refs[:n_in], *refs[n_in + len(after) :])


def partner(values):
    lane = lax.broadcasted_iota(jnp.int32, values.shape, 1)
    half = HD // 2
    return jnp.where(
        lane % HD < half,
        pltpu.roll(values, LANES - half, 1),
        pltpu.roll(values, half, 1),
    )


def attend_kernel(
    spot_ref, x0, x1, x2, x3, pack_ref, cos_ref, sin_ref,
    attn_ref, q_ref, k_ref, v_ref, lse_ref, w_ref, gain_ref, mixed_ref,
):
    rows = x0.shape[0]
    col, prefix = spot_ref[0], spot_ref[1]
    for part in range(8):
        span = pl.ds(part * LANES, LANES)
        w_ref[span, :] = pack_ref[part, :LANES, :]
        gain_ref[0:1, span] = pack_ref[part, LANES : LANES + 1, :LANES].astype(F32)
        gain_ref[1:2, span] = pack_ref[part, LANES : LANES + 1, LANES : 2 * LANES].astype(F32)
    gain = gain_ref[0:1, :]
    for step, chunk in enumerate((x0, x1, x2, x3)):
        source = lax.rem(col - step + 4, 4)
        x = chunk[...].astype(F32)
        scale = lax.rsqrt(jnp.mean(x * x, axis=1, keepdims=True) + EPS)
        attn_ref[pl.ds(pl.multiple_of(source * rows, rows), rows), :] = (x * scale * gain).astype(BF16)
    for tile in range(4):
        span = pl.ds(tile * rows, rows)
        qkv = dot_nn(attn_ref[span, :], w_ref[...])
        cosine, sine = cos_ref[span, :], sin_ref[span, :]
        for block in range(3):
            v = qkv[:, block * LANES : (block + 1) * LANES]
            y = v * cosine + partner(v) * sine
            if block < 2:
                y = (y * HD ** (-0.5)).astype(BF16)
                q_ref[2 * block, span, :] = y[:, :HD]
                q_ref[2 * block + 1, span, :] = y[:, HD:]
            else:
                y = y.astype(BF16)
                k_ref[0, span, :] = y[:, :HD]
                k_ref[1, span, :] = y[:, HD:]
        v = qkv[:, 3 * LANES :].astype(BF16)
        v_ref[0, span, :] = v[:, :HD]
        v_ref[1, span, :] = v[:, HD:]
    total = 4 * rows
    for tile in range(4):
        span = pl.ds(tile * rows, rows)
        keys = max((tile + 1) * rows, total // 2)
        key_spot = lax.broadcasted_iota(jnp.int32, (rows, keys), 1)
        query_spot = lax.broadcasted_iota(jnp.int32, (rows, keys), 0) + tile * rows
        allowed = (key_spot <= query_spot) | (key_spot < prefix)
        for pair in range(2):
            k, v = k_ref[pair, pl.ds(0, keys), :], v_ref[pair, pl.ds(0, keys), :]
            outs = []
            for head in (2 * pair, 2 * pair + 1):
                scores = jnp.where(allowed, dot_nt(q_ref[head, span, :], k), NEGATIVE)
                highest = jnp.max(scores, axis=1, keepdims=True)
                expo = jnp.exp(scores - highest)
                summed = jnp.sum(expo, axis=1, keepdims=True)
                outs.append(dot_nn(expo.astype(BF16), v) * (1.0 / summed))
                lse_ref[span, head : head + 1] = highest + jnp.log(summed)
            mixed_ref[span, pair * LANES : (pair + 1) * LANES] = jnp.concatenate(outs, axis=1).astype(BF16)


def attend(spots, chunks, pack, cosine, sine, after=()):
    rows = chunks[0].shape[0]
    seq = 4 * rows
    shapes = (
        jax.ShapeDtypeStruct((seq, D), BF16),
        jax.ShapeDtypeStruct((4, seq, HD), BF16),
        jax.ShapeDtypeStruct((2, seq, HD), BF16),
        jax.ShapeDtypeStruct((2, seq, HD), BF16),
        jax.ShapeDtypeStruct((seq, 4), F32),
        jax.ShapeDtypeStruct((D, 512), BF16),
        jax.ShapeDtypeStruct((2, D), F32),
        jax.ShapeDtypeStruct((seq, 256), BF16),
    )
    return pl.pallas_call(
        behind(attend_kernel, 8, after),
        out_shape=shapes,
        in_specs=[in_smem()] + [in_vmem()] * 7 + [in_hbm()] * len(after),
        out_specs=tuple(in_vmem() for _ in shapes),
        compiler_params=pltpu.CompilerParams(vmem_limit_bytes=VMEM_MOST),
        cost_estimate=cost(10),
    )(spots, *chunks, pack, cosine, sine, *after)


def attend_back_kernel(
    spot_ref, grad_ref, mixed_ref, q_ref, k_ref, v_ref, lse_ref, attn_ref, w_ref, cos_ref, sin_ref, gain_ref,
    wgrad_ref, in0, in1, in2, in3, dqkv_ref, dk_ref, dv_ref, dq_ref, mg_ref,
):
    seq = attn_ref.shape[0]
    rows = seq // 4
    prefix = spot_ref[1]
    for tile in range(4):
        span = pl.ds(tile * rows, rows)
        for pair in range(2):
            g = grad_ref[span, pair * LANES : (pair + 1) * LANES]
            mg_ref[2 * pair, span, :] = g[:, :HD]
            mg_ref[2 * pair + 1, span, :] = g[:, HD:]
    dk_ref[...] = jnp.zeros_like(dk_ref)
    dv_ref[...] = jnp.zeros_like(dv_ref)
    for tile in range(4):
        span = pl.ds(tile * rows, rows)
        keys = max((tile + 1) * rows, seq // 2)
        key_spot = lax.broadcasted_iota(jnp.int32, (rows, keys), 1)
        query_spot = lax.broadcasted_iota(jnp.int32, (rows, keys), 0) + tile * rows
        allowed = (key_spot <= query_spot) | (key_spot < prefix)
        for pair in range(2):
            k, v = k_ref[pair, pl.ds(0, keys), :], v_ref[pair, pl.ds(0, keys), :]
            both = grad_ref[span, pair * LANES : (pair + 1) * LANES].astype(F32) * mixed_ref[
                span, pair * LANES : (pair + 1) * LANES
            ].astype(F32)
            outs = []
            for at, head in enumerate((2 * pair, 2 * pair + 1)):
                q, g = q_ref[head, span, :], mg_ref[head, span, :]
                delta = jnp.sum(both[:, at * HD : (at + 1) * HD], axis=1, keepdims=True)
                scores = jnp.where(allowed, dot_nt(q, k), NEGATIVE)
                probs = jnp.exp(scores - lse_ref[span, head : head + 1])
                score_grad = (probs * (dot_nt(g, v) - delta)).astype(BF16)
                dv_ref[pair, pl.ds(0, keys), :] += dot_tn(probs.astype(BF16), g)
                dk_ref[pair, pl.ds(0, keys), :] += dot_tn(score_grad, q)
                outs.append(dot_nn(score_grad, k) * HD ** (-0.5))
            dq_ref[span, pair * LANES : (pair + 1) * LANES] = jnp.concatenate(outs, axis=1)
    for tile in range(4):
        span = pl.ds(tile * rows, rows)
        cosine, sine = cos_ref[span, :], sin_ref[span, :]
        for block in range(3):
            if block < 2:
                g = dq_ref[span, block * LANES : (block + 1) * LANES]
            else:
                g = jnp.concatenate([dk_ref[0, span, :], dk_ref[1, span, :]], axis=1)
            dqkv_ref[span, block * LANES : (block + 1) * LANES] = (g * cosine - partner(g) * sine).astype(BF16)
        dqkv_ref[span, 3 * LANES :] = jnp.concatenate([dv_ref[0, span, :], dv_ref[1, span, :]], axis=1).astype(BF16)
    gain_total = jnp.zeros((1, D), F32)
    for step, out in enumerate((in0, in1, in2, in3)):
        source = lax.rem(spot_ref[0] - step + 4, 4)
        span = pl.ds(pl.multiple_of(source * rows, rows), rows)
        back = dot_nt(dqkv_ref[span, :], w_ref[...])
        out[...] = back.astype(BF16)
        gain_total = gain_total + jnp.sum(back * attn_ref[span, :].astype(F32), axis=0, keepdims=True)
    gain_total = gain_total / gain_ref[0:1, :]
    for part in range(8):
        span = pl.ds(part * LANES, LANES)
        wgrad_ref[part, LANES:, :LANES] = jnp.broadcast_to(gain_total[:, part * LANES : (part + 1) * LANES], (8, LANES)).astype(BF16)
        wgrad_ref[part, LANES:, LANES:] = jnp.zeros((8, 3 * LANES), BF16)
        wgrad_ref[part, :LANES, :] = dot_tn(attn_ref[:, span], dqkv_ref[...]).astype(BF16)


def attend_back(spots, grads, mixed, q, k, v, lse, attn_in, w_qkv, cosine, sine, gain, after=()):
    seq = attn_in.shape[0]
    shapes = (
        jax.ShapeDtypeStruct((8, 136, 512), BF16),
    ) + (jax.ShapeDtypeStruct((seq // 4, D), BF16),) * 4
    return pl.pallas_call(
        behind(attend_back_kernel, 12, after),
        out_shape=shapes,
        in_specs=[in_smem()] + [in_vmem()] * 11 + [in_hbm()] * len(after),
        out_specs=tuple(in_vmem() for _ in shapes),
        scratch_shapes=[
            pltpu.VMEM((seq, 512), BF16),
            pltpu.VMEM((2, seq, HD), F32),
            pltpu.VMEM((2, seq, HD), F32),
            pltpu.VMEM((seq, 256), F32),
            pltpu.VMEM((4, seq, HD), BF16),
        ],
        compiler_params=pltpu.CompilerParams(vmem_limit_bytes=VMEM_MOST),
        cost_estimate=cost(16),
    )(spots, grads, mixed, q, k, v, lse, attn_in, w_qkv, cosine, sine, gain, *after)


def route_kernel(
    spot_ref, mixed_ref, x_ref, pack_ref, gain_ref, ids_ref, order_ref,
    resid_ref, send_ref, gates_ref, kept_ref, wo_ref, wr_ref, wr_wide,
):
    rows = x_ref.shape[0]
    wr_wide[...] = jnp.zeros_like(wr_wide)
    for row in range(8):
        span = pl.ds(row * LANES, LANES)
        for col in range(4):
            wo_ref[span, col * 256 : (col + 1) * 256] = pack_ref[row, col, :LANES, :]
            wr_wide[col * 8 : (col + 1) * 8, span] = pack_ref[row, col, LANES:, :LANES].astype(F32)
    wr_ref[...] = wr_wide[...].astype(BF16)
    resid = x_ref[...].astype(F32)
    for part in range(4):
        resid = resid + dot_nn(mixed_ref[pl.ds(part * rows, rows), :], wo_ref[part * 256 : (part + 1) * 256, :])
    resid_ref[...] = resid
    scale = lax.rsqrt(jnp.mean(resid * resid, axis=1, keepdims=True) + EPS)
    moe_in = (resid * scale * gain_ref[1:2, :]).astype(BF16)
    send_ref[:, :D] = moe_in
    logits = dot_nt(moe_in, wr_ref[...])
    lane = lax.broadcasted_iota(jnp.int32, (rows, LANES), 1)
    chosen = jnp.zeros((rows, LANES), jnp.bool_)
    for choice in range(TOPK):
        chosen = chosen | (ids_ref[:, choice : choice + 1] == lane)
    picked = jnp.where(chosen, logits, NEGATIVE)
    expo = jnp.exp(picked - jnp.max(picked, axis=1, keepdims=True))
    gates = expo / jnp.sum(expo, axis=1, keepdims=True)
    first = lax.broadcasted_iota(jnp.int32, (rows, rows), 0)
    second = lax.broadcasted_iota(jnp.int32, (rows, rows), 1)
    place = (first == order_ref[...]).astype(BF16)
    sooner = dot_nn(place, (second < first).astype(BF16)).astype(BF16)
    sooner = dot_nt(sooner, place).astype(BF16)
    slot = dot_nn(sooner, chosen.astype(BF16))
    kept = (chosen & (slot < CAP)).astype(F32)
    gates_ref[...] = gates
    kept_ref[...] = kept
    send_ref[:, D:] = dot_nn((gates * kept).astype(BF16), relabel(spot_ref[2])).astype(BF16)


def relabel(row):
    first = lax.broadcasted_iota(jnp.int32, (LANES, LANES), 0)
    second = lax.broadcasted_iota(jnp.int32, (LANES, LANES), 1)
    return (first == (second ^ (row * 4))).astype(BF16)


def route(spots, mixed, x, pack, gain, ids, order, after=()):
    rows = x.shape[0]
    shapes = (
        jax.ShapeDtypeStruct((rows, D), F32),
        jax.ShapeDtypeStruct((rows, D + LANES), BF16),
        jax.ShapeDtypeStruct((rows, LANES), F32),
        jax.ShapeDtypeStruct((rows, LANES), F32),
        jax.ShapeDtypeStruct((D, D), BF16),
        jax.ShapeDtypeStruct((LANES, D), BF16),
    )
    return pl.pallas_call(
        behind(route_kernel, 7, after),
        out_shape=shapes,
        in_specs=[in_smem()] + [in_vmem()] * 6 + [in_hbm()] * len(after),
        out_specs=tuple(in_vmem() for _ in shapes),
        scratch_shapes=[pltpu.VMEM((LANES, D), F32)],
        compiler_params=pltpu.CompilerParams(vmem_limit_bytes=VMEM_MOST),
        cost_estimate=cost(2),
    )(spots, mixed, x, pack, gain, ids, order, *after)


def expert_kernel(x_ref, g_ref, *refs):
    weights, refs = refs[:10], refs[10:]
    back_ref, hg_ref, hu_ref, act_ref, out_acc, in_acc, gate_acc, held, sems = refs
    step = pl.program_id(0)
    count = held.shape[1]
    wide = count * LANES

    def fetch(at, slot):
        for k in range(8):

            @pl.when(at == k)
            def _():
                for i in range(2):
                    half = weights[k].at[pl.ds(2 * i, 2)] if k < 6 else weights[2 * k - 6 + i]
                    pltpu.make_async_copy(half, held.at[slot, pl.ds(2 * i, 2)], sems.at[slot, i]).start()

    @pl.when(step == 0)
    def _():
        fetch(step, 0)
        out_acc[...] = jnp.zeros_like(out_acc)
        in_acc[...] = jnp.zeros_like(in_acc)
        gate_acc[...] = jnp.zeros_like(gate_acc)

    now = lax.rem(step, 2)
    for i in range(2):
        pltpu.make_async_copy(weights[6], held.at[now, pl.ds(2 * i, 2)], sems.at[now, i]).wait()
    fetch(step + 1, 1 - now)

    join = lambda kind: jnp.concatenate([held[now, i, kind] for i in range(count)], axis=1)
    wg, wu, wd = join(0), join(1), join(2)
    x = x_ref[:, :D]
    expert = lax.broadcasted_iota(jnp.int32, (LANES, wide), 0)
    column = lax.broadcasted_iota(jnp.int32, (LANES, wide), 1)
    spread = (expert == step * count + column // LANES).astype(BF16)
    gate = dot_nn(x_ref[:, D:], spread)
    hidden_gate = dot_nn(x, wg)
    hidden_up = dot_nn(x, wu)
    act_grad = dot_nn(g_ref[...], wd)
    sigma = 0.5 * jnp.tanh(0.5 * hidden_gate) + 0.5
    swish = hidden_gate * sigma
    active = swish * hidden_up
    gate_acc[...] += dot_nt((active * act_grad).astype(BF16), spread)
    gated = (active * gate).astype(BF16)
    act_ref[...] = gated
    out_acc[...] += dot_nt(gated, wd)
    act_grad = act_grad * gate
    up_grad = (act_grad * swish).astype(BF16)
    gate_grad = (act_grad * hidden_up * (sigma + swish * (1.0 - sigma))).astype(BF16)
    hg_ref[...] = gate_grad
    hu_ref[...] = up_grad
    in_acc[...] += dot_nt(gate_grad, wg) + dot_nt(up_grad, wu)

    @pl.when(step == pl.num_programs(0) - 1)
    def _():
        back_ref[:, :D] = in_acc[...].astype(BF16)
        back_ref[:, D : 2 * D] = out_acc[...].astype(BF16)
        back_ref[:, 2 * D :] = gate_acc[...].astype(BF16)


def experts(x, g, weights, after=()):
    rows = x.shape[0]
    count = 4
    steps = 8
    wide = count * LANES
    hidden = pl.BlockSpec((rows, wide), lambda i: (0, i))
    whole = lambda width: pl.BlockSpec((rows, width), lambda i: (0, 0))
    return pl.pallas_call(
        behind(expert_kernel, 12, after),
        out_shape=(jax.ShapeDtypeStruct((rows, 2 * D + LANES), BF16),)
        + (jax.ShapeDtypeStruct((rows, steps * wide), BF16),) * 3,
        grid_spec=pltpu.PrefetchScalarGridSpec(
            num_scalar_prefetch=0,
            grid=(steps,),
            in_specs=[whole(D + LANES), whole(D)] + [in_hbm()] * (10 + len(after)),
            out_specs=(whole(2 * D + LANES), hidden, hidden, hidden),
            scratch_shapes=[
                pltpu.VMEM((rows, D), F32),
                pltpu.VMEM((rows, D), F32),
                pltpu.VMEM((rows, LANES), F32),
                pltpu.VMEM((2, count, 3, D, LANES), BF16),
                pltpu.SemaphoreType.DMA((2, 2)),
            ],
        ),
        compiler_params=pltpu.CompilerParams(vmem_limit_bytes=VMEM_MOST),
        cost_estimate=cost(21),
    )(x, g, *weights, *after)


def flip_kernel(x0, x1, x2, x3, g0, g1, g2, g3, xt_ref, gt_ref):
    rows = x0.shape[0]
    for at, (x, g) in enumerate(zip((x0, x1, x2, x3), (g0, g1, g2, g3))):
        xt_ref[:, at * rows : (at + 1) * rows] = x[:, :D].T
        gt_ref[:, at * rows : (at + 1) * rows] = g[...].T


def flip(xs, gs, after=()):
    seq = 4 * xs[0].shape[0]
    return pl.pallas_call(
        behind(flip_kernel, 8, after),
        out_shape=(jax.ShapeDtypeStruct((D, seq), BF16),) * 2,
        in_specs=[in_vmem()] * 8 + [in_hbm()] * len(after),
        out_specs=(in_vmem(),) * 2,
        compiler_params=pltpu.CompilerParams(vmem_limit_bytes=VMEM_MOST),
        cost_estimate=cost(2),
    )(*xs, *gs, *after)


def expert_wgrad_kernel(places, added, late, xt_ref, gt_ref, *refs):
    hidden, refs = refs[:12], refs[12:]
    count = len(places)
    n_extra = len({place[0] for place in added if place}) + len(late)
    plain = [k for k, place in enumerate(added) if not place]
    extras, refs = refs[:n_extra], refs[n_extra:]
    n_out = len({which for which, _ in places})
    outs, refs = refs[:n_out], refs[n_out:]
    held, out_sems, got, in_sems = refs
    step = pl.program_id(0)
    now = lax.rem(step, 2)

    def fetch(at, slot):
        for k, place in enumerate(added):
            if not place:
                continue
            which, half = place

            @pl.when(at == k)
            def _():
                pltpu.make_async_copy(extras[which].at[half], got.at[slot, 0], in_sems.at[slot, 0]).start()
                if k in late:
                    pltpu.make_async_copy(extras[late[k]].at[0], got.at[slot, 1], in_sems.at[slot, 1]).start()

    if added:

        @pl.when(step == 0)
        def _():
            fetch(step, 0)

        fetch(step + 1, 1 - now)

    def sent(slot):
        pltpu.make_async_copy(held.at[slot], outs[0].at[0], out_sems.at[slot]).wait()

    @pl.when(step >= 2)
    def _():
        sent(now)

    first = functools.reduce(jnp.logical_and, [step != k for k in plain], step >= 0)
    second = functools.reduce(jnp.logical_or, [step == k for k in late], False)
    if added:

        @pl.when(functools.reduce(jnp.logical_and, [step != k for k in plain], step >= 0))
        def _():
            pltpu.make_async_copy(extras[0].at[0], got.at[now, 0], in_sems.at[now, 0]).wait()

        for k in late:

            @pl.when(step == k)
            def _():
                pltpu.make_async_copy(extras[0].at[0], got.at[now, 1], in_sems.at[now, 1]).wait()


    for kind, left in enumerate((xt_ref, xt_ref, gt_ref)):
        joined = jnp.concatenate([part[...] for part in hidden[kind * 4 : kind * 4 + 4]], axis=0)
        product = dot_nn(left[...], joined)
        for i in range(2):
            piece = product[:, i * LANES : (i + 1) * LANES]
            if plain:
                piece = piece + jnp.where(first, got[now, 0, i, kind].astype(F32), 0.0)
            elif added:
                piece = piece + got[now, 0, i, kind].astype(F32)
            if late:
                piece = piece + jnp.where(second, got[now, 1, i, kind].astype(F32), 0.0)
            held[now, i, kind] = piece.astype(BF16)

    for k, (which, half) in enumerate(places):

        @pl.when(step == k)
        def _():
            pltpu.make_async_copy(held.at[now], outs[which].at[half], out_sems.at[now]).start()

    @pl.when(step == count - 1)
    def _():
        sent(now)
        if count > 1:
            sent(1 - now)


def expert_wgrads(flipped, hidden, entries, places, extras=(), added=(), late=None, after=(), into=None, halves=None):
    rows = hidden[0][0].shape[0]
    wide = 2 * LANES
    seq = flipped[0].shape[1]
    count = len(entries)

    def entry(i):
        place = entries[0]
        for k in range(1, count):
            place = jnp.where(i == k, entries[k], place)
        return (0, place)

    lane = pl.BlockSpec((rows, wide), entry)
    whole = pl.BlockSpec((D, seq), lambda i: (0, 0))
    kernel = functools.partial(expert_wgrad_kernel, places, added, late or {})
    if into is not None:
        after = [into, *after]
    sizes = halves or [sum(which == o for which, _ in places) for o in range(max(which for which, _ in places) + 1)]
    return pl.pallas_call(
        behind(kernel, 14 + len(extras), after),
        grid=(count,),
        out_shape=tuple(jax.ShapeDtypeStruct((size, 2, 3, D, LANES), BF16) for size in sizes),
        in_specs=[whole] * 2 + [lane] * 12 + [in_hbm()] * (len(extras) + len(after)),
        out_specs=(in_hbm(),) * len(sizes),
        scratch_shapes=[
            pltpu.VMEM((2, 2, 3, D, LANES), BF16),
            pltpu.SemaphoreType.DMA((2,)),
            pltpu.VMEM((2, 2, 2, 3, D, LANES), BF16),
            pltpu.SemaphoreType.DMA((2, 2)),
        ],
        compiler_params=pltpu.CompilerParams(vmem_limit_bytes=VMEM_MOST),
        cost_estimate=cost(2.2 * count),
        input_output_aliases={} if into is None else {14 + len(extras): 0},
    )(*flipped, *hidden[0], *hidden[1], *hidden[2], *extras, *after)


def expert_total_kernel(own_ref, xa_ref, xb_ref, ya_ref, yb_ref, gate_ref, up_ref, down_ref):
    for kind, out in enumerate((gate_ref, up_ref, down_ref)):
        for half, (x_ref, y_ref) in enumerate(((xa_ref, ya_ref), (xb_ref, yb_ref))):
            out[half, 0] = (
                own_ref[half, 0, kind].astype(F32) + x_ref[0, 0, kind].astype(F32) + y_ref[0, 0, kind].astype(F32)
            )


def expert_total(after, own, *parts):
    block = pl.BlockSpec((2, 1, 3, D, LANES), lambda i: (0, i, 0, 0, 0))
    part = pl.BlockSpec((1, 1, 3, D, LANES), lambda i: (0, i, 0, 0, 0))
    out = pl.BlockSpec((2, 1, D, LANES), lambda i: (0, i, 0, 0))
    sums = pl.pallas_call(
        behind(expert_total_kernel, 5, after),
        grid=(2,),
        out_shape=(jax.ShapeDtypeStruct((2, 2, D, LANES), F32),) * 3,
        in_specs=[block] + [part] * 4 + [in_hbm()] * len(after),
        out_specs=(out,) * 3,
        compiler_params=pltpu.CompilerParams(vmem_limit_bytes=VMEM_MOST),
        cost_estimate=cost(5),
    )(own, *parts, *after)
    return [total.reshape(4, D, LANES) for total in sums]


def halves_kernel(x_ref, y_ref, low_ref, high_ref):
    low_ref[...] = y_ref[...]
    high_ref[...] = x_ref[...]


def halves(from_x, from_y, after):
    half = jax.ShapeDtypeStruct((2, 3, D, LANES), BF16)
    first = pl.BlockSpec((1, 1, D, LANES), lambda i, j: (i, j, 0, 0))
    second = pl.BlockSpec((1, 1, D, LANES), lambda i, j: (i + 2, j, 0, 0))
    return pl.pallas_call(
        behind(halves_kernel, 2, after),
        grid=(2, 3),
        out_shape=(half, half),
        in_specs=[second, first] + [in_hbm()] * len(after),
        out_specs=(first,) * 2,
        compiler_params=pltpu.CompilerParams(vmem_limit_bytes=VMEM_MOST),
        cost_estimate=cost(3),
    )(from_x, from_y, *after)


def turn_kernel(
    spot_ref, came_ref, back_ref, gates_ref, kept_ref, resid_ref, gain_ref, g_ref, wr_ref, wo_ref, send_ref,
    out_ref, resid_grad_ref, branch_ref, mixed_grad_ref, small_ref,
):
    rows = resid_ref.shape[0]
    gates = gates_ref[...]
    both = lambda span: came_ref[:, span].astype(F32) + back_ref[:, span].astype(F32)
    out_ref[...] = resid_ref[...] + both(slice(D, 2 * D))
    gate_grad = dot_nn(both(slice(2 * D, None)).astype(BF16), relabel(spot_ref[2])) * kept_ref[...]
    logit_grad = gates * (gate_grad - jnp.sum(gates * gate_grad, axis=1, keepdims=True))
    logit_grad = logit_grad.astype(BF16)
    moe_grad = both(slice(0, D)) + dot_nn(logit_grad, wr_ref[...])
    resid = resid_ref[...]
    scale = lax.rsqrt(jnp.mean(resid * resid, axis=1, keepdims=True) + EPS)
    normed = resid * scale
    small_ref[LANES:, :] = jnp.broadcast_to(jnp.sum(moe_grad * normed, axis=0, keepdims=True), (8, D))
    small_ref[:LANES, :] = dot_tn(logit_grad, send_ref[:, :D])
    inner = moe_grad * gain_ref[1:2, :]
    grad = g_ref[...].astype(F32) + scale * (inner - normed * jnp.mean(inner * normed, axis=1, keepdims=True))
    resid_grad_ref[...] = grad
    branch = grad.astype(BF16)
    branch_ref[...] = branch
    for part in range(4):
        mixed_grad_ref[pl.ds(part * rows, rows), :] = dot_nt(
            branch, wo_ref[part * 256 : (part + 1) * 256, :]
        ).astype(BF16)


def turn(spots, came, back, gates, kept, resid, gain, g, wr, wo, send, after=()):
    rows = resid.shape[0]
    shapes = (
        jax.ShapeDtypeStruct((rows, D), F32),
        jax.ShapeDtypeStruct((rows, D), F32),
        jax.ShapeDtypeStruct((rows, D), BF16),
        jax.ShapeDtypeStruct((4 * rows, 256), BF16),
        jax.ShapeDtypeStruct((LANES + 8, D), F32),
    )
    return pl.pallas_call(
        behind(turn_kernel, 11, after),
        out_shape=shapes,
        in_specs=[in_smem()] + [in_vmem()] * 10 + [in_hbm()] * len(after),
        out_specs=tuple(in_vmem() for _ in shapes),
        compiler_params=pltpu.CompilerParams(vmem_limit_bytes=VMEM_MOST),
        cost_estimate=cost(2),
    )(spots, came, back, gates, kept, resid, gain, g, wr, wo, send, *after)


def out_wgrad_kernel(mixed_ref, branch_ref, small_ref, pack_ref):
    rows = branch_ref.shape[0]
    for part in range(4):
        product = dot_tn(mixed_ref[pl.ds(part * rows, rows), :], branch_ref[...]).astype(BF16)
        pack_ref[2 * part, :LANES, :] = product[:LANES]
        pack_ref[2 * part + 1, :LANES, :] = product[LANES:]
    for row in range(8):
        span = pl.ds(row * LANES, LANES)
        for col in range(4):
            pack_ref[row, LANES:, col * 256 : col * 256 + LANES] = small_ref[col * 8 : col * 8 + 8, span].astype(BF16)
            pack_ref[row, LANES:, col * 256 + LANES : col * 256 + 256] = small_ref[LANES:, span].astype(BF16)


def out_wgrad(mixed, branch, small, after=()):
    return pl.pallas_call(
        behind(out_wgrad_kernel, 3, after),
        out_shape=jax.ShapeDtypeStruct((8, LANES + 8, D), BF16),
        in_specs=[in_vmem()] * 3 + [in_hbm()] * len(after),
        out_specs=in_vmem(),
        compiler_params=pltpu.CompilerParams(vmem_limit_bytes=VMEM_MOST),
        cost_estimate=cost(3),
    )(mixed, branch, small, *after)


def unpack_kernel(sum_ref, query_ref, key_ref, value_ref, gain_ref):
    query_ref[...] = sum_ref[:LANES, :256].astype(F32)
    key_ref[...] = sum_ref[:LANES, 256:384].astype(F32)
    value_ref[...] = sum_ref[:LANES, 384:].astype(F32)
    gain_ref[...] = sum_ref[LANES:, :LANES].astype(F32)


def unpack(sums, after):
    return pl.pallas_call(
        behind(unpack_kernel, 1, after),
        out_shape=tuple(jax.ShapeDtypeStruct(shape, F32) for shape in ((LANES, 256), (LANES, LANES), (LANES, LANES), (8, LANES))),
        in_specs=[in_vmem()] + [in_hbm()] * len(after),
        out_specs=(in_vmem(),) * 4,
        compiler_params=pltpu.CompilerParams(vmem_limit_bytes=VMEM_MOST),
        cost_estimate=cost(2),
    )(sums, *after)


def ring_gather(value, n_col):
    steps = [(i, (i + 1) % n_col) for i in range(n_col)]
    chunks = [value]
    for _ in range(n_col - 1):
        chunks.append(lax.ppermute(chunks[-1], "col", steps))
    return chunks


def ring_sum(parts, n_col):
    steps = [(i, (i + 1) % n_col) for i in range(n_col)]
    total = parts[1]
    for part in parts[2:] + parts[:1]:
        total = lax.ppermute(total, "col", steps).astype(F32) + part.astype(F32)
        if part is not parts[0]:
            total = total.astype(BF16)
    return total


def shift_all(parts, n_col):
    return [
        lax.ppermute(part, "col", [(i, (i + s) % n_col) for i in range(n_col)]) if s else part
        for s, part in enumerate(parts)
    ]


def hold(value, *until):
    return lax.optimization_barrier((value, *until))[0]


CORE, ACROSS_X, ACROSS_Y = 1, 2, 4


def swap(value, mask):
    return lax.ppermute(value, "row", [(i, i ^ mask) for i in range(8)])


def fast(
    block_in,
    attn_gain,
    moe_gain,
    w_query,
    w_key,
    w_value,
    w_out,
    w_router,
    w_gate,
    w_up,
    w_down,
    expert_ids,
    fill_order,
    prefix_len,
    out_grad,
):
    rows = block_in.shape[0]
    n_col = lax.axis_size("col")
    col = lax.axis_index("col")
    row = lax.axis_index("row")
    seq = rows * n_col
    spots = jnp.stack([col.astype(jnp.int32), prefix_len[0], row.astype(jnp.int32)])
    gains = jnp.concatenate([attn_gain, moe_gain, jnp.zeros((256,), BF16)])[None]
    pack_qkv = jnp.concatenate(
        [jnp.concatenate([w_query, w_key, w_value], axis=1), gains, jnp.zeros((7, 512), BF16)], axis=0
    )
    pack_out = jnp.concatenate([w_out, jnp.pad(w_router.T, ((0, 0), (0, 256 - LANES)))], axis=0)
    pack_out = lax.all_gather(pack_out, "col", axis=0)
    pack_qkv = lax.all_gather(pack_qkv, "row", axis=0)
    pack_out = lax.all_gather(pack_out, "row", axis=0)
    cosine, sine = rope_tables(0, seq)
    cosine = jnp.tile(cosine, (1, 4))
    sine = jnp.concatenate([-sine, sine, -sine, sine], axis=1)
    ring = [(i, (i + 1) % n_col) for i in range(n_col)]
    x_chunks = [block_in, lax.ppermute(block_in, "col", ring)]
    x_chunks += ring_gather(hold(x_chunks[1], cosine, sine), n_col)[1:3]
    own = jnp.stack([w_gate, w_up, w_down], axis=1)
    from_x, from_y, other = swap(own, ACROSS_X), swap(own, ACROSS_Y), swap(own, CORE)

    attn_in, q, k, v, lse, w_qkv, gains, mixed_all = attend(spots, x_chunks, pack_qkv, cosine, sine, [other])
    g_chunks = [out_grad, lax.ppermute(hold(out_grad, x_chunks[3]), "col", ring)]
    g_chunks += ring_gather(hold(g_chunks[1], attn_in), n_col)[1:3]
    mixed_own = lax.all_to_all(mixed_all, "col", split_axis=0, concat_axis=0, tiled=True)
    low, high = halves(from_x, from_y, [g_chunks[2]])
    resid, send, gates, kept, wo, wr = route(
        spots, mixed_own, block_in, pack_out, gains, expert_ids, fill_order, [low]
    )
    far = swap(low, ACROSS_X), swap(high, ACROSS_Y)
    weights = [own, other, from_x, swap(from_x, CORE), from_y, swap(from_y, CORE), *far]

    send_chunks = [send, *ring_gather(hold(send, g_chunks[3]), n_col)[1:]]
    weights += [swap(hold(part, send_chunks[2]), CORE) for part in far]
    results, backs, back = {}, [], None
    steps = [(i, (i + 1) % n_col) for i in range(n_col)]
    order = (1, 2, 3, 0)
    for at, chunk in enumerate(order):
        after = [results[order[at - 1]][1]] if at else [send_chunks[3]]
        if at >= 2:
            after.append(backs[at - 2])
        if at == 2:
            flipped = flip(send_chunks, g_chunks, [results[2][1]])
            after.append(flipped[0])
        results[chunk] = experts(send_chunks[chunk], g_chunks[chunk], weights, after)
        if chunk:
            part = results[chunk][0]
            back = part if back is None else (back.astype(F32) + part.astype(F32)).astype(BF16)
            back = lax.ppermute(back, "col", steps)
            backs.append(back)
    results = [results[chunk] for chunk in range(n_col)]

    hidden = [[result[kind] for result in results] for kind in (1, 2, 3)]
    wgrads = functools.partial(expert_wgrads, flipped, hidden)
    (p7,) = wgrads((14, 15), ((0, 0), (0, 1)), after=[backs[2]])
    r7 = swap(p7, CORE)
    (p5,) = wgrads((10, 11), ((0, 2), (0, 3)), after=[p7], halves=[4])
    (p53,) = wgrads((6, 7), ((0, 0), (0, 1)), after=[r7], into=p5, halves=[4])
    r53 = swap(p53, CORE)
    q6 = wgrads((12, 13), ((0, 0), (1, 0)), [r7], ((0, 0), (0, 1)), after=[p53])
    far_x, far_y = swap(q6[0], ACROSS_X), swap(q6[1], ACROSS_Y)
    block_out, resid_grad, branch, mixed_grad, small = turn(
        spots, backs[2], results[0][0], gates, kept, resid, gains, out_grad, wr, wo, send, q6[:1]
    )
    mixed_grads = lax.all_to_all(mixed_grad, "col", split_axis=0, concat_axis=0, tiled=True)
    pack = out_wgrad(mixed_own, branch, small)
    out_sum = lax.psum_scatter(pack, "row", scatter_dimension=0, tiled=True)
    q2a, q4b, p1 = wgrads(
        (4, 9, 2, 3),
        ((0, 0), (1, 0), (2, 0), (2, 1)),
        [r53],
        ((0, 0), (0, 3), None, None),
        after=[pack, mixed_grads, far_x, far_y],
    )
    r1 = swap(p1, CORE)
    x2a, y4b = swap(q2a, ACROSS_X), swap(q4b, ACROSS_Y)
    q2b, q4a = wgrads((5, 8), ((0, 0), (1, 0)), [r53, far_y, far_x], ((0, 1), (0, 2)), {0: 1, 1: 2}, [q2a])
    x2b, y4a = swap(q2b, ACROSS_X), swap(q4a, ACROSS_Y)
    qkv_wgrad, *back_parts = attend_back(
        spots, mixed_grads, mixed_all, q, k, v, lse, attn_in, w_qkv, cosine, sine, gains, [q2b]
    )
    (q0,) = wgrads((0, 1), ((0, 0), (0, 1)), [r1], ((0, 0), (0, 1)), after=[qkv_wgrad])
    moving = lax.ppermute(back_parts[1], "col", steps)
    moving = (hold(moving, q0, x2a, y4b).astype(F32) + back_parts[2].astype(F32)).astype(BF16)
    moving = lax.ppermute(moving, "col", steps)
    moving = (moving.astype(F32) + back_parts[3].astype(F32)).astype(BF16)
    third_step = moving
    last_step = lax.ppermute(moving, "col", steps)
    attn_grad = last_step.astype(F32) + back_parts[0].astype(F32)
    x_rows = block_in.astype(F32)
    scale = lax.rsqrt(jnp.mean(x_rows * x_rows, axis=1, keepdims=True) + EPS)
    normed = x_rows * scale
    inner = attn_grad * gains[:1]
    block_in_grad = resid_grad + scale * (inner - normed * jnp.mean(inner * normed, axis=1, keepdims=True))
    gate_sum, up_sum, down_sum = expert_total([third_step], q0, x2a, x2b, y4a, y4b)

    qkv_sum = lax.psum_scatter(qkv_wgrad, "row", scatter_dimension=0, tiled=True)[0]
    *qkv_sums, gain_one = unpack(qkv_sum, [last_step])
    out_sum = lax.psum_scatter(hold(out_sum, q2b), "col", scatter_dimension=2, tiled=True)[0].astype(F32)
    gain_one_sum = functools.reduce(jnp.add, shift_all([gain_one] * n_col, n_col))[0]
    return (
        block_out,
        block_in_grad,
        gain_one_sum,
        out_sum[LANES, LANES:],
        *qkv_sums,
        out_sum[:LANES],
        out_sum[LANES:, :LANES].T,
        gate_sum,
        up_sum,
        down_sum,
    )


def takes_fast(mesh):
    n_row, n_col = mesh.shape["row"], mesh.shape["col"]
    return n_row == 8 and n_col == 4


def solution(mesh):
    in_specs = (
        P(("row", "col"), None),
        P("row"),
        P("row"),
        P("row", "col"),
        P("row", "col"),
        P("row", "col"),
        P("row", "col"),
        P("row", "col"),
        P("row", None, "col"),
        P("row", None, "col"),
        P("row", None, "col"),
        P(("row", "col"), None),
        P(("row", "col"), None),
        P("row"),
        P(("row", "col"), None),
    )
    out_specs = (
        P(("row", "col"), None),
        P(("row", "col"), None),
        P("row"),
        P("row"),
        P("row", "col"),
        P("row", "col"),
        P("row", "col"),
        P("row", "col"),
        P("row", "col"),
        P("row", None, "col"),
        P("row", None, "col"),
        P("row", None, "col"),
    )
    local = fast if takes_fast(mesh) else general
    return jax.shard_map(local, mesh=mesh, in_specs=in_specs, out_specs=out_specs, check_vma=False)
```

```python
import functools

import jax
import jax.numpy as jnp
from jax import lax
from jax.experimental import pallas as pl
from jax.experimental.pallas import tpu as pltpu
from jax.sharding import PartitionSpec as P

D = 1024
H = 16
KVH = 8
HD = 64
E = 32
TOPK = 8
CAP = 80


EPS = 1e-06
NEGATIVE = -1e30


def cross_rows(left, right):
    return lax.dot_general(
        left, right, (((0,), (0,)), ((), ())), preferred_element_type=jnp.float32
    )


def times_back(left, right):
    return lax.dot_general(
        left, right, (((1,), (1,)), ((), ())), preferred_element_type=jnp.float32
    )


def rope_tables(first_position, count):
    position = (first_position + jnp.arange(count, dtype=jnp.int32)).astype(jnp.float32)
    inverse = 10000.0 ** (-jnp.arange(HD // 2, dtype=jnp.float32) * 2.0 / HD)
    angle = position[:, None] * inverse[None, :]
    return (jnp.cos(angle), jnp.sin(angle))


def rotate(values, cosine, sine):
    half = HD // 2
    first, second = (values[..., :half], values[..., half:])
    cos_rows = cosine[:, None, :]
    sin_rows = sine[:, None, :]
    return jnp.concatenate(
        [first * cos_rows - second * sin_rows, second * cos_rows + first * sin_rows], axis=-1
    )


def rotate_back(grads, cosine, sine):
    half = HD // 2
    first, second = (grads[..., :half], grads[..., half:])
    cos_rows = cosine[:, None, :]
    sin_rows = sine[:, None, :]
    return jnp.concatenate(
        [first * cos_rows + second * sin_rows, second * cos_rows - first * sin_rows], axis=-1
    )


def norm_rows(values, gain):
    scale = lax.rsqrt(jnp.mean(values * values, axis=1, keepdims=True) + EPS)
    normed = values * scale
    return (normed, scale, (normed * gain).astype(jnp.bfloat16))


def norm_back(grad_in, normed, scale, gain):
    gain_grad = jnp.sum(grad_in * normed, axis=0)
    inner = grad_in * gain
    return (scale * (inner - normed * jnp.mean(inner * normed, axis=1, keepdims=True)), gain_grad)


def to_heads(rows, count, group):
    return rows.reshape(count, KVH, group, HD).transpose(1, 2, 0, 3).reshape(KVH, group * count, HD)


def from_heads(heads, count, group):
    return heads.reshape(KVH, group, count, HD).transpose(2, 0, 1, 3).reshape(count, H, HD)


def general(
    block_in,
    attn_gain,
    moe_gain,
    w_query,
    w_key,
    w_value,
    w_out,
    w_router,
    w_gate,
    w_up,
    w_down,
    expert_ids,
    fill_order,
    prefix_len,
    out_grad,
):
    tok_rows = block_in.shape[0]
    n_col = lax.axis_size("col")
    col_index = lax.axis_index("col")
    seq_rows = tok_rows * n_col
    group = H // KVH
    scale_attn = HD ** (-0.5)
    bf16 = jnp.bfloat16
    f32 = jnp.float32
    shared = (
        lax.all_gather(w_query, "row", axis=0, tiled=True),
        lax.all_gather(w_key, "row", axis=0, tiled=True),
        lax.all_gather(w_value, "row", axis=0, tiled=True),
        lax.all_gather(w_out, "row", axis=0, tiled=True),
        lax.all_gather(w_router, "row", axis=0, tiled=True),
        lax.all_gather(attn_gain, "row", axis=0, tiled=True),
        lax.all_gather(moe_gain, "row", axis=0, tiled=True),
    )
    wq_full, wk_full, wv_full, wo_full, wr_full = (
        lax.all_gather(shared[0], "col", axis=1, tiled=True),
        lax.all_gather(shared[1], "col", axis=1, tiled=True),
        lax.all_gather(shared[2], "col", axis=1, tiled=True),
        lax.all_gather(shared[3], "col", axis=1, tiled=True),
        lax.all_gather(shared[4], "col", axis=1, tiled=True),
    )
    gain_one = shared[5].astype(f32)
    gain_two = shared[6].astype(f32)
    x_rows = block_in.astype(f32)
    normed_one, scale_one, attn_in = norm_rows(x_rows, gain_one)
    query = jnp.dot(attn_in, wq_full, preferred_element_type=f32)
    key = jnp.dot(attn_in, wk_full, preferred_element_type=f32)
    value = jnp.dot(attn_in, wv_full, preferred_element_type=f32).astype(bf16)
    cosine, sine = rope_tables(col_index * tok_rows, tok_rows)
    query_rot = rotate(query.reshape(tok_rows, H, HD), cosine, sine).astype(bf16)
    key_rot = (
        rotate(key.reshape(tok_rows, KVH, HD), cosine, sine)
        .astype(bf16)
        .reshape(tok_rows, KVH * HD)
    )
    keys_all, values_all = (
        lax.all_gather(key_rot, "col", axis=0, tiled=True),
        lax.all_gather(value, "col", axis=0, tiled=True),
    )
    prefix = prefix_len[0]
    query_spot = col_index * tok_rows + jnp.arange(tok_rows, dtype=jnp.int32)
    key_spot = jnp.arange(seq_rows, dtype=jnp.int32)
    allowed = (key_spot[None, :] <= query_spot[:, None]) | (key_spot[None, :] < prefix)
    allowed_rows = jnp.tile(allowed, (group, 1))
    query_heads = to_heads(query_rot.reshape(tok_rows, H * HD), tok_rows, group)
    key_heads = keys_all.reshape(seq_rows, KVH, HD).transpose(1, 0, 2)
    value_heads = values_all.reshape(seq_rows, KVH, HD).transpose(1, 0, 2)

    def attend(pieces):
        queries, keys, values = pieces
        scores = times_back(queries, keys) * scale_attn
        scores = jnp.where(allowed_rows, scores, NEGATIVE)
        highest = jnp.max(scores, axis=1, keepdims=True)
        expo = jnp.exp(scores - highest)
        total = jnp.sum(expo, axis=1, keepdims=True)
        weights = (expo / total).astype(bf16)
        mixed_heads = jnp.dot(weights, values, preferred_element_type=f32).astype(bf16)
        return (mixed_heads, (highest + jnp.log(total))[:, 0])

    mixed_heads, lse_heads = lax.map(attend, (query_heads, key_heads, value_heads))
    mixed = from_heads(mixed_heads, tok_rows, group).reshape(tok_rows, H * HD)
    resid = x_rows + jnp.dot(mixed, wo_full, preferred_element_type=f32)
    normed_two, scale_two, moe_in = norm_rows(resid, gain_two)
    logits = jnp.dot(moe_in, wr_full, preferred_element_type=f32)
    choice_hot = (expert_ids[:, :, None] == jnp.arange(E, dtype=jnp.int32)).astype(f32)
    picked = jnp.sum(choice_hot * logits[:, None, :], axis=2)
    highest = jnp.max(picked, axis=1, keepdims=True)
    expo = jnp.exp(picked - highest)
    gates = expo / jnp.sum(expo, axis=1, keepdims=True)
    order = fill_order[0]
    ranked = expert_ids[order]
    onehot = (ranked.reshape(-1, 1) == jnp.arange(E, dtype=jnp.int32)).astype(jnp.int32)
    before = jnp.cumsum(onehot, axis=0) - onehot
    ranked_slot = jnp.sum(before * onehot, axis=1).reshape(tok_rows, TOPK)
    slot = jnp.zeros((tok_rows, TOPK), jnp.int32).at[order].set(ranked_slot)
    kept = slot < CAP
    dest_grid = jnp.where(kept, expert_ids * CAP + slot, E * CAP)
    pair_ids = jnp.arange(tok_rows * TOPK, dtype=jnp.int32)
    slot_pair = (
        jnp.full((E * CAP + 1,), tok_rows * TOPK, jnp.int32)
        .at[dest_grid.reshape(-1)]
        .set(pair_ids)[: E * CAP]
    )
    slot_token = slot_pair // TOPK
    gate_slot = jnp.concatenate([gates.reshape(-1), jnp.zeros((1,), f32)])[slot_pair]
    moe_pad = jnp.concatenate([moe_in, jnp.zeros((1, D), bf16)])
    dispatch = moe_pad[slot_token].reshape(E, CAP, D)
    received = lax.all_to_all(dispatch, "row", split_axis=0, concat_axis=1, tiled=True)
    gate_w, up_w, down_w = (
        lax.all_gather(w_gate, "col", axis=2, tiled=True),
        lax.all_gather(w_up, "col", axis=2, tiled=True),
        lax.all_gather(w_down, "col", axis=2, tiled=True),
    )
    hidden_gate = jnp.einsum("erd,edf->erf", received, gate_w, preferred_element_type=f32)
    hidden_up = jnp.einsum("erd,edf->erf", received, up_w, preferred_element_type=f32)
    active = (jax.nn.silu(hidden_gate) * hidden_up).astype(bf16)
    expert_out = jnp.einsum("erf,edf->erd", active, down_w, preferred_element_type=f32).astype(bf16)
    returned = lax.all_to_all(expert_out, "row", split_axis=1, concat_axis=0, tiled=True)
    out_pad = jnp.concatenate([returned.reshape(E * CAP, D), jnp.zeros((1, D), bf16)])
    pair_out = out_pad[dest_grid]
    weight_pair = gates * kept.astype(f32)
    moe_out = jnp.zeros((tok_rows, D), f32)
    for choice_index in range(TOPK):
        moe_out = moe_out + weight_pair[:, choice_index : choice_index + 1] * pair_out[
            :, choice_index
        ].astype(f32)
    block_out = resid + moe_out
    grad_out = out_grad.astype(f32)
    gate_grad = jnp.stack(
        [
            jnp.sum(pair_out[:, choice_index].astype(f32) * grad_out, axis=1)
            for choice_index in range(TOPK)
        ],
        axis=1,
    )
    grad_pad = jnp.concatenate([grad_out, jnp.zeros((1, D), f32)])
    slot_grad = (gate_slot[:, None] * grad_pad[slot_token]).astype(bf16).reshape(E, CAP, D)
    out_grads = lax.all_to_all(slot_grad, "row", split_axis=0, concat_axis=1, tiled=True)
    act_grad = jnp.einsum("erd,edf->erf", out_grads, down_w, preferred_element_type=f32)
    sigma = jax.nn.sigmoid(hidden_gate)
    gate_h_grad = (act_grad * hidden_up * sigma * (1.0 + hidden_gate * (1.0 - sigma))).astype(bf16)
    up_h_grad = (act_grad * hidden_gate * sigma).astype(bf16)
    down_wgrad = jnp.einsum("erd,erf->edf", out_grads, active, preferred_element_type=f32)
    gate_wgrad = jnp.einsum("erd,erf->edf", received, gate_h_grad, preferred_element_type=f32)
    up_wgrad = jnp.einsum("erd,erf->edf", received, up_h_grad, preferred_element_type=f32)
    in_grad = (
        jnp.einsum("erf,edf->erd", gate_h_grad, gate_w, preferred_element_type=f32)
        + jnp.einsum("erf,edf->erd", up_h_grad, up_w, preferred_element_type=f32)
    ).astype(bf16)
    back_rows = lax.all_to_all(in_grad, "row", split_axis=1, concat_axis=0, tiled=True)
    gate_sum, up_sum, down_sum = (
        lax.psum_scatter(
            gate_wgrad.astype(jnp.bfloat16), "col", scatter_dimension=2, tiled=True
        ).astype(jnp.float32),
        lax.psum_scatter(
            up_wgrad.astype(jnp.bfloat16), "col", scatter_dimension=2, tiled=True
        ).astype(jnp.float32),
        lax.psum_scatter(
            down_wgrad.astype(jnp.bfloat16), "col", scatter_dimension=2, tiled=True
        ).astype(jnp.float32),
    )
    back_pad = jnp.concatenate([back_rows.reshape(E * CAP, D), jnp.zeros((1, D), bf16)])
    pair_back = back_pad[dest_grid]
    moe_in_grad = jnp.zeros((tok_rows, D), f32)
    for choice_index in range(TOPK):
        moe_in_grad = moe_in_grad + pair_back[:, choice_index].astype(f32)
    picked_grad = gates * (gate_grad - jnp.sum(gates * gate_grad, axis=1, keepdims=True))
    logit_grad = jnp.sum(choice_hot * picked_grad[:, :, None], axis=1).astype(bf16)
    router_wgrad = cross_rows(moe_in, logit_grad)
    moe_in_grad = moe_in_grad + times_back(logit_grad, wr_full)
    norm_two_grad, gain_two_grad = norm_back(moe_in_grad, normed_two, scale_two, gain_two)
    resid_grad = grad_out + norm_two_grad
    branch_grad = resid_grad.astype(bf16)
    out_wgrad = cross_rows(mixed, branch_grad)
    mixed_grad = times_back(branch_grad, wo_full).astype(bf16)
    grad_heads = to_heads(mixed_grad, tok_rows, group)

    def query_side(pieces):
        queries, keys, values, lse_rows, grad_rows = pieces
        scores = jnp.where(allowed_rows, times_back(queries, keys) * scale_attn, NEGATIVE)
        probs = jnp.exp(scores - lse_rows[:, None])
        prob_grad = times_back(grad_rows, values)
        delta = jnp.sum(probs * prob_grad, axis=1, keepdims=True)
        score_grad = (probs * (prob_grad - delta)).astype(bf16)
        query_grad = jnp.dot(score_grad, keys, preferred_element_type=f32) * scale_attn
        return (query_grad, delta[:, 0], score_grad, probs)

    def both_sides(pieces):
        queries, keys, values, lse_rows, grad_rows = pieces
        query_grad, delta, score_grad, probs = query_side(pieces)
        key_grad = cross_rows(score_grad, queries) * scale_attn
        value_grad = cross_rows(probs.astype(bf16), grad_rows)
        return (query_grad, key_grad, value_grad)

    query_rot_grad, key_parts, value_parts = lax.map(
        both_sides, (query_heads, key_heads, value_heads, lse_heads, grad_heads)
    )
    key_rot_grad, value_grad = (
        lax.psum_scatter(
            key_parts.transpose(1, 0, 2).reshape(seq_rows, KVH * HD).astype(jnp.bfloat16),
            "col",
            scatter_dimension=0,
            tiled=True,
        ).astype(jnp.float32),
        lax.psum_scatter(
            value_parts.transpose(1, 0, 2).reshape(seq_rows, KVH * HD).astype(jnp.bfloat16),
            "col",
            scatter_dimension=0,
            tiled=True,
        ).astype(jnp.float32),
    )
    query_grad = (
        rotate_back(from_heads(query_rot_grad, tok_rows, group), cosine, sine)
        .reshape(tok_rows, H * HD)
        .astype(bf16)
    )
    key_grad = (
        rotate_back(key_rot_grad.reshape(tok_rows, KVH, HD), cosine, sine)
        .reshape(tok_rows, KVH * HD)
        .astype(bf16)
    )
    value_grad = value_grad.astype(bf16)
    query_wgrad = cross_rows(attn_in, query_grad)
    key_wgrad = cross_rows(attn_in, key_grad)
    value_wgrad = cross_rows(attn_in, value_grad)
    attn_in_grad = (
        times_back(query_grad, wq_full)
        + times_back(key_grad, wk_full)
        + times_back(value_grad, wv_full)
    )
    norm_one_grad, gain_one_grad = norm_back(attn_in_grad, normed_one, scale_one, gain_one)
    block_in_grad = resid_grad + norm_one_grad
    spread_one = jnp.broadcast_to(gain_one_grad[:, None], (D, n_col))
    spread_two = jnp.broadcast_to(gain_two_grad[:, None], (D, n_col))
    col_sums = (
        lax.psum_scatter(
            query_wgrad.astype(jnp.bfloat16), "col", scatter_dimension=1, tiled=True
        ).astype(jnp.float32),
        lax.psum_scatter(
            key_wgrad.astype(jnp.bfloat16), "col", scatter_dimension=1, tiled=True
        ).astype(jnp.float32),
        lax.psum_scatter(
            value_wgrad.astype(jnp.bfloat16), "col", scatter_dimension=1, tiled=True
        ).astype(jnp.float32),
        lax.psum_scatter(
            out_wgrad.astype(jnp.bfloat16), "col", scatter_dimension=1, tiled=True
        ).astype(jnp.float32),
        lax.psum_scatter(
            router_wgrad.astype(jnp.bfloat16), "col", scatter_dimension=1, tiled=True
        ).astype(jnp.float32),
        lax.psum_scatter(
            spread_one.astype(jnp.bfloat16), "col", scatter_dimension=1, tiled=True
        ).astype(jnp.float32),
        lax.psum_scatter(
            spread_two.astype(jnp.bfloat16), "col", scatter_dimension=1, tiled=True
        ).astype(jnp.float32),
    )
    row_sums = (
        lax.psum_scatter(
            col_sums[0].astype(jnp.bfloat16), "row", scatter_dimension=0, tiled=True
        ).astype(jnp.float32),
        lax.psum_scatter(
            col_sums[1].astype(jnp.bfloat16), "row", scatter_dimension=0, tiled=True
        ).astype(jnp.float32),
        lax.psum_scatter(
            col_sums[2].astype(jnp.bfloat16), "row", scatter_dimension=0, tiled=True
        ).astype(jnp.float32),
        lax.psum_scatter(
            col_sums[3].astype(jnp.bfloat16), "row", scatter_dimension=0, tiled=True
        ).astype(jnp.float32),
        lax.psum_scatter(
            col_sums[4].astype(jnp.bfloat16), "row", scatter_dimension=0, tiled=True
        ).astype(jnp.float32),
        lax.psum_scatter(
            col_sums[5].astype(jnp.bfloat16), "row", scatter_dimension=0, tiled=True
        ).astype(jnp.float32),
        lax.psum_scatter(
            col_sums[6].astype(jnp.bfloat16), "row", scatter_dimension=0, tiled=True
        ).astype(jnp.float32),
    )
    return (
        block_out,
        block_in_grad,
        row_sums[5][:, 0],
        row_sums[6][:, 0],
        row_sums[0],
        row_sums[1],
        row_sums[2],
        row_sums[3],
        row_sums[4],
        gate_sum,
        up_sum,
        down_sum,
    )


F32 = jnp.float32
BF16 = jnp.bfloat16
MIB = 1024 * 1024
LANES = 128
VMEM_MOST = 60 * MIB
COST_SCALE = 10**6


def cost(microseconds):
    return pl.CostEstimate(flops=int(microseconds * COST_SCALE), bytes_accessed=10**5, transcendentals=0)


def dot_nn(a, b):
    return lax.dot_general(a, b, (((1,), (0,)), ((), ())), preferred_element_type=F32)


def dot_nt(a, b):
    return lax.dot_general(a, b, (((1,), (1,)), ((), ())), preferred_element_type=F32)


def dot_tn(a, b):
    return lax.dot_general(a, b, (((0,), (0,)), ((), ())), preferred_element_type=F32)


def in_vmem():
    return pl.BlockSpec(memory_space=pltpu.VMEM)


def in_smem():
    return pl.BlockSpec(memory_space=pltpu.SMEM)


def in_hbm():
    return pl.BlockSpec(memory_space=pl.ANY)


def behind(kernel, n_in, after):
    if not after:
        return kernel
    return lambda *refs: kernel(*refs[:n_in], *refs[n_in + len(after) :])


def partner(values):
    lane = lax.broadcasted_iota(jnp.int32, values.shape, 1)
    half = HD // 2
    return jnp.where(
        lane % HD < half,
        pltpu.roll(values, LANES - half, 1),
        pltpu.roll(values, half, 1),
    )


def attend_kernel(
    spot_ref, x0, x1, x2, x3, pack_ref, cos_ref, sin_ref,
    attn_ref, q_ref, k_ref, v_ref, lse_ref, w_ref, gain_ref, mixed_ref,
):
    rows = x0.shape[0]
    col, prefix = spot_ref[0], spot_ref[1]
    for part in range(8):
        span = pl.ds(part * LANES, LANES)
        w_ref[span, :] = pack_ref[part, :LANES, :]
        gain_ref[0:1, span] = pack_ref[part, LANES : LANES + 1, :LANES].astype(F32)
        gain_ref[1:2, span] = pack_ref[part, LANES : LANES + 1, LANES : 2 * LANES].astype(F32)
    gain = gain_ref[0:1, :]
    for step, chunk in enumerate((x0, x1, x2, x3)):
        source = lax.rem(col - step + 4, 4)
        x = chunk[...].astype(F32)
        scale = lax.rsqrt(jnp.mean(x * x, axis=1, keepdims=True) + EPS)
        attn_ref[pl.ds(pl.multiple_of(source * rows, rows), rows), :] = (x * scale * gain).astype(BF16)
    for tile in range(4):
        span = pl.ds(tile * rows, rows)
        qkv = dot_nn(attn_ref[span, :], w_ref[...])
        cosine, sine = cos_ref[span, :], sin_ref[span, :]
        for block in range(3):
            v = qkv[:, block * LANES : (block + 1) * LANES]
            y = v * cosine + partner(v) * sine
            if block < 2:
                y = (y * HD ** (-0.5)).astype(BF16)
                q_ref[2 * block, span, :] = y[:, :HD]
                q_ref[2 * block + 1, span, :] = y[:, HD:]
            else:
                y = y.astype(BF16)
                k_ref[0, span, :] = y[:, :HD]
                k_ref[1, span, :] = y[:, HD:]
        v = qkv[:, 3 * LANES :].astype(BF16)
        v_ref[0, span, :] = v[:, :HD]
        v_ref[1, span, :] = v[:, HD:]
    total = 4 * rows
    for tile in range(4):
        span = pl.ds(tile * rows, rows)
        keys = max((tile + 1) * rows, total // 2)
        key_spot = lax.broadcasted_iota(jnp.int32, (rows, keys), 1)
        query_spot = lax.broadcasted_iota(jnp.int32, (rows, keys), 0) + tile * rows
        allowed = (key_spot <= query_spot) | (key_spot < prefix)
        for pair in range(2):
            k, v = k_ref[pair, pl.ds(0, keys), :], v_ref[pair, pl.ds(0, keys), :]
            outs = []
            for head in (2 * pair, 2 * pair + 1):
                scores = jnp.where(allowed, dot_nt(q_ref[head, span, :], k), NEGATIVE)
                highest = jnp.max(scores, axis=1, keepdims=True)
                expo = jnp.exp(scores - highest)
                summed = jnp.sum(expo, axis=1, keepdims=True)
                outs.append(dot_nn(expo.astype(BF16), v) * (1.0 / summed))
                lse_ref[span, head : head + 1] = highest + jnp.log(summed)
            mixed_ref[span, pair * LANES : (pair + 1) * LANES] = jnp.concatenate(outs, axis=1).astype(BF16)


def attend(spots, chunks, pack, cosine, sine, after=()):
    rows = chunks[0].shape[0]
    seq = 4 * rows
    shapes = (
        jax.ShapeDtypeStruct((seq, D), BF16),
        jax.ShapeDtypeStruct((4, seq, HD), BF16),
        jax.ShapeDtypeStruct((2, seq, HD), BF16),
        jax.ShapeDtypeStruct((2, seq, HD), BF16),
        jax.ShapeDtypeStruct((seq, 4), F32),
        jax.ShapeDtypeStruct((D, 512), BF16),
        jax.ShapeDtypeStruct((2, D), F32),
        jax.ShapeDtypeStruct((seq, 256), BF16),
    )
    return pl.pallas_call(
        behind(attend_kernel, 8, after),
        out_shape=shapes,
        in_specs=[in_smem()] + [in_vmem()] * 7 + [in_hbm()] * len(after),
        out_specs=tuple(in_vmem() for _ in shapes),
        compiler_params=pltpu.CompilerParams(vmem_limit_bytes=VMEM_MOST),
        cost_estimate=cost(10),
    )(spots, *chunks, pack, cosine, sine, *after)


def attend_back_kernel(
    spot_ref, grad_ref, mixed_ref, q_ref, k_ref, v_ref, lse_ref, attn_ref, w_ref, cos_ref, sin_ref, gain_ref,
    wgrad_ref, in0, in1, in2, in3, dqkv_ref, dk_ref, dv_ref, dq_ref, mg_ref,
):
    seq = attn_ref.shape[0]
    rows = seq // 4
    prefix = spot_ref[1]
    for tile in range(4):
        span = pl.ds(tile * rows, rows)
        for pair in range(2):
            g = grad_ref[span, pair * LANES : (pair + 1) * LANES]
            mg_ref[2 * pair, span, :] = g[:, :HD]
            mg_ref[2 * pair + 1, span, :] = g[:, HD:]
    dk_ref[...] = jnp.zeros_like(dk_ref)
    dv_ref[...] = jnp.zeros_like(dv_ref)
    for tile in range(4):
        span = pl.ds(tile * rows, rows)
        keys = max((tile + 1) * rows, seq // 2)
        key_spot = lax.broadcasted_iota(jnp.int32, (rows, keys), 1)
        query_spot = lax.broadcasted_iota(jnp.int32, (rows, keys), 0) + tile * rows
        allowed = (key_spot <= query_spot) | (key_spot < prefix)
        for pair in range(2):
            k, v = k_ref[pair, pl.ds(0, keys), :], v_ref[pair, pl.ds(0, keys), :]
            both = grad_ref[span, pair * LANES : (pair + 1) * LANES].astype(F32) * mixed_ref[
                span, pair * LANES : (pair + 1) * LANES
            ].astype(F32)
            outs = []
            for at, head in enumerate((2 * pair, 2 * pair + 1)):
                q, g = q_ref[head, span, :], mg_ref[head, span, :]
                delta = jnp.sum(both[:, at * HD : (at + 1) * HD], axis=1, keepdims=True)
                scores = jnp.where(allowed, dot_nt(q, k), NEGATIVE)
                probs = jnp.exp(scores - lse_ref[span, head : head + 1])
                score_grad = (probs * (dot_nt(g, v) - delta)).astype(BF16)
                dv_ref[pair, pl.ds(0, keys), :] += dot_tn(probs.astype(BF16), g)
                dk_ref[pair, pl.ds(0, keys), :] += dot_tn(score_grad, q)
                outs.append(dot_nn(score_grad, k) * HD ** (-0.5))
            dq_ref[span, pair * LANES : (pair + 1) * LANES] = jnp.concatenate(outs, axis=1)
    for tile in range(4):
        span = pl.ds(tile * rows, rows)
        cosine, sine = cos_ref[span, :], sin_ref[span, :]
        for block in range(3):
            if block < 2:
                g = dq_ref[span, block * LANES : (block + 1) * LANES]
            else:
                g = jnp.concatenate([dk_ref[0, span, :], dk_ref[1, span, :]], axis=1)
            dqkv_ref[span, block * LANES : (block + 1) * LANES] = (g * cosine - partner(g) * sine).astype(BF16)
        dqkv_ref[span, 3 * LANES :] = jnp.concatenate([dv_ref[0, span, :], dv_ref[1, span, :]], axis=1).astype(BF16)
    gain_total = jnp.zeros((1, D), F32)
    for step, out in enumerate((in0, in1, in2, in3)):
        source = lax.rem(spot_ref[0] - step + 4, 4)
        span = pl.ds(pl.multiple_of(source * rows, rows), rows)
        back = dot_nt(dqkv_ref[span, :], w_ref[...])
        out[...] = back.astype(BF16)
        gain_total = gain_total + jnp.sum(back * attn_ref[span, :].astype(F32), axis=0, keepdims=True)
    gain_total = gain_total / gain_ref[0:1, :]
    for part in range(8):
        span = pl.ds(part * LANES, LANES)
        wgrad_ref[part, LANES:, :LANES] = jnp.broadcast_to(gain_total[:, part * LANES : (part + 1) * LANES], (8, LANES)).astype(BF16)
        wgrad_ref[part, LANES:, LANES:] = jnp.zeros((8, 3 * LANES), BF16)
        wgrad_ref[part, :LANES, :] = dot_tn(attn_ref[:, span], dqkv_ref[...]).astype(BF16)


def attend_back(spots, grads, mixed, q, k, v, lse, attn_in, w_qkv, cosine, sine, gain, after=()):
    seq = attn_in.shape[0]
    shapes = (
        jax.ShapeDtypeStruct((8, 136, 512), BF16),
    ) + (jax.ShapeDtypeStruct((seq // 4, D), BF16),) * 4
    return pl.pallas_call(
        behind(attend_back_kernel, 12, after),
        out_shape=shapes,
        in_specs=[in_smem()] + [in_vmem()] * 11 + [in_hbm()] * len(after),
        out_specs=tuple(in_vmem() for _ in shapes),
        scratch_shapes=[
            pltpu.VMEM((seq, 512), BF16),
            pltpu.VMEM((2, seq, HD), F32),
            pltpu.VMEM((2, seq, HD), F32),
            pltpu.VMEM((seq, 256), F32),
            pltpu.VMEM((4, seq, HD), BF16),
        ],
        compiler_params=pltpu.CompilerParams(vmem_limit_bytes=VMEM_MOST),
        cost_estimate=cost(16),
    )(spots, grads, mixed, q, k, v, lse, attn_in, w_qkv, cosine, sine, gain, *after)


def route_kernel(
    spot_ref, mixed_ref, x_ref, pack_ref, gain_ref, ids_ref, order_ref,
    resid_ref, send_ref, gates_ref, kept_ref, wo_ref, wr_ref, wr_wide,
):
    rows = x_ref.shape[0]
    wr_wide[...] = jnp.zeros_like(wr_wide)
    for row in range(8):
        span = pl.ds(row * LANES, LANES)
        for col in range(4):
            wo_ref[span, col * 256 : (col + 1) * 256] = pack_ref[row, col, :LANES, :]
            wr_wide[col * 8 : (col + 1) * 8, span] = pack_ref[row, col, LANES:, :LANES].astype(F32)
    wr_ref[...] = wr_wide[...].astype(BF16)
    resid = x_ref[...].astype(F32)
    for part in range(4):
        resid = resid + dot_nn(mixed_ref[pl.ds(part * rows, rows), :], wo_ref[part * 256 : (part + 1) * 256, :])
    resid_ref[...] = resid
    scale = lax.rsqrt(jnp.mean(resid * resid, axis=1, keepdims=True) + EPS)
    moe_in = (resid * scale * gain_ref[1:2, :]).astype(BF16)
    send_ref[:, :D] = moe_in
    logits = dot_nt(moe_in, wr_ref[...])
    lane = lax.broadcasted_iota(jnp.int32, (rows, LANES), 1)
    chosen = jnp.zeros((rows, LANES), jnp.bool_)
    for choice in range(TOPK):
        chosen = chosen | (ids_ref[:, choice : choice + 1] == lane)
    picked = jnp.where(chosen, logits, NEGATIVE)
    expo = jnp.exp(picked - jnp.max(picked, axis=1, keepdims=True))
    gates = expo / jnp.sum(expo, axis=1, keepdims=True)
    first = lax.broadcasted_iota(jnp.int32, (rows, rows), 0)
    second = lax.broadcasted_iota(jnp.int32, (rows, rows), 1)
    place = (first == order_ref[...]).astype(BF16)
    sooner = dot_nn(place, (second < first).astype(BF16)).astype(BF16)
    sooner = dot_nt(sooner, place).astype(BF16)
    slot = dot_nn(sooner, chosen.astype(BF16))
    kept = (chosen & (slot < CAP)).astype(F32)
    gates_ref[...] = gates
    kept_ref[...] = kept
    send_ref[:, D:] = dot_nn((gates * kept).astype(BF16), relabel(spot_ref[2])).astype(BF16)


def relabel(row):
    first = lax.broadcasted_iota(jnp.int32, (LANES, LANES), 0)
    second = lax.broadcasted_iota(jnp.int32, (LANES, LANES), 1)
    return (first == (second ^ (row * 4))).astype(BF16)


def route(spots, mixed, x, pack, gain, ids, order, after=()):
    rows = x.shape[0]
    shapes = (
        jax.ShapeDtypeStruct((rows, D), F32),
        jax.ShapeDtypeStruct((rows, D + LANES), BF16),
        jax.ShapeDtypeStruct((rows, LANES), F32),
        jax.ShapeDtypeStruct((rows, LANES), F32),
        jax.ShapeDtypeStruct((D, D), BF16),
        jax.ShapeDtypeStruct((LANES, D), BF16),
    )
    return pl.pallas_call(
        behind(route_kernel, 7, after),
        out_shape=shapes,
        in_specs=[in_smem()] + [in_vmem()] * 6 + [in_hbm()] * len(after),
        out_specs=tuple(in_vmem() for _ in shapes),
        scratch_shapes=[pltpu.VMEM((LANES, D), F32)],
        compiler_params=pltpu.CompilerParams(vmem_limit_bytes=VMEM_MOST),
        cost_estimate=cost(2),
    )(spots, mixed, x, pack, gain, ids, order, *after)


def expert_kernel(x_ref, g_ref, *refs):
    weights, refs = refs[:10], refs[10:]
    back_ref, hg_ref, hu_ref, act_ref, out_acc, in_acc, gate_acc, held, sems = refs
    step = pl.program_id(0)
    count = held.shape[1]
    wide = count * LANES

    def fetch(at, slot):
        for k in range(8):

            @pl.when(at == k)
            def _():
                for i in range(2):
                    half = weights[k].at[pl.ds(2 * i, 2)] if k < 6 else weights[2 * k - 6 + i]
                    pltpu.make_async_copy(half, held.at[slot, pl.ds(2 * i, 2)], sems.at[slot, i]).start()

    @pl.when(step == 0)
    def _():
        fetch(step, 0)
        out_acc[...] = jnp.zeros_like(out_acc)
        in_acc[...] = jnp.zeros_like(in_acc)
        gate_acc[...] = jnp.zeros_like(gate_acc)

    now = lax.rem(step, 2)
    for i in range(2):
        pltpu.make_async_copy(weights[6], held.at[now, pl.ds(2 * i, 2)], sems.at[now, i]).wait()
    fetch(step + 1, 1 - now)

    join = lambda kind: jnp.concatenate([held[now, i, kind] for i in range(count)], axis=1)
    wg, wu, wd = join(0), join(1), join(2)
    x = x_ref[:, :D]
    expert = lax.broadcasted_iota(jnp.int32, (LANES, wide), 0)
    column = lax.broadcasted_iota(jnp.int32, (LANES, wide), 1)
    spread = (expert == step * count + column // LANES).astype(BF16)
    gate = dot_nn(x_ref[:, D:], spread)
    hidden_gate = dot_nn(x, wg)
    hidden_up = dot_nn(x, wu)
    act_grad = dot_nn(g_ref[...], wd)
    sigma = 0.5 * jnp.tanh(0.5 * hidden_gate) + 0.5
    swish = hidden_gate * sigma
    active = swish * hidden_up
    gate_acc[...] += dot_nt((active * act_grad).astype(BF16), spread)
    gated = (active * gate).astype(BF16)
    act_ref[...] = gated
    out_acc[...] += dot_nt(gated, wd)
    act_grad = act_grad * gate
    up_grad = (act_grad * swish).astype(BF16)
    gate_grad = (act_grad * hidden_up * (sigma + swish * (1.0 - sigma))).astype(BF16)
    hg_ref[...] = gate_grad
    hu_ref[...] = up_grad
    in_acc[...] += dot_nt(gate_grad, wg) + dot_nt(up_grad, wu)

    @pl.when(step == pl.num_programs(0) - 1)
    def _():
        back_ref[:, :D] = in_acc[...].astype(BF16)
        back_ref[:, D : 2 * D] = out_acc[...].astype(BF16)
        back_ref[:, 2 * D :] = gate_acc[...].astype(BF16)


def experts(x, g, weights, after=()):
    rows = x.shape[0]
    count = 4
    steps = 8
    wide = count * LANES
    hidden = pl.BlockSpec((rows, wide), lambda i: (0, i))
    whole = lambda width: pl.BlockSpec((rows, width), lambda i: (0, 0))
    return pl.pallas_call(
        behind(expert_kernel, 12, after),
        out_shape=(jax.ShapeDtypeStruct((rows, 2 * D + LANES), BF16),)
        + (jax.ShapeDtypeStruct((rows, steps * wide), BF16),) * 3,
        grid_spec=pltpu.PrefetchScalarGridSpec(
            num_scalar_prefetch=0,
            grid=(steps,),
            in_specs=[whole(D + LANES), whole(D)] + [in_hbm()] * (10 + len(after)),
            out_specs=(whole(2 * D + LANES), hidden, hidden, hidden),
            scratch_shapes=[
                pltpu.VMEM((rows, D), F32),
                pltpu.VMEM((rows, D), F32),
                pltpu.VMEM((rows, LANES), F32),
                pltpu.VMEM((2, count, 3, D, LANES), BF16),
                pltpu.SemaphoreType.DMA((2, 2)),
            ],
        ),
        compiler_params=pltpu.CompilerParams(vmem_limit_bytes=VMEM_MOST),
        cost_estimate=cost(21),
    )(x, g, *weights, *after)


def flip_kernel(x0, x1, x2, x3, g0, g1, g2, g3, xt_ref, gt_ref):
    rows = x0.shape[0]
    for at, (x, g) in enumerate(zip((x0, x1, x2, x3), (g0, g1, g2, g3))):
        xt_ref[:, at * rows : (at + 1) * rows] = x[:, :D].T
        gt_ref[:, at * rows : (at + 1) * rows] = g[...].T


def flip(xs, gs, after=()):
    seq = 4 * xs[0].shape[0]
    return pl.pallas_call(
        behind(flip_kernel, 8, after),
        out_shape=(jax.ShapeDtypeStruct((D, seq), BF16),) * 2,
        in_specs=[in_vmem()] * 8 + [in_hbm()] * len(after),
        out_specs=(in_vmem(),) * 2,
        compiler_params=pltpu.CompilerParams(vmem_limit_bytes=VMEM_MOST),
        cost_estimate=cost(2),
    )(*xs, *gs, *after)


def expert_wgrad_kernel(places, added, late, xt_ref, gt_ref, *refs):
    hidden, refs = refs[:12], refs[12:]
    count = len(places)
    n_extra = len({place[0] for place in added if place}) + len(late)
    plain = [k for k, place in enumerate(added) if not place]
    extras, refs = refs[:n_extra], refs[n_extra:]
    n_out = len({which for which, _ in places})
    outs, refs = refs[:n_out], refs[n_out:]
    held, out_sems, got, in_sems = refs
    step = pl.program_id(0)
    now = lax.rem(step, 2)

    def fetch(at, slot):
        for k, place in enumerate(added):
            if not place:
                continue
            which, half = place

            @pl.when(at == k)
            def _():
                pltpu.make_async_copy(extras[which].at[half], got.at[slot, 0], in_sems.at[slot, 0]).start()
                if k in late:
                    pltpu.make_async_copy(extras[late[k]].at[0], got.at[slot, 1], in_sems.at[slot, 1]).start()

    if added:

        @pl.when(step == 0)
        def _():
            fetch(step, 0)

        fetch(step + 1, 1 - now)

    def sent(slot):
        pltpu.make_async_copy(held.at[slot], outs[0].at[0], out_sems.at[slot]).wait()

    @pl.when(step >= 2)
    def _():
        sent(now)

    first = functools.reduce(jnp.logical_and, [step != k for k in plain], step >= 0)
    second = functools.reduce(jnp.logical_or, [step == k for k in late], False)
    if added:

        @pl.when(functools.reduce(jnp.logical_and, [step != k for k in plain], step >= 0))
        def _():
            pltpu.make_async_copy(extras[0].at[0], got.at[now, 0], in_sems.at[now, 0]).wait()

        for k in late:

            @pl.when(step == k)
            def _():
                pltpu.make_async_copy(extras[0].at[0], got.at[now, 1], in_sems.at[now, 1]).wait()


    for kind, left in enumerate((xt_ref, xt_ref, gt_ref)):
        joined = jnp.concatenate([part[...] for part in hidden[kind * 4 : kind * 4 + 4]], axis=0)
        product = dot_nn(left[...], joined)
        for i in range(2):
            piece = product[:, i * LANES : (i + 1) * LANES]
            if plain:
                piece = piece + jnp.where(first, got[now, 0, i, kind].astype(F32), 0.0)
            elif added:
                piece = piece + got[now, 0, i, kind].astype(F32)
            if late:
                piece = piece + jnp.where(second, got[now, 1, i, kind].astype(F32), 0.0)
            held[now, i, kind] = piece.astype(BF16)

    for k, (which, half) in enumerate(places):

        @pl.when(step == k)
        def _():
            pltpu.make_async_copy(held.at[now], outs[which].at[half], out_sems.at[now]).start()

    @pl.when(step == count - 1)
    def _():
        sent(now)
        if count > 1:
            sent(1 - now)


def expert_wgrads(flipped, hidden, entries, places, extras=(), added=(), late=None, after=(), into=None, halves=None):
    rows = hidden[0][0].shape[0]
    wide = 2 * LANES
    seq = flipped[0].shape[1]
    count = len(entries)

    def entry(i):
        place = entries[0]
        for k in range(1, count):
            place = jnp.where(i == k, entries[k], place)
        return (0, place)

    lane = pl.BlockSpec((rows, wide), entry)
    whole = pl.BlockSpec((D, seq), lambda i: (0, 0))
    kernel = functools.partial(expert_wgrad_kernel, places, added, late or {})
    if into is not None:
        after = [into, *after]
    sizes = halves or [sum(which == o for which, _ in places) for o in range(max(which for which, _ in places) + 1)]
    return pl.pallas_call(
        behind(kernel, 14 + len(extras), after),
        grid=(count,),
        out_shape=tuple(jax.ShapeDtypeStruct((size, 2, 3, D, LANES), BF16) for size in sizes),
        in_specs=[whole] * 2 + [lane] * 12 + [in_hbm()] * (len(extras) + len(after)),
        out_specs=(in_hbm(),) * len(sizes),
        scratch_shapes=[
            pltpu.VMEM((2, 2, 3, D, LANES), BF16),
            pltpu.SemaphoreType.DMA((2,)),
            pltpu.VMEM((2, 2, 2, 3, D, LANES), BF16),
            pltpu.SemaphoreType.DMA((2, 2)),
        ],
        compiler_params=pltpu.CompilerParams(vmem_limit_bytes=VMEM_MOST),
        cost_estimate=cost(2.2 * count),
        input_output_aliases={} if into is None else {14 + len(extras): 0},
    )(*flipped, *hidden[0], *hidden[1], *hidden[2], *extras, *after)


def expert_total_kernel(own_ref, xa_ref, xb_ref, ya_ref, yb_ref, gate_ref, up_ref, down_ref):
    for kind, out in enumerate((gate_ref, up_ref, down_ref)):
        for half, (x_ref, y_ref) in enumerate(((xa_ref, ya_ref), (xb_ref, yb_ref))):
            out[half, 0] = (
                own_ref[half, 0, kind].astype(F32) + x_ref[0, 0, kind].astype(F32) + y_ref[0, 0, kind].astype(F32)
            )


def expert_total(after, own, *parts):
    block = pl.BlockSpec((2, 1, 3, D, LANES), lambda i: (0, i, 0, 0, 0))
    part = pl.BlockSpec((1, 1, 3, D, LANES), lambda i: (0, i, 0, 0, 0))
    out = pl.BlockSpec((2, 1, D, LANES), lambda i: (0, i, 0, 0))
    sums = pl.pallas_call(
        behind(expert_total_kernel, 5, after),
        grid=(2,),
        out_shape=(jax.ShapeDtypeStruct((2, 2, D, LANES), F32),) * 3,
        in_specs=[block] + [part] * 4 + [in_hbm()] * len(after),
        out_specs=(out,) * 3,
        compiler_params=pltpu.CompilerParams(vmem_limit_bytes=VMEM_MOST),
        cost_estimate=cost(5),
    )(own, *parts, *after)
    return [total.reshape(4, D, LANES) for total in sums]


def halves_kernel(x_ref, y_ref, low_ref, high_ref):
    low_ref[...] = y_ref[...]
    high_ref[...] = x_ref[...]


def halves(from_x, from_y, after):
    half = jax.ShapeDtypeStruct((2, 3, D, LANES), BF16)
    first = pl.BlockSpec((1, 1, D, LANES), lambda i, j: (i, j, 0, 0))
    second = pl.BlockSpec((1, 1, D, LANES), lambda i, j: (i + 2, j, 0, 0))
    return pl.pallas_call(
        behind(halves_kernel, 2, after),
        grid=(2, 3),
        out_shape=(half, half),
        in_specs=[second, first] + [in_hbm()] * len(after),
        out_specs=(first,) * 2,
        compiler_params=pltpu.CompilerParams(vmem_limit_bytes=VMEM_MOST),
        cost_estimate=cost(3),
    )(from_x, from_y, *after)


def turn_kernel(
    spot_ref, came_ref, back_ref, gates_ref, kept_ref, resid_ref, gain_ref, g_ref, wr_ref, wo_ref, send_ref,
    out_ref, resid_grad_ref, branch_ref, mixed_grad_ref, small_ref,
):
    rows = resid_ref.shape[0]
    gates = gates_ref[...]
    both = lambda span: came_ref[:, span].astype(F32) + back_ref[:, span].astype(F32)
    out_ref[...] = resid_ref[...] + both(slice(D, 2 * D))
    gate_grad = dot_nn(both(slice(2 * D, None)).astype(BF16), relabel(spot_ref[2])) * kept_ref[...]
    logit_grad = gates * (gate_grad - jnp.sum(gates * gate_grad, axis=1, keepdims=True))
    logit_grad = logit_grad.astype(BF16)
    moe_grad = both(slice(0, D)) + dot_nn(logit_grad, wr_ref[...])
    resid = resid_ref[...]
    scale = lax.rsqrt(jnp.mean(resid * resid, axis=1, keepdims=True) + EPS)
    normed = resid * scale
    small_ref[LANES:, :] = jnp.broadcast_to(jnp.sum(moe_grad * normed, axis=0, keepdims=True), (8, D))
    small_ref[:LANES, :] = dot_tn(logit_grad, send_ref[:, :D])
    inner = moe_grad * gain_ref[1:2, :]
    grad = g_ref[...].astype(F32) + scale * (inner - normed * jnp.mean(inner * normed, axis=1, keepdims=True))
    resid_grad_ref[...] = grad
    branch = grad.astype(BF16)
    branch_ref[...] = branch
    for part in range(4):
        mixed_grad_ref[pl.ds(part * rows, rows), :] = dot_nt(
            branch, wo_ref[part * 256 : (part + 1) * 256, :]
        ).astype(BF16)


def turn(spots, came, back, gates, kept, resid, gain, g, wr, wo, send, after=()):
    rows = resid.shape[0]
    shapes = (
        jax.ShapeDtypeStruct((rows, D), F32),
        jax.ShapeDtypeStruct((rows, D), F32),
        jax.ShapeDtypeStruct((rows, D), BF16),
        jax.ShapeDtypeStruct((4 * rows, 256), BF16),
        jax.ShapeDtypeStruct((LANES + 8, D), F32),
    )
    return pl.pallas_call(
        behind(turn_kernel, 11, after),
        out_shape=shapes,
        in_specs=[in_smem()] + [in_vmem()] * 10 + [in_hbm()] * len(after),
        out_specs=tuple(in_vmem() for _ in shapes),
        compiler_params=pltpu.CompilerParams(vmem_limit_bytes=VMEM_MOST),
        cost_estimate=cost(2),
    )(spots, came, back, gates, kept, resid, gain, g, wr, wo, send, *after)


def out_wgrad_kernel(mixed_ref, branch_ref, small_ref, pack_ref):
    rows = branch_ref.shape[0]
    for part in range(4):
        product = dot_tn(mixed_ref[pl.ds(part * rows, rows), :], branch_ref[...]).astype(BF16)
        pack_ref[2 * part, :LANES, :] = product[:LANES]
        pack_ref[2 * part + 1, :LANES, :] = product[LANES:]
    for row in range(8):
        span = pl.ds(row * LANES, LANES)
        for col in range(4):
            pack_ref[row, LANES:, col * 256 : col * 256 + LANES] = small_ref[col * 8 : col * 8 + 8, span].astype(BF16)
            pack_ref[row, LANES:, col * 256 + LANES : col * 256 + 256] = small_ref[LANES:, span].astype(BF16)


def out_wgrad(mixed, branch, small, after=()):
    return pl.pallas_call(
        behind(out_wgrad_kernel, 3, after),
        out_shape=jax.ShapeDtypeStruct((8, LANES + 8, D), BF16),
        in_specs=[in_vmem()] * 3 + [in_hbm()] * len(after),
        out_specs=in_vmem(),
        compiler_params=pltpu.CompilerParams(vmem_limit_bytes=VMEM_MOST),
        cost_estimate=cost(3),
    )(mixed, branch, small, *after)


def unpack_kernel(sum_ref, query_ref, key_ref, value_ref, gain_ref):
    query_ref[...] = sum_ref[:LANES, :256].astype(F32)
    key_ref[...] = sum_ref[:LANES, 256:384].astype(F32)
    value_ref[...] = sum_ref[:LANES, 384:].astype(F32)
    gain_ref[...] = sum_ref[LANES:, :LANES].astype(F32)


def unpack(sums, after):
    return pl.pallas_call(
        behind(unpack_kernel, 1, after),
        out_shape=tuple(jax.ShapeDtypeStruct(shape, F32) for shape in ((LANES, 256), (LANES, LANES), (LANES, LANES), (8, LANES))),
        in_specs=[in_vmem()] + [in_hbm()] * len(after),
        out_specs=(in_vmem(),) * 4,
        compiler_params=pltpu.CompilerParams(vmem_limit_bytes=VMEM_MOST),
        cost_estimate=cost(2),
    )(sums, *after)


def ring_gather(value, n_col):
    steps = [(i, (i + 1) % n_col) for i in range(n_col)]
    chunks = [value]
    for _ in range(n_col - 1):
        chunks.append(lax.ppermute(chunks[-1], "col", steps))
    return chunks


def ring_sum(parts, n_col):
    steps = [(i, (i + 1) % n_col) for i in range(n_col)]
    total = parts[1]
    for part in parts[2:] + parts[:1]:
        total = lax.ppermute(total, "col", steps).astype(F32) + part.astype(F32)
        if part is not parts[0]:
            total = total.astype(BF16)
    return total


def shift_all(parts, n_col):
    return [
        lax.ppermute(part, "col", [(i, (i + s) % n_col) for i in range(n_col)]) if s else part
        for s, part in enumerate(parts)
    ]


def hold(value, *until):
    return lax.optimization_barrier((value, *until))[0]


CORE, ACROSS_X, ACROSS_Y = 1, 2, 4


def swap(value, mask):
    return lax.ppermute(value, "row", [(i, i ^ mask) for i in range(8)])


def fast(
    block_in,
    attn_gain,
    moe_gain,
    w_query,
    w_key,
    w_value,
    w_out,
    w_router,
    w_gate,
    w_up,
    w_down,
    expert_ids,
    fill_order,
    prefix_len,
    out_grad,
):
    rows = block_in.shape[0]
    n_col = lax.axis_size("col")
    col = lax.axis_index("col")
    row = lax.axis_index("row")
    seq = rows * n_col
    spots = jnp.stack([col.astype(jnp.int32), prefix_len[0], row.astype(jnp.int32)])
    gains = jnp.concatenate([attn_gain, moe_gain, jnp.zeros((256,), BF16)])[None]
    pack_qkv = jnp.concatenate(
        [jnp.concatenate([w_query, w_key, w_value], axis=1), gains, jnp.zeros((7, 512), BF16)], axis=0
    )
    pack_out = jnp.concatenate([w_out, jnp.pad(w_router.T, ((0, 0), (0, 256 - LANES)))], axis=0)
    pack_out = lax.all_gather(pack_out, "col", axis=0)
    pack_qkv = lax.all_gather(pack_qkv, "row", axis=0)
    pack_out = lax.all_gather(pack_out, "row", axis=0)
    cosine, sine = rope_tables(0, seq)
    cosine = jnp.tile(cosine, (1, 4))
    sine = jnp.concatenate([-sine, sine, -sine, sine], axis=1)
    ring = [(i, (i + 1) % n_col) for i in range(n_col)]
    x_chunks = [block_in, lax.ppermute(block_in, "col", ring)]
    x_chunks += ring_gather(hold(x_chunks[1], cosine, sine), n_col)[1:3]
    own = jnp.stack([w_gate, w_up, w_down], axis=1)
    from_x, from_y, other = swap(own, ACROSS_X), swap(own, ACROSS_Y), swap(own, CORE)

    attn_in, q, k, v, lse, w_qkv, gains, mixed_all = attend(spots, x_chunks, pack_qkv, cosine, sine, [other])
    g_chunks = [out_grad, lax.ppermute(hold(out_grad, x_chunks[3]), "col", ring)]
    g_chunks += ring_gather(hold(g_chunks[1], attn_in), n_col)[1:3]
    mixed_own = lax.all_to_all(mixed_all, "col", split_axis=0, concat_axis=0, tiled=True)
    low, high = halves(from_x, from_y, [g_chunks[2]])
    resid, send, gates, kept, wo, wr = route(
        spots, mixed_own, block_in, pack_out, gains, expert_ids, fill_order, [low]
    )
    far = swap(low, ACROSS_X), swap(high, ACROSS_Y)
    weights = [own, other, from_x, swap(from_x, CORE), from_y, swap(from_y, CORE), *far]

    send_chunks = [send, *ring_gather(hold(send, g_chunks[3]), n_col)[1:]]
    weights += [swap(hold(part, send_chunks[2]), CORE) for part in far]
    results, backs, back = {}, [], None
    steps = [(i, (i + 1) % n_col) for i in range(n_col)]
    order = (1, 2, 3, 0)
    for at, chunk in enumerate(order):
        after = [results[order[at - 1]][1]] if at else [send_chunks[3]]
        if at >= 2:
            after.append(backs[at - 2])
        if at == 2:
            flipped = flip(send_chunks, g_chunks, [results[2][1]])
            after.append(flipped[0])
        results[chunk] = experts(send_chunks[chunk], g_chunks[chunk], weights, after)
        if chunk:
            part = results[chunk][0]
            back = part if back is None else (back.astype(F32) + part.astype(F32)).astype(BF16)
            back = lax.ppermute(back, "col", steps)
            backs.append(back)
    results = [results[chunk] for chunk in range(n_col)]

    hidden = [[result[kind] for result in results] for kind in (1, 2, 3)]
    wgrads = functools.partial(expert_wgrads, flipped, hidden)
    (p7,) = wgrads((14, 15), ((0, 0), (0, 1)), after=[backs[2]])
    r7 = swap(p7, CORE)
    (p5,) = wgrads((10, 11), ((0, 2), (0, 3)), after=[p7], halves=[4])
    (p53,) = wgrads((6, 7), ((0, 0), (0, 1)), after=[r7], into=p5, halves=[4])
    r53 = swap(p53, CORE)
    q6 = wgrads((12, 13), ((0, 0), (1, 0)), [r7], ((0, 0), (0, 1)), after=[p53])
    far_x, far_y = swap(q6[0], ACROSS_X), swap(q6[1], ACROSS_Y)
    block_out, resid_grad, branch, mixed_grad, small = turn(
        spots, backs[2], results[0][0], gates, kept, resid, gains, out_grad, wr, wo, send, q6[:1]
    )
    mixed_grads = lax.all_to_all(mixed_grad, "col", split_axis=0, concat_axis=0, tiled=True)
    pack = out_wgrad(mixed_own, branch, small)
    out_sum = lax.psum_scatter(pack, "row", scatter_dimension=0, tiled=True)
    q2a, q4b, q2b, q4a, p1 = wgrads(
        (4, 9, 5, 8, 2, 3),
        ((0, 0), (1, 0), (2, 0), (3, 0), (4, 0), (4, 1)),
        [r53, far_y, far_x],
        ((0, 0), (0, 3), (0, 1), (0, 2), None, None),
        {2: 1, 3: 2},
        [pack, mixed_grads],
    )
    x2a, y4b = swap(q2a, ACROSS_X), swap(q4b, ACROSS_Y)
    r1 = swap(p1, CORE)
    x2b, y4a = swap(q2b, ACROSS_X), swap(q4a, ACROSS_Y)
    qkv_wgrad, *back_parts = attend_back(
        spots, mixed_grads, mixed_all, q, k, v, lse, attn_in, w_qkv, cosine, sine, gains, [q2b]
    )
    (q0,) = wgrads((0, 1), ((0, 0), (0, 1)), [r1], ((0, 0), (0, 1)), after=[qkv_wgrad])
    moving = lax.ppermute(back_parts[1], "col", steps)
    moving = (hold(moving, q0, x2a, y4b).astype(F32) + back_parts[2].astype(F32)).astype(BF16)
    moving = lax.ppermute(moving, "col", steps)
    moving = (moving.astype(F32) + back_parts[3].astype(F32)).astype(BF16)
    third_step = moving
    last_step = lax.ppermute(moving, "col", steps)
    attn_grad = last_step.astype(F32) + back_parts[0].astype(F32)
    x_rows = block_in.astype(F32)
    scale = lax.rsqrt(jnp.mean(x_rows * x_rows, axis=1, keepdims=True) + EPS)
    normed = x_rows * scale
    inner = attn_grad * gains[:1]
    block_in_grad = resid_grad + scale * (inner - normed * jnp.mean(inner * normed, axis=1, keepdims=True))
    gate_sum, up_sum, down_sum = expert_total([third_step], q0, x2a, x2b, y4a, y4b)

    qkv_sum = lax.psum_scatter(qkv_wgrad, "row", scatter_dimension=0, tiled=True)[0]
    *qkv_sums, gain_one = unpack(qkv_sum, [last_step])
    out_sum = lax.psum_scatter(hold(out_sum, q2b), "col", scatter_dimension=2, tiled=True)[0].astype(F32)
    gain_one_sum = functools.reduce(jnp.add, shift_all([gain_one] * n_col, n_col))[0]
    return (
        block_out,
        block_in_grad,
        gain_one_sum,
        out_sum[LANES, LANES:],
        *qkv_sums,
        out_sum[:LANES],
        out_sum[LANES:, :LANES].T,
        gate_sum,
        up_sum,
        down_sum,
    )


def takes_fast(mesh):
    n_row, n_col = mesh.shape["row"], mesh.shape["col"]
    return n_row == 8 and n_col == 4


def solution(mesh):
    in_specs = (
        P(("row", "col"), None),
        P("row"),
        P("row"),
        P("row", "col"),
        P("row", "col"),
        P("row", "col"),
        P("row", "col"),
        P("row", "col"),
        P("row", None, "col"),
        P("row", None, "col"),
        P("row", None, "col"),
        P(("row", "col"), None),
        P(("row", "col"), None),
        P("row"),
        P(("row", "col"), None),
    )
    out_specs = (
        P(("row", "col"), None),
        P(("row", "col"), None),
        P("row"),
        P("row"),
        P("row", "col"),
        P("row", "col"),
        P("row", "col"),
        P("row", "col"),
        P("row", "col"),
        P("row", None, "col"),
        P("row", None, "col"),
        P("row", None, "col"),
    )
    local = fast if takes_fast(mesh) else general
    return jax.shard_map(local, mesh=mesh, in_specs=in_specs, out_specs=out_specs, check_vma=False)
```

```python
import functools

import jax
import jax.numpy as jnp
from jax import lax
from jax.experimental import pallas as pl
from jax.experimental.pallas import tpu as pltpu
from jax.sharding import PartitionSpec as P

D = 1024
H = 16
KVH = 8
HD = 64
E = 32
TOPK = 8
CAP = 80


EPS = 1e-06
NEGATIVE = -1e30


def cross_rows(left, right):
    return lax.dot_general(
        left, right, (((0,), (0,)), ((), ())), preferred_element_type=jnp.float32
    )


def times_back(left, right):
    return lax.dot_general(
        left, right, (((1,), (1,)), ((), ())), preferred_element_type=jnp.float32
    )


def rope_tables(first_position, count):
    position = (first_position + jnp.arange(count, dtype=jnp.int32)).astype(jnp.float32)
    inverse = 10000.0 ** (-jnp.arange(HD // 2, dtype=jnp.float32) * 2.0 / HD)
    angle = position[:, None] * inverse[None, :]
    return (jnp.cos(angle), jnp.sin(angle))


def rotate(values, cosine, sine):
    half = HD // 2
    first, second = (values[..., :half], values[..., half:])
    cos_rows = cosine[:, None, :]
    sin_rows = sine[:, None, :]
    return jnp.concatenate(
        [first * cos_rows - second * sin_rows, second * cos_rows + first * sin_rows], axis=-1
    )


def rotate_back(grads, cosine, sine):
    half = HD // 2
    first, second = (grads[..., :half], grads[..., half:])
    cos_rows = cosine[:, None, :]
    sin_rows = sine[:, None, :]
    return jnp.concatenate(
        [first * cos_rows + second * sin_rows, second * cos_rows - first * sin_rows], axis=-1
    )


def norm_rows(values, gain):
    scale = lax.rsqrt(jnp.mean(values * values, axis=1, keepdims=True) + EPS)
    normed = values * scale
    return (normed, scale, (normed * gain).astype(jnp.bfloat16))


def norm_back(grad_in, normed, scale, gain):
    gain_grad = jnp.sum(grad_in * normed, axis=0)
    inner = grad_in * gain
    return (scale * (inner - normed * jnp.mean(inner * normed, axis=1, keepdims=True)), gain_grad)


def to_heads(rows, count, group):
    return rows.reshape(count, KVH, group, HD).transpose(1, 2, 0, 3).reshape(KVH, group * count, HD)


def from_heads(heads, count, group):
    return heads.reshape(KVH, group, count, HD).transpose(2, 0, 1, 3).reshape(count, H, HD)


def general(
    block_in,
    attn_gain,
    moe_gain,
    w_query,
    w_key,
    w_value,
    w_out,
    w_router,
    w_gate,
    w_up,
    w_down,
    expert_ids,
    fill_order,
    prefix_len,
    out_grad,
):
    tok_rows = block_in.shape[0]
    n_col = lax.axis_size("col")
    col_index = lax.axis_index("col")
    seq_rows = tok_rows * n_col
    group = H // KVH
    scale_attn = HD ** (-0.5)
    bf16 = jnp.bfloat16
    f32 = jnp.float32
    shared = (
        lax.all_gather(w_query, "row", axis=0, tiled=True),
        lax.all_gather(w_key, "row", axis=0, tiled=True),
        lax.all_gather(w_value, "row", axis=0, tiled=True),
        lax.all_gather(w_out, "row", axis=0, tiled=True),
        lax.all_gather(w_router, "row", axis=0, tiled=True),
        lax.all_gather(attn_gain, "row", axis=0, tiled=True),
        lax.all_gather(moe_gain, "row", axis=0, tiled=True),
    )
    wq_full, wk_full, wv_full, wo_full, wr_full = (
        lax.all_gather(shared[0], "col", axis=1, tiled=True),
        lax.all_gather(shared[1], "col", axis=1, tiled=True),
        lax.all_gather(shared[2], "col", axis=1, tiled=True),
        lax.all_gather(shared[3], "col", axis=1, tiled=True),
        lax.all_gather(shared[4], "col", axis=1, tiled=True),
    )
    gain_one = shared[5].astype(f32)
    gain_two = shared[6].astype(f32)
    x_rows = block_in.astype(f32)
    normed_one, scale_one, attn_in = norm_rows(x_rows, gain_one)
    query = jnp.dot(attn_in, wq_full, preferred_element_type=f32)
    key = jnp.dot(attn_in, wk_full, preferred_element_type=f32)
    value = jnp.dot(attn_in, wv_full, preferred_element_type=f32).astype(bf16)
    cosine, sine = rope_tables(col_index * tok_rows, tok_rows)
    query_rot = rotate(query.reshape(tok_rows, H, HD), cosine, sine).astype(bf16)
    key_rot = (
        rotate(key.reshape(tok_rows, KVH, HD), cosine, sine)
        .astype(bf16)
        .reshape(tok_rows, KVH * HD)
    )
    keys_all, values_all = (
        lax.all_gather(key_rot, "col", axis=0, tiled=True),
        lax.all_gather(value, "col", axis=0, tiled=True),
    )
    prefix = prefix_len[0]
    query_spot = col_index * tok_rows + jnp.arange(tok_rows, dtype=jnp.int32)
    key_spot = jnp.arange(seq_rows, dtype=jnp.int32)
    allowed = (key_spot[None, :] <= query_spot[:, None]) | (key_spot[None, :] < prefix)
    allowed_rows = jnp.tile(allowed, (group, 1))
    query_heads = to_heads(query_rot.reshape(tok_rows, H * HD), tok_rows, group)
    key_heads = keys_all.reshape(seq_rows, KVH, HD).transpose(1, 0, 2)
    value_heads = values_all.reshape(seq_rows, KVH, HD).transpose(1, 0, 2)

    def attend(pieces):
        queries, keys, values = pieces
        scores = times_back(queries, keys) * scale_attn
        scores = jnp.where(allowed_rows, scores, NEGATIVE)
        highest = jnp.max(scores, axis=1, keepdims=True)
        expo = jnp.exp(scores - highest)
        total = jnp.sum(expo, axis=1, keepdims=True)
        weights = (expo / total).astype(bf16)
        mixed_heads = jnp.dot(weights, values, preferred_element_type=f32).astype(bf16)
        return (mixed_heads, (highest + jnp.log(total))[:, 0])

    mixed_heads, lse_heads = lax.map(attend, (query_heads, key_heads, value_heads))
    mixed = from_heads(mixed_heads, tok_rows, group).reshape(tok_rows, H * HD)
    resid = x_rows + jnp.dot(mixed, wo_full, preferred_element_type=f32)
    normed_two, scale_two, moe_in = norm_rows(resid, gain_two)
    logits = jnp.dot(moe_in, wr_full, preferred_element_type=f32)
    choice_hot = (expert_ids[:, :, None] == jnp.arange(E, dtype=jnp.int32)).astype(f32)
    picked = jnp.sum(choice_hot * logits[:, None, :], axis=2)
    highest = jnp.max(picked, axis=1, keepdims=True)
    expo = jnp.exp(picked - highest)
    gates = expo / jnp.sum(expo, axis=1, keepdims=True)
    order = fill_order[0]
    ranked = expert_ids[order]
    onehot = (ranked.reshape(-1, 1) == jnp.arange(E, dtype=jnp.int32)).astype(jnp.int32)
    before = jnp.cumsum(onehot, axis=0) - onehot
    ranked_slot = jnp.sum(before * onehot, axis=1).reshape(tok_rows, TOPK)
    slot = jnp.zeros((tok_rows, TOPK), jnp.int32).at[order].set(ranked_slot)
    kept = slot < CAP
    dest_grid = jnp.where(kept, expert_ids * CAP + slot, E * CAP)
    pair_ids = jnp.arange(tok_rows * TOPK, dtype=jnp.int32)
    slot_pair = (
        jnp.full((E * CAP + 1,), tok_rows * TOPK, jnp.int32)
        .at[dest_grid.reshape(-1)]
        .set(pair_ids)[: E * CAP]
    )
    slot_token = slot_pair // TOPK
    gate_slot = jnp.concatenate([gates.reshape(-1), jnp.zeros((1,), f32)])[slot_pair]
    moe_pad = jnp.concatenate([moe_in, jnp.zeros((1, D), bf16)])
    dispatch = moe_pad[slot_token].reshape(E, CAP, D)
    received = lax.all_to_all(dispatch, "row", split_axis=0, concat_axis=1, tiled=True)
    gate_w, up_w, down_w = (
        lax.all_gather(w_gate, "col", axis=2, tiled=True),
        lax.all_gather(w_up, "col", axis=2, tiled=True),
        lax.all_gather(w_down, "col", axis=2, tiled=True),
    )
    hidden_gate = jnp.einsum("erd,edf->erf", received, gate_w, preferred_element_type=f32)
    hidden_up = jnp.einsum("erd,edf->erf", received, up_w, preferred_element_type=f32)
    active = (jax.nn.silu(hidden_gate) * hidden_up).astype(bf16)
    expert_out = jnp.einsum("erf,edf->erd", active, down_w, preferred_element_type=f32).astype(bf16)
    returned = lax.all_to_all(expert_out, "row", split_axis=1, concat_axis=0, tiled=True)
    out_pad = jnp.concatenate([returned.reshape(E * CAP, D), jnp.zeros((1, D), bf16)])
    pair_out = out_pad[dest_grid]
    weight_pair = gates * kept.astype(f32)
    moe_out = jnp.zeros((tok_rows, D), f32)
    for choice_index in range(TOPK):
        moe_out = moe_out + weight_pair[:, choice_index : choice_index + 1] * pair_out[
            :, choice_index
        ].astype(f32)
    block_out = resid + moe_out
    grad_out = out_grad.astype(f32)
    gate_grad = jnp.stack(
        [
            jnp.sum(pair_out[:, choice_index].astype(f32) * grad_out, axis=1)
            for choice_index in range(TOPK)
        ],
        axis=1,
    )
    grad_pad = jnp.concatenate([grad_out, jnp.zeros((1, D), f32)])
    slot_grad = (gate_slot[:, None] * grad_pad[slot_token]).astype(bf16).reshape(E, CAP, D)
    out_grads = lax.all_to_all(slot_grad, "row", split_axis=0, concat_axis=1, tiled=True)
    act_grad = jnp.einsum("erd,edf->erf", out_grads, down_w, preferred_element_type=f32)
    sigma = jax.nn.sigmoid(hidden_gate)
    gate_h_grad = (act_grad * hidden_up * sigma * (1.0 + hidden_gate * (1.0 - sigma))).astype(bf16)
    up_h_grad = (act_grad * hidden_gate * sigma).astype(bf16)
    down_wgrad = jnp.einsum("erd,erf->edf", out_grads, active, preferred_element_type=f32)
    gate_wgrad = jnp.einsum("erd,erf->edf", received, gate_h_grad, preferred_element_type=f32)
    up_wgrad = jnp.einsum("erd,erf->edf", received, up_h_grad, preferred_element_type=f32)
    in_grad = (
        jnp.einsum("erf,edf->erd", gate_h_grad, gate_w, preferred_element_type=f32)
        + jnp.einsum("erf,edf->erd", up_h_grad, up_w, preferred_element_type=f32)
    ).astype(bf16)
    back_rows = lax.all_to_all(in_grad, "row", split_axis=1, concat_axis=0, tiled=True)
    gate_sum, up_sum, down_sum = (
        lax.psum_scatter(
            gate_wgrad.astype(jnp.bfloat16), "col", scatter_dimension=2, tiled=True
        ).astype(jnp.float32),
        lax.psum_scatter(
            up_wgrad.astype(jnp.bfloat16), "col", scatter_dimension=2, tiled=True
        ).astype(jnp.float32),
        lax.psum_scatter(
            down_wgrad.astype(jnp.bfloat16), "col", scatter_dimension=2, tiled=True
        ).astype(jnp.float32),
    )
    back_pad = jnp.concatenate([back_rows.reshape(E * CAP, D), jnp.zeros((1, D), bf16)])
    pair_back = back_pad[dest_grid]
    moe_in_grad = jnp.zeros((tok_rows, D), f32)
    for choice_index in range(TOPK):
        moe_in_grad = moe_in_grad + pair_back[:, choice_index].astype(f32)
    picked_grad = gates * (gate_grad - jnp.sum(gates * gate_grad, axis=1, keepdims=True))
    logit_grad = jnp.sum(choice_hot * picked_grad[:, :, None], axis=1).astype(bf16)
    router_wgrad = cross_rows(moe_in, logit_grad)
    moe_in_grad = moe_in_grad + times_back(logit_grad, wr_full)
    norm_two_grad, gain_two_grad = norm_back(moe_in_grad, normed_two, scale_two, gain_two)
    resid_grad = grad_out + norm_two_grad
    branch_grad = resid_grad.astype(bf16)
    out_wgrad = cross_rows(mixed, branch_grad)
    mixed_grad = times_back(branch_grad, wo_full).astype(bf16)
    grad_heads = to_heads(mixed_grad, tok_rows, group)

    def query_side(pieces):
        queries, keys, values, lse_rows, grad_rows = pieces
        scores = jnp.where(allowed_rows, times_back(queries, keys) * scale_attn, NEGATIVE)
        probs = jnp.exp(scores - lse_rows[:, None])
        prob_grad = times_back(grad_rows, values)
        delta = jnp.sum(probs * prob_grad, axis=1, keepdims=True)
        score_grad = (probs * (prob_grad - delta)).astype(bf16)
        query_grad = jnp.dot(score_grad, keys, preferred_element_type=f32) * scale_attn
        return (query_grad, delta[:, 0], score_grad, probs)

    def both_sides(pieces):
        queries, keys, values, lse_rows, grad_rows = pieces
        query_grad, delta, score_grad, probs = query_side(pieces)
        key_grad = cross_rows(score_grad, queries) * scale_attn
        value_grad = cross_rows(probs.astype(bf16), grad_rows)
        return (query_grad, key_grad, value_grad)

    query_rot_grad, key_parts, value_parts = lax.map(
        both_sides, (query_heads, key_heads, value_heads, lse_heads, grad_heads)
    )
    key_rot_grad, value_grad = (
        lax.psum_scatter(
            key_parts.transpose(1, 0, 2).reshape(seq_rows, KVH * HD).astype(jnp.bfloat16),
            "col",
            scatter_dimension=0,
            tiled=True,
        ).astype(jnp.float32),
        lax.psum_scatter(
            value_parts.transpose(1, 0, 2).reshape(seq_rows, KVH * HD).astype(jnp.bfloat16),
            "col",
            scatter_dimension=0,
            tiled=True,
        ).astype(jnp.float32),
    )
    query_grad = (
        rotate_back(from_heads(query_rot_grad, tok_rows, group), cosine, sine)
        .reshape(tok_rows, H * HD)
        .astype(bf16)
    )
    key_grad = (
        rotate_back(key_rot_grad.reshape(tok_rows, KVH, HD), cosine, sine)
        .reshape(tok_rows, KVH * HD)
        .astype(bf16)
    )
    value_grad = value_grad.astype(bf16)
    query_wgrad = cross_rows(attn_in, query_grad)
    key_wgrad = cross_rows(attn_in, key_grad)
    value_wgrad = cross_rows(attn_in, value_grad)
    attn_in_grad = (
        times_back(query_grad, wq_full)
        + times_back(key_grad, wk_full)
        + times_back(value_grad, wv_full)
    )
    norm_one_grad, gain_one_grad = norm_back(attn_in_grad, normed_one, scale_one, gain_one)
    block_in_grad = resid_grad + norm_one_grad
    spread_one = jnp.broadcast_to(gain_one_grad[:, None], (D, n_col))
    spread_two = jnp.broadcast_to(gain_two_grad[:, None], (D, n_col))
    col_sums = (
        lax.psum_scatter(
            query_wgrad.astype(jnp.bfloat16), "col", scatter_dimension=1, tiled=True
        ).astype(jnp.float32),
        lax.psum_scatter(
            key_wgrad.astype(jnp.bfloat16), "col", scatter_dimension=1, tiled=True
        ).astype(jnp.float32),
        lax.psum_scatter(
            value_wgrad.astype(jnp.bfloat16), "col", scatter_dimension=1, tiled=True
        ).astype(jnp.float32),
        lax.psum_scatter(
            out_wgrad.astype(jnp.bfloat16), "col", scatter_dimension=1, tiled=True
        ).astype(jnp.float32),
        lax.psum_scatter(
            router_wgrad.astype(jnp.bfloat16), "col", scatter_dimension=1, tiled=True
        ).astype(jnp.float32),
        lax.psum_scatter(
            spread_one.astype(jnp.bfloat16), "col", scatter_dimension=1, tiled=True
        ).astype(jnp.float32),
        lax.psum_scatter(
            spread_two.astype(jnp.bfloat16), "col", scatter_dimension=1, tiled=True
        ).astype(jnp.float32),
    )
    row_sums = (
        lax.psum_scatter(
            col_sums[0].astype(jnp.bfloat16), "row", scatter_dimension=0, tiled=True
        ).astype(jnp.float32),
        lax.psum_scatter(
            col_sums[1].astype(jnp.bfloat16), "row", scatter_dimension=0, tiled=True
        ).astype(jnp.float32),
        lax.psum_scatter(
            col_sums[2].astype(jnp.bfloat16), "row", scatter_dimension=0, tiled=True
        ).astype(jnp.float32),
        lax.psum_scatter(
            col_sums[3].astype(jnp.bfloat16), "row", scatter_dimension=0, tiled=True
        ).astype(jnp.float32),
        lax.psum_scatter(
            col_sums[4].astype(jnp.bfloat16), "row", scatter_dimension=0, tiled=True
        ).astype(jnp.float32),
        lax.psum_scatter(
            col_sums[5].astype(jnp.bfloat16), "row", scatter_dimension=0, tiled=True
        ).astype(jnp.float32),
        lax.psum_scatter(
            col_sums[6].astype(jnp.bfloat16), "row", scatter_dimension=0, tiled=True
        ).astype(jnp.float32),
    )
    return (
        block_out,
        block_in_grad,
        row_sums[5][:, 0],
        row_sums[6][:, 0],
        row_sums[0],
        row_sums[1],
        row_sums[2],
        row_sums[3],
        row_sums[4],
        gate_sum,
        up_sum,
        down_sum,
    )


F32 = jnp.float32
BF16 = jnp.bfloat16
MIB = 1024 * 1024
LANES = 128
VMEM_MOST = 60 * MIB
COST_SCALE = 10**6


def cost(microseconds):
    return pl.CostEstimate(flops=int(microseconds * COST_SCALE), bytes_accessed=10**5, transcendentals=0)


def dot_nn(a, b):
    return lax.dot_general(a, b, (((1,), (0,)), ((), ())), preferred_element_type=F32)


def dot_nt(a, b):
    return lax.dot_general(a, b, (((1,), (1,)), ((), ())), preferred_element_type=F32)


def dot_tn(a, b):
    return lax.dot_general(a, b, (((0,), (0,)), ((), ())), preferred_element_type=F32)


def in_vmem():
    return pl.BlockSpec(memory_space=pltpu.VMEM)


def in_smem():
    return pl.BlockSpec(memory_space=pltpu.SMEM)


def in_hbm():
    return pl.BlockSpec(memory_space=pl.ANY)


def behind(kernel, n_in, after):
    if not after:
        return kernel
    return lambda *refs: kernel(*refs[:n_in], *refs[n_in + len(after) :])


def partner(values):
    lane = lax.broadcasted_iota(jnp.int32, values.shape, 1)
    half = HD // 2
    return jnp.where(
        lane % HD < half,
        pltpu.roll(values, LANES - half, 1),
        pltpu.roll(values, half, 1),
    )


def attend_kernel(
    spot_ref, x0, x1, x2, x3, pack_ref, cos_ref, sin_ref,
    attn_ref, q_ref, k_ref, v_ref, lse_ref, w_ref, gain_ref, mixed_ref,
):
    rows = x0.shape[0]
    col, prefix = spot_ref[0], spot_ref[1]
    for part in range(8):
        span = pl.ds(part * LANES, LANES)
        w_ref[span, :] = pack_ref[part, :LANES, :]
        gain_ref[0:1, span] = pack_ref[part, LANES : LANES + 1, :LANES].astype(F32)
        gain_ref[1:2, span] = pack_ref[part, LANES : LANES + 1, LANES : 2 * LANES].astype(F32)
    gain = gain_ref[0:1, :]
    for step, chunk in enumerate((x0, x1, x2, x3)):
        source = lax.rem(col - step + 4, 4)
        x = chunk[...].astype(F32)
        scale = lax.rsqrt(jnp.mean(x * x, axis=1, keepdims=True) + EPS)
        attn_ref[pl.ds(pl.multiple_of(source * rows, rows), rows), :] = (x * scale * gain).astype(BF16)
    for tile in range(4):
        span = pl.ds(tile * rows, rows)
        qkv = dot_nn(attn_ref[span, :], w_ref[...])
        cosine, sine = cos_ref[span, :], sin_ref[span, :]
        for block in range(3):
            v = qkv[:, block * LANES : (block + 1) * LANES]
            y = v * cosine + partner(v) * sine
            if block < 2:
                y = (y * HD ** (-0.5)).astype(BF16)
                q_ref[2 * block, span, :] = y[:, :HD]
                q_ref[2 * block + 1, span, :] = y[:, HD:]
            else:
                y = y.astype(BF16)
                k_ref[0, span, :] = y[:, :HD]
                k_ref[1, span, :] = y[:, HD:]
        v = qkv[:, 3 * LANES :].astype(BF16)
        v_ref[0, span, :] = v[:, :HD]
        v_ref[1, span, :] = v[:, HD:]
    total = 4 * rows
    for tile in range(4):
        span = pl.ds(tile * rows, rows)
        keys = max((tile + 1) * rows, total // 2)
        key_spot = lax.broadcasted_iota(jnp.int32, (rows, keys), 1)
        query_spot = lax.broadcasted_iota(jnp.int32, (rows, keys), 0) + tile * rows
        allowed = (key_spot <= query_spot) | (key_spot < prefix)
        for pair in range(2):
            k, v = k_ref[pair, pl.ds(0, keys), :], v_ref[pair, pl.ds(0, keys), :]
            outs = []
            for head in (2 * pair, 2 * pair + 1):
                scores = jnp.where(allowed, dot_nt(q_ref[head, span, :], k), NEGATIVE)
                highest = jnp.max(scores, axis=1, keepdims=True)
                expo = jnp.exp(scores - highest)
                summed = jnp.sum(expo, axis=1, keepdims=True)
                outs.append(dot_nn(expo.astype(BF16), v) * (1.0 / summed))
                lse_ref[span, head : head + 1] = highest + jnp.log(summed)
            mixed_ref[span, pair * LANES : (pair + 1) * LANES] = jnp.concatenate(outs, axis=1).astype(BF16)


def attend(spots, chunks, pack, cosine, sine, after=()):
    rows = chunks[0].shape[0]
    seq = 4 * rows
    shapes = (
        jax.ShapeDtypeStruct((seq, D), BF16),
        jax.ShapeDtypeStruct((4, seq, HD), BF16),
        jax.ShapeDtypeStruct((2, seq, HD), BF16),
        jax.ShapeDtypeStruct((2, seq, HD), BF16),
        jax.ShapeDtypeStruct((seq, 4), F32),
        jax.ShapeDtypeStruct((D, 512), BF16),
        jax.ShapeDtypeStruct((2, D), F32),
        jax.ShapeDtypeStruct((seq, 256), BF16),
    )
    return pl.pallas_call(
        behind(attend_kernel, 8, after),
        out_shape=shapes,
        in_specs=[in_smem()] + [in_vmem()] * 7 + [in_hbm()] * len(after),
        out_specs=tuple(in_vmem() for _ in shapes),
        compiler_params=pltpu.CompilerParams(vmem_limit_bytes=VMEM_MOST),
        cost_estimate=cost(10),
    )(spots, *chunks, pack, cosine, sine, *after)


def attend_back_kernel(
    spot_ref, grad_ref, mixed_ref, q_ref, k_ref, v_ref, lse_ref, attn_ref, w_ref, cos_ref, sin_ref, gain_ref,
    wgrad_ref, in0, in1, in2, in3, dqkv_ref, dk_ref, dv_ref, dq_ref, mg_ref,
):
    seq = attn_ref.shape[0]
    rows = seq // 4
    prefix = spot_ref[1]
    for tile in range(4):
        span = pl.ds(tile * rows, rows)
        for pair in range(2):
            g = grad_ref[span, pair * LANES : (pair + 1) * LANES]
            mg_ref[2 * pair, span, :] = g[:, :HD]
            mg_ref[2 * pair + 1, span, :] = g[:, HD:]
    dk_ref[...] = jnp.zeros_like(dk_ref)
    dv_ref[...] = jnp.zeros_like(dv_ref)
    for tile in range(4):
        span = pl.ds(tile * rows, rows)
        keys = max((tile + 1) * rows, seq // 2)
        key_spot = lax.broadcasted_iota(jnp.int32, (rows, keys), 1)
        query_spot = lax.broadcasted_iota(jnp.int32, (rows, keys), 0) + tile * rows
        allowed = (key_spot <= query_spot) | (key_spot < prefix)
        for pair in range(2):
            k, v = k_ref[pair, pl.ds(0, keys), :], v_ref[pair, pl.ds(0, keys), :]
            both = grad_ref[span, pair * LANES : (pair + 1) * LANES].astype(F32) * mixed_ref[
                span, pair * LANES : (pair + 1) * LANES
            ].astype(F32)
            outs = []
            for at, head in enumerate((2 * pair, 2 * pair + 1)):
                q, g = q_ref[head, span, :], mg_ref[head, span, :]
                delta = jnp.sum(both[:, at * HD : (at + 1) * HD], axis=1, keepdims=True)
                scores = jnp.where(allowed, dot_nt(q, k), NEGATIVE)
                probs = jnp.exp(scores - lse_ref[span, head : head + 1])
                score_grad = (probs * (dot_nt(g, v) - delta)).astype(BF16)
                dv_ref[pair, pl.ds(0, keys), :] += dot_tn(probs.astype(BF16), g)
                dk_ref[pair, pl.ds(0, keys), :] += dot_tn(score_grad, q)
                outs.append(dot_nn(score_grad, k) * HD ** (-0.5))
            dq_ref[span, pair * LANES : (pair + 1) * LANES] = jnp.concatenate(outs, axis=1)
    for tile in range(4):
        span = pl.ds(tile * rows, rows)
        cosine, sine = cos_ref[span, :], sin_ref[span, :]
        for block in range(3):
            if block < 2:
                g = dq_ref[span, block * LANES : (block + 1) * LANES]
            else:
                g = jnp.concatenate([dk_ref[0, span, :], dk_ref[1, span, :]], axis=1)
            dqkv_ref[span, block * LANES : (block + 1) * LANES] = (g * cosine - partner(g) * sine).astype(BF16)
        dqkv_ref[span, 3 * LANES :] = jnp.concatenate([dv_ref[0, span, :], dv_ref[1, span, :]], axis=1).astype(BF16)
    gain_total = jnp.zeros((1, D), F32)
    for step, out in enumerate((in0, in1, in2, in3)):
        source = lax.rem(spot_ref[0] - step + 4, 4)
        span = pl.ds(pl.multiple_of(source * rows, rows), rows)
        back = dot_nt(dqkv_ref[span, :], w_ref[...])
        out[...] = back.astype(BF16)
        gain_total = gain_total + jnp.sum(back * attn_ref[span, :].astype(F32), axis=0, keepdims=True)
    gain_total = gain_total / gain_ref[0:1, :]
    for part in range(8):
        span = pl.ds(part * LANES, LANES)
        wgrad_ref[part, LANES:, :LANES] = jnp.broadcast_to(gain_total[:, part * LANES : (part + 1) * LANES], (8, LANES)).astype(BF16)
        wgrad_ref[part, LANES:, LANES:] = jnp.zeros((8, 3 * LANES), BF16)
        wgrad_ref[part, :LANES, :] = dot_tn(attn_ref[:, span], dqkv_ref[...]).astype(BF16)


def attend_back(spots, grads, mixed, q, k, v, lse, attn_in, w_qkv, cosine, sine, gain, after=()):
    seq = attn_in.shape[0]
    shapes = (
        jax.ShapeDtypeStruct((8, 136, 512), BF16),
    ) + (jax.ShapeDtypeStruct((seq // 4, D), BF16),) * 4
    return pl.pallas_call(
        behind(attend_back_kernel, 12, after),
        out_shape=shapes,
        in_specs=[in_smem()] + [in_vmem()] * 11 + [in_hbm()] * len(after),
        out_specs=tuple(in_vmem() for _ in shapes),
        scratch_shapes=[
            pltpu.VMEM((seq, 512), BF16),
            pltpu.VMEM((2, seq, HD), F32),
            pltpu.VMEM((2, seq, HD), F32),
            pltpu.VMEM((seq, 256), F32),
            pltpu.VMEM((4, seq, HD), BF16),
        ],
        compiler_params=pltpu.CompilerParams(vmem_limit_bytes=VMEM_MOST),
        cost_estimate=cost(16),
    )(spots, grads, mixed, q, k, v, lse, attn_in, w_qkv, cosine, sine, gain, *after)


def route_kernel(
    spot_ref, mixed_ref, x_ref, pack_ref, gain_ref, ids_ref, order_ref,
    resid_ref, send_ref, gates_ref, kept_ref, wo_ref, wr_ref, wr_wide,
):
    rows = x_ref.shape[0]
    wr_wide[...] = jnp.zeros_like(wr_wide)
    for row in range(8):
        span = pl.ds(row * LANES, LANES)
        for col in range(4):
            wo_ref[span, col * 256 : (col + 1) * 256] = pack_ref[row, col, :LANES, :]
            wr_wide[col * 8 : (col + 1) * 8, span] = pack_ref[row, col, LANES:, :LANES].astype(F32)
    wr_ref[...] = wr_wide[...].astype(BF16)
    resid = x_ref[...].astype(F32)
    for part in range(4):
        resid = resid + dot_nn(mixed_ref[pl.ds(part * rows, rows), :], wo_ref[part * 256 : (part + 1) * 256, :])
    resid_ref[...] = resid
    scale = lax.rsqrt(jnp.mean(resid * resid, axis=1, keepdims=True) + EPS)
    moe_in = (resid * scale * gain_ref[1:2, :]).astype(BF16)
    send_ref[:, :D] = moe_in
    logits = dot_nt(moe_in, wr_ref[...])
    lane = lax.broadcasted_iota(jnp.int32, (rows, LANES), 1)
    chosen = jnp.zeros((rows, LANES), jnp.bool_)
    for choice in range(TOPK):
        chosen = chosen | (ids_ref[:, choice : choice + 1] == lane)
    picked = jnp.where(chosen, logits, NEGATIVE)
    expo = jnp.exp(picked - jnp.max(picked, axis=1, keepdims=True))
    gates = expo / jnp.sum(expo, axis=1, keepdims=True)
    first = lax.broadcasted_iota(jnp.int32, (rows, rows), 0)
    second = lax.broadcasted_iota(jnp.int32, (rows, rows), 1)
    place = (first == order_ref[...]).astype(BF16)
    sooner = dot_nn(place, (second < first).astype(BF16)).astype(BF16)
    sooner = dot_nt(sooner, place).astype(BF16)
    slot = dot_nn(sooner, chosen.astype(BF16))
    kept = (chosen & (slot < CAP)).astype(F32)
    gates_ref[...] = gates
    kept_ref[...] = kept
    send_ref[:, D:] = dot_nn((gates * kept).astype(BF16), relabel(spot_ref[2])).astype(BF16)


def relabel(row):
    first = lax.broadcasted_iota(jnp.int32, (LANES, LANES), 0)
    second = lax.broadcasted_iota(jnp.int32, (LANES, LANES), 1)
    return (first == (second ^ (row * 4))).astype(BF16)


def route(spots, mixed, x, pack, gain, ids, order, after=()):
    rows = x.shape[0]
    shapes = (
        jax.ShapeDtypeStruct((rows, D), F32),
        jax.ShapeDtypeStruct((rows, D + LANES), BF16),
        jax.ShapeDtypeStruct((rows, LANES), F32),
        jax.ShapeDtypeStruct((rows, LANES), F32),
        jax.ShapeDtypeStruct((D, D), BF16),
        jax.ShapeDtypeStruct((LANES, D), BF16),
    )
    return pl.pallas_call(
        behind(route_kernel, 7, after),
        out_shape=shapes,
        in_specs=[in_smem()] + [in_vmem()] * 6 + [in_hbm()] * len(after),
        out_specs=tuple(in_vmem() for _ in shapes),
        scratch_shapes=[pltpu.VMEM((LANES, D), F32)],
        compiler_params=pltpu.CompilerParams(vmem_limit_bytes=VMEM_MOST),
        cost_estimate=cost(2),
    )(spots, mixed, x, pack, gain, ids, order, *after)


def expert_kernel(x_ref, g_ref, *refs):
    weights, refs = refs[:10], refs[10:]
    back_ref, hg_ref, hu_ref, act_ref, out_acc, in_acc, gate_acc, held, sems = refs
    step = pl.program_id(0)
    count = held.shape[1]
    wide = count * LANES

    def fetch(at, slot):
        for k in range(8):

            @pl.when(at == k)
            def _():
                for i in range(2):
                    half = weights[k].at[pl.ds(2 * i, 2)] if k < 6 else weights[2 * k - 6 + i]
                    pltpu.make_async_copy(half, held.at[slot, pl.ds(2 * i, 2)], sems.at[slot, i]).start()

    @pl.when(step == 0)
    def _():
        fetch(step, 0)
        out_acc[...] = jnp.zeros_like(out_acc)
        in_acc[...] = jnp.zeros_like(in_acc)
        gate_acc[...] = jnp.zeros_like(gate_acc)

    now = lax.rem(step, 2)
    for i in range(2):
        pltpu.make_async_copy(weights[6], held.at[now, pl.ds(2 * i, 2)], sems.at[now, i]).wait()
    fetch(step + 1, 1 - now)

    join = lambda kind: jnp.concatenate([held[now, i, kind] for i in range(count)], axis=1)
    wg, wu, wd = join(0), join(1), join(2)
    x = x_ref[:, :D]
    expert = lax.broadcasted_iota(jnp.int32, (LANES, wide), 0)
    column = lax.broadcasted_iota(jnp.int32, (LANES, wide), 1)
    spread = (expert == step * count + column // LANES).astype(BF16)
    gate = dot_nn(x_ref[:, D:], spread)
    hidden_gate = dot_nn(x, wg)
    hidden_up = dot_nn(x, wu)
    act_grad = dot_nn(g_ref[...], wd)
    sigma = 0.5 * jnp.tanh(0.5 * hidden_gate) + 0.5
    swish = hidden_gate * sigma
    active = swish * hidden_up
    gate_acc[...] += dot_nt((active * act_grad).astype(BF16), spread)
    gated = (active * gate).astype(BF16)
    act_ref[...] = gated
    out_acc[...] += dot_nt(gated, wd)
    act_grad = act_grad * gate
    up_grad = (act_grad * swish).astype(BF16)
    gate_grad = (act_grad * hidden_up * (sigma + swish * (1.0 - sigma))).astype(BF16)
    hg_ref[...] = gate_grad
    hu_ref[...] = up_grad
    in_acc[...] += dot_nt(gate_grad, wg) + dot_nt(up_grad, wu)

    @pl.when(step == pl.num_programs(0) - 1)
    def _():
        back_ref[:, :D] = in_acc[...].astype(BF16)
        back_ref[:, D : 2 * D] = out_acc[...].astype(BF16)
        back_ref[:, 2 * D :] = gate_acc[...].astype(BF16)


def experts(x, g, weights, after=()):
    rows = x.shape[0]
    count = 4
    steps = 8
    wide = count * LANES
    hidden = pl.BlockSpec((rows, wide), lambda i: (0, i))
    whole = lambda width: pl.BlockSpec((rows, width), lambda i: (0, 0))
    return pl.pallas_call(
        behind(expert_kernel, 12, after),
        out_shape=(jax.ShapeDtypeStruct((rows, 2 * D + LANES), BF16),)
        + (jax.ShapeDtypeStruct((rows, steps * wide), BF16),) * 3,
        grid_spec=pltpu.PrefetchScalarGridSpec(
            num_scalar_prefetch=0,
            grid=(steps,),
            in_specs=[whole(D + LANES), whole(D)] + [in_hbm()] * (10 + len(after)),
            out_specs=(whole(2 * D + LANES), hidden, hidden, hidden),
            scratch_shapes=[
                pltpu.VMEM((rows, D), F32),
                pltpu.VMEM((rows, D), F32),
                pltpu.VMEM((rows, LANES), F32),
                pltpu.VMEM((2, count, 3, D, LANES), BF16),
                pltpu.SemaphoreType.DMA((2, 2)),
            ],
        ),
        compiler_params=pltpu.CompilerParams(vmem_limit_bytes=VMEM_MOST),
        cost_estimate=cost(21),
    )(x, g, *weights, *after)


def flip_kernel(x0, x1, x2, x3, g0, g1, g2, g3, xt_ref, gt_ref):
    rows = x0.shape[0]
    for at, (x, g) in enumerate(zip((x0, x1, x2, x3), (g0, g1, g2, g3))):
        xt_ref[:, at * rows : (at + 1) * rows] = x[:, :D].T
        gt_ref[:, at * rows : (at + 1) * rows] = g[...].T


def flip(xs, gs, after=()):
    seq = 4 * xs[0].shape[0]
    return pl.pallas_call(
        behind(flip_kernel, 8, after),
        out_shape=(jax.ShapeDtypeStruct((D, seq), BF16),) * 2,
        in_specs=[in_vmem()] * 8 + [in_hbm()] * len(after),
        out_specs=(in_vmem(),) * 2,
        compiler_params=pltpu.CompilerParams(vmem_limit_bytes=VMEM_MOST),
        cost_estimate=cost(2),
    )(*xs, *gs, *after)


def expert_wgrad_kernel(places, added, late, xt_ref, gt_ref, *refs):
    hidden, refs = refs[:12], refs[12:]
    count = len(places)
    n_extra = len({place[0] for place in added if place}) + len(late)
    plain = [k for k, place in enumerate(added) if not place]
    extras, refs = refs[:n_extra], refs[n_extra:]
    n_out = len({which for which, _ in places})
    outs, refs = refs[:n_out], refs[n_out:]
    held, out_sems, got, in_sems = refs
    step = pl.program_id(0)
    now = lax.rem(step, 2)

    def fetch(at, slot):
        for k, place in enumerate(added):
            if not place:
                continue
            which, half = place

            @pl.when(at == k)
            def _():
                pltpu.make_async_copy(extras[which].at[half], got.at[slot, 0], in_sems.at[slot, 0]).start()
                if k in late:
                    pltpu.make_async_copy(extras[late[k]].at[0], got.at[slot, 1], in_sems.at[slot, 1]).start()

    if added:

        @pl.when(step == 0)
        def _():
            fetch(step, 0)

        fetch(step + 1, 1 - now)

    def sent(slot):
        pltpu.make_async_copy(held.at[slot], outs[0].at[0], out_sems.at[slot]).wait()

    @pl.when(step >= 2)
    def _():
        sent(now)

    first = functools.reduce(jnp.logical_and, [step != k for k in plain], step >= 0)
    second = functools.reduce(jnp.logical_or, [step == k for k in late], False)
    if added:

        @pl.when(functools.reduce(jnp.logical_and, [step != k for k in plain], step >= 0))
        def _():
            pltpu.make_async_copy(extras[0].at[0], got.at[now, 0], in_sems.at[now, 0]).wait()

        for k in late:

            @pl.when(step == k)
            def _():
                pltpu.make_async_copy(extras[0].at[0], got.at[now, 1], in_sems.at[now, 1]).wait()


    for kind, left in enumerate((xt_ref, xt_ref, gt_ref)):
        joined = jnp.concatenate([part[...] for part in hidden[kind * 4 : kind * 4 + 4]], axis=0)
        product = dot_nn(left[...], joined)
        for i in range(2):
            piece = product[:, i * LANES : (i + 1) * LANES]
            if plain:
                piece = piece + jnp.where(first, got[now, 0, i, kind].astype(F32), 0.0)
            elif added:
                piece = piece + got[now, 0, i, kind].astype(F32)
            if late:
                piece = piece + jnp.where(second, got[now, 1, i, kind].astype(F32), 0.0)
            held[now, i, kind] = piece.astype(BF16)

    for k, (which, half) in enumerate(places):

        @pl.when(step == k)
        def _():
            pltpu.make_async_copy(held.at[now], outs[which].at[half], out_sems.at[now]).start()

    @pl.when(step == count - 1)
    def _():
        sent(now)
        if count > 1:
            sent(1 - now)


def expert_wgrads(flipped, hidden, entries, places, extras=(), added=(), late=None, after=(), into=None, halves=None):
    rows = hidden[0][0].shape[0]
    wide = 2 * LANES
    seq = flipped[0].shape[1]
    count = len(entries)

    def entry(i):
        place = entries[0]
        for k in range(1, count):
            place = jnp.where(i == k, entries[k], place)
        return (0, place)

    lane = pl.BlockSpec((rows, wide), entry)
    whole = pl.BlockSpec((D, seq), lambda i: (0, 0))
    kernel = functools.partial(expert_wgrad_kernel, places, added, late or {})
    if into is not None:
        after = [into, *after]
    sizes = halves or [sum(which == o for which, _ in places) for o in range(max(which for which, _ in places) + 1)]
    return pl.pallas_call(
        behind(kernel, 14 + len(extras), after),
        grid=(count,),
        out_shape=tuple(jax.ShapeDtypeStruct((size, 2, 3, D, LANES), BF16) for size in sizes),
        in_specs=[whole] * 2 + [lane] * 12 + [in_hbm()] * (len(extras) + len(after)),
        out_specs=(in_hbm(),) * len(sizes),
        scratch_shapes=[
            pltpu.VMEM((2, 2, 3, D, LANES), BF16),
            pltpu.SemaphoreType.DMA((2,)),
            pltpu.VMEM((2, 2, 2, 3, D, LANES), BF16),
            pltpu.SemaphoreType.DMA((2, 2)),
        ],
        compiler_params=pltpu.CompilerParams(vmem_limit_bytes=VMEM_MOST),
        cost_estimate=cost(2.2 * count),
        input_output_aliases={} if into is None else {14 + len(extras): 0},
    )(*flipped, *hidden[0], *hidden[1], *hidden[2], *extras, *after)


def expert_total_kernel(own_ref, xa_ref, xb_ref, ya_ref, yb_ref, gate_ref, up_ref, down_ref):
    for kind, out in enumerate((gate_ref, up_ref, down_ref)):
        for half, (x_ref, y_ref) in enumerate(((xa_ref, ya_ref), (xb_ref, yb_ref))):
            out[half, 0] = (
                own_ref[half, 0, kind].astype(F32) + x_ref[0, 0, kind].astype(F32) + y_ref[0, 0, kind].astype(F32)
            )


def expert_total(after, own, *parts):
    block = pl.BlockSpec((2, 1, 3, D, LANES), lambda i: (0, i, 0, 0, 0))
    part = pl.BlockSpec((1, 1, 3, D, LANES), lambda i: (0, i, 0, 0, 0))
    out = pl.BlockSpec((2, 1, D, LANES), lambda i: (0, i, 0, 0))
    sums = pl.pallas_call(
        behind(expert_total_kernel, 5, after),
        grid=(2,),
        out_shape=(jax.ShapeDtypeStruct((2, 2, D, LANES), F32),) * 3,
        in_specs=[block] + [part] * 4 + [in_hbm()] * len(after),
        out_specs=(out,) * 3,
        compiler_params=pltpu.CompilerParams(vmem_limit_bytes=VMEM_MOST),
        cost_estimate=cost(5),
    )(own, *parts, *after)
    return [total.reshape(4, D, LANES) for total in sums]


def halves_kernel(x_ref, y_ref, low_ref, high_ref):
    low_ref[...] = y_ref[...]
    high_ref[...] = x_ref[...]


def halves(from_x, from_y, after):
    half = jax.ShapeDtypeStruct((2, 3, D, LANES), BF16)
    first = pl.BlockSpec((1, 1, D, LANES), lambda i, j: (i, j, 0, 0))
    second = pl.BlockSpec((1, 1, D, LANES), lambda i, j: (i + 2, j, 0, 0))
    return pl.pallas_call(
        behind(halves_kernel, 2, after),
        grid=(2, 3),
        out_shape=(half, half),
        in_specs=[second, first] + [in_hbm()] * len(after),
        out_specs=(first,) * 2,
        compiler_params=pltpu.CompilerParams(vmem_limit_bytes=VMEM_MOST),
        cost_estimate=cost(3),
    )(from_x, from_y, *after)


def turn_kernel(
    spot_ref, came_ref, back_ref, gates_ref, kept_ref, resid_ref, gain_ref, g_ref, wr_ref, wo_ref, send_ref,
    out_ref, resid_grad_ref, branch_ref, mixed_grad_ref, small_ref,
):
    rows = resid_ref.shape[0]
    gates = gates_ref[...]
    both = lambda span: came_ref[:, span].astype(F32) + back_ref[:, span].astype(F32)
    out_ref[...] = resid_ref[...] + both(slice(D, 2 * D))
    gate_grad = dot_nn(both(slice(2 * D, None)).astype(BF16), relabel(spot_ref[2])) * kept_ref[...]
    logit_grad = gates * (gate_grad - jnp.sum(gates * gate_grad, axis=1, keepdims=True))
    logit_grad = logit_grad.astype(BF16)
    moe_grad = both(slice(0, D)) + dot_nn(logit_grad, wr_ref[...])
    resid = resid_ref[...]
    scale = lax.rsqrt(jnp.mean(resid * resid, axis=1, keepdims=True) + EPS)
    normed = resid * scale
    small_ref[LANES:, :] = jnp.broadcast_to(jnp.sum(moe_grad * normed, axis=0, keepdims=True), (8, D))
    small_ref[:LANES, :] = dot_tn(logit_grad, send_ref[:, :D])
    inner = moe_grad * gain_ref[1:2, :]
    grad = g_ref[...].astype(F32) + scale * (inner - normed * jnp.mean(inner * normed, axis=1, keepdims=True))
    resid_grad_ref[...] = grad
    branch = grad.astype(BF16)
    branch_ref[...] = branch
    for part in range(4):
        mixed_grad_ref[pl.ds(part * rows, rows), :] = dot_nt(
            branch, wo_ref[part * 256 : (part + 1) * 256, :]
        ).astype(BF16)


def turn(spots, came, back, gates, kept, resid, gain, g, wr, wo, send, after=()):
    rows = resid.shape[0]
    shapes = (
        jax.ShapeDtypeStruct((rows, D), F32),
        jax.ShapeDtypeStruct((rows, D), F32),
        jax.ShapeDtypeStruct((rows, D), BF16),
        jax.ShapeDtypeStruct((4 * rows, 256), BF16),
        jax.ShapeDtypeStruct((LANES + 8, D), F32),
    )
    return pl.pallas_call(
        behind(turn_kernel, 11, after),
        out_shape=shapes,
        in_specs=[in_smem()] + [in_vmem()] * 10 + [in_hbm()] * len(after),
        out_specs=tuple(in_vmem() for _ in shapes),
        compiler_params=pltpu.CompilerParams(vmem_limit_bytes=VMEM_MOST),
        cost_estimate=cost(2),
    )(spots, came, back, gates, kept, resid, gain, g, wr, wo, send, *after)


def out_wgrad_kernel(mixed_ref, branch_ref, small_ref, pack_ref):
    rows = branch_ref.shape[0]
    for part in range(4):
        product = dot_tn(mixed_ref[pl.ds(part * rows, rows), :], branch_ref[...]).astype(BF16)
        pack_ref[2 * part, :LANES, :] = product[:LANES]
        pack_ref[2 * part + 1, :LANES, :] = product[LANES:]
    for row in range(8):
        span = pl.ds(row * LANES, LANES)
        for col in range(4):
            pack_ref[row, LANES:, col * 256 : col * 256 + LANES] = small_ref[col * 8 : col * 8 + 8, span].astype(BF16)
            pack_ref[row, LANES:, col * 256 + LANES : col * 256 + 256] = small_ref[LANES:, span].astype(BF16)


def out_wgrad(mixed, branch, small, after=()):
    return pl.pallas_call(
        behind(out_wgrad_kernel, 3, after),
        out_shape=jax.ShapeDtypeStruct((8, LANES + 8, D), BF16),
        in_specs=[in_vmem()] * 3 + [in_hbm()] * len(after),
        out_specs=in_vmem(),
        compiler_params=pltpu.CompilerParams(vmem_limit_bytes=VMEM_MOST),
        cost_estimate=cost(3),
    )(mixed, branch, small, *after)


def unpack_kernel(sum_ref, query_ref, key_ref, value_ref, gain_ref):
    query_ref[...] = sum_ref[:LANES, :256].astype(F32)
    key_ref[...] = sum_ref[:LANES, 256:384].astype(F32)
    value_ref[...] = sum_ref[:LANES, 384:].astype(F32)
    gain_ref[...] = sum_ref[LANES:, :LANES].astype(F32)


def unpack(sums, after):
    return pl.pallas_call(
        behind(unpack_kernel, 1, after),
        out_shape=tuple(jax.ShapeDtypeStruct(shape, F32) for shape in ((LANES, 256), (LANES, LANES), (LANES, LANES), (8, LANES))),
        in_specs=[in_vmem()] + [in_hbm()] * len(after),
        out_specs=(in_vmem(),) * 4,
        compiler_params=pltpu.CompilerParams(vmem_limit_bytes=VMEM_MOST),
        cost_estimate=cost(2),
    )(sums, *after)


def ring_gather(value, n_col):
    steps = [(i, (i + 1) % n_col) for i in range(n_col)]
    chunks = [value]
    for _ in range(n_col - 1):
        chunks.append(lax.ppermute(chunks[-1], "col", steps))
    return chunks


def ring_sum(parts, n_col):
    steps = [(i, (i + 1) % n_col) for i in range(n_col)]
    total = parts[1]
    for part in parts[2:] + parts[:1]:
        total = lax.ppermute(total, "col", steps).astype(F32) + part.astype(F32)
        if part is not parts[0]:
            total = total.astype(BF16)
    return total


def shift_all(parts, n_col):
    return [
        lax.ppermute(part, "col", [(i, (i + s) % n_col) for i in range(n_col)]) if s else part
        for s, part in enumerate(parts)
    ]


def hold(value, *until):
    return lax.optimization_barrier((value, *until))[0]


CORE, ACROSS_X, ACROSS_Y = 1, 2, 4


def swap(value, mask):
    return lax.ppermute(value, "row", [(i, i ^ mask) for i in range(8)])


def fast(
    block_in,
    attn_gain,
    moe_gain,
    w_query,
    w_key,
    w_value,
    w_out,
    w_router,
    w_gate,
    w_up,
    w_down,
    expert_ids,
    fill_order,
    prefix_len,
    out_grad,
):
    rows = block_in.shape[0]
    n_col = lax.axis_size("col")
    col = lax.axis_index("col")
    row = lax.axis_index("row")
    seq = rows * n_col
    spots = jnp.stack([col.astype(jnp.int32), prefix_len[0], row.astype(jnp.int32)])
    gains = jnp.concatenate([attn_gain, moe_gain, jnp.zeros((256,), BF16)])[None]
    pack_qkv = jnp.concatenate(
        [jnp.concatenate([w_query, w_key, w_value], axis=1), gains, jnp.zeros((7, 512), BF16)], axis=0
    )
    pack_out = jnp.concatenate([w_out, jnp.pad(w_router.T, ((0, 0), (0, 256 - LANES)))], axis=0)
    pack_out = lax.all_gather(pack_out, "col", axis=0)
    pack_qkv = lax.all_gather(pack_qkv, "row", axis=0)
    pack_out = lax.all_gather(pack_out, "row", axis=0)
    cosine, sine = rope_tables(0, seq)
    cosine = jnp.tile(cosine, (1, 4))
    sine = jnp.concatenate([-sine, sine, -sine, sine], axis=1)
    ring = [(i, (i + 1) % n_col) for i in range(n_col)]
    x_chunks = [block_in, lax.ppermute(block_in, "col", ring)]
    x_chunks += ring_gather(hold(x_chunks[1], cosine, sine), n_col)[1:3]
    own = jnp.stack([w_gate, w_up, w_down], axis=1)
    from_x, from_y, other = swap(own, ACROSS_X), swap(own, ACROSS_Y), swap(own, CORE)

    attn_in, q, k, v, lse, w_qkv, gains, mixed_all = attend(spots, x_chunks, pack_qkv, cosine, sine, [other])
    g_chunks = [out_grad, lax.ppermute(hold(out_grad, x_chunks[3]), "col", ring)]
    g_chunks += ring_gather(hold(g_chunks[1], attn_in), n_col)[1:3]
    mixed_own = lax.all_to_all(mixed_all, "col", split_axis=0, concat_axis=0, tiled=True)
    low, high = halves(from_x, from_y, [g_chunks[2]])
    resid, send, gates, kept, wo, wr = route(
        spots, mixed_own, block_in, pack_out, gains, expert_ids, fill_order, [low]
    )
    far = swap(low, ACROSS_X), swap(high, ACROSS_Y)
    weights = [own, other, from_x, swap(from_x, CORE), from_y, swap(from_y, CORE), *far]

    send_chunks = [send, *ring_gather(hold(send, g_chunks[3]), n_col)[1:]]
    weights += [swap(hold(part, send_chunks[2]), CORE) for part in far]
    results, backs, back = {}, [], None
    steps = [(i, (i + 1) % n_col) for i in range(n_col)]
    order = (1, 2, 3, 0)
    for at, chunk in enumerate(order):
        after = [results[order[at - 1]][1]] if at else [send_chunks[3]]
        if at >= 2:
            after.append(backs[at - 2])
        if at == 2:
            flipped = flip(send_chunks, g_chunks, [results[2][1]])
            after.append(flipped[0])
        results[chunk] = experts(send_chunks[chunk], g_chunks[chunk], weights, after)
        if chunk:
            part = results[chunk][0]
            back = part if back is None else (back.astype(F32) + part.astype(F32)).astype(BF16)
            back = lax.ppermute(back, "col", steps)
            backs.append(back)
    results = [results[chunk] for chunk in range(n_col)]

    hidden = [[result[kind] for result in results] for kind in (1, 2, 3)]
    wgrads = functools.partial(expert_wgrads, flipped, hidden)
    (p7,) = wgrads((14, 15), ((0, 0), (0, 1)), after=[backs[2]])
    r7 = swap(p7, CORE)
    (p5,) = wgrads((10, 11), ((0, 2), (0, 3)), after=[p7], halves=[4])
    (p53,) = wgrads((6, 7), ((0, 0), (0, 1)), after=[r7], into=p5, halves=[4])
    r53 = swap(p53, CORE)
    q6 = wgrads((12, 13), ((0, 0), (1, 0)), [r7], ((0, 0), (0, 1)), after=[p53])
    far_x, far_y = swap(q6[0], ACROSS_X), swap(q6[1], ACROSS_Y)
    block_out, resid_grad, branch, mixed_grad, small = turn(
        spots, backs[2], results[0][0], gates, kept, resid, gains, out_grad, wr, wo, send, q6[:1]
    )
    mixed_grads = lax.all_to_all(mixed_grad, "col", split_axis=0, concat_axis=0, tiled=True)
    pack = out_wgrad(mixed_own, branch, small)
    out_sum = lax.psum_scatter(pack, "row", scatter_dimension=0, tiled=True)
    q2a, q4b, q2b, q4a, p1 = wgrads(
        (4, 9, 5, 8, 2, 3),
        ((0, 0), (1, 0), (2, 0), (3, 0), (4, 0), (4, 1)),
        [r53, far_y, far_x],
        ((0, 0), (0, 3), (0, 1), (0, 2), None, None),
        {2: 1, 3: 2},
        [pack, mixed_grads],
    )
    x2a, y4b = swap(q2a, ACROSS_X), swap(q4b, ACROSS_Y)
    r1 = swap(p1, CORE)
    x2b, y4a = swap(q2b, ACROSS_X), swap(q4a, ACROSS_Y)
    qkv_wgrad, *back_parts = attend_back(
        spots, mixed_grads, mixed_all, q, k, v, lse, attn_in, w_qkv, cosine, sine, gains, [q2b]
    )
    (q0,) = wgrads((0, 1), ((0, 0), (0, 1)), [r1], ((0, 0), (0, 1)), after=[qkv_wgrad])
    moving = lax.ppermute(back_parts[1], "col", steps)
    moving = (hold(moving, q0, x2a, y4b).astype(F32) + back_parts[2].astype(F32)).astype(BF16)
    moving = lax.ppermute(moving, "col", steps)
    moving = (moving.astype(F32) + back_parts[3].astype(F32)).astype(BF16)
    third_step = moving
    last_step = lax.ppermute(moving, "col", steps)
    attn_grad = last_step.astype(F32) + back_parts[0].astype(F32)
    x_rows = block_in.astype(F32)
    scale = lax.rsqrt(jnp.mean(x_rows * x_rows, axis=1, keepdims=True) + EPS)
    normed = x_rows * scale
    inner = attn_grad * gains[:1]
    block_in_grad = resid_grad + scale * (inner - normed * jnp.mean(inner * normed, axis=1, keepdims=True))

    qkv_sum = lax.psum_scatter(qkv_wgrad, "row", scatter_dimension=0, tiled=True)[0]
    *qkv_sums, gain_one = unpack(qkv_sum, [last_step])
    out_sum = lax.psum_scatter(hold(out_sum, q2b), "col", scatter_dimension=2, tiled=True)[0].astype(F32)
    gain_one_sum = functools.reduce(jnp.add, shift_all([gain_one] * n_col, n_col))
    gate_sum, up_sum, down_sum = expert_total([block_in_grad, gain_one_sum], q0, x2a, x2b, y4a, y4b)
    return (
        block_out,
        block_in_grad,
        gain_one_sum[0],
        out_sum[LANES, LANES:],
        *qkv_sums,
        out_sum[:LANES],
        out_sum[LANES:, :LANES].T,
        gate_sum,
        up_sum,
        down_sum,
    )


def takes_fast(mesh):
    n_row, n_col = mesh.shape["row"], mesh.shape["col"]
    return n_row == 8 and n_col == 4


def solution(mesh):
    in_specs = (
        P(("row", "col"), None),
        P("row"),
        P("row"),
        P("row", "col"),
        P("row", "col"),
        P("row", "col"),
        P("row", "col"),
        P("row", "col"),
        P("row", None, "col"),
        P("row", None, "col"),
        P("row", None, "col"),
        P(("row", "col"), None),
        P(("row", "col"), None),
        P("row"),
        P(("row", "col"), None),
    )
    out_specs = (
        P(("row", "col"), None),
        P(("row", "col"), None),
        P("row"),
        P("row"),
        P("row", "col"),
        P("row", "col"),
        P("row", "col"),
        P("row", "col"),
        P("row", "col"),
        P("row", None, "col"),
        P("row", None, "col"),
        P("row", None, "col"),
    )
    local = fast if takes_fast(mesh) else general
    return jax.shard_map(local, mesh=mesh, in_specs=in_specs, out_specs=out_specs, check_vma=False)
```

```python
import functools

import jax
import jax.numpy as jnp
from jax import lax
from jax.experimental import pallas as pl
from jax.experimental.pallas import tpu as pltpu
from jax.sharding import PartitionSpec as P

D = 1024
H = 16
KVH = 8
HD = 64
E = 32
TOPK = 8
CAP = 80


EPS = 1e-06
NEGATIVE = -1e30


def cross_rows(left, right):
    return lax.dot_general(
        left, right, (((0,), (0,)), ((), ())), preferred_element_type=jnp.float32
    )


def times_back(left, right):
    return lax.dot_general(
        left, right, (((1,), (1,)), ((), ())), preferred_element_type=jnp.float32
    )


def rope_tables(first_position, count):
    position = (first_position + jnp.arange(count, dtype=jnp.int32)).astype(jnp.float32)
    inverse = 10000.0 ** (-jnp.arange(HD // 2, dtype=jnp.float32) * 2.0 / HD)
    angle = position[:, None] * inverse[None, :]
    return (jnp.cos(angle), jnp.sin(angle))


def rotate(values, cosine, sine):
    half = HD // 2
    first, second = (values[..., :half], values[..., half:])
    cos_rows = cosine[:, None, :]
    sin_rows = sine[:, None, :]
    return jnp.concatenate(
        [first * cos_rows - second * sin_rows, second * cos_rows + first * sin_rows], axis=-1
    )


def rotate_back(grads, cosine, sine):
    half = HD // 2
    first, second = (grads[..., :half], grads[..., half:])
    cos_rows = cosine[:, None, :]
    sin_rows = sine[:, None, :]
    return jnp.concatenate(
        [first * cos_rows + second * sin_rows, second * cos_rows - first * sin_rows], axis=-1
    )


def norm_rows(values, gain):
    scale = lax.rsqrt(jnp.mean(values * values, axis=1, keepdims=True) + EPS)
    normed = values * scale
    return (normed, scale, (normed * gain).astype(jnp.bfloat16))


def norm_back(grad_in, normed, scale, gain):
    gain_grad = jnp.sum(grad_in * normed, axis=0)
    inner = grad_in * gain
    return (scale * (inner - normed * jnp.mean(inner * normed, axis=1, keepdims=True)), gain_grad)


def to_heads(rows, count, group):
    return rows.reshape(count, KVH, group, HD).transpose(1, 2, 0, 3).reshape(KVH, group * count, HD)


def from_heads(heads, count, group):
    return heads.reshape(KVH, group, count, HD).transpose(2, 0, 1, 3).reshape(count, H, HD)


def general(
    block_in,
    attn_gain,
    moe_gain,
    w_query,
    w_key,
    w_value,
    w_out,
    w_router,
    w_gate,
    w_up,
    w_down,
    expert_ids,
    fill_order,
    prefix_len,
    out_grad,
):
    tok_rows = block_in.shape[0]
    n_col = lax.axis_size("col")
    col_index = lax.axis_index("col")
    seq_rows = tok_rows * n_col
    group = H // KVH
    scale_attn = HD ** (-0.5)
    bf16 = jnp.bfloat16
    f32 = jnp.float32
    shared = (
        lax.all_gather(w_query, "row", axis=0, tiled=True),
        lax.all_gather(w_key, "row", axis=0, tiled=True),
        lax.all_gather(w_value, "row", axis=0, tiled=True),
        lax.all_gather(w_out, "row", axis=0, tiled=True),
        lax.all_gather(w_router, "row", axis=0, tiled=True),
        lax.all_gather(attn_gain, "row", axis=0, tiled=True),
        lax.all_gather(moe_gain, "row", axis=0, tiled=True),
    )
    wq_full, wk_full, wv_full, wo_full, wr_full = (
        lax.all_gather(shared[0], "col", axis=1, tiled=True),
        lax.all_gather(shared[1], "col", axis=1, tiled=True),
        lax.all_gather(shared[2], "col", axis=1, tiled=True),
        lax.all_gather(shared[3], "col", axis=1, tiled=True),
        lax.all_gather(shared[4], "col", axis=1, tiled=True),
    )
    gain_one = shared[5].astype(f32)
    gain_two = shared[6].astype(f32)
    x_rows = block_in.astype(f32)
    normed_one, scale_one, attn_in = norm_rows(x_rows, gain_one)
    query = jnp.dot(attn_in, wq_full, preferred_element_type=f32)
    key = jnp.dot(attn_in, wk_full, preferred_element_type=f32)
    value = jnp.dot(attn_in, wv_full, preferred_element_type=f32).astype(bf16)
    cosine, sine = rope_tables(col_index * tok_rows, tok_rows)
    query_rot = rotate(query.reshape(tok_rows, H, HD), cosine, sine).astype(bf16)
    key_rot = (
        rotate(key.reshape(tok_rows, KVH, HD), cosine, sine)
        .astype(bf16)
        .reshape(tok_rows, KVH * HD)
    )
    keys_all, values_all = (
        lax.all_gather(key_rot, "col", axis=0, tiled=True),
        lax.all_gather(value, "col", axis=0, tiled=True),
    )
    prefix = prefix_len[0]
    query_spot = col_index * tok_rows + jnp.arange(tok_rows, dtype=jnp.int32)
    key_spot = jnp.arange(seq_rows, dtype=jnp.int32)
    allowed = (key_spot[None, :] <= query_spot[:, None]) | (key_spot[None, :] < prefix)
    allowed_rows = jnp.tile(allowed, (group, 1))
    query_heads = to_heads(query_rot.reshape(tok_rows, H * HD), tok_rows, group)
    key_heads = keys_all.reshape(seq_rows, KVH, HD).transpose(1, 0, 2)
    value_heads = values_all.reshape(seq_rows, KVH, HD).transpose(1, 0, 2)

    def attend(pieces):
        queries, keys, values = pieces
        scores = times_back(queries, keys) * scale_attn
        scores = jnp.where(allowed_rows, scores, NEGATIVE)
        highest = jnp.max(scores, axis=1, keepdims=True)
        expo = jnp.exp(scores - highest)
        total = jnp.sum(expo, axis=1, keepdims=True)
        weights = (expo / total).astype(bf16)
        mixed_heads = jnp.dot(weights, values, preferred_element_type=f32).astype(bf16)
        return (mixed_heads, (highest + jnp.log(total))[:, 0])

    mixed_heads, lse_heads = lax.map(attend, (query_heads, key_heads, value_heads))
    mixed = from_heads(mixed_heads, tok_rows, group).reshape(tok_rows, H * HD)
    resid = x_rows + jnp.dot(mixed, wo_full, preferred_element_type=f32)
    normed_two, scale_two, moe_in = norm_rows(resid, gain_two)
    logits = jnp.dot(moe_in, wr_full, preferred_element_type=f32)
    choice_hot = (expert_ids[:, :, None] == jnp.arange(E, dtype=jnp.int32)).astype(f32)
    picked = jnp.sum(choice_hot * logits[:, None, :], axis=2)
    highest = jnp.max(picked, axis=1, keepdims=True)
    expo = jnp.exp(picked - highest)
    gates = expo / jnp.sum(expo, axis=1, keepdims=True)
    order = fill_order[0]
    ranked = expert_ids[order]
    onehot = (ranked.reshape(-1, 1) == jnp.arange(E, dtype=jnp.int32)).astype(jnp.int32)
    before = jnp.cumsum(onehot, axis=0) - onehot
    ranked_slot = jnp.sum(before * onehot, axis=1).reshape(tok_rows, TOPK)
    slot = jnp.zeros((tok_rows, TOPK), jnp.int32).at[order].set(ranked_slot)
    kept = slot < CAP
    dest_grid = jnp.where(kept, expert_ids * CAP + slot, E * CAP)
    pair_ids = jnp.arange(tok_rows * TOPK, dtype=jnp.int32)
    slot_pair = (
        jnp.full((E * CAP + 1,), tok_rows * TOPK, jnp.int32)
        .at[dest_grid.reshape(-1)]
        .set(pair_ids)[: E * CAP]
    )
    slot_token = slot_pair // TOPK
    gate_slot = jnp.concatenate([gates.reshape(-1), jnp.zeros((1,), f32)])[slot_pair]
    moe_pad = jnp.concatenate([moe_in, jnp.zeros((1, D), bf16)])
    dispatch = moe_pad[slot_token].reshape(E, CAP, D)
    received = lax.all_to_all(dispatch, "row", split_axis=0, concat_axis=1, tiled=True)
    gate_w, up_w, down_w = (
        lax.all_gather(w_gate, "col", axis=2, tiled=True),
        lax.all_gather(w_up, "col", axis=2, tiled=True),
        lax.all_gather(w_down, "col", axis=2, tiled=True),
    )
    hidden_gate = jnp.einsum("erd,edf->erf", received, gate_w, preferred_element_type=f32)
    hidden_up = jnp.einsum("erd,edf->erf", received, up_w, preferred_element_type=f32)
    active = (jax.nn.silu(hidden_gate) * hidden_up).astype(bf16)
    expert_out = jnp.einsum("erf,edf->erd", active, down_w, preferred_element_type=f32).astype(bf16)
    returned = lax.all_to_all(expert_out, "row", split_axis=1, concat_axis=0, tiled=True)
    out_pad = jnp.concatenate([returned.reshape(E * CAP, D), jnp.zeros((1, D), bf16)])
    pair_out = out_pad[dest_grid]
    weight_pair = gates * kept.astype(f32)
    moe_out = jnp.zeros((tok_rows, D), f32)
    for choice_index in range(TOPK):
        moe_out = moe_out + weight_pair[:, choice_index : choice_index + 1] * pair_out[
            :, choice_index
        ].astype(f32)
    block_out = resid + moe_out
    grad_out = out_grad.astype(f32)
    gate_grad = jnp.stack(
        [
            jnp.sum(pair_out[:, choice_index].astype(f32) * grad_out, axis=1)
            for choice_index in range(TOPK)
        ],
        axis=1,
    )
    grad_pad = jnp.concatenate([grad_out, jnp.zeros((1, D), f32)])
    slot_grad = (gate_slot[:, None] * grad_pad[slot_token]).astype(bf16).reshape(E, CAP, D)
    out_grads = lax.all_to_all(slot_grad, "row", split_axis=0, concat_axis=1, tiled=True)
    act_grad = jnp.einsum("erd,edf->erf", out_grads, down_w, preferred_element_type=f32)
    sigma = jax.nn.sigmoid(hidden_gate)
    gate_h_grad = (act_grad * hidden_up * sigma * (1.0 + hidden_gate * (1.0 - sigma))).astype(bf16)
    up_h_grad = (act_grad * hidden_gate * sigma).astype(bf16)
    down_wgrad = jnp.einsum("erd,erf->edf", out_grads, active, preferred_element_type=f32)
    gate_wgrad = jnp.einsum("erd,erf->edf", received, gate_h_grad, preferred_element_type=f32)
    up_wgrad = jnp.einsum("erd,erf->edf", received, up_h_grad, preferred_element_type=f32)
    in_grad = (
        jnp.einsum("erf,edf->erd", gate_h_grad, gate_w, preferred_element_type=f32)
        + jnp.einsum("erf,edf->erd", up_h_grad, up_w, preferred_element_type=f32)
    ).astype(bf16)
    back_rows = lax.all_to_all(in_grad, "row", split_axis=1, concat_axis=0, tiled=True)
    gate_sum, up_sum, down_sum = (
        lax.psum_scatter(
            gate_wgrad.astype(jnp.bfloat16), "col", scatter_dimension=2, tiled=True
        ).astype(jnp.float32),
        lax.psum_scatter(
            up_wgrad.astype(jnp.bfloat16), "col", scatter_dimension=2, tiled=True
        ).astype(jnp.float32),
        lax.psum_scatter(
            down_wgrad.astype(jnp.bfloat16), "col", scatter_dimension=2, tiled=True
        ).astype(jnp.float32),
    )
    back_pad = jnp.concatenate([back_rows.reshape(E * CAP, D), jnp.zeros((1, D), bf16)])
    pair_back = back_pad[dest_grid]
    moe_in_grad = jnp.zeros((tok_rows, D), f32)
    for choice_index in range(TOPK):
        moe_in_grad = moe_in_grad + pair_back[:, choice_index].astype(f32)
    picked_grad = gates * (gate_grad - jnp.sum(gates * gate_grad, axis=1, keepdims=True))
    logit_grad = jnp.sum(choice_hot * picked_grad[:, :, None], axis=1).astype(bf16)
    router_wgrad = cross_rows(moe_in, logit_grad)
    moe_in_grad = moe_in_grad + times_back(logit_grad, wr_full)
    norm_two_grad, gain_two_grad = norm_back(moe_in_grad, normed_two, scale_two, gain_two)
    resid_grad = grad_out + norm_two_grad
    branch_grad = resid_grad.astype(bf16)
    out_wgrad = cross_rows(mixed, branch_grad)
    mixed_grad = times_back(branch_grad, wo_full).astype(bf16)
    grad_heads = to_heads(mixed_grad, tok_rows, group)

    def query_side(pieces):
        queries, keys, values, lse_rows, grad_rows = pieces
        scores = jnp.where(allowed_rows, times_back(queries, keys) * scale_attn, NEGATIVE)
        probs = jnp.exp(scores - lse_rows[:, None])
        prob_grad = times_back(grad_rows, values)
        delta = jnp.sum(probs * prob_grad, axis=1, keepdims=True)
        score_grad = (probs * (prob_grad - delta)).astype(bf16)
        query_grad = jnp.dot(score_grad, keys, preferred_element_type=f32) * scale_attn
        return (query_grad, delta[:, 0], score_grad, probs)

    def both_sides(pieces):
        queries, keys, values, lse_rows, grad_rows = pieces
        query_grad, delta, score_grad, probs = query_side(pieces)
        key_grad = cross_rows(score_grad, queries) * scale_attn
        value_grad = cross_rows(probs.astype(bf16), grad_rows)
        return (query_grad, key_grad, value_grad)

    query_rot_grad, key_parts, value_parts = lax.map(
        both_sides, (query_heads, key_heads, value_heads, lse_heads, grad_heads)
    )
    key_rot_grad, value_grad = (
        lax.psum_scatter(
            key_parts.transpose(1, 0, 2).reshape(seq_rows, KVH * HD).astype(jnp.bfloat16),
            "col",
            scatter_dimension=0,
            tiled=True,
        ).astype(jnp.float32),
        lax.psum_scatter(
            value_parts.transpose(1, 0, 2).reshape(seq_rows, KVH * HD).astype(jnp.bfloat16),
            "col",
            scatter_dimension=0,
            tiled=True,
        ).astype(jnp.float32),
    )
    query_grad = (
        rotate_back(from_heads(query_rot_grad, tok_rows, group), cosine, sine)
        .reshape(tok_rows, H * HD)
        .astype(bf16)
    )
    key_grad = (
        rotate_back(key_rot_grad.reshape(tok_rows, KVH, HD), cosine, sine)
        .reshape(tok_rows, KVH * HD)
        .astype(bf16)
    )
    value_grad = value_grad.astype(bf16)
    query_wgrad = cross_rows(attn_in, query_grad)
    key_wgrad = cross_rows(attn_in, key_grad)
    value_wgrad = cross_rows(attn_in, value_grad)
    attn_in_grad = (
        times_back(query_grad, wq_full)
        + times_back(key_grad, wk_full)
        + times_back(value_grad, wv_full)
    )
    norm_one_grad, gain_one_grad = norm_back(attn_in_grad, normed_one, scale_one, gain_one)
    block_in_grad = resid_grad + norm_one_grad
    spread_one = jnp.broadcast_to(gain_one_grad[:, None], (D, n_col))
    spread_two = jnp.broadcast_to(gain_two_grad[:, None], (D, n_col))
    col_sums = (
        lax.psum_scatter(
            query_wgrad.astype(jnp.bfloat16), "col", scatter_dimension=1, tiled=True
        ).astype(jnp.float32),
        lax.psum_scatter(
            key_wgrad.astype(jnp.bfloat16), "col", scatter_dimension=1, tiled=True
        ).astype(jnp.float32),
        lax.psum_scatter(
            value_wgrad.astype(jnp.bfloat16), "col", scatter_dimension=1, tiled=True
        ).astype(jnp.float32),
        lax.psum_scatter(
            out_wgrad.astype(jnp.bfloat16), "col", scatter_dimension=1, tiled=True
        ).astype(jnp.float32),
        lax.psum_scatter(
            router_wgrad.astype(jnp.bfloat16), "col", scatter_dimension=1, tiled=True
        ).astype(jnp.float32),
        lax.psum_scatter(
            spread_one.astype(jnp.bfloat16), "col", scatter_dimension=1, tiled=True
        ).astype(jnp.float32),
        lax.psum_scatter(
            spread_two.astype(jnp.bfloat16), "col", scatter_dimension=1, tiled=True
        ).astype(jnp.float32),
    )
    row_sums = (
        lax.psum_scatter(
            col_sums[0].astype(jnp.bfloat16), "row", scatter_dimension=0, tiled=True
        ).astype(jnp.float32),
        lax.psum_scatter(
            col_sums[1].astype(jnp.bfloat16), "row", scatter_dimension=0, tiled=True
        ).astype(jnp.float32),
        lax.psum_scatter(
            col_sums[2].astype(jnp.bfloat16), "row", scatter_dimension=0, tiled=True
        ).astype(jnp.float32),
        lax.psum_scatter(
            col_sums[3].astype(jnp.bfloat16), "row", scatter_dimension=0, tiled=True
        ).astype(jnp.float32),
        lax.psum_scatter(
            col_sums[4].astype(jnp.bfloat16), "row", scatter_dimension=0, tiled=True
        ).astype(jnp.float32),
        lax.psum_scatter(
            col_sums[5].astype(jnp.bfloat16), "row", scatter_dimension=0, tiled=True
        ).astype(jnp.float32),
        lax.psum_scatter(
            col_sums[6].astype(jnp.bfloat16), "row", scatter_dimension=0, tiled=True
        ).astype(jnp.float32),
    )
    return (
        block_out,
        block_in_grad,
        row_sums[5][:, 0],
        row_sums[6][:, 0],
        row_sums[0],
        row_sums[1],
        row_sums[2],
        row_sums[3],
        row_sums[4],
        gate_sum,
        up_sum,
        down_sum,
    )


F32 = jnp.float32
BF16 = jnp.bfloat16
MIB = 1024 * 1024
LANES = 128
VMEM_MOST = 60 * MIB
COST_SCALE = 10**6


def cost(microseconds):
    return pl.CostEstimate(flops=int(microseconds * COST_SCALE), bytes_accessed=10**5, transcendentals=0)


def dot_nn(a, b):
    return lax.dot_general(a, b, (((1,), (0,)), ((), ())), preferred_element_type=F32)


def dot_nt(a, b):
    return lax.dot_general(a, b, (((1,), (1,)), ((), ())), preferred_element_type=F32)


def dot_tn(a, b):
    return lax.dot_general(a, b, (((0,), (0,)), ((), ())), preferred_element_type=F32)


def in_vmem():
    return pl.BlockSpec(memory_space=pltpu.VMEM)


def in_smem():
    return pl.BlockSpec(memory_space=pltpu.SMEM)


def in_hbm():
    return pl.BlockSpec(memory_space=pl.ANY)


def behind(kernel, n_in, after):
    if not after:
        return kernel
    return lambda *refs: kernel(*refs[:n_in], *refs[n_in + len(after) :])


def partner(values):
    lane = lax.broadcasted_iota(jnp.int32, values.shape, 1)
    half = HD // 2
    return jnp.where(
        lane % HD < half,
        pltpu.roll(values, LANES - half, 1),
        pltpu.roll(values, half, 1),
    )


def attend_kernel(
    spot_ref, x0, x1, x2, x3, pack_ref, cos_ref, sin_ref,
    attn_ref, q_ref, k_ref, v_ref, lse_ref, w_ref, gain_ref, mixed_ref,
):
    rows = x0.shape[0]
    col, prefix = spot_ref[0], spot_ref[1]
    for part in range(8):
        span = pl.ds(part * LANES, LANES)
        w_ref[span, :] = pack_ref[part, :LANES, :]
        gain_ref[0:1, span] = pack_ref[part, LANES : LANES + 1, :LANES].astype(F32)
        gain_ref[1:2, span] = pack_ref[part, LANES : LANES + 1, LANES : 2 * LANES].astype(F32)
    gain = gain_ref[0:1, :]
    for step, chunk in enumerate((x0, x1, x2, x3)):
        source = lax.rem(col - step + 4, 4)
        x = chunk[...].astype(F32)
        scale = lax.rsqrt(jnp.mean(x * x, axis=1, keepdims=True) + EPS)
        attn_ref[pl.ds(pl.multiple_of(source * rows, rows), rows), :] = (x * scale * gain).astype(BF16)
    for tile in range(4):
        span = pl.ds(tile * rows, rows)
        qkv = dot_nn(attn_ref[span, :], w_ref[...])
        cosine, sine = cos_ref[span, :], sin_ref[span, :]
        for block in range(3):
            v = qkv[:, block * LANES : (block + 1) * LANES]
            y = v * cosine + partner(v) * sine
            if block < 2:
                y = (y * HD ** (-0.5)).astype(BF16)
                q_ref[2 * block, span, :] = y[:, :HD]
                q_ref[2 * block + 1, span, :] = y[:, HD:]
            else:
                y = y.astype(BF16)
                k_ref[0, span, :] = y[:, :HD]
                k_ref[1, span, :] = y[:, HD:]
        v = qkv[:, 3 * LANES :].astype(BF16)
        v_ref[0, span, :] = v[:, :HD]
        v_ref[1, span, :] = v[:, HD:]
    total = 4 * rows
    for tile in range(4):
        span = pl.ds(tile * rows, rows)
        keys = max((tile + 1) * rows, total // 2)
        key_spot = lax.broadcasted_iota(jnp.int32, (rows, keys), 1)
        query_spot = lax.broadcasted_iota(jnp.int32, (rows, keys), 0) + tile * rows
        allowed = (key_spot <= query_spot) | (key_spot < prefix)
        for pair in range(2):
            k, v = k_ref[pair, pl.ds(0, keys), :], v_ref[pair, pl.ds(0, keys), :]
            outs = []
            for head in (2 * pair, 2 * pair + 1):
                scores = jnp.where(allowed, dot_nt(q_ref[head, span, :], k), NEGATIVE)
                highest = jnp.max(scores, axis=1, keepdims=True)
                expo = jnp.exp(scores - highest)
                summed = jnp.sum(expo, axis=1, keepdims=True)
                outs.append(dot_nn(expo.astype(BF16), v) * (1.0 / summed))
                lse_ref[span, head : head + 1] = highest + jnp.log(summed)
            mixed_ref[span, pair * LANES : (pair + 1) * LANES] = jnp.concatenate(outs, axis=1).astype(BF16)


def attend(spots, chunks, pack, cosine, sine, after=()):
    rows = chunks[0].shape[0]
    seq = 4 * rows
    shapes = (
        jax.ShapeDtypeStruct((seq, D), BF16),
        jax.ShapeDtypeStruct((4, seq, HD), BF16),
        jax.ShapeDtypeStruct((2, seq, HD), BF16),
        jax.ShapeDtypeStruct((2, seq, HD), BF16),
        jax.ShapeDtypeStruct((seq, 4), F32),
        jax.ShapeDtypeStruct((D, 512), BF16),
        jax.ShapeDtypeStruct((2, D), F32),
        jax.ShapeDtypeStruct((seq, 256), BF16),
    )
    return pl.pallas_call(
        behind(attend_kernel, 8, after),
        out_shape=shapes,
        in_specs=[in_smem()] + [in_vmem()] * 7 + [in_hbm()] * len(after),
        out_specs=tuple(in_vmem() for _ in shapes),
        compiler_params=pltpu.CompilerParams(vmem_limit_bytes=VMEM_MOST),
        cost_estimate=cost(10),
    )(spots, *chunks, pack, cosine, sine, *after)


def attend_back_kernel(
    spot_ref, grad_ref, mixed_ref, q_ref, k_ref, v_ref, lse_ref, attn_ref, w_ref, cos_ref, sin_ref, gain_ref,
    wgrad_ref, in0, in1, in2, in3, dqkv_ref, dk_ref, dv_ref, dq_ref, mg_ref,
):
    seq = attn_ref.shape[0]
    rows = seq // 4
    prefix = spot_ref[1]
    for tile in range(4):
        span = pl.ds(tile * rows, rows)
        for pair in range(2):
            g = grad_ref[span, pair * LANES : (pair + 1) * LANES]
            mg_ref[2 * pair, span, :] = g[:, :HD]
            mg_ref[2 * pair + 1, span, :] = g[:, HD:]
    dk_ref[...] = jnp.zeros_like(dk_ref)
    dv_ref[...] = jnp.zeros_like(dv_ref)
    for tile in range(4):
        span = pl.ds(tile * rows, rows)
        keys = max((tile + 1) * rows, seq // 2)
        key_spot = lax.broadcasted_iota(jnp.int32, (rows, keys), 1)
        query_spot = lax.broadcasted_iota(jnp.int32, (rows, keys), 0) + tile * rows
        allowed = (key_spot <= query_spot) | (key_spot < prefix)
        for pair in range(2):
            k, v = k_ref[pair, pl.ds(0, keys), :], v_ref[pair, pl.ds(0, keys), :]
            both = grad_ref[span, pair * LANES : (pair + 1) * LANES].astype(F32) * mixed_ref[
                span, pair * LANES : (pair + 1) * LANES
            ].astype(F32)
            outs = []
            for at, head in enumerate((2 * pair, 2 * pair + 1)):
                q, g = q_ref[head, span, :], mg_ref[head, span, :]
                delta = jnp.sum(both[:, at * HD : (at + 1) * HD], axis=1, keepdims=True)
                scores = jnp.where(allowed, dot_nt(q, k), NEGATIVE)
                probs = jnp.exp(scores - lse_ref[span, head : head + 1])
                score_grad = (probs * (dot_nt(g, v) - delta)).astype(BF16)
                dv_ref[pair, pl.ds(0, keys), :] += dot_tn(probs.astype(BF16), g)
                dk_ref[pair, pl.ds(0, keys), :] += dot_tn(score_grad, q)
                outs.append(dot_nn(score_grad, k) * HD ** (-0.5))
            dq_ref[span, pair * LANES : (pair + 1) * LANES] = jnp.concatenate(outs, axis=1)
    for tile in range(4):
        span = pl.ds(tile * rows, rows)
        cosine, sine = cos_ref[span, :], sin_ref[span, :]
        for block in range(3):
            if block < 2:
                g = dq_ref[span, block * LANES : (block + 1) * LANES]
            else:
                g = jnp.concatenate([dk_ref[0, span, :], dk_ref[1, span, :]], axis=1)
            dqkv_ref[span, block * LANES : (block + 1) * LANES] = (g * cosine - partner(g) * sine).astype(BF16)
        dqkv_ref[span, 3 * LANES :] = jnp.concatenate([dv_ref[0, span, :], dv_ref[1, span, :]], axis=1).astype(BF16)
    gain_total = jnp.zeros((1, D), F32)
    for step, out in enumerate((in0, in1, in2, in3)):
        source = lax.rem(spot_ref[0] - step + 4, 4)
        span = pl.ds(pl.multiple_of(source * rows, rows), rows)
        back = dot_nt(dqkv_ref[span, :], w_ref[...])
        out[...] = back.astype(BF16)
        gain_total = gain_total + jnp.sum(back * attn_ref[span, :].astype(F32), axis=0, keepdims=True)
    gain_total = gain_total / gain_ref[0:1, :]
    for part in range(8):
        span = pl.ds(part * LANES, LANES)
        wgrad_ref[part, LANES:, :LANES] = jnp.broadcast_to(gain_total[:, part * LANES : (part + 1) * LANES], (8, LANES)).astype(BF16)
        wgrad_ref[part, LANES:, LANES:] = jnp.zeros((8, 3 * LANES), BF16)
        wgrad_ref[part, :LANES, :] = dot_tn(attn_ref[:, span], dqkv_ref[...]).astype(BF16)


def attend_back(spots, grads, mixed, q, k, v, lse, attn_in, w_qkv, cosine, sine, gain, after=()):
    seq = attn_in.shape[0]
    shapes = (
        jax.ShapeDtypeStruct((8, 136, 512), BF16),
    ) + (jax.ShapeDtypeStruct((seq // 4, D), BF16),) * 4
    return pl.pallas_call(
        behind(attend_back_kernel, 12, after),
        out_shape=shapes,
        in_specs=[in_smem()] + [in_vmem()] * 11 + [in_hbm()] * len(after),
        out_specs=tuple(in_vmem() for _ in shapes),
        scratch_shapes=[
            pltpu.VMEM((seq, 512), BF16),
            pltpu.VMEM((2, seq, HD), F32),
            pltpu.VMEM((2, seq, HD), F32),
            pltpu.VMEM((seq, 256), F32),
            pltpu.VMEM((4, seq, HD), BF16),
        ],
        compiler_params=pltpu.CompilerParams(vmem_limit_bytes=VMEM_MOST),
        cost_estimate=cost(16),
    )(spots, grads, mixed, q, k, v, lse, attn_in, w_qkv, cosine, sine, gain, *after)


def route_kernel(
    spot_ref, mixed_ref, x_ref, pack_ref, gain_ref, ids_ref, order_ref,
    resid_ref, send_ref, gates_ref, kept_ref, wo_ref, wr_ref, wr_wide,
):
    rows = x_ref.shape[0]
    wr_wide[...] = jnp.zeros_like(wr_wide)
    for row in range(8):
        span = pl.ds(row * LANES, LANES)
        for col in range(4):
            wo_ref[span, col * 256 : (col + 1) * 256] = pack_ref[row, col, :LANES, :]
            wr_wide[col * 8 : (col + 1) * 8, span] = pack_ref[row, col, LANES:, :LANES].astype(F32)
    wr_ref[...] = wr_wide[...].astype(BF16)
    resid = x_ref[...].astype(F32)
    for part in range(4):
        resid = resid + dot_nn(mixed_ref[pl.ds(part * rows, rows), :], wo_ref[part * 256 : (part + 1) * 256, :])
    resid_ref[...] = resid
    scale = lax.rsqrt(jnp.mean(resid * resid, axis=1, keepdims=True) + EPS)
    moe_in = (resid * scale * gain_ref[1:2, :]).astype(BF16)
    send_ref[:, :D] = moe_in
    logits = dot_nt(moe_in, wr_ref[...])
    lane = lax.broadcasted_iota(jnp.int32, (rows, LANES), 1)
    chosen = jnp.zeros((rows, LANES), jnp.bool_)
    for choice in range(TOPK):
        chosen = chosen | (ids_ref[:, choice : choice + 1] == lane)
    picked = jnp.where(chosen, logits, NEGATIVE)
    expo = jnp.exp(picked - jnp.max(picked, axis=1, keepdims=True))
    gates = expo / jnp.sum(expo, axis=1, keepdims=True)
    first = lax.broadcasted_iota(jnp.int32, (rows, rows), 0)
    second = lax.broadcasted_iota(jnp.int32, (rows, rows), 1)
    place = (first == order_ref[...]).astype(BF16)
    sooner = dot_nn(place, (second < first).astype(BF16)).astype(BF16)
    sooner = dot_nt(sooner, place).astype(BF16)
    slot = dot_nn(sooner, chosen.astype(BF16))
    kept = (chosen & (slot < CAP)).astype(F32)
    gates_ref[...] = gates
    kept_ref[...] = kept
    send_ref[:, D:] = dot_nn((gates * kept).astype(BF16), relabel(spot_ref[2])).astype(BF16)


def relabel(row):
    first = lax.broadcasted_iota(jnp.int32, (LANES, LANES), 0)
    second = lax.broadcasted_iota(jnp.int32, (LANES, LANES), 1)
    return (first == (second ^ (row * 4))).astype(BF16)


def route(spots, mixed, x, pack, gain, ids, order, after=()):
    rows = x.shape[0]
    shapes = (
        jax.ShapeDtypeStruct((rows, D), F32),
        jax.ShapeDtypeStruct((rows, D + LANES), BF16),
        jax.ShapeDtypeStruct((rows, LANES), F32),
        jax.ShapeDtypeStruct((rows, LANES), F32),
        jax.ShapeDtypeStruct((D, D), BF16),
        jax.ShapeDtypeStruct((LANES, D), BF16),
    )
    return pl.pallas_call(
        behind(route_kernel, 7, after),
        out_shape=shapes,
        in_specs=[in_smem()] + [in_vmem()] * 6 + [in_hbm()] * len(after),
        out_specs=tuple(in_vmem() for _ in shapes),
        scratch_shapes=[pltpu.VMEM((LANES, D), F32)],
        compiler_params=pltpu.CompilerParams(vmem_limit_bytes=VMEM_MOST),
        cost_estimate=cost(2),
    )(spots, mixed, x, pack, gain, ids, order, *after)


def expert_kernel(x_ref, g_ref, *refs):
    weights, refs = refs[:10], refs[10:]
    back_ref, hg_ref, hu_ref, act_ref, out_acc, in_acc, gate_acc, held, sems = refs
    step = pl.program_id(0)
    count = held.shape[1]
    wide = count * LANES

    def fetch(at, slot):
        for k in range(8):

            @pl.when(at == k)
            def _():
                for i in range(2):
                    half = weights[k].at[pl.ds(2 * i, 2)] if k < 6 else weights[2 * k - 6 + i]
                    pltpu.make_async_copy(half, held.at[slot, pl.ds(2 * i, 2)], sems.at[slot, i]).start()

    @pl.when(step == 0)
    def _():
        fetch(step, 0)
        out_acc[...] = jnp.zeros_like(out_acc)
        in_acc[...] = jnp.zeros_like(in_acc)
        gate_acc[...] = jnp.zeros_like(gate_acc)

    now = lax.rem(step, 2)
    for i in range(2):
        pltpu.make_async_copy(weights[6], held.at[now, pl.ds(2 * i, 2)], sems.at[now, i]).wait()
    fetch(step + 1, 1 - now)

    join = lambda kind: jnp.concatenate([held[now, i, kind] for i in range(count)], axis=1)
    wg, wu, wd = join(0), join(1), join(2)
    x = x_ref[:, :D]
    expert = lax.broadcasted_iota(jnp.int32, (LANES, wide), 0)
    column = lax.broadcasted_iota(jnp.int32, (LANES, wide), 1)
    spread = (expert == step * count + column // LANES).astype(BF16)
    gate = dot_nn(x_ref[:, D:], spread)
    hidden_gate = dot_nn(x, wg)
    hidden_up = dot_nn(x, wu)
    act_grad = dot_nn(g_ref[...], wd)
    sigma = 0.5 * jnp.tanh(0.5 * hidden_gate) + 0.5
    swish = hidden_gate * sigma
    active = swish * hidden_up
    gate_acc[...] += dot_nt((active * act_grad).astype(BF16), spread)
    gated = (active * gate).astype(BF16)
    act_ref[...] = gated
    out_acc[...] += dot_nt(gated, wd)
    act_grad = act_grad * gate
    up_grad = (act_grad * swish).astype(BF16)
    gate_grad = (act_grad * hidden_up * (sigma + swish * (1.0 - sigma))).astype(BF16)
    hg_ref[...] = gate_grad
    hu_ref[...] = up_grad
    in_acc[...] += dot_nt(gate_grad, wg) + dot_nt(up_grad, wu)

    @pl.when(step == pl.num_programs(0) - 1)
    def _():
        back_ref[:, :D] = in_acc[...].astype(BF16)
        back_ref[:, D : 2 * D] = out_acc[...].astype(BF16)
        back_ref[:, 2 * D :] = gate_acc[...].astype(BF16)


def experts(x, g, weights, after=()):
    rows = x.shape[0]
    count = 4
    steps = 8
    wide = count * LANES
    hidden = pl.BlockSpec((rows, wide), lambda i: (0, i))
    whole = lambda width: pl.BlockSpec((rows, width), lambda i: (0, 0))
    return pl.pallas_call(
        behind(expert_kernel, 12, after),
        out_shape=(jax.ShapeDtypeStruct((rows, 2 * D + LANES), BF16),)
        + (jax.ShapeDtypeStruct((rows, steps * wide), BF16),) * 3,
        grid_spec=pltpu.PrefetchScalarGridSpec(
            num_scalar_prefetch=0,
            grid=(steps,),
            in_specs=[whole(D + LANES), whole(D)] + [in_hbm()] * (10 + len(after)),
            out_specs=(whole(2 * D + LANES), hidden, hidden, hidden),
            scratch_shapes=[
                pltpu.VMEM((rows, D), F32),
                pltpu.VMEM((rows, D), F32),
                pltpu.VMEM((rows, LANES), F32),
                pltpu.VMEM((2, count, 3, D, LANES), BF16),
                pltpu.SemaphoreType.DMA((2, 2)),
            ],
        ),
        compiler_params=pltpu.CompilerParams(vmem_limit_bytes=VMEM_MOST),
        cost_estimate=cost(21),
    )(x, g, *weights, *after)


def flip_kernel(x0, x1, x2, x3, g0, g1, g2, g3, xt_ref, gt_ref):
    rows = x0.shape[0]
    for at, (x, g) in enumerate(zip((x0, x1, x2, x3), (g0, g1, g2, g3))):
        xt_ref[:, at * rows : (at + 1) * rows] = x[:, :D].T
        gt_ref[:, at * rows : (at + 1) * rows] = g[...].T


def flip(xs, gs, after=()):
    seq = 4 * xs[0].shape[0]
    return pl.pallas_call(
        behind(flip_kernel, 8, after),
        out_shape=(jax.ShapeDtypeStruct((D, seq), BF16),) * 2,
        in_specs=[in_vmem()] * 8 + [in_hbm()] * len(after),
        out_specs=(in_vmem(),) * 2,
        compiler_params=pltpu.CompilerParams(vmem_limit_bytes=VMEM_MOST),
        cost_estimate=cost(2),
    )(*xs, *gs, *after)


def expert_wgrad_kernel(places, added, late, xt_ref, gt_ref, *refs):
    hidden, refs = refs[:12], refs[12:]
    count = len(places)
    n_extra = len({place[0] for place in added if place}) + len(late)
    plain = [k for k, place in enumerate(added) if not place]
    extras, refs = refs[:n_extra], refs[n_extra:]
    n_out = len({which for which, _ in places})
    outs, refs = refs[:n_out], refs[n_out:]
    held, out_sems, got, in_sems = refs
    step = pl.program_id(0)
    now = lax.rem(step, 2)

    def fetch(at, slot):
        for k, place in enumerate(added):
            if not place:
                continue
            which, half = place

            @pl.when(at == k)
            def _():
                pltpu.make_async_copy(extras[which].at[half], got.at[slot, 0], in_sems.at[slot, 0]).start()
                if k in late:
                    pltpu.make_async_copy(extras[late[k]].at[0], got.at[slot, 1], in_sems.at[slot, 1]).start()

    if added:

        @pl.when(step == 0)
        def _():
            fetch(step, 0)

        fetch(step + 1, 1 - now)

    def sent(slot):
        pltpu.make_async_copy(held.at[slot], outs[0].at[0], out_sems.at[slot]).wait()

    @pl.when(step >= 2)
    def _():
        sent(now)

    first = functools.reduce(jnp.logical_and, [step != k for k in plain], step >= 0)
    second = functools.reduce(jnp.logical_or, [step == k for k in late], False)
    if added:

        @pl.when(functools.reduce(jnp.logical_and, [step != k for k in plain], step >= 0))
        def _():
            pltpu.make_async_copy(extras[0].at[0], got.at[now, 0], in_sems.at[now, 0]).wait()

        for k in late:

            @pl.when(step == k)
            def _():
                pltpu.make_async_copy(extras[0].at[0], got.at[now, 1], in_sems.at[now, 1]).wait()


    for kind, left in enumerate((xt_ref, xt_ref, gt_ref)):
        joined = jnp.concatenate([part[...] for part in hidden[kind * 4 : kind * 4 + 4]], axis=0)
        product = dot_nn(left[...], joined)
        for i in range(2):
            piece = product[:, i * LANES : (i + 1) * LANES]
            if plain:
                piece = piece + jnp.where(first, got[now, 0, i, kind].astype(F32), 0.0)
            elif added:
                piece = piece + got[now, 0, i, kind].astype(F32)
            if late:
                piece = piece + jnp.where(second, got[now, 1, i, kind].astype(F32), 0.0)
            held[now, i, kind] = piece.astype(BF16)

    for k, (which, half) in enumerate(places):

        @pl.when(step == k)
        def _():
            pltpu.make_async_copy(held.at[now], outs[which].at[half], out_sems.at[now]).start()

    @pl.when(step == count - 1)
    def _():
        sent(now)
        if count > 1:
            sent(1 - now)


def expert_wgrads(flipped, hidden, entries, places, extras=(), added=(), late=None, after=(), into=None, halves=None):
    rows = hidden[0][0].shape[0]
    wide = 2 * LANES
    seq = flipped[0].shape[1]
    count = len(entries)

    def entry(i):
        place = entries[0]
        for k in range(1, count):
            place = jnp.where(i == k, entries[k], place)
        return (0, place)

    lane = pl.BlockSpec((rows, wide), entry)
    whole = pl.BlockSpec((D, seq), lambda i: (0, 0))
    kernel = functools.partial(expert_wgrad_kernel, places, added, late or {})
    if into is not None:
        after = [into, *after]
    sizes = halves or [sum(which == o for which, _ in places) for o in range(max(which for which, _ in places) + 1)]
    return pl.pallas_call(
        behind(kernel, 14 + len(extras), after),
        grid=(count,),
        out_shape=tuple(jax.ShapeDtypeStruct((size, 2, 3, D, LANES), BF16) for size in sizes),
        in_specs=[whole] * 2 + [lane] * 12 + [in_hbm()] * (len(extras) + len(after)),
        out_specs=(in_hbm(),) * len(sizes),
        scratch_shapes=[
            pltpu.VMEM((2, 2, 3, D, LANES), BF16),
            pltpu.SemaphoreType.DMA((2,)),
            pltpu.VMEM((2, 2, 2, 3, D, LANES), BF16),
            pltpu.SemaphoreType.DMA((2, 2)),
        ],
        compiler_params=pltpu.CompilerParams(vmem_limit_bytes=VMEM_MOST),
        cost_estimate=cost(2.2 * count),
        input_output_aliases={} if into is None else {14 + len(extras): 0},
    )(*flipped, *hidden[0], *hidden[1], *hidden[2], *extras, *after)


def expert_total_kernel(own_ref, xa_ref, xb_ref, ya_ref, yb_ref, gate_ref, up_ref, down_ref):
    for kind, out in enumerate((gate_ref, up_ref, down_ref)):
        for half, (x_ref, y_ref) in enumerate(((xa_ref, ya_ref), (xb_ref, yb_ref))):
            out[half, 0] = (
                own_ref[half, 0, kind].astype(F32) + x_ref[0, 0, kind].astype(F32) + y_ref[0, 0, kind].astype(F32)
            )


def expert_total(after, own, *parts):
    block = pl.BlockSpec((2, 1, 3, D, LANES), lambda i: (0, i, 0, 0, 0))
    part = pl.BlockSpec((1, 1, 3, D, LANES), lambda i: (0, i, 0, 0, 0))
    out = pl.BlockSpec((2, 1, D, LANES), lambda i: (0, i, 0, 0))
    sums = pl.pallas_call(
        behind(expert_total_kernel, 5, after),
        grid=(2,),
        out_shape=(jax.ShapeDtypeStruct((2, 2, D, LANES), F32),) * 3,
        in_specs=[block] + [part] * 4 + [in_hbm()] * len(after),
        out_specs=(out,) * 3,
        compiler_params=pltpu.CompilerParams(vmem_limit_bytes=VMEM_MOST),
        cost_estimate=cost(5),
    )(own, *parts, *after)
    return [total.reshape(4, D, LANES) for total in sums]


def halves_kernel(x_ref, y_ref, low_ref, high_ref):
    low_ref[...] = y_ref[...]
    high_ref[...] = x_ref[...]


def halves(from_x, from_y, after):
    half = jax.ShapeDtypeStruct((2, 3, D, LANES), BF16)
    first = pl.BlockSpec((1, 1, D, LANES), lambda i, j: (i, j, 0, 0))
    second = pl.BlockSpec((1, 1, D, LANES), lambda i, j: (i + 2, j, 0, 0))
    return pl.pallas_call(
        behind(halves_kernel, 2, after),
        grid=(2, 3),
        out_shape=(half, half),
        in_specs=[second, first] + [in_hbm()] * len(after),
        out_specs=(first,) * 2,
        compiler_params=pltpu.CompilerParams(vmem_limit_bytes=VMEM_MOST),
        cost_estimate=cost(3),
    )(from_x, from_y, *after)


def turn_kernel(
    spot_ref, came_ref, back_ref, gates_ref, kept_ref, resid_ref, gain_ref, g_ref, wr_ref, wo_ref, send_ref,
    out_ref, resid_grad_ref, branch_ref, mixed_grad_ref, small_ref,
):
    rows = resid_ref.shape[0]
    gates = gates_ref[...]
    both = lambda span: came_ref[:, span].astype(F32) + back_ref[:, span].astype(F32)
    out_ref[...] = resid_ref[...] + both(slice(D, 2 * D))
    gate_grad = dot_nn(both(slice(2 * D, None)).astype(BF16), relabel(spot_ref[2])) * kept_ref[...]
    logit_grad = gates * (gate_grad - jnp.sum(gates * gate_grad, axis=1, keepdims=True))
    logit_grad = logit_grad.astype(BF16)
    moe_grad = both(slice(0, D)) + dot_nn(logit_grad, wr_ref[...])
    resid = resid_ref[...]
    scale = lax.rsqrt(jnp.mean(resid * resid, axis=1, keepdims=True) + EPS)
    normed = resid * scale
    small_ref[LANES:, :] = jnp.broadcast_to(jnp.sum(moe_grad * normed, axis=0, keepdims=True), (8, D))
    small_ref[:LANES, :] = dot_tn(logit_grad, send_ref[:, :D])
    inner = moe_grad * gain_ref[1:2, :]
    grad = g_ref[...].astype(F32) + scale * (inner - normed * jnp.mean(inner * normed, axis=1, keepdims=True))
    resid_grad_ref[...] = grad
    branch = grad.astype(BF16)
    branch_ref[...] = branch
    for part in range(4):
        mixed_grad_ref[pl.ds(part * rows, rows), :] = dot_nt(
            branch, wo_ref[part * 256 : (part + 1) * 256, :]
        ).astype(BF16)


def turn(spots, came, back, gates, kept, resid, gain, g, wr, wo, send, after=()):
    rows = resid.shape[0]
    shapes = (
        jax.ShapeDtypeStruct((rows, D), F32),
        jax.ShapeDtypeStruct((rows, D), F32),
        jax.ShapeDtypeStruct((rows, D), BF16),
        jax.ShapeDtypeStruct((4 * rows, 256), BF16),
        jax.ShapeDtypeStruct((LANES + 8, D), F32),
    )
    return pl.pallas_call(
        behind(turn_kernel, 11, after),
        out_shape=shapes,
        in_specs=[in_smem()] + [in_vmem()] * 10 + [in_hbm()] * len(after),
        out_specs=tuple(in_vmem() for _ in shapes),
        compiler_params=pltpu.CompilerParams(vmem_limit_bytes=VMEM_MOST),
        cost_estimate=cost(2),
    )(spots, came, back, gates, kept, resid, gain, g, wr, wo, send, *after)


def out_wgrad_kernel(mixed_ref, branch_ref, small_ref, pack_ref):
    rows = branch_ref.shape[0]
    for part in range(4):
        product = dot_tn(mixed_ref[pl.ds(part * rows, rows), :], branch_ref[...]).astype(BF16)
        pack_ref[2 * part, :LANES, :] = product[:LANES]
        pack_ref[2 * part + 1, :LANES, :] = product[LANES:]
    for row in range(8):
        span = pl.ds(row * LANES, LANES)
        for col in range(4):
            pack_ref[row, LANES:, col * 256 : col * 256 + LANES] = small_ref[col * 8 : col * 8 + 8, span].astype(BF16)
            pack_ref[row, LANES:, col * 256 + LANES : col * 256 + 256] = small_ref[LANES:, span].astype(BF16)


def out_wgrad(mixed, branch, small, after=()):
    return pl.pallas_call(
        behind(out_wgrad_kernel, 3, after),
        out_shape=jax.ShapeDtypeStruct((8, LANES + 8, D), BF16),
        in_specs=[in_vmem()] * 3 + [in_hbm()] * len(after),
        out_specs=in_vmem(),
        compiler_params=pltpu.CompilerParams(vmem_limit_bytes=VMEM_MOST),
        cost_estimate=cost(3),
    )(mixed, branch, small, *after)


def unpack_kernel(sum_ref, query_ref, key_ref, value_ref, gain_ref):
    query_ref[...] = sum_ref[:LANES, :256].astype(F32)
    key_ref[...] = sum_ref[:LANES, 256:384].astype(F32)
    value_ref[...] = sum_ref[:LANES, 384:].astype(F32)
    gain_ref[...] = sum_ref[LANES:, :LANES].astype(F32)


def unpack(sums, after):
    return pl.pallas_call(
        behind(unpack_kernel, 1, after),
        out_shape=tuple(jax.ShapeDtypeStruct(shape, F32) for shape in ((LANES, 256), (LANES, LANES), (LANES, LANES), (8, LANES))),
        in_specs=[in_vmem()] + [in_hbm()] * len(after),
        out_specs=(in_vmem(),) * 4,
        compiler_params=pltpu.CompilerParams(vmem_limit_bytes=VMEM_MOST),
        cost_estimate=cost(2),
    )(sums, *after)


def ring_gather(value, n_col):
    steps = [(i, (i + 1) % n_col) for i in range(n_col)]
    chunks = [value]
    for _ in range(n_col - 1):
        chunks.append(lax.ppermute(chunks[-1], "col", steps))
    return chunks


def ring_sum(parts, n_col):
    steps = [(i, (i + 1) % n_col) for i in range(n_col)]
    total = parts[1]
    for part in parts[2:] + parts[:1]:
        total = lax.ppermute(total, "col", steps).astype(F32) + part.astype(F32)
        if part is not parts[0]:
            total = total.astype(BF16)
    return total


def shift_all(parts, n_col):
    return [
        lax.ppermute(part, "col", [(i, (i + s) % n_col) for i in range(n_col)]) if s else part
        for s, part in enumerate(parts)
    ]


def hold(value, *until):
    return lax.optimization_barrier((value, *until))[0]


CORE, ACROSS_X, ACROSS_Y = 1, 2, 4


def swap(value, mask):
    return lax.ppermute(value, "row", [(i, i ^ mask) for i in range(8)])


def fast(
    block_in,
    attn_gain,
    moe_gain,
    w_query,
    w_key,
    w_value,
    w_out,
    w_router,
    w_gate,
    w_up,
    w_down,
    expert_ids,
    fill_order,
    prefix_len,
    out_grad,
):
    rows = block_in.shape[0]
    n_col = lax.axis_size("col")
    col = lax.axis_index("col")
    row = lax.axis_index("row")
    seq = rows * n_col
    spots = jnp.stack([col.astype(jnp.int32), prefix_len[0], row.astype(jnp.int32)])
    gains = jnp.concatenate([attn_gain, moe_gain, jnp.zeros((256,), BF16)])[None]
    pack_qkv = jnp.concatenate(
        [jnp.concatenate([w_query, w_key, w_value], axis=1), gains, jnp.zeros((7, 512), BF16)], axis=0
    )
    pack_out = jnp.concatenate([w_out, jnp.pad(w_router.T, ((0, 0), (0, 256 - LANES)))], axis=0)
    pack_out = lax.all_gather(pack_out, "col", axis=0)
    pack_qkv = lax.all_gather(pack_qkv, "row", axis=0)
    pack_out = lax.all_gather(pack_out, "row", axis=0)
    cosine, sine = rope_tables(0, seq)
    cosine = jnp.tile(cosine, (1, 4))
    sine = jnp.concatenate([-sine, sine, -sine, sine], axis=1)
    ring = [(i, (i + 1) % n_col) for i in range(n_col)]
    x_chunks = [block_in, lax.ppermute(block_in, "col", ring)]
    x_chunks += ring_gather(hold(x_chunks[1], cosine, sine), n_col)[1:3]
    own = jnp.stack([w_gate, w_up, w_down], axis=1)
    from_x, from_y, other = swap(own, ACROSS_X), swap(own, ACROSS_Y), swap(own, CORE)

    attn_in, q, k, v, lse, w_qkv, gains, mixed_all = attend(spots, x_chunks, pack_qkv, cosine, sine, [other])
    g_chunks = [out_grad, lax.ppermute(hold(out_grad, x_chunks[3]), "col", ring)]
    g_chunks += ring_gather(hold(g_chunks[1], attn_in), n_col)[1:3]
    mixed_own = lax.all_to_all(mixed_all, "col", split_axis=0, concat_axis=0, tiled=True)
    low, high = halves(from_x, from_y, [g_chunks[2]])
    resid, send, gates, kept, wo, wr = route(
        spots, mixed_own, block_in, pack_out, gains, expert_ids, fill_order, [low]
    )
    far = swap(low, ACROSS_X), swap(high, ACROSS_Y)
    weights = [own, other, from_x, swap(from_x, CORE), from_y, swap(from_y, CORE), *far]

    send_chunks = [send, *ring_gather(hold(send, g_chunks[3]), n_col)[1:]]
    weights += [swap(hold(part, send_chunks[2]), CORE) for part in far]
    results, backs, back = {}, [], None
    steps = [(i, (i + 1) % n_col) for i in range(n_col)]
    order = (1, 2, 3, 0)
    for at, chunk in enumerate(order):
        after = [results[order[at - 1]][1]] if at else [send_chunks[3]]
        if at >= 2:
            after.append(backs[at - 2])
        if at == 2:
            flipped = flip(send_chunks, g_chunks, [results[2][1]])
            after.append(flipped[0])
        results[chunk] = experts(send_chunks[chunk], g_chunks[chunk], weights, after)
        if chunk:
            part = results[chunk][0]
            back = part if back is None else (back.astype(F32) + part.astype(F32)).astype(BF16)
            back = lax.ppermute(back, "col", steps)
            backs.append(back)
    results = [results[chunk] for chunk in range(n_col)]

    hidden = [[result[kind] for result in results] for kind in (1, 2, 3)]
    wgrads = functools.partial(expert_wgrads, flipped, hidden)
    (p7,) = wgrads((14, 15), ((0, 0), (0, 1)), after=[backs[2]])
    r7 = swap(p7, CORE)
    (p5,) = wgrads((10, 11), ((0, 2), (0, 3)), after=[p7], halves=[4])
    (p53,) = wgrads((6, 7), ((0, 0), (0, 1)), after=[r7], into=p5, halves=[4])
    r53 = swap(p53, CORE)
    q6 = wgrads((12, 13), ((0, 0), (1, 0)), [r7], ((0, 0), (0, 1)), after=[p53])
    far_x, far_y = swap(q6[0], ACROSS_X), swap(q6[1], ACROSS_Y)
    block_out, resid_grad, branch, mixed_grad, small = turn(
        spots, backs[2], results[0][0], gates, kept, resid, gains, out_grad, wr, wo, send, q6[:1]
    )
    mixed_grads = lax.all_to_all(mixed_grad, "col", split_axis=0, concat_axis=0, tiled=True)
    pack = out_wgrad(mixed_own, branch, small)
    out_sum = lax.psum_scatter(pack, "row", scatter_dimension=0, tiled=True)
    q2a, q4b, q2b, q4a, p1 = wgrads(
        (4, 9, 5, 8, 2, 3),
        ((0, 0), (1, 0), (2, 0), (3, 0), (4, 0), (4, 1)),
        [r53, far_y, far_x],
        ((0, 0), (0, 3), (0, 1), (0, 2), None, None),
        {2: 1, 3: 2},
        [pack, mixed_grads],
    )
    x2a, y4b = swap(q2a, ACROSS_X), swap(q4b, ACROSS_Y)
    r1 = swap(p1, CORE)
    x2b, y4a = swap(q2b, ACROSS_X), swap(q4a, ACROSS_Y)
    qkv_wgrad, *back_parts = attend_back(
        spots, mixed_grads, mixed_all, q, k, v, lse, attn_in, w_qkv, cosine, sine, gains, [q2b]
    )
    (q0,) = wgrads((0, 1), ((0, 0), (0, 1)), [r1], ((0, 0), (0, 1)), after=[qkv_wgrad])
    moving = lax.ppermute(back_parts[1], "col", steps)
    moving = (hold(moving, x2a, y4b).astype(F32) + back_parts[2].astype(F32)).astype(BF16)
    moving = lax.ppermute(moving, "col", steps)
    moving = (hold(moving, q0).astype(F32) + back_parts[3].astype(F32)).astype(BF16)
    third_step = moving
    last_step = lax.ppermute(moving, "col", steps)
    attn_grad = last_step.astype(F32) + back_parts[0].astype(F32)
    x_rows = block_in.astype(F32)
    scale = lax.rsqrt(jnp.mean(x_rows * x_rows, axis=1, keepdims=True) + EPS)
    normed = x_rows * scale
    inner = attn_grad * gains[:1]
    block_in_grad = resid_grad + scale * (inner - normed * jnp.mean(inner * normed, axis=1, keepdims=True))

    qkv_sum = lax.psum_scatter(qkv_wgrad, "row", scatter_dimension=0, tiled=True)[0]
    *qkv_sums, gain_one = unpack(qkv_sum, [last_step])
    out_sum = lax.psum_scatter(hold(out_sum, q2b), "col", scatter_dimension=2, tiled=True)[0].astype(F32)
    gain_one_sum = functools.reduce(jnp.add, shift_all([gain_one] * n_col, n_col))
    gate_sum, up_sum, down_sum = expert_total([block_in_grad, gain_one_sum], q0, x2a, x2b, y4a, y4b)
    return (
        block_out,
        block_in_grad,
        gain_one_sum[0],
        out_sum[LANES, LANES:],
        *qkv_sums,
        out_sum[:LANES],
        out_sum[LANES:, :LANES].T,
        gate_sum,
        up_sum,
        down_sum,
    )


def takes_fast(mesh):
    n_row, n_col = mesh.shape["row"], mesh.shape["col"]
    return n_row == 8 and n_col == 4


def solution(mesh):
    in_specs = (
        P(("row", "col"), None),
        P("row"),
        P("row"),
        P("row", "col"),
        P("row", "col"),
        P("row", "col"),
        P("row", "col"),
        P("row", "col"),
        P("row", None, "col"),
        P("row", None, "col"),
        P("row", None, "col"),
        P(("row", "col"), None),
        P(("row", "col"), None),
        P("row"),
        P(("row", "col"), None),
    )
    out_specs = (
        P(("row", "col"), None),
        P(("row", "col"), None),
        P("row"),
        P("row"),
        P("row", "col"),
        P("row", "col"),
        P("row", "col"),
        P("row", "col"),
        P("row", "col"),
        P("row", None, "col"),
        P("row", None, "col"),
        P("row", None, "col"),
    )
    local = fast if takes_fast(mesh) else general
    return jax.shard_map(local, mesh=mesh, in_specs=in_specs, out_specs=out_specs, check_vma=False)
```
